32 devices in a mesh: seq: 8 (over z, x), exp: 4 (over y, core).
Axes of the slice: x: 2, y: 2, z: 4, core: 2. Of those that a mesh axis runs over, the one named last changes fastest.
Arguments:
- stream: bfloat16 [4096, 2048], P(('seq', 'exp')), may hold values from -6 to 6
- moe_gain: float32 [2048], replicated, may hold values from 0.1 to 1.9
- expert_ids: int32 [4096, 10], P(('seq', 'exp')), may hold values from 0 to 63, all different within a row; in each aligned block of 128 rows (0 to 127, 128 to 255, ...) at most 24 rows name the same one
- expert_weights: float32 [4096, 10], P(('seq', 'exp')), may hold values from 0.02 to 0.3
- gate_up_weight: bfloat16 [64, 2048, 1024], P(('seq', 'exp')), may hold values from -0.125 to 0.125
- down: bfloat16 [64, 512, 2048], P(('seq', 'exp')), may hold values from -0.25 to 0.25
- mixer_gain: float32 [2048], replicated, may hold values from 0.1 to 1.9
- qkv_weight: bfloat16 [3, 2048, 4096], P(None, None, 'exp'), may hold values from -0.125 to 0.125
- decay_log: float32 [4096, 32], P('seq', 'exp'), may hold values from -2 to 0
- write_rate: float32 [4096, 32], P('seq', 'exp'), may hold values from 0 to 1
Outputs:
- mixed: bfloat16 [4096, 2048], P(('seq', 'exp'))
- core: float32 [4096, 4096], P('seq', 'exp')
The draws below stay inside these ranges and needn't reach their ends.
Inputs may be any that keep to these rules, and one draw needn't show every extreme that they name: `expert_ids`: each token names 10 different experts. Among the 128 tokens of one device at most 24 name the same expert, and in every draw some expert is named by exactly 24 tokens of some device.
All inputs are finite; a program needn't handle non-finite values.
Results may differ from the reference program's by a relative error of at most 0.0081.
Values may be sent and summed in bfloat16 or wider, within the bound.
No kernel may reach another device: no remote copies, remote signals or barrier semaphores. Data moves between devices by JAX's collectives and lax.ppermute only.
A program may use at most 128 MiB of HBM per device.

```python
import math
import jax
import jax.numpy as jnp
import numpy as np
from jax import lax

D = 2048
FFE = 512
TOPK = 10
HEADS = 32
DK = 128
TOK_DEV = 128
EXPERTS = 64
CAP = 24
TOKENS = 4096
N_SEQ = 8
N_EXP = 4


def head_speed(key, share):
    return jax.random.uniform(jax.random.fold_in(key, 101), (HEADS,)) < share


def draw_decay_log(key, part):
    share = 0.5
    fast = head_speed(key, share)
    keys = jax.random.split(jax.random.fold_in(key, 202), 6)
    block_factor = jnp.exp(jax.random.uniform(keys[0], (TOKENS // TOK_DEV, HEADS), minval=math.log(0.6), maxval=math.log(1.6)))
    block_factor = jnp.repeat(block_factor, TOK_DEV, axis=0, total_repeat_length=TOKENS)
    rough = jax.random.uniform(keys[1], (TOKENS, HEADS), minval=0.5, maxval=1.5)
    fast_rate = jax.random.uniform(keys[2], (HEADS,), minval=1.0 / 45.0, maxval=1.0 / 35.0)
    slow_rate = jax.random.uniform(keys[3], (HEADS,), minval=0.05, maxval=0.2) / TOKENS
    delta_step_size = jnp.where(fast, fast_rate, slow_rate)[None, :] * block_factor * rough
    bucket_number = jax.random.randint(keys[4], (2, HEADS), 0, TOKENS)
    kept_indicator = jax.random.uniform(keys[5], (2, HEADS), minval=0.5, maxval=0.8)
    element_offsets = jnp.arange(TOKENS, dtype=jnp.int32)[:, None]
    element_batch = jnp.where(element_offsets == bucket_number[0][None, :], jnp.log(kept_indicator[0])[None, :], 0.0)
    element_batch = element_batch + jnp.where(element_offsets == bucket_number[1][None, :], jnp.log(kept_indicator[1])[None, :], 0.0)
    return (element_batch - delta_step_size).astype(jnp.float32)


def draw_write_rate(key, part):
    share = 0.5
    fast = head_speed(key, share)
    keys = jax.random.split(jax.random.fold_in(key, 404), 3)
    fast_level = jax.random.uniform(keys[0], (HEADS,), minval=0.2, maxval=0.9)
    slow_level = jax.random.uniform(keys[1], (HEADS,), minval=0.3, maxval=1.0) * DK / TOKENS
    rough = jax.random.uniform(keys[2], (TOKENS, HEADS), minval=0.7, maxval=1.0)
    return (jnp.where(fast, fast_level, slow_level)[None, :] * rough).astype(jnp.float32)


def level_of(stream_key, extent, pieces, smallest, largest):
    level = 1.0
    for dim, shards_of in pieces:
        steps = jax.random.uniform(jax.random.fold_in(jax.random.fold_in(stream_key, 6), dim), (shards_of,), jnp.float32, smallest / len(pieces), largest / len(pieces))
        level = level * jnp.repeat(jnp.exp(steps), extent[dim] // shards_of).reshape((-1,) + (1,) * (len(extent) - 1 - dim))
    return level


def deal_out(own_key, own, number, rows, count, top, reach, lean):
    sequence = jax.random.permutation(own_key, count)
    packed, usual = shares(count, rows * top, reach, lean, True), shares(count, rows * top, reach, lean, False)
    places = jnp.arange(count)

    def named(sizes, turn):
        used = int((sizes > 0).sum())
        fixed = max(1, used // 4)
        shifted = fixed + (places - fixed + turn * (used - fixed)) % max(1, count - fixed)
        return jnp.zeros((count,), jnp.int32).at[sequence[jnp.where(places < fixed, places, shifted)]].set(jnp.asarray(sizes, jnp.int32))

    sizes = jnp.where(number % 4 == 0, named(packed, number // 4), named(usual, number - number // 4 - 1))
    mixed = jax.random.permutation(jax.random.fold_in(own, 3), count)
    source_of, taker = mixed[0:count // 2 * 2:2], mixed[1:count // 2 * 2:2]
    margin = jnp.minimum(sizes[source_of] - 1, reach - sizes[taker]) // 2
    margin = jnp.where((source_of == sequence[0]) | (taker == sequence[0]) | (sizes[taker] == 0), 0, jnp.maximum(margin, 0))
    shifted = jax.random.randint(jax.random.fold_in(own, 4), (count // 2,), 0, 1 << 20) % (margin + 1)
    sizes = sizes.at[source_of].add(-shifted).at[taker].add(shifted)
    members = jnp.searchsorted(jnp.cumsum(sizes), jnp.arange(rows * top), side="right").astype(jnp.int32)
    table = members.reshape(top, rows).T
    table = table[jax.random.permutation(jax.random.fold_in(own, 1), rows)]
    turn = jax.random.randint(jax.random.fold_in(own, 2), (rows, 1), 0, top)
    return jnp.take_along_axis(table, (jnp.arange(top)[None, :] + turn) % top, axis=1)


def shares(count, total, bound, skew, full):
    loads = [(1 << 20) // math.isqrt(grade ** skew) + 1 for grade in range(1, count + 1)]
    largest = bound if full else min(bound, max(-(-total // count), total * loads[0] // sum(loads)))
    least = 1 if total - largest >= count - 1 else 0
    holding, surplus = [largest] + [least] * (count - 1), total - largest - least * (count - 1)
    while surplus > 0:
        candidates = [i for i in range(1, count) if holding[i] < largest] or [i for i in range(1, count) if holding[i] < bound]
        pool, remaining = sum([loads[i] for i in candidates]), surplus
        for i in candidates:
            extra = min(bound - holding[i], max(1, remaining * loads[i] // pool), surplus)
            holding[i] = holding[i] + extra
            surplus = surplus - extra
    return np.array(holding)


def normal_values(rng, extent, deviation, reach, cuts=(), held_as=jnp.bfloat16):
    entries = deviation * jax.random.normal(rng, extent, jnp.float32)
    if cuts:
        entries = entries * level_of(rng, extent, cuts, -0.22, 0.18)
    return jnp.clip(entries, -reach, reach).astype(held_as)


def setup_inputs(seed: int = 0) -> dict:
    key_list = jax.random.split(jax.random.key(seed), 11)
    stream = normal_values(key_list[0], (TOKENS, D), 1.0, 6.0, ((0, 32),))
    moe_gain = jnp.clip(1.0 + 0.18 * jax.random.normal(key_list[1], (D,), jnp.float32), 0.1, 1.9)
    expert_ids_keys = jax.random.split(jax.random.fold_in(key_list[2], 1), TOKENS // TOK_DEV)
    expert_ids_turns = jax.random.permutation(jax.random.fold_in(key_list[2], 3), TOKENS // TOK_DEV)
    expert_ids = jax.vmap(lambda own, number: deal_out(jax.random.fold_in(key_list[2], 2), own, number, TOK_DEV, EXPERTS, TOPK, CAP, 2))(expert_ids_keys, expert_ids_turns).reshape((TOKENS, TOPK))
    expert_weights = jnp.clip(0.02 + 0.28 * jax.random.uniform(key_list[3], (TOKENS, TOPK), jnp.float32) ** level_of(key_list[3], (TOKENS, TOPK), ((0, 32),), -0.2, 0.2), 0.02, 0.3)
    gate_up_weight = normal_values(key_list[4], (EXPERTS, D, 2 * FFE), D ** -0.5, 0.125, ((0, 32),))
    down = normal_values(key_list[5], (EXPERTS, FFE, D), FFE ** -0.5, 0.25, ((0, 32),))
    mixer_gain = jnp.clip(1.0 + 0.18 * jax.random.normal(key_list[6], (D,), jnp.float32), 0.1, 1.9)
    qkv_weight = normal_values(key_list[7], (3, D, HEADS * DK), D ** -0.5, 0.125, ((2, 4),))
    decay_log = draw_decay_log(jax.random.fold_in(key_list[10], 71), 0)
    write_rate = draw_write_rate(jax.random.fold_in(key_list[10], 71), 0)
    return dict(stream=stream, moe_gain=moe_gain, expert_ids=expert_ids, expert_weights=expert_weights, gate_up_weight=gate_up_weight, down=down, mixer_gain=mixer_gain, qkv_weight=qkv_weight, decay_log=decay_log, write_rate=write_rate)


def rms_scale(values, gain):
    wide = values.astype(jnp.float32)
    return wide * lax.rsqrt(lax.optimization_barrier(jnp.mean(wide * wide, axis=-1, keepdims=True)) + 1e-06) * gain

def unit_rows(values):
    return values * lax.rsqrt(lax.optimization_barrier(jnp.sum(values * values, axis=-1, keepdims=True)) + 1e-06)

def reference(stream, moe_gain, expert_ids, expert_weights, gate_up_weight, down, mixer_gain, qkv_weight, decay_log, write_rate):
    normed = rms_scale(stream, moe_gain).astype(jnp.bfloat16)
    flat_ids = expert_ids.reshape(-1)
    flat_weights = expert_weights.reshape(-1)
    total = flat_ids.shape[0]
    most = CAP * N_SEQ * N_EXP
    order = jnp.arange(total, dtype=jnp.int32)

    def single_specialist(accum, expert):
        match = flat_ids == expert
        position = jnp.cumsum(match.astype(jnp.int32)) - 1
        target = jnp.where(match, position, most)
        picked = jnp.zeros((most,), jnp.int32).at[target].set(order, mode='drop')
        live = jnp.arange(most, dtype=jnp.int32) < jnp.sum(match.astype(jnp.int32))
        rows = normed[picked // TOPK].astype(jnp.float32)
        both = jnp.dot(rows, gate_up_weight[expert].astype(jnp.float32))
        hidden = (jax.nn.silu(both[:, :FFE]) * both[:, FFE:]).astype(jnp.bfloat16)
        hidden = lax.optimization_barrier(hidden).astype(jnp.float32)
        result = jnp.dot(hidden, down[expert].astype(jnp.float32)).astype(jnp.bfloat16)
        result = lax.optimization_barrier(result).astype(jnp.float32)
        scale = jnp.where(live, flat_weights[picked], 0.0)
        accum = accum.at[picked // TOPK].add(result * scale[:, None])
        return (accum, None)
    moe, _ = lax.scan(single_specialist, jnp.zeros((TOKENS, D), jnp.float32), jnp.arange(EXPERTS, dtype=jnp.int32))
    mixed = (stream.astype(jnp.float32) + moe).astype(jnp.bfloat16)
    normed_mix = rms_scale(mixed, mixer_gain).astype(jnp.bfloat16)
    normed_mix = lax.optimization_barrier(normed_mix).astype(jnp.float32)
    query = unit_rows(jnp.dot(normed_mix, qkv_weight[0].astype(jnp.float32)).reshape(TOKENS, HEADS, DK))
    key = unit_rows(jnp.dot(normed_mix, qkv_weight[1].astype(jnp.float32)).reshape(TOKENS, HEADS, DK))
    value = jnp.dot(normed_mix, qkv_weight[2].astype(jnp.float32)).reshape(TOKENS, HEADS, DK)
    highest = lax.Precision.HIGHEST

    def advance(state, inputs):
        query_t, key_t, value_t, decay_t, learning_speed_now = inputs
        recall = jnp.einsum('hd,hde->he', key_t, state, precision=highest)
        state = jnp.exp(decay_t)[:, None, None] * (state - learning_speed_now[:, None, None] * key_t[:, :, None] * recall[:, None, :])
        state = state + learning_speed_now[:, None, None] * key_t[:, :, None] * value_t[:, None, :]
        return (state, jnp.einsum('hd,hde->he', query_t, state, precision=highest))
    start = jnp.zeros((HEADS, DK, DK), jnp.float32)
    _, outputs = lax.scan(advance, start, (query, key, value, decay_log, write_rate))
    return (mixed, outputs.reshape(TOKENS, HEADS * DK))
```

```python
from functools import partial

import jax
import jax.numpy as jnp
from jax import lax
from jax.experimental import pallas as pl
from jax.experimental.pallas import tpu as pltpu
from jax.sharding import PartitionSpec as P

CH = 128
VMEM_LIMIT = 56 * 1024 * 1024
BF = jnp.bfloat16
F32 = jnp.float32


def rms_scale(values, gain):
    wide = values.astype(F32)
    return wide * lax.rsqrt(jnp.mean(wide * wide, axis=-1, keepdims=True) + 1e-06) * gain


def dot(a, b):
    return jnp.dot(a, b, preferred_element_type=F32)


def split(a):
    high = a.astype(BF)
    return high, (a - high.astype(F32)).astype(BF)


def left_pair(a):
    high, low = split(a)
    return jnp.concatenate([high, low], axis=1)


def right_pair(b):
    high, low = split(b)
    row = jnp.concatenate([high, low], axis=1)
    return jnp.concatenate([row, row], axis=0)


def wide_product(a, b):
    columns = b.shape[1]
    both = dot(left_pair(a), right_pair(b))
    return both[:, :columns] + both[:, columns:]


def moe_kernel(capacity, first_ref, meta_ref, x_ref, gate_up_ref, down_ref, out_ref, rows_ref, back_ref):
    blocks, twice, tok = meta_ref.shape
    choose = twice // 2
    local_experts = gate_up_ref.shape[0]
    expert_width = down_ref.shape[1]
    pairs = blocks // 2
    pair_rows = rows_ref.shape[1] // pairs
    first = first_ref[0]
    matched, weights = [], []
    for block in range(blocks):
        ids = meta_ref[block, :choose, :]
        scale = meta_ref[block, choose:, :]
        for e in range(local_experts):
            hit = ids == (first + e).astype(F32)
            matched.append(jnp.max(jnp.where(hit, 1.0, 0.0), axis=0, keepdims=True))
            weights.append(jnp.sum(jnp.where(hit, scale, 0.0), axis=0, keepdims=True))
    match = jnp.concatenate(matched, axis=0)
    before = lax.broadcasted_iota(jnp.int32, (tok, tok), 0) < lax.broadcasted_iota(
        jnp.int32, (tok, tok), 1
    )
    rank = dot(match.astype(BF), jnp.where(before, 1.0, 0.0).astype(BF))
    rank = jnp.where(match > 0.5, rank, -1e4)
    row_number = lax.broadcasted_iota(jnp.int32, (pair_rows, 2 * tok), 0).astype(F32)
    picks = []
    for pair in range(pairs):
        x_pair = x_ref[pair * 2 * tok : (pair + 1) * 2 * tok, :]
        for e in range(local_experts):
            low = 2 * pair * local_experts + e
            high = low + local_experts
            place = jnp.concatenate(
                [rank[low : low + 1], rank[high : high + 1] + float(capacity)], axis=1
            )
            pick = jnp.where(row_number == place, 1.0, 0.0)
            picks.append(pick)
            rows_ref[e, pair * pair_rows : (pair + 1) * pair_rows, :] = dot(
                pick.astype(BF), x_pair
            ).astype(BF)
    for e in range(local_experts):
        both = dot(rows_ref[e], gate_up_ref[e])
        gate = both[:, :expert_width]
        hidden = (gate / (1.0 + jnp.exp(-gate)) * both[:, expert_width:]).astype(BF)
        back_ref[e] = dot(hidden, down_ref[e]).astype(BF)
    for pair in range(pairs):
        scaled, rows = [], []
        for e in range(local_experts):
            low = 2 * pair * local_experts + e
            high = low + local_experts
            weight = jnp.concatenate([weights[low], weights[high]], axis=1)
            scaled.append(picks[pair * local_experts + e] * weight)
            rows.append(back_ref[e, pair * pair_rows : (pair + 1) * pair_rows, :])
        high_part, low_part = split(jnp.concatenate(scaled, axis=0))
        left = jnp.concatenate([high_part, low_part], axis=0)
        right = jnp.concatenate(rows + rows, axis=0)
        out_ref[pair * 2 * tok : (pair + 1) * 2 * tok, :] = lax.dot_general(
            left, right, (((0,), (0,)), ((), ())), preferred_element_type=F32
        ).astype(BF)


def experts(gathered, meta, first, gate_up_weight, down, capacity):
    rows, width = gathered.shape
    blocks, twice, tok = meta.shape
    local_experts, _, double = gate_up_weight.shape
    group = min(8, blocks)
    pair_rows = -(-2 * capacity // 16) * 16
    held = group // 2 * pair_rows
    once = pl.Buffered(1)
    return pl.pallas_call(
        partial(moe_kernel, capacity),
        grid=(blocks // group,),
        in_specs=[
            pl.BlockSpec(memory_space=pltpu.SMEM),
            pl.BlockSpec((group, twice, tok), lambda i: (i, 0, 0)),
            pl.BlockSpec((group * tok, width), lambda i: (i, 0)),
            pl.BlockSpec(gate_up_weight.shape, lambda i: (0, 0, 0), pipeline_mode=once),
            pl.BlockSpec(down.shape, lambda i: (0, 0, 0), pipeline_mode=once),
        ],
        out_specs=pl.BlockSpec((group * tok, width), lambda i: (i, 0)),
        out_shape=jax.ShapeDtypeStruct((rows, width), BF),
        scratch_shapes=[
            pltpu.VMEM((local_experts, held, width), BF),
            pltpu.VMEM((local_experts, held, width), BF),
        ],
        compiler_params=pltpu.CompilerParams(vmem_limit_bytes=VMEM_LIMIT),
        cost_estimate=pl.CostEstimate(
            flops=2 * blocks * capacity * local_experts * width * double * 3 // 2,
            bytes_accessed=4 * rows * width + 2 * (gate_up_weight.size + down.size),
            transcendentals=0,
        ),
        name="experts",
    )(first, meta, gathered, gate_up_weight, down)


def unit_rows(values):
    return values * lax.rsqrt(jnp.sum(values * values, axis=-1, keepdims=True) + 1e-06)


def mixer_kernel(q_ref, k_ref, v_ref, sum_ref, rate_ref, enter_ref, local_ref, end_ref):
    length, dim = q_ref.shape[1:]
    blocks = length // CH
    span = range(blocks)
    rows = lax.broadcasted_iota(jnp.int32, (CH, CH), 0)
    columns = lax.broadcasted_iota(jnp.int32, (CH, CH), 1)
    strict = rows > columns
    inclusive = rows >= columns
    identity = jnp.where(rows == columns, 1.0, 0.0)
    cut = [slice(n * CH, (n + 1) * CH) for n in span]
    query = [unit_rows(q_ref[0, cut[n], :]) for n in span]
    key = [unit_rows(k_ref[0, cut[n], :]) for n in span]
    value = [v_ref[0, cut[n], :] for n in span]
    across = [jnp.broadcast_to(sum_ref[0, n : n + 1, :], (CH, CH)) for n in span]
    down_rows = [across[n].T for n in span]
    rate = [jnp.broadcast_to(rate_ref[0, n : n + 1, :], (CH, CH)).T for n in span]
    fade = [jnp.exp(jnp.where(inclusive, down_rows[n] - across[n], 0.0)) for n in span]
    growth = [jnp.exp(down_rows[n]) for n in span]
    last = [jnp.broadcast_to(down_rows[n][CH - 1 : CH, :], (CH, CH)) for n in span]
    remaining = [jnp.exp(last[n] - down_rows[n]) for n in span]
    whole = [jnp.exp(last[n]) for n in span]
    both = []
    for n in span:
        high, low = split(key[n])
        left = jnp.concatenate(
            [jnp.concatenate([high, low], axis=1), left_pair(query[n])], axis=0
        )
        hh = jnp.concatenate([high, high], axis=1)
        ll = jnp.concatenate([low, low], axis=1)
        right_t = jnp.concatenate([hh, ll], axis=0)
        got = lax.dot_general(left, right_t, (((1,), (1,)), ((), ())), preferred_element_type=F32)
        both.append(got[:, :CH] + got[:, CH:])
    lower = [jnp.where(strict, rate[n] * fade[n] * both[n][:CH], 0.0) for n in span]
    masked = [jnp.where(inclusive, fade[n] * both[n][CH:], 0.0) for n in span]

    def ring(size):
        shared = (rows // (2 * size)) == (columns // (2 * size))
        return shared & (rows // size % 2 == 1) & (columns // size % 2 == 0)

    inverse = [identity - jnp.where(ring(1), lower[n], 0.0) for n in span]
    size = 2
    while size < CH:
        here = ring(size)
        step = [wide_product(jnp.where(here, lower[n], 0.0), inverse[n]) for n in span]
        inverse = [inverse[n] - wide_product(inverse[n], step[n]) for n in span]
        size *= 2
    solved = [
        wide_product(
            inverse[n],
            jnp.concatenate([rate[n] * growth[n] * key[n], rate[n] * value[n]], axis=1),
        )
        for n in span
    ]
    ended = [wide_product((remaining[n] * key[n]).T, solved[n]) for n in span]
    probed = [wide_product(masked[n], solved[n]) for n in span]
    state = None
    for n in span:
        entering = growth[n] * query[n] - probed[n][:, :dim]
        output = probed[n][:, dim:]
        transition = whole[n] * identity - ended[n][:, :dim]
        written = ended[n][:, dim:]
        if n == 0:
            state = jnp.concatenate([transition, written], axis=1)
        else:
            moved = wide_product(jnp.concatenate([entering, transition], axis=0), state)
            entering = moved[:CH, :dim]
            output = output + moved[:CH, dim:]
            state = jnp.concatenate([moved[CH:, :dim], moved[CH:, dim:] + written], axis=1)
        enter_ref[cut[n], :] = entering
        local_ref[cut[n], :] = output
    end_ref[0] = state


def mixer(projected, sums, rates):
    _, length, columns = projected.shape
    heads, blocks, _ = sums.shape
    dim = columns // heads
    part = lambda p: pl.BlockSpec((1, length, dim), lambda h, p=p: (p, 0, h))
    per_head = pl.BlockSpec((1, blocks, CH), lambda h: (h, 0, 0))
    per_column = pl.BlockSpec((length, dim), lambda h: (0, h))
    return pl.pallas_call(
        mixer_kernel,
        grid=(heads,),
        in_specs=[part(0), part(1), part(2), per_head, per_head],
        out_specs=[per_column, per_column, pl.BlockSpec((1, dim, 2 * dim), lambda h: (h, 0, 0))],
        out_shape=[
            jax.ShapeDtypeStruct((length, columns), F32),
            jax.ShapeDtypeStruct((length, columns), F32),
            jax.ShapeDtypeStruct((heads, dim, 2 * dim), F32),
        ],
        compiler_params=pltpu.CompilerParams(vmem_limit_bytes=VMEM_LIMIT),
        name="mixer",
    )(projected, projected, projected, sums, rates)


def carry_kernel(ends_ref, states_ref):
    segments, dim, _ = ends_ref.shape
    state = jnp.zeros((dim, dim), F32)
    for s in range(segments):
        states_ref[s] = state
        if s < segments - 1:
            state = wide_product(ends_ref[s, :, :dim], state) + ends_ref[s, :, dim:]


def carry(ends):
    segments, dim, _ = ends.shape
    return pl.pallas_call(
        carry_kernel,
        out_shape=jax.ShapeDtypeStruct((segments, dim, dim), F32),
        compiler_params=pltpu.CompilerParams(vmem_limit_bytes=VMEM_LIMIT),
        name="carry",
    )(ends)


def finish_kernel(enter_ref, local_ref, state_ref, core_ref):
    core_ref[...] = local_ref[...] + wide_product(enter_ref[...], state_ref[0])


def finish(entering, local_out, states):
    length, columns = entering.shape
    heads, dim, _ = states.shape
    per_column = pl.BlockSpec((length, dim), lambda h: (0, h))
    return pl.pallas_call(
        finish_kernel,
        grid=(heads,),
        in_specs=[per_column, per_column, pl.BlockSpec((1, dim, dim), lambda h: (h, 0, 0))],
        out_specs=per_column,
        out_shape=jax.ShapeDtypeStruct((length, columns), F32),
        compiler_params=pltpu.CompilerParams(vmem_limit_bytes=VMEM_LIMIT),
        name="finish",
    )(entering, local_out, states)


def relay(ends, seq_count):
    dim = ends.shape[1]
    pairs = [(i, i + 1) for i in range(seq_count - 1)]

    def step(_, incoming):
        outgoing = (
            jnp.einsum("hij,hjk->hik", ends[..., :dim], incoming, precision=lax.Precision.HIGHEST)
            + ends[..., dim:]
        )
        return lax.ppermute(outgoing, "seq", pairs)

    return lax.fori_loop(0, seq_count - 1, step, jnp.zeros_like(ends[..., :dim]))


def route_all(normed, expert_ids, expert_weights, gate_up_weight, down, capacity):
    axes = ("seq", "exp")
    tok_rows = normed.shape[0]
    me = lax.axis_index("seq") * lax.axis_size("exp") + lax.axis_index("exp")
    first = (me * gate_up_weight.shape[0]).astype(jnp.int32).reshape(1)
    meta = jnp.concatenate([expert_ids.astype(F32).T, expert_weights.T], axis=0)
    meta = lax.all_gather(meta, axes, axis=0, tiled=False)
    gathered = lax.all_gather(normed, axes, axis=0, tiled=True)
    partial_sums = experts(gathered, meta, first, gate_up_weight, down, capacity)
    return lax.psum_scatter(partial_sums, axes, scatter_dimension=0, tiled=True).astype(F32)


def route_some(normed, expert_ids, expert_weights, gate_up_weight, down, capacity):
    axes = ("seq", "exp")
    tok_rows, width = normed.shape
    choose = expert_ids.shape[1]
    local_experts = gate_up_weight.shape[0]
    expert_width = down.shape[1]
    devices = lax.axis_size("seq") * lax.axis_size("exp")
    experts_all = local_experts * devices
    flat_ids = expert_ids.reshape(-1)
    onehot = (flat_ids[:, None] == jnp.arange(experts_all, dtype=jnp.int32)[None, :]).astype(
        jnp.int32
    )
    rank = jnp.sum(jnp.cumsum(onehot, axis=0) * onehot, axis=1) - 1
    slot = flat_ids * capacity + rank
    token_of = jnp.arange(tok_rows * choose, dtype=jnp.int32) // choose
    send = jnp.zeros((experts_all * capacity, width), BF).at[slot].set(normed[token_of])
    both = jnp.einsum(
        "secd,edf->secf",
        lax.all_to_all(
            send.reshape(devices, local_experts, capacity, width),
            axes,
            split_axis=0,
            concat_axis=0,
            tiled=True,
        ),
        gate_up_weight,
        preferred_element_type=F32,
    )
    hidden = (jax.nn.silu(both[..., :expert_width]) * both[..., expert_width:]).astype(BF)
    back = lax.all_to_all(
        jnp.einsum("secf,efd->secd", hidden, down, preferred_element_type=F32).astype(BF),
        axes,
        split_axis=0,
        concat_axis=0,
        tiled=True,
    )
    back_rows = back.reshape(experts_all * capacity, width)[slot].astype(F32)
    return jnp.sum(
        back_rows.reshape(tok_rows, choose, width) * expert_weights[:, :, None], axis=1
    )


def local(
    stream,
    moe_gain,
    expert_ids,
    expert_weights,
    gate_up_weight,
    down,
    mixer_gain,
    qkv_weight,
    decay_log,
    write_rate,
):
    tok_rows, width = stream.shape
    choose = expert_ids.shape[1]
    seq_count = lax.axis_size("seq")
    devices = seq_count * lax.axis_size("exp")
    experts_all = gate_up_weight.shape[0] * devices
    capacity = max(2, (tok_rows * choose * 6 + experts_all * 5 - 1) // (experts_all * 5))
    normed = rms_scale(stream, moe_gain).astype(BF)
    route = route_all if devices * tok_rows * width * 4 <= 40 * 2**20 else route_some
    moe = route(normed, expert_ids, expert_weights, gate_up_weight, down, capacity)
    mixed = (stream.astype(F32) + moe).astype(BF)
    normed_mix = rms_scale(mixed, mixer_gain).astype(BF)
    projected = jnp.einsum(
        "rd,pde->pre",
        lax.all_gather(normed_mix, "exp", axis=0, tiled=True),
        qkv_weight,
        preferred_element_type=F32,
    )
    length = projected.shape[1]
    heads = decay_log.shape[1]
    blocks = length // CH
    sums = jnp.cumsum(decay_log.T.reshape(heads, blocks, CH), axis=-1)
    rates = write_rate.T.reshape(heads, blocks, CH)
    entering, local_out, ends = mixer(projected, sums, rates)
    if heads % seq_count == 0:
        dim = ends.shape[1]
        each = heads // seq_count
        held = lax.all_to_all(ends, "seq", split_axis=0, concat_axis=0, tiled=True)
        held = held.reshape(seq_count, each, dim, 2 * dim)
        states = jnp.stack([carry(held[:, i]) for i in range(each)], axis=1)
        arriving = lax.all_to_all(
            states.reshape(seq_count * each, dim, dim), "seq", split_axis=0, concat_axis=0, tiled=True
        )
    else:
        arriving = relay(ends, seq_count)
    return (mixed, finish(entering, local_out, arriving))


def solution(mesh):
    in_specs = (
        P(("seq", "exp"), None),
        P(),
        P(("seq", "exp"), None),
        P(("seq", "exp"), None),
        P(("seq", "exp"), None, None),
        P(("seq", "exp"), None, None),
        P(),
        P(None, None, "exp"),
        P("seq", "exp"),
        P("seq", "exp"),
    )
    out_specs = (P(("seq", "exp"), None), P("seq", "exp"))
    return jax.shard_map(local, mesh=mesh, in_specs=in_specs, out_specs=out_specs, check_vma=False)
```

```python
from functools import partial

import jax
import jax.numpy as jnp
from jax import lax
from jax.experimental import pallas as pl
from jax.experimental.pallas import tpu as pltpu
from jax.sharding import PartitionSpec as P

CH = 128
ROUTE_STEP = 16
VMEM_LIMIT = 56 * 1024 * 1024
BF = jnp.bfloat16
F32 = jnp.float32


def rms_scale(values, gain):
    wide = values.astype(F32)
    return wide * lax.rsqrt(jnp.mean(wide * wide, axis=-1, keepdims=True) + 1e-06) * gain


def dot(a, b):
    return jnp.dot(a, b, preferred_element_type=F32)


def split(a):
    high = a.astype(BF)
    return high, (a - high.astype(F32)).astype(BF)


def left_pair(a):
    high, low = split(a)
    return jnp.concatenate([high, low], axis=1)


def right_pair(b):
    high, low = split(b)
    row = jnp.concatenate([high, low], axis=1)
    return jnp.concatenate([row, row], axis=0)


def wide_product(a, b):
    columns = b.shape[1]
    both = dot(left_pair(a), right_pair(b))
    return both[:, :columns] + both[:, columns:]


def moe_kernel(capacity, choose, *refs):
    first_ref, *block_refs = refs[:5]
    weight_refs = refs[5:9]
    out_refs = refs[9:13]
    gate_up_ref, down_ref, rows_ref, back_ref, sem = refs[13:]
    tok, wide = block_refs[0].shape
    width = rows_ref.shape[2]
    experts_here = gate_up_ref.shape[0]
    half = experts_here // 2
    expert_width = down_ref.shape[1]
    pair_rows = rows_ref.shape[1] // 2

    copies = []
    for e in range(experts_here):
        side, at = divmod(e, half)
        fetch_in = pltpu.make_async_copy(
            weight_refs[2 * side].at[at], gate_up_ref.at[e], sem.at[0, e]
        )
        fetch_out = pltpu.make_async_copy(
            weight_refs[2 * side + 1].at[at], down_ref.at[e], sem.at[1, e]
        )
        fetch_in.start()
        fetch_out.start()
        copies.append((fetch_in, fetch_out))

    matched, weights = [], []
    for block_ref in block_refs:
        routing = block_ref[:, width:].astype(F32).T
        ids = routing[:choose]
        scale = routing[ROUTE_STEP : ROUTE_STEP + choose]
        scale = scale + routing[2 * ROUTE_STEP : 2 * ROUTE_STEP + choose]
        for e in range(experts_here):
            side, at = divmod(e, half)
            hit = ids == (first_ref[side] + at).astype(F32)
            matched.append(jnp.max(jnp.where(hit, 1.0, 0.0), axis=0, keepdims=True))
            weights.append(jnp.sum(jnp.where(hit, scale, 0.0), axis=0, keepdims=True))
    match = jnp.concatenate(matched, axis=0)
    before = lax.broadcasted_iota(jnp.int32, (tok, tok), 0) < lax.broadcasted_iota(
        jnp.int32, (tok, tok), 1
    )
    rank = dot(match.astype(BF), jnp.where(before, 1.0, 0.0).astype(BF))
    rank = jnp.where(match > 0.5, rank, -1e4)
    row_number = lax.broadcasted_iota(jnp.int32, (pair_rows, 2 * tok), 0).astype(F32)
    picks = []
    for pair in range(2):
        x_pair = jnp.concatenate(
            [block_refs[2 * pair][:, :width], block_refs[2 * pair + 1][:, :width]], axis=0
        )
        here = []
        for e in range(experts_here):
            low = 2 * pair * experts_here + e
            high = low + experts_here
            place = jnp.concatenate(
                [rank[low : low + 1], rank[high : high + 1] + float(capacity)], axis=1
            )
            here.append(jnp.where(row_number == place, 1.0, 0.0))
        picks.append(here)
        chosen = dot(jnp.concatenate(here, axis=0).astype(BF), x_pair).astype(BF)
        for e in range(experts_here):
            rows_ref[e, pair * pair_rows : (pair + 1) * pair_rows, :] = chosen[
                e * pair_rows : (e + 1) * pair_rows
            ]
    for e in range(experts_here):
        copies[e][0].wait()
        both = dot(rows_ref[e], gate_up_ref[e])
        gate = both[:, :expert_width]
        hidden = (gate / (1.0 + jnp.exp(-gate)) * both[:, expert_width:]).astype(BF)
        copies[e][1].wait()
        back_ref[e] = dot(hidden, down_ref[e]).astype(BF)
    for pair in range(2):
        scaled, rows = [], []
        for e in range(experts_here):
            low = 2 * pair * experts_here + e
            high = low + experts_here
            weight = jnp.concatenate([weights[low], weights[high]], axis=1)
            scaled.append(picks[pair][e] * weight)
            rows.append(back_ref[e, pair * pair_rows : (pair + 1) * pair_rows, :])
        high_part, low_part = split(jnp.concatenate(scaled, axis=0))
        left = jnp.concatenate([high_part, low_part], axis=0)
        right = jnp.concatenate(rows + rows, axis=0)
        summed = lax.dot_general(
            left, right, (((0,), (0,)), ((), ())), preferred_element_type=F32
        ).astype(BF)
        out_refs[2 * pair][...] = summed[:tok]
        out_refs[2 * pair + 1][...] = summed[tok:]


def experts(blocks, first, weights, capacity, choose):
    tok, wide = blocks[0].shape
    gate_up_weight, down = weights[:2]
    local_experts, width, double = gate_up_weight.shape
    here = 2 * local_experts
    pair_rows = -(-2 * capacity // 16) * 16
    whole = pl.BlockSpec(memory_space=pltpu.VMEM)
    return pl.pallas_call(
        partial(moe_kernel, capacity, choose),
        in_specs=[pl.BlockSpec(memory_space=pltpu.SMEM)]
        + [whole] * 4
        + [pl.BlockSpec(memory_space=pl.ANY)] * 4,
        out_specs=[whole] * 4,
        out_shape=[jax.ShapeDtypeStruct((tok, width), BF)] * 4,
        scratch_shapes=[
            pltpu.VMEM((here,) + gate_up_weight.shape[1:], BF),
            pltpu.VMEM((here,) + down.shape[1:], BF),
            pltpu.VMEM((here, 2 * pair_rows, width), BF),
            pltpu.VMEM((here, 2 * pair_rows, width), BF),
            pltpu.SemaphoreType.DMA((2, here)),
        ],
        compiler_params=pltpu.CompilerParams(vmem_limit_bytes=VMEM_LIMIT),
        cost_estimate=pl.CostEstimate(
            flops=2 * here * 2 * pair_rows * width * double * 3,
            bytes_accessed=4 * (gate_up_weight.size + down.size),
            transcendentals=0,
        ),
        name="experts",
    )(first, *blocks, *weights)


def unit_rows(values):
    return values * lax.rsqrt(jnp.sum(values * values, axis=-1, keepdims=True) + 1e-06)


def mixer_kernel(q_ref, k_ref, v_ref, sum_ref, rate_ref, enter_ref, local_ref, end_ref):
    length, dim = q_ref.shape[1:]
    blocks = length // CH
    span = range(blocks)
    rows = lax.broadcasted_iota(jnp.int32, (CH, CH), 0)
    columns = lax.broadcasted_iota(jnp.int32, (CH, CH), 1)
    strict = rows > columns
    inclusive = rows >= columns
    identity = jnp.where(rows == columns, 1.0, 0.0)
    cut = [slice(n * CH, (n + 1) * CH) for n in span]
    query = [unit_rows(q_ref[0, cut[n], :]) for n in span]
    key = [unit_rows(k_ref[0, cut[n], :]) for n in span]
    value = [v_ref[0, cut[n], :] for n in span]
    across = [jnp.broadcast_to(sum_ref[0, n : n + 1, :], (CH, CH)) for n in span]
    down_rows = [across[n].T for n in span]
    rate = [jnp.broadcast_to(rate_ref[0, n : n + 1, :], (CH, CH)).T for n in span]
    fade = [jnp.exp(jnp.where(inclusive, down_rows[n] - across[n], 0.0)) for n in span]
    growth = [jnp.exp(down_rows[n]) for n in span]
    last = [jnp.broadcast_to(down_rows[n][CH - 1 : CH, :], (CH, CH)) for n in span]
    remaining = [jnp.exp(last[n] - down_rows[n]) for n in span]
    whole = [jnp.exp(last[n]) for n in span]
    both = []
    for n in span:
        high, low = split(key[n])
        left = jnp.concatenate(
            [jnp.concatenate([high, low], axis=1), left_pair(query[n])], axis=0
        )
        hh = jnp.concatenate([high, high], axis=1)
        ll = jnp.concatenate([low, low], axis=1)
        right_t = jnp.concatenate([hh, ll], axis=0)
        got = lax.dot_general(left, right_t, (((1,), (1,)), ((), ())), preferred_element_type=F32)
        both.append(got[:, :CH] + got[:, CH:])
    lower = [jnp.where(strict, rate[n] * fade[n] * both[n][:CH], 0.0) for n in span]
    masked = [jnp.where(inclusive, fade[n] * both[n][CH:], 0.0) for n in span]

    def ring(size):
        shared = (rows // (2 * size)) == (columns // (2 * size))
        return shared & (rows // size % 2 == 1) & (columns // size % 2 == 0)

    inverse = [identity - jnp.where(ring(1), lower[n], 0.0) for n in span]
    size = 2
    while size < CH:
        here = ring(size)
        step = [wide_product(jnp.where(here, lower[n], 0.0), inverse[n]) for n in span]
        inverse = [inverse[n] - wide_product(inverse[n], step[n]) for n in span]
        size *= 2
    solved = [
        wide_product(
            inverse[n],
            jnp.concatenate([rate[n] * growth[n] * key[n], rate[n] * value[n]], axis=1),
        )
        for n in span
    ]
    ended = [wide_product((remaining[n] * key[n]).T, solved[n]) for n in span]
    probed = [wide_product(masked[n], solved[n]) for n in span]
    state = None
    total_decay = None
    for n in span:
        entering = growth[n] * query[n] - probed[n][:, :dim]
        output = probed[n][:, dim:]
        transition = whole[n] * identity - ended[n][:, :dim]
        written = ended[n][:, dim:]
        if n == 0:
            state = jnp.concatenate([transition, written], axis=1)
            total_decay = whole[n]
        else:
            moved = wide_product(jnp.concatenate([entering, transition], axis=0), state)
            entering = moved[:CH, :dim]
            output = output + moved[:CH, dim:]
            state = jnp.concatenate([moved[CH:, :dim], moved[CH:, dim:] + written], axis=1)
            total_decay = total_decay * whole[n]
        enter_ref[cut[n], :] = entering
        local_ref[cut[n], :] = output
    end_ref[0, :dim, :dim] = (total_decay * identity - state[:, :dim]).astype(BF)
    end_ref[0, :dim, dim:] = state[:, dim:].astype(BF)
    end_ref[0, dim:, :] = left_pair(total_decay[:16])


def mixer(projected, sums, rates):
    _, length, columns = projected.shape
    heads, blocks, _ = sums.shape
    dim = columns // heads
    part = lambda p: pl.BlockSpec((1, length, dim), lambda h, p=p: (p, 0, h))
    per_head = pl.BlockSpec((1, blocks, CH), lambda h: (h, 0, 0))
    per_column = pl.BlockSpec((length, dim), lambda h: (0, h))
    return pl.pallas_call(
        mixer_kernel,
        grid=(heads,),
        in_specs=[part(0), part(1), part(2), per_head, per_head],
        out_specs=[per_column, per_column, pl.BlockSpec((1, dim + 16, 2 * dim), lambda h: (h, 0, 0))],
        out_shape=[
            jax.ShapeDtypeStruct((length, columns), F32),
            jax.ShapeDtypeStruct((length, columns), F32),
            jax.ShapeDtypeStruct((heads, dim + 16, 2 * dim), BF),
        ],
        compiler_params=pltpu.CompilerParams(vmem_limit_bytes=VMEM_LIMIT),
        name="mixer",
    )(projected, projected, projected, sums, rates)


def carry_kernel(ends_ref, states_ref):
    segments, _, double = ends_ref.shape
    dim = double // 2
    state = jnp.zeros((dim, dim), F32)
    for s in range(segments):
        states_ref[s] = state.astype(BF)
        if s < segments - 1:
            decay = ends_ref[s, dim : dim + 1, :].astype(F32)
            decay = decay[:, :dim] + decay[:, dim:]
            removed = dot(ends_ref[s, :dim, :dim], left_pair(state))
            removed = removed[:, :dim] + removed[:, dim:]
            state = decay * state - removed + ends_ref[s, :dim, dim:].astype(F32)


def carry(ends):
    segments, _, double = ends.shape
    return pl.pallas_call(
        carry_kernel,
        out_shape=jax.ShapeDtypeStruct((segments, double // 2, double // 2), BF),
        compiler_params=pltpu.CompilerParams(vmem_limit_bytes=VMEM_LIMIT),
        name="carry",
    )(ends)


def finish_kernel(enter_ref, local_ref, state_ref, core_ref):
    state = state_ref[0]
    core_ref[...] = local_ref[...] + dot(
        left_pair(enter_ref[...]), jnp.concatenate([state, state], axis=0)
    )


def finish(entering, local_out, states):
    length, columns = entering.shape
    heads, dim, _ = states.shape
    per_column = pl.BlockSpec((length, dim), lambda h: (0, h))
    return pl.pallas_call(
        finish_kernel,
        grid=(heads,),
        in_specs=[per_column, per_column, pl.BlockSpec((1, dim, dim), lambda h: (h, 0, 0))],
        out_specs=per_column,
        out_shape=jax.ShapeDtypeStruct((length, columns), F32),
        compiler_params=pltpu.CompilerParams(vmem_limit_bytes=VMEM_LIMIT),
        name="finish",
    )(entering, local_out, states)


def relay(ends, seq_count):
    dim = ends.shape[2] // 2
    pairs = [(i, i + 1) for i in range(seq_count - 1)]
    removed, written = ends[:, :dim, :dim].astype(F32), ends[:, :dim, dim:].astype(F32)
    decay = ends[:, dim, :1].astype(F32) + ends[:, dim, dim : dim + 1].astype(F32)

    def step(_, incoming):
        outgoing = decay[:, :, None] * incoming + written
        outgoing = outgoing - jnp.einsum(
            "hij,hjk->hik", removed, incoming, precision=lax.Precision.HIGHEST
        )
        return lax.ppermute(outgoing, "seq", pairs)

    return lax.fori_loop(0, seq_count - 1, step, jnp.zeros_like(written)).astype(BF)


def move(values, change):
    exp_count = lax.axis_size("exp")
    pairs = []
    for s in range(lax.axis_size("seq")):
        for e in range(exp_count):
            to_s, to_e = change(s, e)
            pairs.append((s * exp_count + e, to_s * exp_count + to_e))
    return lax.ppermute(values, ("seq", "exp"), pairs)


def over_x(values):
    return move(values, lambda s, e: (s ^ 1, e))


def over_y(values):
    return move(values, lambda s, e: (s, e ^ 2))


def over_core(values):
    return move(values, lambda s, e: (s, e ^ 1))


def along_z(values, by):
    count = lax.axis_size("seq")
    return move(values, lambda s, e: ((s + 2 * by) % count, e))


def added(*terms):
    total = terms[0].astype(F32)
    for term in terms[1:]:
        total = total + term.astype(F32)
    return total


def route_waves(normed, expert_ids, expert_weights, gate_up_weight, down, capacity):
    tok_rows, width = normed.shape
    choose = expert_ids.shape[1]
    local_experts = gate_up_weight.shape[0]
    me = lax.axis_index("seq") * lax.axis_size("exp") + lax.axis_index("exp")
    first = (jnp.stack([me, me ^ 1]) * local_experts).astype(jnp.int32)
    gap = jnp.zeros((tok_rows, ROUTE_STEP - choose), BF)
    high, low = split(expert_weights)
    tail = jnp.zeros((tok_rows, 128 - 3 * ROUTE_STEP), BF)
    block = jnp.concatenate(
        [normed, expert_ids.astype(BF), gap, high, gap, low, gap, tail], axis=1
    )
    weights = (gate_up_weight, down, over_core(gate_up_weight), over_core(down))
    total = None
    for wave in range(lax.axis_size("seq") // 2):
        if wave:
            block = along_z(block, 1)
        one, two = (over_x, over_y) if wave % 2 == 0 else (over_y, over_x)
        by_one = one(block)
        by_two = two(block)
        both = two(by_one)
        own, sum_one, sum_two, sum_both = experts(
            (block, by_one, by_two, both), first, weights, capacity, choose
        )
        passed = added(sum_one, two(sum_both)).astype(BF)
        here = added(own, two(sum_two), one(passed))
        if wave:
            here = along_z(here.astype(BF), -wave).astype(F32)
        total = here if total is None else total + here
    return total


def route_some(normed, expert_ids, expert_weights, gate_up_weight, down, capacity):
    axes = ("seq", "exp")
    tok_rows, width = normed.shape
    choose = expert_ids.shape[1]
    local_experts = gate_up_weight.shape[0]
    expert_width = down.shape[1]
    devices = lax.axis_size("seq") * lax.axis_size("exp")
    experts_all = local_experts * devices
    flat_ids = expert_ids.reshape(-1)
    onehot = (flat_ids[:, None] == jnp.arange(experts_all, dtype=jnp.int32)[None, :]).astype(
        jnp.int32
    )
    rank = jnp.sum(jnp.cumsum(onehot, axis=0) * onehot, axis=1) - 1
    slot = flat_ids * capacity + rank
    token_of = jnp.arange(tok_rows * choose, dtype=jnp.int32) // choose
    send = jnp.zeros((experts_all * capacity, width), BF).at[slot].set(normed[token_of])
    both = jnp.einsum(
        "secd,edf->secf",
        lax.all_to_all(
            send.reshape(devices, local_experts, capacity, width),
            axes,
            split_axis=0,
            concat_axis=0,
            tiled=True,
        ),
        gate_up_weight,
        preferred_element_type=F32,
    )
    hidden = (jax.nn.silu(both[..., :expert_width]) * both[..., expert_width:]).astype(BF)
    back = lax.all_to_all(
        jnp.einsum("secf,efd->secd", hidden, down, preferred_element_type=F32).astype(BF),
        axes,
        split_axis=0,
        concat_axis=0,
        tiled=True,
    )
    back_rows = back.reshape(experts_all * capacity, width)[slot].astype(F32)
    return jnp.sum(
        back_rows.reshape(tok_rows, choose, width) * expert_weights[:, :, None], axis=1
    )


def local(
    stream,
    moe_gain,
    expert_ids,
    expert_weights,
    gate_up_weight,
    down,
    mixer_gain,
    qkv_weight,
    decay_log,
    write_rate,
):
    tok_rows, width = stream.shape
    choose = expert_ids.shape[1]
    seq_count = lax.axis_size("seq")
    devices = seq_count * lax.axis_size("exp")
    experts_all = gate_up_weight.shape[0] * devices
    capacity = max(2, (tok_rows * choose * 6 + experts_all * 5 - 1) // (experts_all * 5))
    normed = rms_scale(stream, moe_gain).astype(BF)
    planes = lax.axis_size("exp") == 4 and seq_count % 2 == 0 and choose <= ROUTE_STEP
    route = route_waves if planes and experts_all <= 256 else route_some
    moe = route(normed, expert_ids, expert_weights, gate_up_weight, down, capacity)
    mixed = (stream.astype(F32) + moe).astype(BF)
    normed_mix = rms_scale(mixed, mixer_gain).astype(BF)
    projected = jnp.einsum(
        "rd,pde->pre",
        lax.all_gather(normed_mix, "exp", axis=0, tiled=True),
        qkv_weight,
        preferred_element_type=F32,
    )
    length = projected.shape[1]
    heads = decay_log.shape[1]
    blocks = length // CH
    sums = jnp.cumsum(decay_log.T.reshape(heads, blocks, CH), axis=-1)
    rates = write_rate.T.reshape(heads, blocks, CH)
    entering, local_out, ends = mixer(projected, sums, rates)
    if heads % seq_count == 0:
        dim = ends.shape[2] // 2
        each = heads // seq_count
        held = lax.all_to_all(ends, "seq", split_axis=0, concat_axis=0, tiled=True)
        held = held.reshape(seq_count, each, dim + 16, 2 * dim)
        states = jnp.stack([carry(held[:, i]) for i in range(each)], axis=1)
        arriving = lax.all_to_all(
            states.reshape(seq_count * each, dim, dim), "seq", split_axis=0, concat_axis=0, tiled=True
        )
    else:
        arriving = relay(ends, seq_count)
    return (mixed, finish(entering, local_out, arriving))


def solution(mesh):
    in_specs = (
        P(("seq", "exp"), None),
        P(),
        P(("seq", "exp"), None),
        P(("seq", "exp"), None),
        P(("seq", "exp"), None, None),
        P(("seq", "exp"), None, None),
        P(),
        P(None, None, "exp"),
        P("seq", "exp"),
        P("seq", "exp"),
    )
    out_specs = (P(("seq", "exp"), None), P("seq", "exp"))
    return jax.shard_map(local, mesh=mesh, in_specs=in_specs, out_specs=out_specs, check_vma=False)
```

```python
from functools import partial

import jax
import jax.numpy as jnp
from jax import lax
from jax.experimental import pallas as pl
from jax.experimental.pallas import tpu as pltpu
from jax.sharding import PartitionSpec as P

CH = 128
ROUTE_STEP = 16
VMEM_LIMIT = 56 * 1024 * 1024
BF = jnp.bfloat16
F32 = jnp.float32


def rms_scale(values, gain):
    wide = values.astype(F32)
    return wide * lax.rsqrt(jnp.mean(wide * wide, axis=-1, keepdims=True) + 1e-06) * gain


def dot(a, b):
    return jnp.dot(a, b, preferred_element_type=F32)


def split(a):
    high = a.astype(BF)
    return high, (a - high.astype(F32)).astype(BF)


def left_pair(a):
    high, low = split(a)
    return jnp.concatenate([high, low], axis=1)


def right_pair(b):
    high, low = split(b)
    row = jnp.concatenate([high, low], axis=1)
    return jnp.concatenate([row, row], axis=0)


def wide_product(a, b):
    columns = b.shape[1]
    both = dot(left_pair(a), right_pair(b))
    return both[:, :columns] + both[:, columns:]


def moe_kernel(capacity, choose, *refs):
    first_ref, *block_refs = refs[:5]
    weight_refs = refs[5:9]
    out_refs = refs[-9:-5]
    gate_up_ref, down_ref, rows_ref, back_ref, sem = refs[-5:]
    tok, wide = block_refs[0].shape
    width = rows_ref.shape[2]
    experts_here = gate_up_ref.shape[0]
    half = experts_here // 2
    expert_width = down_ref.shape[1]
    pair_rows = rows_ref.shape[1] // 2

    copies = []
    for e in range(experts_here):
        side, at = divmod(e, half)
        fetch_in = pltpu.make_async_copy(
            weight_refs[2 * side].at[at], gate_up_ref.at[e], sem.at[0, e]
        )
        fetch_out = pltpu.make_async_copy(
            weight_refs[2 * side + 1].at[at], down_ref.at[e], sem.at[1, e]
        )
        fetch_in.start()
        fetch_out.start()
        copies.append((fetch_in, fetch_out))

    matched, weights = [], []
    for block_ref in block_refs:
        routing = block_ref[:, width:].astype(F32).T
        ids = routing[:choose]
        scale = routing[ROUTE_STEP : ROUTE_STEP + choose]
        scale = scale + routing[2 * ROUTE_STEP : 2 * ROUTE_STEP + choose]
        for e in range(experts_here):
            side, at = divmod(e, half)
            hit = ids == (first_ref[side] + at).astype(F32)
            matched.append(jnp.max(jnp.where(hit, 1.0, 0.0), axis=0, keepdims=True))
            weights.append(jnp.sum(jnp.where(hit, scale, 0.0), axis=0, keepdims=True))
    match = jnp.concatenate(matched, axis=0)
    before = lax.broadcasted_iota(jnp.int32, (tok, tok), 0) < lax.broadcasted_iota(
        jnp.int32, (tok, tok), 1
    )
    rank = dot(match.astype(BF), jnp.where(before, 1.0, 0.0).astype(BF))
    rank = jnp.where(match > 0.5, rank, -1e4)
    row_number = lax.broadcasted_iota(jnp.int32, (pair_rows, 2 * tok), 0).astype(F32)
    picks = []
    for pair in range(2):
        x_pair = jnp.concatenate(
            [block_refs[2 * pair][:, :width], block_refs[2 * pair + 1][:, :width]], axis=0
        )
        here = []
        for e in range(experts_here):
            low = 2 * pair * experts_here + e
            high = low + experts_here
            place = jnp.concatenate(
                [rank[low : low + 1], rank[high : high + 1] + float(capacity)], axis=1
            )
            here.append(jnp.where(row_number == place, 1.0, 0.0))
        picks.append(here)
        chosen = dot(jnp.concatenate(here, axis=0).astype(BF), x_pair).astype(BF)
        for e in range(experts_here):
            rows_ref[e, pair * pair_rows : (pair + 1) * pair_rows, :] = chosen[
                e * pair_rows : (e + 1) * pair_rows
            ]
    for e in range(experts_here):
        copies[e][0].wait()
        both = dot(rows_ref[e], gate_up_ref[e])
        gate = both[:, :expert_width]
        hidden = (gate / (1.0 + jnp.exp(-gate)) * both[:, expert_width:]).astype(BF)
        copies[e][1].wait()
        back_ref[e] = dot(hidden, down_ref[e]).astype(BF)
    for pair in range(2):
        scaled, rows = [], []
        for e in range(experts_here):
            low = 2 * pair * experts_here + e
            high = low + experts_here
            weight = jnp.concatenate([weights[low], weights[high]], axis=1)
            scaled.append(picks[pair][e] * weight)
            rows.append(back_ref[e, pair * pair_rows : (pair + 1) * pair_rows, :])
        high_part, low_part = split(jnp.concatenate(scaled, axis=0))
        left = jnp.concatenate([high_part, low_part], axis=0)
        right = jnp.concatenate(rows + rows, axis=0)
        summed = lax.dot_general(
            left, right, (((0,), (0,)), ((), ())), preferred_element_type=F32
        ).astype(BF)
        out_refs[2 * pair][...] = summed[:tok]
        out_refs[2 * pair + 1][...] = summed[tok:]


def experts(blocks, first, weights, after, capacity, choose):
    tok, wide = blocks[0].shape
    gate_up_weight, down = weights[:2]
    local_experts, width, double = gate_up_weight.shape
    here = 2 * local_experts
    pair_rows = -(-2 * capacity // 16) * 16
    whole = pl.BlockSpec(memory_space=pltpu.VMEM)
    return pl.pallas_call(
        partial(moe_kernel, capacity, choose),
        in_specs=[pl.BlockSpec(memory_space=pltpu.SMEM)]
        + [whole] * 4
        + [pl.BlockSpec(memory_space=pl.ANY)] * (4 + len(after)),
        out_specs=[whole] * 4,
        out_shape=[jax.ShapeDtypeStruct((tok, width), BF)] * 4,
        scratch_shapes=[
            pltpu.VMEM((here,) + gate_up_weight.shape[1:], BF),
            pltpu.VMEM((here,) + down.shape[1:], BF),
            pltpu.VMEM((here, 2 * pair_rows, width), BF),
            pltpu.VMEM((here, 2 * pair_rows, width), BF),
            pltpu.SemaphoreType.DMA((2, here)),
        ],
        compiler_params=pltpu.CompilerParams(vmem_limit_bytes=VMEM_LIMIT),
        cost_estimate=pl.CostEstimate(
            flops=2 * here * 2 * pair_rows * width * double * 3,
            bytes_accessed=4 * (gate_up_weight.size + down.size),
            transcendentals=0,
        ),
        name="experts",
    )(first, *blocks, *weights, *after)


def unit_rows(values):
    return values * lax.rsqrt(jnp.sum(values * values, axis=-1, keepdims=True) + 1e-06)


def mixer_kernel(q_ref, k_ref, v_ref, sum_ref, rate_ref, enter_ref, local_ref, end_ref):
    length, dim = q_ref.shape[1:]
    blocks = length // CH
    span = range(blocks)
    rows = lax.broadcasted_iota(jnp.int32, (CH, CH), 0)
    columns = lax.broadcasted_iota(jnp.int32, (CH, CH), 1)
    strict = rows > columns
    inclusive = rows >= columns
    identity = jnp.where(rows == columns, 1.0, 0.0)
    cut = [slice(n * CH, (n + 1) * CH) for n in span]
    query = [unit_rows(q_ref[0, cut[n], :]) for n in span]
    key = [unit_rows(k_ref[0, cut[n], :]) for n in span]
    value = [v_ref[0, cut[n], :] for n in span]
    across = [jnp.broadcast_to(sum_ref[0, n : n + 1, :], (CH, CH)) for n in span]
    down_rows = [across[n].T for n in span]
    rate = [jnp.broadcast_to(rate_ref[0, n : n + 1, :], (CH, CH)).T for n in span]
    fade = [jnp.exp(jnp.where(inclusive, down_rows[n] - across[n], 0.0)) for n in span]
    growth = [jnp.exp(down_rows[n]) for n in span]
    last = [jnp.broadcast_to(down_rows[n][CH - 1 : CH, :], (CH, CH)) for n in span]
    remaining = [jnp.exp(last[n] - down_rows[n]) for n in span]
    whole = [jnp.exp(last[n]) for n in span]
    both = []
    for n in span:
        high, low = split(key[n])
        left = jnp.concatenate(
            [jnp.concatenate([high, low], axis=1), left_pair(query[n])], axis=0
        )
        hh = jnp.concatenate([high, high], axis=1)
        ll = jnp.concatenate([low, low], axis=1)
        right_t = jnp.concatenate([hh, ll], axis=0)
        got = lax.dot_general(left, right_t, (((1,), (1,)), ((), ())), preferred_element_type=F32)
        both.append(got[:, :CH] + got[:, CH:])
    lower = [jnp.where(strict, rate[n] * fade[n] * both[n][:CH], 0.0) for n in span]
    masked = [jnp.where(inclusive, fade[n] * both[n][CH:], 0.0) for n in span]

    def ring(size):
        shared = (rows // (2 * size)) == (columns // (2 * size))
        return shared & (rows // size % 2 == 1) & (columns // size % 2 == 0)

    inverse = [identity - jnp.where(ring(1), lower[n], 0.0) for n in span]
    size = 2
    while size < CH:
        here = ring(size)
        step = [wide_product(jnp.where(here, lower[n], 0.0), inverse[n]) for n in span]
        inverse = [inverse[n] - wide_product(inverse[n], step[n]) for n in span]
        size *= 2
    solved = [
        wide_product(
            inverse[n],
            jnp.concatenate([rate[n] * growth[n] * key[n], rate[n] * value[n]], axis=1),
        )
        for n in span
    ]
    ended = [wide_product((remaining[n] * key[n]).T, solved[n]) for n in span]
    probed = [wide_product(masked[n], solved[n]) for n in span]
    state = None
    total_decay = None
    for n in span:
        entering = growth[n] * query[n] - probed[n][:, :dim]
        output = probed[n][:, dim:]
        transition = whole[n] * identity - ended[n][:, :dim]
        written = ended[n][:, dim:]
        if n == 0:
            state = jnp.concatenate([transition, written], axis=1)
            total_decay = whole[n]
        else:
            moved = wide_product(jnp.concatenate([entering, transition], axis=0), state)
            entering = moved[:CH, :dim]
            output = output + moved[:CH, dim:]
            state = jnp.concatenate([moved[CH:, :dim], moved[CH:, dim:] + written], axis=1)
            total_decay = total_decay * whole[n]
        enter_ref[cut[n], :] = entering
        local_ref[cut[n], :] = output
    end_ref[0, :dim, :dim] = (total_decay * identity - state[:, :dim]).astype(BF)
    end_ref[0, :dim, dim:] = state[:, dim:].astype(BF)
    end_ref[0, dim:, :] = left_pair(total_decay[:16])


def mixer(projected, sums, rates):
    _, length, columns = projected.shape
    heads, blocks, _ = sums.shape
    dim = columns // heads
    part = lambda p: pl.BlockSpec((1, length, dim), lambda h, p=p: (p, 0, h))
    per_head = pl.BlockSpec((1, blocks, CH), lambda h: (h, 0, 0))
    per_column = pl.BlockSpec((length, dim), lambda h: (0, h))
    return pl.pallas_call(
        mixer_kernel,
        grid=(heads,),
        in_specs=[part(0), part(1), part(2), per_head, per_head],
        out_specs=[per_column, per_column, pl.BlockSpec((1, dim + 16, 2 * dim), lambda h: (h, 0, 0))],
        out_shape=[
            jax.ShapeDtypeStruct((length, columns), F32),
            jax.ShapeDtypeStruct((length, columns), F32),
            jax.ShapeDtypeStruct((heads, dim + 16, 2 * dim), BF),
        ],
        compiler_params=pltpu.CompilerParams(vmem_limit_bytes=VMEM_LIMIT),
        name="mixer",
    )(projected, projected, projected, sums, rates)


def carry_kernel(ends_ref, states_ref):
    segments, _, double = ends_ref.shape
    dim = double // 2
    state = jnp.zeros((dim, dim), F32)
    for s in range(segments):
        states_ref[s] = state.astype(BF)
        if s < segments - 1:
            decay = ends_ref[s, dim : dim + 1, :].astype(F32)
            decay = decay[:, :dim] + decay[:, dim:]
            removed = dot(ends_ref[s, :dim, :dim], left_pair(state))
            removed = removed[:, :dim] + removed[:, dim:]
            state = decay * state - removed + ends_ref[s, :dim, dim:].astype(F32)


def carry(ends):
    segments, _, double = ends.shape
    return pl.pallas_call(
        carry_kernel,
        out_shape=jax.ShapeDtypeStruct((segments, double // 2, double // 2), BF),
        compiler_params=pltpu.CompilerParams(vmem_limit_bytes=VMEM_LIMIT),
        name="carry",
    )(ends)


def finish_kernel(enter_ref, local_ref, state_ref, core_ref):
    state = state_ref[0]
    core_ref[...] = local_ref[...] + dot(
        left_pair(enter_ref[...]), jnp.concatenate([state, state], axis=0)
    )


def finish(entering, local_out, states):
    length, columns = entering.shape
    heads, dim, _ = states.shape
    per_column = pl.BlockSpec((length, dim), lambda h: (0, h))
    return pl.pallas_call(
        finish_kernel,
        grid=(heads,),
        in_specs=[per_column, per_column, pl.BlockSpec((1, dim, dim), lambda h: (h, 0, 0))],
        out_specs=per_column,
        out_shape=jax.ShapeDtypeStruct((length, columns), F32),
        compiler_params=pltpu.CompilerParams(vmem_limit_bytes=VMEM_LIMIT),
        name="finish",
    )(entering, local_out, states)


def relay(ends, seq_count):
    dim = ends.shape[2] // 2
    pairs = [(i, i + 1) for i in range(seq_count - 1)]
    removed, written = ends[:, :dim, :dim].astype(F32), ends[:, :dim, dim:].astype(F32)
    decay = ends[:, dim, :1].astype(F32) + ends[:, dim, dim : dim + 1].astype(F32)

    def step(_, incoming):
        outgoing = decay[:, :, None] * incoming + written
        outgoing = outgoing - jnp.einsum(
            "hij,hjk->hik", removed, incoming, precision=lax.Precision.HIGHEST
        )
        return lax.ppermute(outgoing, "seq", pairs)

    return lax.fori_loop(0, seq_count - 1, step, jnp.zeros_like(written)).astype(BF)


def move(values, change):
    exp_count = lax.axis_size("exp")
    pairs = []
    for s in range(lax.axis_size("seq")):
        for e in range(exp_count):
            to_s, to_e = change(s, e)
            pairs.append((s * exp_count + e, to_s * exp_count + to_e))
    return lax.ppermute(values, ("seq", "exp"), pairs)


def over_x(values):
    return move(values, lambda s, e: (s ^ 1, e))


def over_y(values):
    return move(values, lambda s, e: (s, e ^ 2))


def over_core(values):
    return move(values, lambda s, e: (s, e ^ 1))


def along_z(values, by):
    count = lax.axis_size("seq")
    return move(values, lambda s, e: ((s + 2 * by) % count, e))


def added(*terms):
    total = terms[0].astype(F32)
    for term in terms[1:]:
        total = total + term.astype(F32)
    return total


def route_waves(normed, expert_ids, expert_weights, gate_up_weight, down, capacity):
    tok_rows, width = normed.shape
    choose = expert_ids.shape[1]
    local_experts = gate_up_weight.shape[0]
    me = lax.axis_index("seq") * lax.axis_size("exp") + lax.axis_index("exp")
    first = (jnp.stack([me, me ^ 1]) * local_experts).astype(jnp.int32)
    gap = jnp.zeros((tok_rows, ROUTE_STEP - choose), BF)
    high, low = split(expert_weights)
    tail = jnp.zeros((tok_rows, 128 - 3 * ROUTE_STEP), BF)
    block = jnp.concatenate(
        [normed, expert_ids.astype(BF), gap, high, gap, low, gap, tail], axis=1
    )
    weights = (gate_up_weight, down, over_core(gate_up_weight), over_core(down))
    total = None
    after = ()
    for wave in range(lax.axis_size("seq") // 2):
        if wave:
            block = along_z(block, 1)
        one, two = (over_x, over_y) if wave % 2 == 0 else (over_y, over_x)
        by_one = one(block)
        by_two = two(block)
        both = two(by_one)
        own, sum_one, sum_two, sum_both = experts(
            (block, by_one, by_two, both), first, weights, after, capacity, choose
        )
        after = (own,)
        passed = added(sum_one, two(sum_both)).astype(BF)
        here = added(own, two(sum_two), one(passed))
        if wave:
            here = along_z(here.astype(BF), -wave).astype(F32)
        total = here if total is None else total + here
    return total


def route_some(normed, expert_ids, expert_weights, gate_up_weight, down, capacity):
    axes = ("seq", "exp")
    tok_rows, width = normed.shape
    choose = expert_ids.shape[1]
    local_experts = gate_up_weight.shape[0]
    expert_width = down.shape[1]
    devices = lax.axis_size("seq") * lax.axis_size("exp")
    experts_all = local_experts * devices
    flat_ids = expert_ids.reshape(-1)
    onehot = (flat_ids[:, None] == jnp.arange(experts_all, dtype=jnp.int32)[None, :]).astype(
        jnp.int32
    )
    rank = jnp.sum(jnp.cumsum(onehot, axis=0) * onehot, axis=1) - 1
    slot = flat_ids * capacity + rank
    token_of = jnp.arange(tok_rows * choose, dtype=jnp.int32) // choose
    send = jnp.zeros((experts_all * capacity, width), BF).at[slot].set(normed[token_of])
    both = jnp.einsum(
        "secd,edf->secf",
        lax.all_to_all(
            send.reshape(devices, local_experts, capacity, width),
            axes,
            split_axis=0,
            concat_axis=0,
            tiled=True,
        ),
        gate_up_weight,
        preferred_element_type=F32,
    )
    hidden = (jax.nn.silu(both[..., :expert_width]) * both[..., expert_width:]).astype(BF)
    back = lax.all_to_all(
        jnp.einsum("secf,efd->secd", hidden, down, preferred_element_type=F32).astype(BF),
        axes,
        split_axis=0,
        concat_axis=0,
        tiled=True,
    )
    back_rows = back.reshape(experts_all * capacity, width)[slot].astype(F32)
    return jnp.sum(
        back_rows.reshape(tok_rows, choose, width) * expert_weights[:, :, None], axis=1
    )


def local(
    stream,
    moe_gain,
    expert_ids,
    expert_weights,
    gate_up_weight,
    down,
    mixer_gain,
    qkv_weight,
    decay_log,
    write_rate,
):
    tok_rows, width = stream.shape
    choose = expert_ids.shape[1]
    seq_count = lax.axis_size("seq")
    devices = seq_count * lax.axis_size("exp")
    experts_all = gate_up_weight.shape[0] * devices
    capacity = max(2, (tok_rows * choose * 6 + experts_all * 5 - 1) // (experts_all * 5))
    normed = rms_scale(stream, moe_gain).astype(BF)
    planes = lax.axis_size("exp") == 4 and seq_count % 2 == 0 and choose <= ROUTE_STEP
    route = route_waves if planes and experts_all <= 256 else route_some
    moe = route(normed, expert_ids, expert_weights, gate_up_weight, down, capacity)
    mixed = (stream.astype(F32) + moe).astype(BF)
    normed_mix = rms_scale(mixed, mixer_gain).astype(BF)
    projected = jnp.einsum(
        "rd,pde->pre",
        lax.all_gather(normed_mix, "exp", axis=0, tiled=True),
        qkv_weight,
        preferred_element_type=F32,
    )
    length = projected.shape[1]
    heads = decay_log.shape[1]
    blocks = length // CH
    sums = jnp.cumsum(decay_log.T.reshape(heads, blocks, CH), axis=-1)
    rates = write_rate.T.reshape(heads, blocks, CH)
    entering, local_out, ends = mixer(projected, sums, rates)
    if heads % seq_count == 0:
        dim = ends.shape[2] // 2
        each = heads // seq_count
        held = lax.all_to_all(ends, "seq", split_axis=0, concat_axis=0, tiled=True)
        held = held.reshape(seq_count, each, dim + 16, 2 * dim)
        states = jnp.stack([carry(held[:, i]) for i in range(each)], axis=1)
        arriving = lax.all_to_all(
            states.reshape(seq_count * each, dim, dim), "seq", split_axis=0, concat_axis=0, tiled=True
        )
    else:
        arriving = relay(ends, seq_count)
    return (mixed, finish(entering, local_out, arriving))


def solution(mesh):
    in_specs = (
        P(("seq", "exp"), None),
        P(),
        P(("seq", "exp"), None),
        P(("seq", "exp"), None),
        P(("seq", "exp"), None, None),
        P(("seq", "exp"), None, None),
        P(),
        P(None, None, "exp"),
        P("seq", "exp"),
        P("seq", "exp"),
    )
    out_specs = (P(("seq", "exp"), None), P("seq", "exp"))
    return jax.shard_map(local, mesh=mesh, in_specs=in_specs, out_specs=out_specs, check_vma=False)
```

```python
from functools import partial

import jax
import jax.numpy as jnp
from jax import lax
from jax.experimental import pallas as pl
from jax.experimental.pallas import tpu as pltpu
from jax.sharding import PartitionSpec as P

CH = 128
ROUTE_STEP = 16
VMEM_LIMIT = 56 * 1024 * 1024
BF = jnp.bfloat16
F32 = jnp.float32


def rms_scale(values, gain):
    wide = values.astype(F32)
    return wide * lax.rsqrt(jnp.mean(wide * wide, axis=-1, keepdims=True) + 1e-06) * gain


def dot(a, b):
    return jnp.dot(a, b, preferred_element_type=F32)


def split(a):
    high = a.astype(BF)
    return high, (a - high.astype(F32)).astype(BF)


def left_pair(a):
    high, low = split(a)
    return jnp.concatenate([high, low], axis=1)


def right_pair(b):
    high, low = split(b)
    row = jnp.concatenate([high, low], axis=1)
    return jnp.concatenate([row, row], axis=0)


def wide_product(a, b):
    columns = b.shape[1]
    both = dot(left_pair(a), right_pair(b))
    return both[:, :columns] + both[:, columns:]


def moe_kernel(capacity, choose, *refs):
    first_ref, *block_refs = refs[:5]
    weight_refs = refs[5:9]
    out_refs = refs[-9:-5]
    gate_up_ref, down_ref, rows_ref, back_ref, sem = refs[-5:]
    tok, wide = block_refs[0].shape
    width = rows_ref.shape[2]
    experts_here = gate_up_ref.shape[0]
    half = experts_here // 2
    expert_width = down_ref.shape[1]
    pair_rows = rows_ref.shape[1] // 2

    copies = []
    for e in range(experts_here):
        side, at = divmod(e, half)
        fetch_in = pltpu.make_async_copy(
            weight_refs[2 * side].at[at], gate_up_ref.at[e], sem.at[0, e]
        )
        fetch_out = pltpu.make_async_copy(
            weight_refs[2 * side + 1].at[at], down_ref.at[e], sem.at[1, e]
        )
        fetch_in.start()
        fetch_out.start()
        copies.append((fetch_in, fetch_out))

    matched, weights = [], []
    for block_ref in block_refs:
        routing = block_ref[:, width:].astype(F32).T
        ids = routing[:choose]
        scale = routing[ROUTE_STEP : ROUTE_STEP + choose]
        scale = scale + routing[2 * ROUTE_STEP : 2 * ROUTE_STEP + choose]
        for e in range(experts_here):
            side, at = divmod(e, half)
            hit = ids == (first_ref[side] + at).astype(F32)
            matched.append(jnp.max(jnp.where(hit, 1.0, 0.0), axis=0, keepdims=True))
            weights.append(jnp.sum(jnp.where(hit, scale, 0.0), axis=0, keepdims=True))
    match = jnp.concatenate(matched, axis=0)
    before = lax.broadcasted_iota(jnp.int32, (tok, tok), 0) < lax.broadcasted_iota(
        jnp.int32, (tok, tok), 1
    )
    rank = dot(match.astype(BF), jnp.where(before, 1.0, 0.0).astype(BF))
    rank = jnp.where(match > 0.5, rank, -1e4)
    row_number = lax.broadcasted_iota(jnp.int32, (pair_rows, 2 * tok), 0).astype(F32)
    picks = []
    for pair in range(2):
        x_pair = jnp.concatenate(
            [block_refs[2 * pair][:, :width], block_refs[2 * pair + 1][:, :width]], axis=0
        )
        here = []
        for e in range(experts_here):
            low = 2 * pair * experts_here + e
            high = low + experts_here
            place = jnp.concatenate(
                [rank[low : low + 1], rank[high : high + 1] + float(capacity)], axis=1
            )
            here.append(jnp.where(row_number == place, 1.0, 0.0))
        picks.append(here)
        chosen = dot(jnp.concatenate(here, axis=0).astype(BF), x_pair).astype(BF)
        for e in range(experts_here):
            rows_ref[e, pair * pair_rows : (pair + 1) * pair_rows, :] = chosen[
                e * pair_rows : (e + 1) * pair_rows
            ]
    for e in range(experts_here):
        copies[e][0].wait()
        both = dot(rows_ref[e], gate_up_ref[e])
        gate = both[:, :expert_width]
        hidden = (gate / (1.0 + jnp.exp(-gate)) * both[:, expert_width:]).astype(BF)
        copies[e][1].wait()
        back_ref[e] = dot(hidden, down_ref[e]).astype(BF)
    for pair in range(2):
        scaled, rows = [], []
        for e in range(experts_here):
            low = 2 * pair * experts_here + e
            high = low + experts_here
            weight = jnp.concatenate([weights[low], weights[high]], axis=1)
            scaled.append(picks[pair][e] * weight)
            rows.append(back_ref[e, pair * pair_rows : (pair + 1) * pair_rows, :])
        high_part, low_part = split(jnp.concatenate(scaled, axis=0))
        left = jnp.concatenate([high_part, low_part], axis=0)
        right = jnp.concatenate(rows + rows, axis=0)
        summed = lax.dot_general(
            left, right, (((0,), (0,)), ((), ())), preferred_element_type=F32
        ).astype(BF)
        out_refs[2 * pair][...] = summed[:tok]
        out_refs[2 * pair + 1][...] = summed[tok:]


def experts(blocks, first, weights, after, capacity, choose):
    tok, wide = blocks[0].shape
    gate_up_weight, down = weights[:2]
    local_experts, width, double = gate_up_weight.shape
    here = 2 * local_experts
    pair_rows = -(-2 * capacity // 16) * 16
    whole = pl.BlockSpec(memory_space=pltpu.VMEM)
    return pl.pallas_call(
        partial(moe_kernel, capacity, choose),
        in_specs=[pl.BlockSpec(memory_space=pltpu.SMEM)]
        + [whole] * 4
        + [pl.BlockSpec(memory_space=pl.ANY)] * (4 + len(after)),
        out_specs=[whole] * 4,
        out_shape=[jax.ShapeDtypeStruct((tok, width), BF)] * 4,
        scratch_shapes=[
            pltpu.VMEM((here,) + gate_up_weight.shape[1:], BF),
            pltpu.VMEM((here,) + down.shape[1:], BF),
            pltpu.VMEM((here, 2 * pair_rows, width), BF),
            pltpu.VMEM((here, 2 * pair_rows, width), BF),
            pltpu.SemaphoreType.DMA((2, here)),
        ],
        compiler_params=pltpu.CompilerParams(vmem_limit_bytes=VMEM_LIMIT),
        cost_estimate=pl.CostEstimate(
            flops=here * pair_rows * width * double // 4,
            bytes_accessed=tok * width,
            transcendentals=0,
        ),
        name="experts",
    )(first, *blocks, *weights, *after)


def unit_rows(values):
    return values * lax.rsqrt(jnp.sum(values * values, axis=-1, keepdims=True) + 1e-06)


def mixer_kernel(q_ref, k_ref, v_ref, sum_ref, rate_ref, enter_ref, local_ref, end_ref):
    length, dim = q_ref.shape[1:]
    blocks = length // CH
    span = range(blocks)
    rows = lax.broadcasted_iota(jnp.int32, (CH, CH), 0)
    columns = lax.broadcasted_iota(jnp.int32, (CH, CH), 1)
    strict = rows > columns
    inclusive = rows >= columns
    identity = jnp.where(rows == columns, 1.0, 0.0)
    cut = [slice(n * CH, (n + 1) * CH) for n in span]
    query = [unit_rows(q_ref[0, cut[n], :]) for n in span]
    key = [unit_rows(k_ref[0, cut[n], :]) for n in span]
    value = [v_ref[0, cut[n], :] for n in span]
    across = [jnp.broadcast_to(sum_ref[0, n : n + 1, :], (CH, CH)) for n in span]
    down_rows = [across[n].T for n in span]
    rate = [jnp.broadcast_to(rate_ref[0, n : n + 1, :], (CH, CH)).T for n in span]
    fade = [jnp.exp(jnp.where(inclusive, down_rows[n] - across[n], 0.0)) for n in span]
    growth = [jnp.exp(down_rows[n]) for n in span]
    last = [jnp.broadcast_to(down_rows[n][CH - 1 : CH, :], (CH, CH)) for n in span]
    remaining = [jnp.exp(last[n] - down_rows[n]) for n in span]
    whole = [jnp.exp(last[n]) for n in span]
    both = []
    for n in span:
        high, low = split(key[n])
        left = jnp.concatenate(
            [jnp.concatenate([high, low], axis=1), left_pair(query[n])], axis=0
        )
        hh = jnp.concatenate([high, high], axis=1)
        ll = jnp.concatenate([low, low], axis=1)
        right_t = jnp.concatenate([hh, ll], axis=0)
        got = lax.dot_general(left, right_t, (((1,), (1,)), ((), ())), preferred_element_type=F32)
        both.append(got[:, :CH] + got[:, CH:])
    lower = [jnp.where(strict, rate[n] * fade[n] * both[n][:CH], 0.0) for n in span]
    masked = [jnp.where(inclusive, fade[n] * both[n][CH:], 0.0) for n in span]

    def ring(size):
        shared = (rows // (2 * size)) == (columns // (2 * size))
        return shared & (rows // size % 2 == 1) & (columns // size % 2 == 0)

    inverse = [identity - jnp.where(ring(1), lower[n], 0.0) for n in span]
    size = 2
    while size < CH:
        here = ring(size)
        step = [wide_product(jnp.where(here, lower[n], 0.0), inverse[n]) for n in span]
        inverse = [inverse[n] - wide_product(inverse[n], step[n]) for n in span]
        size *= 2
    solved = [
        wide_product(
            inverse[n],
            jnp.concatenate([rate[n] * growth[n] * key[n], rate[n] * value[n]], axis=1),
        )
        for n in span
    ]
    ended = [wide_product((remaining[n] * key[n]).T, solved[n]) for n in span]
    probed = [wide_product(masked[n], solved[n]) for n in span]
    state = None
    total_decay = None
    for n in span:
        entering = growth[n] * query[n] - probed[n][:, :dim]
        output = probed[n][:, dim:]
        transition = whole[n] * identity - ended[n][:, :dim]
        written = ended[n][:, dim:]
        if n == 0:
            state = jnp.concatenate([transition, written], axis=1)
            total_decay = whole[n]
        else:
            moved = wide_product(jnp.concatenate([entering, transition], axis=0), state)
            entering = moved[:CH, :dim]
            output = output + moved[:CH, dim:]
            state = jnp.concatenate([moved[CH:, :dim], moved[CH:, dim:] + written], axis=1)
            total_decay = total_decay * whole[n]
        enter_ref[cut[n], :] = entering
        local_ref[cut[n], :] = output
    end_ref[0, :dim, :dim] = (total_decay * identity - state[:, :dim]).astype(BF)
    end_ref[0, :dim, dim:] = state[:, dim:].astype(BF)
    end_ref[0, dim:, :] = left_pair(total_decay[:16])


def mixer(projected, sums, rates):
    _, length, columns = projected.shape
    heads, blocks, _ = sums.shape
    dim = columns // heads
    part = lambda p: pl.BlockSpec((1, length, dim), lambda h, p=p: (p, 0, h))
    per_head = pl.BlockSpec((1, blocks, CH), lambda h: (h, 0, 0))
    per_column = pl.BlockSpec((length, dim), lambda h: (0, h))
    return pl.pallas_call(
        mixer_kernel,
        grid=(heads,),
        in_specs=[part(0), part(1), part(2), per_head, per_head],
        out_specs=[per_column, per_column, pl.BlockSpec((1, dim + 16, 2 * dim), lambda h: (h, 0, 0))],
        out_shape=[
            jax.ShapeDtypeStruct((length, columns), F32),
            jax.ShapeDtypeStruct((length, columns), F32),
            jax.ShapeDtypeStruct((heads, dim + 16, 2 * dim), BF),
        ],
        compiler_params=pltpu.CompilerParams(vmem_limit_bytes=VMEM_LIMIT),
        name="mixer",
    )(projected, projected, projected, sums, rates)


def carry_kernel(ends_ref, states_ref):
    segments, _, double = ends_ref.shape
    dim = double // 2
    state = jnp.zeros((dim, dim), F32)
    for s in range(segments):
        states_ref[s] = state.astype(BF)
        if s < segments - 1:
            decay = ends_ref[s, dim : dim + 1, :].astype(F32)
            decay = decay[:, :dim] + decay[:, dim:]
            removed = dot(ends_ref[s, :dim, :dim], left_pair(state))
            removed = removed[:, :dim] + removed[:, dim:]
            state = decay * state - removed + ends_ref[s, :dim, dim:].astype(F32)


def carry(ends):
    segments, _, double = ends.shape
    return pl.pallas_call(
        carry_kernel,
        out_shape=jax.ShapeDtypeStruct((segments, double // 2, double // 2), BF),
        compiler_params=pltpu.CompilerParams(vmem_limit_bytes=VMEM_LIMIT),
        name="carry",
    )(ends)


def finish_kernel(enter_ref, local_ref, state_ref, core_ref):
    state = state_ref[0]
    core_ref[...] = local_ref[...] + dot(
        left_pair(enter_ref[...]), jnp.concatenate([state, state], axis=0)
    )


def finish(entering, local_out, states):
    length, columns = entering.shape
    heads, dim, _ = states.shape
    per_column = pl.BlockSpec((length, dim), lambda h: (0, h))
    return pl.pallas_call(
        finish_kernel,
        grid=(heads,),
        in_specs=[per_column, per_column, pl.BlockSpec((1, dim, dim), lambda h: (h, 0, 0))],
        out_specs=per_column,
        out_shape=jax.ShapeDtypeStruct((length, columns), F32),
        compiler_params=pltpu.CompilerParams(vmem_limit_bytes=VMEM_LIMIT),
        name="finish",
    )(entering, local_out, states)


def relay(ends, seq_count):
    dim = ends.shape[2] // 2
    pairs = [(i, i + 1) for i in range(seq_count - 1)]
    removed, written = ends[:, :dim, :dim].astype(F32), ends[:, :dim, dim:].astype(F32)
    decay = ends[:, dim, :1].astype(F32) + ends[:, dim, dim : dim + 1].astype(F32)

    def step(_, incoming):
        outgoing = decay[:, :, None] * incoming + written
        outgoing = outgoing - jnp.einsum(
            "hij,hjk->hik", removed, incoming, precision=lax.Precision.HIGHEST
        )
        return lax.ppermute(outgoing, "seq", pairs)

    return lax.fori_loop(0, seq_count - 1, step, jnp.zeros_like(written)).astype(BF)


def move(values, change):
    exp_count = lax.axis_size("exp")
    pairs = []
    for s in range(lax.axis_size("seq")):
        for e in range(exp_count):
            to_s, to_e = change(s, e)
            pairs.append((s * exp_count + e, to_s * exp_count + to_e))
    return lax.ppermute(values, ("seq", "exp"), pairs)


def over_x(values):
    return move(values, lambda s, e: (s ^ 1, e))


def over_y(values):
    return move(values, lambda s, e: (s, e ^ 2))


def over_core(values):
    return move(values, lambda s, e: (s, e ^ 1))


def along_z(values, by):
    count = lax.axis_size("seq")
    return move(values, lambda s, e: ((s + 2 * by) % count, e))


def added(*terms):
    total = terms[0].astype(F32)
    for term in terms[1:]:
        total = total + term.astype(F32)
    return total


def route_waves(normed, expert_ids, expert_weights, gate_up_weight, down, capacity):
    tok_rows, width = normed.shape
    choose = expert_ids.shape[1]
    local_experts = gate_up_weight.shape[0]
    me = lax.axis_index("seq") * lax.axis_size("exp") + lax.axis_index("exp")
    first = (jnp.stack([me, me ^ 1]) * local_experts).astype(jnp.int32)
    gap = jnp.zeros((tok_rows, ROUTE_STEP - choose), BF)
    high, low = split(expert_weights)
    tail = jnp.zeros((tok_rows, 128 - 3 * ROUTE_STEP), BF)
    block = jnp.concatenate(
        [normed, expert_ids.astype(BF), gap, high, gap, low, gap, tail], axis=1
    )
    weights = (gate_up_weight, down, over_core(gate_up_weight), over_core(down))
    total = None
    due = [(), (), (), ()]
    diagonal = sum_below = None
    for wave in range(lax.axis_size("seq") // 2):
        if wave:
            block = along_z(block, 1)
        one, two = (over_x, over_y) if wave % 4 < 2 else (over_y, over_x)
        by_one = one(block)
        by_two = two(block)
        diagonal = two(by_one) if wave % 2 == 0 else along_z(diagonal, 1)
        own, sum_one, sum_two, sum_both = experts(
            (block, by_one, by_two, diagonal), first, weights, due[0], capacity, choose
        )
        due = due[1:] + [()]
        due[0] += (own,)
        from_two = two(sum_two)
        if wave % 2 == 0:
            sum_below = along_z(sum_both, 1)
            here = added(own, from_two, one(sum_one))
            due[1] += (from_two, sum_below)
        else:
            sum_both = added(sum_both, sum_below).astype(BF)
            passed = added(sum_one, two(sum_both)).astype(BF)
            here = added(own, from_two, one(passed))
            due[1] += (from_two, passed)
        if wave:
            here = along_z(here.astype(BF), -wave).astype(F32)
        total = here if total is None else total + here
    return total


def route_some(normed, expert_ids, expert_weights, gate_up_weight, down, capacity):
    axes = ("seq", "exp")
    tok_rows, width = normed.shape
    choose = expert_ids.shape[1]
    local_experts = gate_up_weight.shape[0]
    expert_width = down.shape[1]
    devices = lax.axis_size("seq") * lax.axis_size("exp")
    experts_all = local_experts * devices
    flat_ids = expert_ids.reshape(-1)
    onehot = (flat_ids[:, None] == jnp.arange(experts_all, dtype=jnp.int32)[None, :]).astype(
        jnp.int32
    )
    rank = jnp.sum(jnp.cumsum(onehot, axis=0) * onehot, axis=1) - 1
    slot = flat_ids * capacity + rank
    token_of = jnp.arange(tok_rows * choose, dtype=jnp.int32) // choose
    send = jnp.zeros((experts_all * capacity, width), BF).at[slot].set(normed[token_of])
    both = jnp.einsum(
        "secd,edf->secf",
        lax.all_to_all(
            send.reshape(devices, local_experts, capacity, width),
            axes,
            split_axis=0,
            concat_axis=0,
            tiled=True,
        ),
        gate_up_weight,
        preferred_element_type=F32,
    )
    hidden = (jax.nn.silu(both[..., :expert_width]) * both[..., expert_width:]).astype(BF)
    back = lax.all_to_all(
        jnp.einsum("secf,efd->secd", hidden, down, preferred_element_type=F32).astype(BF),
        axes,
        split_axis=0,
        concat_axis=0,
        tiled=True,
    )
    back_rows = back.reshape(experts_all * capacity, width)[slot].astype(F32)
    return jnp.sum(
        back_rows.reshape(tok_rows, choose, width) * expert_weights[:, :, None], axis=1
    )


def local(
    stream,
    moe_gain,
    expert_ids,
    expert_weights,
    gate_up_weight,
    down,
    mixer_gain,
    qkv_weight,
    decay_log,
    write_rate,
):
    tok_rows, width = stream.shape
    choose = expert_ids.shape[1]
    seq_count = lax.axis_size("seq")
    devices = seq_count * lax.axis_size("exp")
    experts_all = gate_up_weight.shape[0] * devices
    capacity = max(2, (tok_rows * choose * 6 + experts_all * 5 - 1) // (experts_all * 5))
    normed = rms_scale(stream, moe_gain).astype(BF)
    planes = lax.axis_size("exp") == 4 and seq_count % 4 == 0 and choose <= ROUTE_STEP
    route = route_waves if planes and experts_all <= 256 else route_some
    moe = route(normed, expert_ids, expert_weights, gate_up_weight, down, capacity)
    mixed = (stream.astype(F32) + moe).astype(BF)
    normed_mix = rms_scale(mixed, mixer_gain).astype(BF)
    projected = jnp.einsum(
        "rd,pde->pre",
        lax.all_gather(normed_mix, "exp", axis=0, tiled=True),
        qkv_weight,
        preferred_element_type=F32,
    )
    length = projected.shape[1]
    heads = decay_log.shape[1]
    blocks = length // CH
    sums = jnp.cumsum(decay_log.T.reshape(heads, blocks, CH), axis=-1)
    rates = write_rate.T.reshape(heads, blocks, CH)
    entering, local_out, ends = mixer(projected, sums, rates)
    if heads % seq_count == 0:
        dim = ends.shape[2] // 2
        each = heads // seq_count
        held = lax.all_to_all(ends, "seq", split_axis=0, concat_axis=0, tiled=True)
        held = held.reshape(seq_count, each, dim + 16, 2 * dim)
        states = jnp.stack([carry(held[:, i]) for i in range(each)], axis=1)
        arriving = lax.all_to_all(
            states.reshape(seq_count * each, dim, dim), "seq", split_axis=0, concat_axis=0, tiled=True
        )
    else:
        arriving = relay(ends, seq_count)
    return (mixed, finish(entering, local_out, arriving))


def solution(mesh):
    in_specs = (
        P(("seq", "exp"), None),
        P(),
        P(("seq", "exp"), None),
        P(("seq", "exp"), None),
        P(("seq", "exp"), None, None),
        P(("seq", "exp"), None, None),
        P(),
        P(None, None, "exp"),
        P("seq", "exp"),
        P("seq", "exp"),
    )
    out_specs = (P(("seq", "exp"), None), P("seq", "exp"))
    return jax.shard_map(local, mesh=mesh, in_specs=in_specs, out_specs=out_specs, check_vma=False)
```

```python
from functools import partial

import jax
import jax.numpy as jnp
from jax import lax
from jax.experimental import pallas as pl
from jax.experimental.pallas import tpu as pltpu
from jax.sharding import PartitionSpec as P

CH = 128
ROUTE_STEP = 16
VMEM_LIMIT = 56 * 1024 * 1024
BF = jnp.bfloat16
F32 = jnp.float32


def rms_scale(values, gain):
    wide = values.astype(F32)
    return wide * lax.rsqrt(jnp.mean(wide * wide, axis=-1, keepdims=True) + 1e-06) * gain


def dot(a, b):
    return jnp.dot(a, b, preferred_element_type=F32)


def split(a):
    high = a.astype(BF)
    return high, (a - high.astype(F32)).astype(BF)


def left_pair(a):
    high, low = split(a)
    return jnp.concatenate([high, low], axis=1)


def right_pair(b):
    high, low = split(b)
    row = jnp.concatenate([high, low], axis=1)
    return jnp.concatenate([row, row], axis=0)


def wide_product(a, b):
    columns = b.shape[1]
    both = dot(left_pair(a), right_pair(b))
    return both[:, :columns] + both[:, columns:]


def moe_kernel(capacity, choose, *refs):
    first_ref, *block_refs = refs[:5]
    weight_refs = refs[5:9]
    out_refs = refs[-9:-5]
    gate_up_ref, down_ref, rows_ref, back_ref, sem = refs[-5:]
    tok, wide = block_refs[0].shape
    width = rows_ref.shape[2]
    experts_here = gate_up_ref.shape[0]
    half = experts_here // 2
    expert_width = down_ref.shape[1]
    pair_rows = rows_ref.shape[1] // 2

    copies = []
    for e in range(experts_here):
        side, at = divmod(e, half)
        fetch_in = pltpu.make_async_copy(
            weight_refs[2 * side].at[at], gate_up_ref.at[e], sem.at[0, e]
        )
        fetch_out = pltpu.make_async_copy(
            weight_refs[2 * side + 1].at[at], down_ref.at[e], sem.at[1, e]
        )
        fetch_in.start()
        fetch_out.start()
        copies.append((fetch_in, fetch_out))

    matched, weights = [], []
    for block_ref in block_refs:
        routing = block_ref[:, width:].astype(F32).T
        ids = routing[:choose]
        scale = routing[ROUTE_STEP : ROUTE_STEP + choose]
        scale = scale + routing[2 * ROUTE_STEP : 2 * ROUTE_STEP + choose]
        for e in range(experts_here):
            side, at = divmod(e, half)
            hit = ids == (first_ref[side] + at).astype(F32)
            matched.append(jnp.max(jnp.where(hit, 1.0, 0.0), axis=0, keepdims=True))
            weights.append(jnp.sum(jnp.where(hit, scale, 0.0), axis=0, keepdims=True))
    match = jnp.concatenate(matched, axis=0)
    before = lax.broadcasted_iota(jnp.int32, (tok, tok), 0) < lax.broadcasted_iota(
        jnp.int32, (tok, tok), 1
    )
    rank = dot(match.astype(BF), jnp.where(before, 1.0, 0.0).astype(BF))
    rank = jnp.where(match > 0.5, rank, -1e4)
    row_number = lax.broadcasted_iota(jnp.int32, (pair_rows, 2 * tok), 0).astype(F32)
    picks = []
    for pair in range(2):
        x_pair = jnp.concatenate(
            [block_refs[2 * pair][:, :width], block_refs[2 * pair + 1][:, :width]], axis=0
        )
        here = []
        for e in range(experts_here):
            low = 2 * pair * experts_here + e
            high = low + experts_here
            place = jnp.concatenate(
                [rank[low : low + 1], rank[high : high + 1] + float(capacity)], axis=1
            )
            here.append(jnp.where(row_number == place, 1.0, 0.0))
        picks.append(here)
        chosen = dot(jnp.concatenate(here, axis=0).astype(BF), x_pair).astype(BF)
        for e in range(experts_here):
            rows_ref[e, pair * pair_rows : (pair + 1) * pair_rows, :] = chosen[
                e * pair_rows : (e + 1) * pair_rows
            ]
    for e in range(experts_here):
        copies[e][0].wait()
        both = dot(rows_ref[e], gate_up_ref[e])
        gate = both[:, :expert_width]
        hidden = (gate / (1.0 + jnp.exp(-gate)) * both[:, expert_width:]).astype(BF)
        copies[e][1].wait()
        back_ref[e] = dot(hidden, down_ref[e]).astype(BF)
    for pair in range(2):
        scaled, rows = [], []
        for e in range(experts_here):
            low = 2 * pair * experts_here + e
            high = low + experts_here
            weight = jnp.concatenate([weights[low], weights[high]], axis=1)
            scaled.append(picks[pair][e] * weight)
            rows.append(back_ref[e, pair * pair_rows : (pair + 1) * pair_rows, :])
        high_part, low_part = split(jnp.concatenate(scaled, axis=0))
        left = jnp.concatenate([high_part, low_part], axis=0)
        right = jnp.concatenate(rows + rows, axis=0)
        summed = lax.dot_general(
            left, right, (((0,), (0,)), ((), ())), preferred_element_type=F32
        ).astype(BF)
        out_refs[2 * pair][...] = summed[:tok]
        out_refs[2 * pair + 1][...] = summed[tok:]


def experts(blocks, first, weights, after, capacity, choose):
    tok, wide = blocks[0].shape
    gate_up_weight, down = weights[:2]
    local_experts, width, double = gate_up_weight.shape
    here = 2 * local_experts
    pair_rows = -(-2 * capacity // 16) * 16
    whole = pl.BlockSpec(memory_space=pltpu.VMEM)
    return pl.pallas_call(
        partial(moe_kernel, capacity, choose),
        in_specs=[pl.BlockSpec(memory_space=pltpu.SMEM)]
        + [whole] * 4
        + [pl.BlockSpec(memory_space=pl.ANY)] * (4 + len(after)),
        out_specs=[whole] * 4,
        out_shape=[jax.ShapeDtypeStruct((tok, width), BF)] * 4,
        scratch_shapes=[
            pltpu.VMEM((here,) + gate_up_weight.shape[1:], BF),
            pltpu.VMEM((here,) + down.shape[1:], BF),
            pltpu.VMEM((here, 2 * pair_rows, width), BF),
            pltpu.VMEM((here, 2 * pair_rows, width), BF),
            pltpu.SemaphoreType.DMA((2, here)),
        ],
        compiler_params=pltpu.CompilerParams(vmem_limit_bytes=VMEM_LIMIT),
        cost_estimate=pl.CostEstimate(
            flops=here * pair_rows * width * double // 4,
            bytes_accessed=tok * width,
            transcendentals=0,
        ),
        name="experts",
    )(first, *blocks, *weights, *after)


def unit_rows(values):
    return values * lax.rsqrt(jnp.sum(values * values, axis=-1, keepdims=True) + 1e-06)


def tiles():
    rows = lax.broadcasted_iota(jnp.int32, (CH, CH), 0)
    columns = lax.broadcasted_iota(jnp.int32, (CH, CH), 1)
    return rows, columns


def against_rows(a, b):
    high, low = split(b)
    right = jnp.concatenate(
        [jnp.concatenate([high, high], axis=1), jnp.concatenate([low, low], axis=1)], axis=0
    )
    both = lax.dot_general(
        left_pair(a), right, (((1,), (1,)), ((), ())), preferred_element_type=F32
    )
    return both[:, : b.shape[0]] + both[:, b.shape[0] :]


def chunk_kernel(place_ref, x_ref, w_ref, sum_ref, rate_ref, *refs):
    q_ref, k_ref, solved_ref, moved_ref = refs[-4:]
    heads, chunks, _ = sum_ref.shape[1:]
    dim = w_ref.shape[2] // heads
    rows, columns = tiles()
    strict = rows > columns
    identity = jnp.where(rows == columns, 1.0, 0.0)
    x = x_ref[...]
    query = dot(x, w_ref[0])
    key = dot(x, w_ref[1])
    value = dot(x, w_ref[2])
    units = [(h, n) for h in range(heads) for n in range(chunks)]

    def part(values, h, n):
        return values[n * CH : (n + 1) * CH, h * dim : (h + 1) * dim]

    keys, values, lowers, rates, growths, remains, wholes = [], [], [], [], [], [], []
    for h, n in units:
        q_ref[n * CH : (n + 1) * CH, h * dim : (h + 1) * dim] = unit_rows(part(query, h, n))
        unit = unit_rows(part(key, h, n))
        k_ref[n * CH : (n + 1) * CH, h * dim : (h + 1) * dim] = unit
        keys.append(unit)
        values.append(part(value, h, n))
    for u, (h, n) in enumerate(units):
        across = jnp.broadcast_to(sum_ref[0, h, n : n + 1, :], (CH, CH))
        along = across.T
        rate = jnp.broadcast_to(rate_ref[0, h, n : n + 1, :], (CH, CH)).T
        last = jnp.broadcast_to(along[CH - 1 : CH, :], (CH, CH))
        fade = jnp.exp(jnp.where(strict, along - across, 0.0))
        rates.append(rate)
        growths.append(jnp.exp(along))
        remains.append(jnp.exp(last - along))
        wholes.append(jnp.exp(last))
        lowers.append(jnp.where(strict, rate * fade * against_rows(keys[u], keys[u]), 0.0))

    def ring(size):
        shared = (rows // (2 * size)) == (columns // (2 * size))
        return shared & (rows // size % 2 == 1) & (columns // size % 2 == 0)

    span = range(len(units))
    inverse = [identity - jnp.where(ring(1), lowers[u], 0.0) for u in span]
    size = 2
    while size < CH:
        here = ring(size)
        step = [wide_product(jnp.where(here, lowers[u], 0.0), inverse[u]) for u in span]
        inverse = [inverse[u] - wide_product(inverse[u], step[u]) for u in span]
        size *= 2
    solved = [
        wide_product(
            inverse[u],
            jnp.concatenate([rates[u] * growths[u] * keys[u], rates[u] * values[u]], axis=1),
        )
        for u in span
    ]
    for u, (h, n) in enumerate(units):
        solved_ref[h, n] = solved[u]
        ended = wide_product((remains[u] * keys[u]).T, solved[u])
        moved_ref[h, n, :, :dim] = wholes[u] * identity - ended[:, :dim]
        moved_ref[h, n, :, dim:] = ended[:, dim:]


def chunks_of(x, place, qkv_weight, sums, rates, before):
    rows, width = x.shape
    _, _, columns = qkv_weight.shape
    parts, heads, chunks, _ = sums.shape
    dim = columns // heads
    step = min(4, heads)
    at_rows = pl.BlockSpec((rows, step * dim), lambda i, place: (place[0], i))
    at_chunks = pl.BlockSpec((step, chunks, CH, 2 * dim), lambda i, place: (i, place[0], 0, 0))
    per_head = pl.BlockSpec((1, step, chunks, CH), lambda i, place: (place[0], i, 0, 0))
    return pl.pallas_call(
        chunk_kernel,
        grid_spec=pltpu.PrefetchScalarGridSpec(
            num_scalar_prefetch=1,
            grid=(heads // step,),
            in_specs=[
                pl.BlockSpec((rows, width), lambda i, place: (0, 0)),
                pl.BlockSpec((3, width, step * dim), lambda i, place: (0, 0, i)),
                per_head,
                per_head,
            ]
            + [pl.BlockSpec(memory_space=pl.ANY)] * len(before),
            out_specs=[at_rows, at_rows, at_chunks, at_chunks],
        ),
        out_shape=[jax.ShapeDtypeStruct((parts * rows, columns), F32)] * 2
        + [jax.ShapeDtypeStruct((heads, parts * chunks, CH, 2 * dim), F32)] * 2,
        input_output_aliases={5 + i: i for i in range(len(before))},
        compiler_params=pltpu.CompilerParams(vmem_limit_bytes=VMEM_LIMIT),
        name="chunks",
    )(place, x, qkv_weight, sums, rates, *before)


def chain_kernel(moved_ref, sum_ref, starts_ref, end_ref):
    heads, chunks, dim, _ = moved_ref.shape
    rows, columns = tiles()
    identity = jnp.where(rows == columns, 1.0, 0.0)
    span = range(heads)
    state = [moved_ref[h, 0] for h in span]
    for n in range(1, chunks):
        for h in span:
            starts_ref[h, n - 1] = state[h]
        moved = [wide_product(moved_ref[h, n, :, :dim], state[h]) for h in span]
        state = [
            jnp.concatenate([moved[h][:, :dim], moved[h][:, dim:] + moved_ref[h, n, :, dim:]], axis=1)
            for h in span
        ]
    for h in span:
        decay = sum_ref[h, 0:1, :]
        for n in range(1, chunks):
            decay = decay + sum_ref[h, n : n + 1, :]
        decay = jnp.exp(jnp.broadcast_to(decay, (CH, CH)).T[CH - 1 : CH, :])
        decay = jnp.broadcast_to(decay, (CH, CH))
        end_ref[h, :dim, :dim] = (decay * identity - state[h][:, :dim]).astype(BF)
        end_ref[h, :dim, dim:] = state[h][:, dim:].astype(BF)
        end_ref[h, dim:, :] = left_pair(decay[:16])


def chain(moved, sums):
    heads, chunks, dim, double = moved.shape
    return pl.pallas_call(
        chain_kernel,
        out_shape=[
            jax.ShapeDtypeStruct((heads, chunks - 1, dim, double), F32),
            jax.ShapeDtypeStruct((heads, dim + 16, double), BF),
        ],
        compiler_params=pltpu.CompilerParams(vmem_limit_bytes=VMEM_LIMIT),
        name="chain",
    )(moved, sums)


def read_kernel(q_ref, k_ref, solved_ref, starts_ref, sum_ref, enter_ref, local_ref):
    heads, chunks, _ = sum_ref.shape
    dim = starts_ref.shape[2]
    rows, columns = tiles()
    inclusive = rows >= columns
    units = [(h, n) for h in range(heads) for n in range(chunks)]
    for h, n in units:
        cut = slice(n * CH, (n + 1) * CH), slice(h * dim, (h + 1) * dim)
        across = jnp.broadcast_to(sum_ref[h, n : n + 1, :], (CH, CH))
        along = across.T
        fade = jnp.exp(jnp.where(inclusive, along - across, 0.0))
        query = q_ref[cut]
        masked = jnp.where(inclusive, fade * against_rows(query, k_ref[cut]), 0.0)
        probed = wide_product(masked, solved_ref[h, n])
        entering = jnp.exp(along) * query - probed[:, :dim]
        output = probed[:, dim:]
        if n:
            begun = wide_product(entering, starts_ref[h, n - 1])
            entering = begun[:, :dim]
            output = output + begun[:, dim:]
        enter_ref[cut] = entering
        local_ref[cut] = output


def read(query, key, solved, starts, sums):
    length, columns = query.shape
    heads, chunks, _ = sums.shape
    dim = columns // heads
    step = 2 if heads % 2 == 0 else 1
    per_column = pl.BlockSpec((length, step * dim), lambda h: (0, h))
    four = lambda h: (h, 0, 0, 0)
    return pl.pallas_call(
        read_kernel,
        grid=(heads // step,),
        in_specs=[
            per_column,
            per_column,
            pl.BlockSpec((step, chunks, CH, 2 * dim), four),
            pl.BlockSpec((step, chunks - 1, dim, 2 * dim), four),
            pl.BlockSpec((step, chunks, CH), lambda h: (h, 0, 0)),
        ],
        out_specs=[per_column, per_column],
        out_shape=[jax.ShapeDtypeStruct((length, columns), F32)] * 2,
        compiler_params=pltpu.CompilerParams(vmem_limit_bytes=VMEM_LIMIT),
        name="read",
    )(query, key, solved, starts, sums)


def carry_kernel(ends_ref, states_ref):
    segments, _, double = ends_ref.shape
    dim = double // 2
    state = jnp.zeros((dim, dim), F32)
    for s in range(segments):
        states_ref[s] = state.astype(BF)
        if s < segments - 1:
            decay = ends_ref[s, dim : dim + 1, :].astype(F32)
            decay = decay[:, :dim] + decay[:, dim:]
            removed = dot(ends_ref[s, :dim, :dim], left_pair(state))
            removed = removed[:, :dim] + removed[:, dim:]
            state = decay * state - removed + ends_ref[s, :dim, dim:].astype(F32)


def carry(ends):
    segments, _, double = ends.shape
    return pl.pallas_call(
        carry_kernel,
        out_shape=jax.ShapeDtypeStruct((segments, double // 2, double // 2), BF),
        compiler_params=pltpu.CompilerParams(vmem_limit_bytes=VMEM_LIMIT),
        name="carry",
    )(ends)


def finish_kernel(enter_ref, local_ref, state_ref, core_ref):
    heads, dim, _ = state_ref.shape
    for h in range(heads):
        cut = slice(h * dim, (h + 1) * dim)
        state = state_ref[h]
        core_ref[:, cut] = local_ref[:, cut] + dot(
            left_pair(enter_ref[:, cut]), jnp.concatenate([state, state], axis=0)
        )


def finish(entering, local_out, states):
    length, columns = entering.shape
    heads, dim, _ = states.shape
    step = 2 if heads % 2 == 0 else 1
    per_column = pl.BlockSpec((length, step * dim), lambda h: (0, h))
    return pl.pallas_call(
        finish_kernel,
        grid=(heads // step,),
        in_specs=[per_column, per_column, pl.BlockSpec((step, dim, dim), lambda h: (h, 0, 0))],
        out_specs=per_column,
        out_shape=jax.ShapeDtypeStruct((length, columns), F32),
        compiler_params=pltpu.CompilerParams(vmem_limit_bytes=VMEM_LIMIT),
        name="finish",
    )(entering, local_out, states)


def relay(ends, seq_count):
    dim = ends.shape[2] // 2
    pairs = [(i, i + 1) for i in range(seq_count - 1)]
    removed, written = ends[:, :dim, :dim].astype(F32), ends[:, :dim, dim:].astype(F32)
    decay = ends[:, dim, :1].astype(F32) + ends[:, dim, dim : dim + 1].astype(F32)

    def step(_, incoming):
        outgoing = decay[:, :, None] * incoming + written
        outgoing = outgoing - jnp.einsum(
            "hij,hjk->hik", removed, incoming, precision=lax.Precision.HIGHEST
        )
        return lax.ppermute(outgoing, "seq", pairs)

    return lax.fori_loop(0, seq_count - 1, step, jnp.zeros_like(written)).astype(BF)


def move(values, change):
    exp_count = lax.axis_size("exp")
    pairs = []
    for s in range(lax.axis_size("seq")):
        for e in range(exp_count):
            to_s, to_e = change(s, e)
            pairs.append((s * exp_count + e, to_s * exp_count + to_e))
    return lax.ppermute(values, ("seq", "exp"), pairs)


def over_x(values):
    return move(values, lambda s, e: (s ^ 1, e))


def over_y(values):
    return move(values, lambda s, e: (s, e ^ 2))


def over_core(values):
    return move(values, lambda s, e: (s, e ^ 1))


def along_z(values, by):
    count = lax.axis_size("seq")
    return move(values, lambda s, e: ((s + 2 * by) % count, e))


def added(*terms):
    total = terms[0].astype(F32)
    for term in terms[1:]:
        total = total + term.astype(F32)
    return total


def route_waves(normed, expert_ids, expert_weights, gate_up_weight, down, capacity):
    tok_rows, width = normed.shape
    choose = expert_ids.shape[1]
    local_experts = gate_up_weight.shape[0]
    me = lax.axis_index("seq") * lax.axis_size("exp") + lax.axis_index("exp")
    first = (jnp.stack([me, me ^ 1]) * local_experts).astype(jnp.int32)
    gap = jnp.zeros((tok_rows, ROUTE_STEP - choose), BF)
    high, low = split(expert_weights)
    tail = jnp.zeros((tok_rows, 128 - 3 * ROUTE_STEP), BF)
    block = jnp.concatenate(
        [normed, expert_ids.astype(BF), gap, high, gap, low, gap, tail], axis=1
    )
    weights = (gate_up_weight, down, over_core(gate_up_weight), over_core(down))
    total = None
    due = [(), (), (), ()]
    diagonal = sum_below = None
    for wave in range(lax.axis_size("seq") // 2):
        if wave:
            block = along_z(block, 1)
        one, two = (over_x, over_y) if wave % 4 < 2 else (over_y, over_x)
        by_one = one(block)
        by_two = two(block)
        diagonal = two(by_one) if wave % 2 == 0 else along_z(diagonal, 1)
        own, sum_one, sum_two, sum_both = experts(
            (block, by_one, by_two, diagonal), first, weights, due[0], capacity, choose
        )
        due = due[1:] + [()]
        due[0] += (own,)
        from_two = two(sum_two)
        if wave % 2 == 0:
            sum_below = along_z(sum_both, 1)
            here = added(own, from_two, one(sum_one))
            due[1] += (from_two, sum_below)
        else:
            sum_both = added(sum_both, sum_below).astype(BF)
            passed = added(sum_one, two(sum_both)).astype(BF)
            here = added(own, from_two, one(passed))
            due[1] += (from_two, passed)
        if wave:
            here = along_z(here.astype(BF), -wave).astype(F32)
        total = here if total is None else total + here
    return total


def route_some(normed, expert_ids, expert_weights, gate_up_weight, down, capacity):
    axes = ("seq", "exp")
    tok_rows, width = normed.shape
    choose = expert_ids.shape[1]
    local_experts = gate_up_weight.shape[0]
    expert_width = down.shape[1]
    devices = lax.axis_size("seq") * lax.axis_size("exp")
    experts_all = local_experts * devices
    flat_ids = expert_ids.reshape(-1)
    onehot = (flat_ids[:, None] == jnp.arange(experts_all, dtype=jnp.int32)[None, :]).astype(
        jnp.int32
    )
    rank = jnp.sum(jnp.cumsum(onehot, axis=0) * onehot, axis=1) - 1
    slot = flat_ids * capacity + rank
    token_of = jnp.arange(tok_rows * choose, dtype=jnp.int32) // choose
    send = jnp.zeros((experts_all * capacity, width), BF).at[slot].set(normed[token_of])
    both = jnp.einsum(
        "secd,edf->secf",
        lax.all_to_all(
            send.reshape(devices, local_experts, capacity, width),
            axes,
            split_axis=0,
            concat_axis=0,
            tiled=True,
        ),
        gate_up_weight,
        preferred_element_type=F32,
    )
    hidden = (jax.nn.silu(both[..., :expert_width]) * both[..., expert_width:]).astype(BF)
    back = lax.all_to_all(
        jnp.einsum("secf,efd->secd", hidden, down, preferred_element_type=F32).astype(BF),
        axes,
        split_axis=0,
        concat_axis=0,
        tiled=True,
    )
    back_rows = back.reshape(experts_all * capacity, width)[slot].astype(F32)
    return jnp.sum(
        back_rows.reshape(tok_rows, choose, width) * expert_weights[:, :, None], axis=1
    )


def local(
    stream,
    moe_gain,
    expert_ids,
    expert_weights,
    gate_up_weight,
    down,
    mixer_gain,
    qkv_weight,
    decay_log,
    write_rate,
):
    tok_rows, width = stream.shape
    choose = expert_ids.shape[1]
    seq_count = lax.axis_size("seq")
    devices = seq_count * lax.axis_size("exp")
    experts_all = gate_up_weight.shape[0] * devices
    capacity = max(2, (tok_rows * choose * 6 + experts_all * 5 - 1) // (experts_all * 5))
    normed = rms_scale(stream, moe_gain).astype(BF)
    planes = lax.axis_size("exp") == 4 and seq_count % 4 == 0 and choose <= ROUTE_STEP
    route = route_waves if planes and experts_all <= 256 else route_some
    moe = route(normed, expert_ids, expert_weights, gate_up_weight, down, capacity)
    mixed = (stream.astype(F32) + moe).astype(BF)
    normed_mix = rms_scale(mixed, mixer_gain).astype(BF)
    heads = decay_log.shape[1]
    blocks = decay_log.shape[0] // CH
    sums = jnp.cumsum(decay_log.T.reshape(heads, blocks, CH), axis=-1)
    rates = write_rate.T.reshape(heads, blocks, CH)
    pairs = blocks // 2
    by_pair = lambda values: values.reshape(heads, pairs, 2, CH).transpose(1, 0, 2, 3)
    if planes:
        core = lax.axis_index("exp") % 2
        side = lax.axis_index("exp") // 2
        from_y = over_y(normed_mix)
        both_sides = [(normed_mix, over_core(normed_mix)), (from_y, over_core(from_y))]
        parts = [
            (
                jnp.concatenate([jnp.where(core == 0, a, b), jnp.where(core == 0, b, a)], axis=0),
                place,
            )
            for (a, b), place in zip(both_sides, (side, 1 - side))
        ]
    else:
        gathered = lax.all_gather(normed_mix, "exp", axis=0, tiled=True)
        parts = [(gathered[2 * CH * i : 2 * CH * (i + 1)], jnp.int32(i)) for i in range(pairs)]
    found = ()
    for x, place in parts:
        found = chunks_of(
            x,
            place.astype(jnp.int32).reshape(1),
            qkv_weight,
            by_pair(sums),
            by_pair(rates),
            found,
        )
    query, key, solved, moved = found
    starts, ends = chain(moved, sums)
    entering, local_out = read(query, key, solved, starts, sums)
    if heads % seq_count == 0:
        dim = ends.shape[2] // 2
        each = heads // seq_count
        held = lax.all_to_all(ends, "seq", split_axis=0, concat_axis=0, tiled=True)
        held = held.reshape(seq_count, each, dim + 16, 2 * dim)
        states = jnp.stack([carry(held[:, i]) for i in range(each)], axis=1)
        arriving = lax.all_to_all(
            states.reshape(seq_count * each, dim, dim), "seq", split_axis=0, concat_axis=0, tiled=True
        )
    else:
        arriving = relay(ends, seq_count)
    return (mixed, finish(entering, local_out, arriving))


def solution(mesh):
    in_specs = (
        P(("seq", "exp"), None),
        P(),
        P(("seq", "exp"), None),
        P(("seq", "exp"), None),
        P(("seq", "exp"), None, None),
        P(("seq", "exp"), None, None),
        P(),
        P(None, None, "exp"),
        P("seq", "exp"),
        P("seq", "exp"),
    )
    out_specs = (P(("seq", "exp"), None), P("seq", "exp"))
    return jax.shard_map(local, mesh=mesh, in_specs=in_specs, out_specs=out_specs, check_vma=False)
```

```python
from functools import partial

import jax
import jax.numpy as jnp
from jax import lax
from jax.experimental import pallas as pl
from jax.experimental.pallas import tpu as pltpu
from jax.sharding import PartitionSpec as P

CH = 128
ROUTE_STEP = 16
VMEM_LIMIT = 56 * 1024 * 1024
BF = jnp.bfloat16
F32 = jnp.float32


def rms_scale(values, gain):
    wide = values.astype(F32)
    return wide * lax.rsqrt(jnp.mean(wide * wide, axis=-1, keepdims=True) + 1e-06) * gain


def dot(a, b):
    return jnp.dot(a, b, preferred_element_type=F32)


def split(a):
    high = a.astype(BF)
    return high, (a - high.astype(F32)).astype(BF)


def left_pair(a):
    high, low = split(a)
    return jnp.concatenate([high, low], axis=1)


def right_pair(b):
    high, low = split(b)
    row = jnp.concatenate([high, low], axis=1)
    return jnp.concatenate([row, row], axis=0)


def wide_product(a, b):
    columns = b.shape[1]
    both = dot(left_pair(a), right_pair(b))
    return both[:, :columns] + both[:, columns:]


def moe_kernel(capacity, choose, *refs):
    first_ref, *block_refs = refs[:5]
    weight_refs = refs[5:9]
    out_refs = refs[-9:-5]
    gate_up_ref, down_ref, rows_ref, back_ref, sem = refs[-5:]
    tok, wide = block_refs[0].shape
    width = rows_ref.shape[2]
    experts_here = gate_up_ref.shape[0]
    half = experts_here // 2
    expert_width = down_ref.shape[1]
    pair_rows = rows_ref.shape[1] // 2

    copies = []
    for e in range(experts_here):
        side, at = divmod(e, half)
        fetch_in = pltpu.make_async_copy(
            weight_refs[2 * side].at[at], gate_up_ref.at[e], sem.at[0, e]
        )
        fetch_out = pltpu.make_async_copy(
            weight_refs[2 * side + 1].at[at], down_ref.at[e], sem.at[1, e]
        )
        fetch_in.start()
        fetch_out.start()
        copies.append((fetch_in, fetch_out))

    matched, weights = [], []
    for block_ref in block_refs:
        routing = block_ref[:, width:].astype(F32).T
        ids = routing[:choose]
        scale = routing[ROUTE_STEP : ROUTE_STEP + choose]
        scale = scale + routing[2 * ROUTE_STEP : 2 * ROUTE_STEP + choose]
        for e in range(experts_here):
            side, at = divmod(e, half)
            hit = ids == (first_ref[side] + at).astype(F32)
            matched.append(jnp.max(jnp.where(hit, 1.0, 0.0), axis=0, keepdims=True))
            weights.append(jnp.sum(jnp.where(hit, scale, 0.0), axis=0, keepdims=True))
    match = jnp.concatenate(matched, axis=0)
    before = lax.broadcasted_iota(jnp.int32, (tok, tok), 0) < lax.broadcasted_iota(
        jnp.int32, (tok, tok), 1
    )
    rank = dot(match.astype(BF), jnp.where(before, 1.0, 0.0).astype(BF))
    rank = jnp.where(match > 0.5, rank, -1e4)
    row_number = lax.broadcasted_iota(jnp.int32, (pair_rows, 2 * tok), 0).astype(F32)
    picks = []
    for pair in range(2):
        x_pair = jnp.concatenate(
            [block_refs[2 * pair][:, :width], block_refs[2 * pair + 1][:, :width]], axis=0
        )
        here = []
        for e in range(experts_here):
            low = 2 * pair * experts_here + e
            high = low + experts_here
            place = jnp.concatenate(
                [rank[low : low + 1], rank[high : high + 1] + float(capacity)], axis=1
            )
            here.append(jnp.where(row_number == place, 1.0, 0.0))
        picks.append(here)
        chosen = dot(jnp.concatenate(here, axis=0).astype(BF), x_pair).astype(BF)
        for e in range(experts_here):
            rows_ref[e, pair * pair_rows : (pair + 1) * pair_rows, :] = chosen[
                e * pair_rows : (e + 1) * pair_rows
            ]
    for e in range(experts_here):
        copies[e][0].wait()
        both = dot(rows_ref[e], gate_up_ref[e])
        gate = both[:, :expert_width]
        hidden = (gate / (1.0 + jnp.exp(-gate)) * both[:, expert_width:]).astype(BF)
        copies[e][1].wait()
        back_ref[e] = dot(hidden, down_ref[e]).astype(BF)
    for pair in range(2):
        scaled, rows = [], []
        for e in range(experts_here):
            low = 2 * pair * experts_here + e
            high = low + experts_here
            weight = jnp.concatenate([weights[low], weights[high]], axis=1)
            scaled.append(picks[pair][e] * weight)
            rows.append(back_ref[e, pair * pair_rows : (pair + 1) * pair_rows, :])
        high_part, low_part = split(jnp.concatenate(scaled, axis=0))
        left = jnp.concatenate([high_part, low_part], axis=0)
        right = jnp.concatenate(rows + rows, axis=0)
        summed = lax.dot_general(
            left, right, (((0,), (0,)), ((), ())), preferred_element_type=F32
        ).astype(BF)
        out_refs[2 * pair][...] = summed[:tok]
        out_refs[2 * pair + 1][...] = summed[tok:]


def experts(blocks, first, weights, after, capacity, choose):
    tok, wide = blocks[0].shape
    gate_up_weight, down = weights[:2]
    local_experts, width, double = gate_up_weight.shape
    here = 2 * local_experts
    pair_rows = -(-2 * capacity // 16) * 16
    whole = pl.BlockSpec(memory_space=pltpu.VMEM)
    return pl.pallas_call(
        partial(moe_kernel, capacity, choose),
        in_specs=[pl.BlockSpec(memory_space=pltpu.SMEM)]
        + [whole] * 4
        + [pl.BlockSpec(memory_space=pl.ANY)] * (4 + len(after)),
        out_specs=[whole] * 4,
        out_shape=[jax.ShapeDtypeStruct((tok, width), BF)] * 4,
        scratch_shapes=[
            pltpu.VMEM((here,) + gate_up_weight.shape[1:], BF),
            pltpu.VMEM((here,) + down.shape[1:], BF),
            pltpu.VMEM((here, 2 * pair_rows, width), BF),
            pltpu.VMEM((here, 2 * pair_rows, width), BF),
            pltpu.SemaphoreType.DMA((2, here)),
        ],
        compiler_params=pltpu.CompilerParams(vmem_limit_bytes=VMEM_LIMIT),
        cost_estimate=pl.CostEstimate(
            flops=here * pair_rows * width * double // 4,
            bytes_accessed=tok * width,
            transcendentals=0,
        ),
        name="experts",
    )(first, *blocks, *weights, *after)


def unit_rows(values):
    return values * lax.rsqrt(jnp.sum(values * values, axis=-1, keepdims=True) + 1e-06)


def tiles():
    rows = lax.broadcasted_iota(jnp.int32, (CH, CH), 0)
    columns = lax.broadcasted_iota(jnp.int32, (CH, CH), 1)
    return rows, columns


def against_rows(a, b):
    high, low = split(b)
    right = jnp.concatenate(
        [jnp.concatenate([high, high], axis=1), jnp.concatenate([low, low], axis=1)], axis=0
    )
    both = lax.dot_general(
        left_pair(a), right, (((1,), (1,)), ((), ())), preferred_element_type=F32
    )
    return both[:, : b.shape[0]] + both[:, b.shape[0] :]


def chunk_kernel(place_ref, x_ref, w_ref, sum_ref, rate_ref, *refs):
    q_ref, k_ref, solved_ref, moved_ref = refs[-4:]
    heads, chunks, _ = sum_ref.shape[1:]
    dim = w_ref.shape[2] // heads
    rows, columns = tiles()
    strict = rows > columns
    identity = jnp.where(rows == columns, 1.0, 0.0)
    x = x_ref[...]
    query = dot(x, w_ref[0])
    key = dot(x, w_ref[1])
    value = dot(x, w_ref[2])
    units = [(h, n) for h in range(heads) for n in range(chunks)]

    def part(values, h, n):
        return values[n * CH : (n + 1) * CH, h * dim : (h + 1) * dim]

    keys, values, lowers, rates, growths, remains, wholes = [], [], [], [], [], [], []
    for h, n in units:
        q_ref[n * CH : (n + 1) * CH, h * dim : (h + 1) * dim] = unit_rows(part(query, h, n))
        unit = unit_rows(part(key, h, n))
        k_ref[n * CH : (n + 1) * CH, h * dim : (h + 1) * dim] = unit
        keys.append(unit)
        values.append(part(value, h, n))
    for u, (h, n) in enumerate(units):
        across = jnp.broadcast_to(sum_ref[0, h, n : n + 1, :], (CH, CH))
        along = across.T
        rate = jnp.broadcast_to(rate_ref[0, h, n : n + 1, :], (CH, CH)).T
        last = jnp.broadcast_to(along[CH - 1 : CH, :], (CH, CH))
        fade = jnp.exp(jnp.where(strict, along - across, 0.0))
        rates.append(rate)
        growths.append(jnp.exp(along))
        remains.append(jnp.exp(last - along))
        wholes.append(jnp.exp(last))
        lowers.append(jnp.where(strict, rate * fade * against_rows(keys[u], keys[u]), 0.0))

    def ring(size):
        shared = (rows // (2 * size)) == (columns // (2 * size))
        return shared & (rows // size % 2 == 1) & (columns // size % 2 == 0)

    span = range(len(units))
    inverse = [identity - jnp.where(ring(1), lowers[u], 0.0) for u in span]
    size = 2
    while size < CH:
        here = ring(size)
        step = [wide_product(jnp.where(here, lowers[u], 0.0), inverse[u]) for u in span]
        inverse = [inverse[u] - wide_product(inverse[u], step[u]) for u in span]
        size *= 2
    solved = [
        wide_product(
            inverse[u],
            jnp.concatenate([rates[u] * growths[u] * keys[u], rates[u] * values[u]], axis=1),
        )
        for u in span
    ]
    for u, (h, n) in enumerate(units):
        solved_ref[h, n] = solved[u]
        ended = wide_product((remains[u] * keys[u]).T, solved[u])
        moved_ref[h, n, :, :dim] = wholes[u] * identity - ended[:, :dim]
        moved_ref[h, n, :, dim:] = ended[:, dim:]


def chunks_of(x, place, qkv_weight, sums, rates, before):
    rows, width = x.shape
    _, _, columns = qkv_weight.shape
    parts, heads, chunks, _ = sums.shape
    dim = columns // heads
    step = min(4, heads)
    at_rows = pl.BlockSpec((rows, step * dim), lambda i, place: (place[0], i))
    at_chunks = pl.BlockSpec((step, chunks, CH, 2 * dim), lambda i, place: (i, place[0], 0, 0))
    per_head = pl.BlockSpec((1, step, chunks, CH), lambda i, place: (place[0], i, 0, 0))
    return pl.pallas_call(
        chunk_kernel,
        grid_spec=pltpu.PrefetchScalarGridSpec(
            num_scalar_prefetch=1,
            grid=(heads // step,),
            in_specs=[
                pl.BlockSpec((rows, width), lambda i, place: (0, 0)),
                pl.BlockSpec((3, width, step * dim), lambda i, place: (0, 0, i)),
                per_head,
                per_head,
            ]
            + [pl.BlockSpec(memory_space=pl.ANY)] * len(before),
            out_specs=[at_rows, at_rows, at_chunks, at_chunks],
        ),
        out_shape=[jax.ShapeDtypeStruct((parts * rows, columns), F32)] * 2
        + [jax.ShapeDtypeStruct((heads, parts * chunks, CH, 2 * dim), F32)] * 2,
        input_output_aliases={5 + i: i for i in range(len(before))},
        compiler_params=pltpu.CompilerParams(vmem_limit_bytes=VMEM_LIMIT),
        name="chunks",
    )(place, x, qkv_weight, sums, rates, *before)


def chain_kernel(moved_ref, sum_ref, starts_ref, end_ref):
    heads, chunks, dim, _ = moved_ref.shape
    rows, columns = tiles()
    identity = jnp.where(rows == columns, 1.0, 0.0)
    span = range(heads)
    state = [moved_ref[h, 0] for h in span]
    for n in range(1, chunks):
        for h in span:
            starts_ref[h, n - 1] = state[h]
        moved = [wide_product(moved_ref[h, n, :, :dim], state[h]) for h in span]
        state = [
            jnp.concatenate([moved[h][:, :dim], moved[h][:, dim:] + moved_ref[h, n, :, dim:]], axis=1)
            for h in span
        ]
    for h in span:
        decay = sum_ref[h, 0:1, :]
        for n in range(1, chunks):
            decay = decay + sum_ref[h, n : n + 1, :]
        decay = jnp.exp(jnp.broadcast_to(decay, (CH, CH)).T[CH - 1 : CH, :])
        decay = jnp.broadcast_to(decay, (CH, CH))
        end_ref[h, :dim, :dim] = (decay * identity - state[h][:, :dim]).astype(BF)
        end_ref[h, :dim, dim:] = state[h][:, dim:].astype(BF)
        end_ref[h, dim:, :] = left_pair(decay[:16])


def chain(moved, sums):
    heads, chunks, dim, double = moved.shape
    return pl.pallas_call(
        chain_kernel,
        out_shape=[
            jax.ShapeDtypeStruct((heads, chunks - 1, dim, double), F32),
            jax.ShapeDtypeStruct((heads, dim + 16, double), BF),
        ],
        compiler_params=pltpu.CompilerParams(vmem_limit_bytes=VMEM_LIMIT),
        name="chain",
    )(moved, sums)


def read_kernel(q_ref, k_ref, solved_ref, starts_ref, sum_ref, enter_ref, local_ref):
    heads, chunks, _ = sum_ref.shape
    dim = starts_ref.shape[2]
    rows, columns = tiles()
    inclusive = rows >= columns
    units = [(h, n) for h in range(heads) for n in range(chunks)]
    for h, n in units:
        cut = slice(n * CH, (n + 1) * CH), slice(h * dim, (h + 1) * dim)
        across = jnp.broadcast_to(sum_ref[h, n : n + 1, :], (CH, CH))
        along = across.T
        fade = jnp.exp(jnp.where(inclusive, along - across, 0.0))
        query = q_ref[cut]
        masked = jnp.where(inclusive, fade * against_rows(query, k_ref[cut]), 0.0)
        probed = wide_product(masked, solved_ref[h, n])
        entering = jnp.exp(along) * query - probed[:, :dim]
        output = probed[:, dim:]
        if n:
            begun = wide_product(entering, starts_ref[h, n - 1])
            entering = begun[:, :dim]
            output = output + begun[:, dim:]
        enter_ref[cut] = entering
        local_ref[cut] = output


def read(query, key, solved, starts, sums):
    length, columns = query.shape
    heads, chunks, _ = sums.shape
    dim = columns // heads
    step = 2 if heads % 2 == 0 else 1
    per_column = pl.BlockSpec((length, step * dim), lambda h: (0, h))
    four = lambda h: (h, 0, 0, 0)
    return pl.pallas_call(
        read_kernel,
        grid=(heads // step,),
        in_specs=[
            per_column,
            per_column,
            pl.BlockSpec((step, chunks, CH, 2 * dim), four),
            pl.BlockSpec((step, chunks - 1, dim, 2 * dim), four),
            pl.BlockSpec((step, chunks, CH), lambda h: (h, 0, 0)),
        ],
        out_specs=[per_column, per_column],
        out_shape=[jax.ShapeDtypeStruct((length, columns), F32)] * 2,
        compiler_params=pltpu.CompilerParams(vmem_limit_bytes=VMEM_LIMIT),
        name="read",
    )(query, key, solved, starts, sums)


def carry_kernel(ends_ref, states_ref):
    segments, _, double = ends_ref.shape
    dim = double // 2
    state = jnp.zeros((dim, dim), F32)
    for s in range(segments):
        states_ref[s] = state.astype(BF)
        if s < segments - 1:
            decay = ends_ref[s, dim : dim + 1, :].astype(F32)
            decay = decay[:, :dim] + decay[:, dim:]
            removed = dot(ends_ref[s, :dim, :dim], left_pair(state))
            removed = removed[:, :dim] + removed[:, dim:]
            state = decay * state - removed + ends_ref[s, :dim, dim:].astype(F32)


def carry(ends):
    segments, _, double = ends.shape
    return pl.pallas_call(
        carry_kernel,
        out_shape=jax.ShapeDtypeStruct((segments, double // 2, double // 2), BF),
        compiler_params=pltpu.CompilerParams(vmem_limit_bytes=VMEM_LIMIT),
        name="carry",
    )(ends)


def finish_kernel(enter_ref, local_ref, state_ref, core_ref):
    heads, dim, _ = state_ref.shape
    for h in range(heads):
        cut = slice(h * dim, (h + 1) * dim)
        state = state_ref[h]
        core_ref[:, cut] = local_ref[:, cut] + dot(
            left_pair(enter_ref[:, cut]), jnp.concatenate([state, state], axis=0)
        )


def finish(entering, local_out, states):
    length, columns = entering.shape
    heads, dim, _ = states.shape
    step = 2 if heads % 2 == 0 else 1
    per_column = pl.BlockSpec((length, step * dim), lambda h: (0, h))
    return pl.pallas_call(
        finish_kernel,
        grid=(heads // step,),
        in_specs=[per_column, per_column, pl.BlockSpec((step, dim, dim), lambda h: (h, 0, 0))],
        out_specs=per_column,
        out_shape=jax.ShapeDtypeStruct((length, columns), F32),
        compiler_params=pltpu.CompilerParams(vmem_limit_bytes=VMEM_LIMIT),
        name="finish",
    )(entering, local_out, states)


def relay(ends, seq_count):
    dim = ends.shape[2] // 2
    pairs = [(i, i + 1) for i in range(seq_count - 1)]
    removed, written = ends[:, :dim, :dim].astype(F32), ends[:, :dim, dim:].astype(F32)
    decay = ends[:, dim, :1].astype(F32) + ends[:, dim, dim : dim + 1].astype(F32)

    def step(_, incoming):
        outgoing = decay[:, :, None] * incoming + written
        outgoing = outgoing - jnp.einsum(
            "hij,hjk->hik", removed, incoming, precision=lax.Precision.HIGHEST
        )
        return lax.ppermute(outgoing, "seq", pairs)

    return lax.fori_loop(0, seq_count - 1, step, jnp.zeros_like(written)).astype(BF)


def move(values, change):
    exp_count = lax.axis_size("exp")
    pairs = []
    for s in range(lax.axis_size("seq")):
        for e in range(exp_count):
            to_s, to_e = change(s, e)
            pairs.append((s * exp_count + e, to_s * exp_count + to_e))
    return lax.ppermute(values, ("seq", "exp"), pairs)


def over_x(values):
    return move(values, lambda s, e: (s ^ 1, e))


def over_y(values):
    return move(values, lambda s, e: (s, e ^ 2))


def over_core(values):
    return move(values, lambda s, e: (s, e ^ 1))


def along_z(values, by):
    count = lax.axis_size("seq")
    return move(values, lambda s, e: ((s + 2 * by) % count, e))


def added(*terms):
    total = terms[0].astype(F32)
    for term in terms[1:]:
        total = total + term.astype(F32)
    return total


def route_waves(normed, expert_ids, expert_weights, gate_up_weight, down, capacity):
    tok_rows, width = normed.shape
    choose = expert_ids.shape[1]
    local_experts = gate_up_weight.shape[0]
    me = lax.axis_index("seq") * lax.axis_size("exp") + lax.axis_index("exp")
    first = (jnp.stack([me, me ^ 1]) * local_experts).astype(jnp.int32)
    gap = jnp.zeros((tok_rows, ROUTE_STEP - choose), BF)
    high, low = split(expert_weights)
    tail = jnp.zeros((tok_rows, 128 - 3 * ROUTE_STEP), BF)
    block = jnp.concatenate(
        [normed, expert_ids.astype(BF), gap, high, gap, low, gap, tail], axis=1
    )
    weights = (gate_up_weight, down, over_core(gate_up_weight), over_core(down))
    waves = range(lax.axis_size("seq") // 2)
    first_way = [over_x if wave % 4 < 2 else over_y for wave in waves]
    second_way = [over_y if wave % 4 < 2 else over_x for wave in waves]
    block = [block]
    for wave in waves[1:]:
        block.append(along_z(block[-1], 1))
    by_one = [first_way[wave](block[wave]) for wave in waves]
    by_two = [second_way[wave](block[wave]) for wave in waves]
    diagonal = []
    for wave in waves:
        diagonal.append(
            along_z(diagonal[-1], 1) if wave % 2 else second_way[wave](by_one[wave])
        )
    due = [() for _ in range(len(waves) + 2)]
    for wave in waves:
        if wave > 1:
            due[wave - 2] += (block[wave],)
            due[wave - 1] += (by_one[wave], by_two[wave])
    home = running = sum_below = None
    for wave in waves:
        own, sum_one, sum_two, sum_both = experts(
            (block[wave], by_one[wave], by_two[wave], diagonal[wave]),
            first,
            weights,
            due[wave],
            capacity,
            choose,
        )
        one, two = first_way[wave], second_way[wave]
        due[wave + 1] += (own,)
        from_two = two(sum_two)
        if wave % 2 == 0:
            sum_below = along_z(sum_both, 1)
            from_one = one(sum_one)
            due[wave + 2] += (from_one, from_two, sum_below)
        else:
            sum_both = added(sum_both, sum_below).astype(BF)
            passed = added(sum_one, two(sum_both)).astype(BF)
            from_one = one(passed)
            due[wave + 2] += (from_two, passed)
        here = added(own, from_two, from_one)
        if wave == 0:
            home = here
        else:
            if running is not None:
                here = here + running.astype(F32)
            running = along_z(here.astype(BF), 1)
    return home + running.astype(F32)


def route_some(normed, expert_ids, expert_weights, gate_up_weight, down, capacity):
    axes = ("seq", "exp")
    tok_rows, width = normed.shape
    choose = expert_ids.shape[1]
    local_experts = gate_up_weight.shape[0]
    expert_width = down.shape[1]
    devices = lax.axis_size("seq") * lax.axis_size("exp")
    experts_all = local_experts * devices
    flat_ids = expert_ids.reshape(-1)
    onehot = (flat_ids[:, None] == jnp.arange(experts_all, dtype=jnp.int32)[None, :]).astype(
        jnp.int32
    )
    rank = jnp.sum(jnp.cumsum(onehot, axis=0) * onehot, axis=1) - 1
    slot = flat_ids * capacity + rank
    token_of = jnp.arange(tok_rows * choose, dtype=jnp.int32) // choose
    send = jnp.zeros((experts_all * capacity, width), BF).at[slot].set(normed[token_of])
    both = jnp.einsum(
        "secd,edf->secf",
        lax.all_to_all(
            send.reshape(devices, local_experts, capacity, width),
            axes,
            split_axis=0,
            concat_axis=0,
            tiled=True,
        ),
        gate_up_weight,
        preferred_element_type=F32,
    )
    hidden = (jax.nn.silu(both[..., :expert_width]) * both[..., expert_width:]).astype(BF)
    back = lax.all_to_all(
        jnp.einsum("secf,efd->secd", hidden, down, preferred_element_type=F32).astype(BF),
        axes,
        split_axis=0,
        concat_axis=0,
        tiled=True,
    )
    back_rows = back.reshape(experts_all * capacity, width)[slot].astype(F32)
    return jnp.sum(
        back_rows.reshape(tok_rows, choose, width) * expert_weights[:, :, None], axis=1
    )


def local(
    stream,
    moe_gain,
    expert_ids,
    expert_weights,
    gate_up_weight,
    down,
    mixer_gain,
    qkv_weight,
    decay_log,
    write_rate,
):
    tok_rows, width = stream.shape
    choose = expert_ids.shape[1]
    seq_count = lax.axis_size("seq")
    devices = seq_count * lax.axis_size("exp")
    experts_all = gate_up_weight.shape[0] * devices
    capacity = max(2, (tok_rows * choose * 6 + experts_all * 5 - 1) // (experts_all * 5))
    normed = rms_scale(stream, moe_gain).astype(BF)
    planes = lax.axis_size("exp") == 4 and seq_count % 4 == 0 and choose <= ROUTE_STEP
    route = route_waves if planes and experts_all <= 256 else route_some
    moe = route(normed, expert_ids, expert_weights, gate_up_weight, down, capacity)
    mixed = (stream.astype(F32) + moe).astype(BF)
    normed_mix = rms_scale(mixed, mixer_gain).astype(BF)
    heads = decay_log.shape[1]
    blocks = decay_log.shape[0] // CH
    sums = jnp.cumsum(decay_log.T.reshape(heads, blocks, CH), axis=-1)
    rates = write_rate.T.reshape(heads, blocks, CH)
    pairs = blocks // 2
    by_pair = lambda values: values.reshape(heads, pairs, 2, CH).transpose(1, 0, 2, 3)
    if planes:
        core = lax.axis_index("exp") % 2
        side = lax.axis_index("exp") // 2
        from_y = over_y(normed_mix)
        both_sides = [(normed_mix, over_core(normed_mix)), (from_y, over_core(from_y))]
        parts = [
            (
                jnp.concatenate([jnp.where(core == 0, a, b), jnp.where(core == 0, b, a)], axis=0),
                place,
            )
            for (a, b), place in zip(both_sides, (side, 1 - side))
        ]
    else:
        gathered = lax.all_gather(normed_mix, "exp", axis=0, tiled=True)
        parts = [(gathered[2 * CH * i : 2 * CH * (i + 1)], jnp.int32(i)) for i in range(pairs)]
    found = ()
    for x, place in parts:
        found = chunks_of(
            x,
            place.astype(jnp.int32).reshape(1),
            qkv_weight,
            by_pair(sums),
            by_pair(rates),
            found,
        )
    query, key, solved, moved = found
    starts, ends = chain(moved, sums)
    entering, local_out = read(query, key, solved, starts, sums)
    if heads % seq_count == 0:
        dim = ends.shape[2] // 2
        each = heads // seq_count
        held = lax.all_to_all(ends, "seq", split_axis=0, concat_axis=0, tiled=True)
        held = held.reshape(seq_count, each, dim + 16, 2 * dim)
        states = jnp.stack([carry(held[:, i]) for i in range(each)], axis=1)
        arriving = lax.all_to_all(
            states.reshape(seq_count * each, dim, dim), "seq", split_axis=0, concat_axis=0, tiled=True
        )
    else:
        arriving = relay(ends, seq_count)
    return (mixed, finish(entering, local_out, arriving))


def solution(mesh):
    in_specs = (
        P(("seq", "exp"), None),
        P(),
        P(("seq", "exp"), None),
        P(("seq", "exp"), None),
        P(("seq", "exp"), None, None),
        P(("seq", "exp"), None, None),
        P(),
        P(None, None, "exp"),
        P("seq", "exp"),
        P("seq", "exp"),
    )
    out_specs = (P(("seq", "exp"), None), P("seq", "exp"))
    return jax.shard_map(local, mesh=mesh, in_specs=in_specs, out_specs=out_specs, check_vma=False)
```

```python
from functools import partial

import jax
import jax.numpy as jnp
from jax import lax
from jax.experimental import pallas as pl
from jax.experimental.pallas import tpu as pltpu
from jax.sharding import PartitionSpec as P

CH = 128
ROUTE_STEP = 16
VMEM_LIMIT = 56 * 1024 * 1024
BF = jnp.bfloat16
F32 = jnp.float32


def rms_scale(values, gain):
    wide = values.astype(F32)
    return wide * lax.rsqrt(jnp.mean(wide * wide, axis=-1, keepdims=True) + 1e-06) * gain


def dot(a, b):
    return jnp.dot(a, b, preferred_element_type=F32)


def split(a):
    high = a.astype(BF)
    return high, (a - high.astype(F32)).astype(BF)


def left_pair(a):
    high, low = split(a)
    return jnp.concatenate([high, low], axis=1)


def right_pair(b):
    high, low = split(b)
    row = jnp.concatenate([high, low], axis=1)
    return jnp.concatenate([row, row], axis=0)


def wide_product(a, b):
    columns = b.shape[1]
    both = dot(left_pair(a), right_pair(b))
    return both[:, :columns] + both[:, columns:]


def moe_kernel(capacity, choose, *refs):
    first_ref, *block_refs = refs[:5]
    weight_refs = refs[5:9]
    out_refs = refs[-9:-5]
    gate_up_ref, down_ref, rows_ref, back_ref, sem = refs[-5:]
    tok, wide = block_refs[0].shape
    width = rows_ref.shape[2]
    experts_here = gate_up_ref.shape[0]
    half = experts_here // 2
    expert_width = down_ref.shape[1]
    pair_rows = rows_ref.shape[1] // 2

    copies = []
    for e in range(experts_here):
        side, at = divmod(e, half)
        fetch_in = pltpu.make_async_copy(
            weight_refs[2 * side].at[at], gate_up_ref.at[e], sem.at[0, e]
        )
        fetch_out = pltpu.make_async_copy(
            weight_refs[2 * side + 1].at[at], down_ref.at[e], sem.at[1, e]
        )
        fetch_in.start()
        fetch_out.start()
        copies.append((fetch_in, fetch_out))

    matched, weights = [], []
    for block_ref in block_refs:
        routing = block_ref[:, width:].astype(F32).T
        ids = routing[:choose]
        scale = routing[ROUTE_STEP : ROUTE_STEP + choose]
        scale = scale + routing[2 * ROUTE_STEP : 2 * ROUTE_STEP + choose]
        for e in range(experts_here):
            side, at = divmod(e, half)
            hit = ids == (first_ref[side] + at).astype(F32)
            matched.append(jnp.max(jnp.where(hit, 1.0, 0.0), axis=0, keepdims=True))
            weights.append(jnp.sum(jnp.where(hit, scale, 0.0), axis=0, keepdims=True))
    match = jnp.concatenate(matched, axis=0)
    before = lax.broadcasted_iota(jnp.int32, (tok, tok), 0) < lax.broadcasted_iota(
        jnp.int32, (tok, tok), 1
    )
    rank = dot(match.astype(BF), jnp.where(before, 1.0, 0.0).astype(BF))
    rank = jnp.where(match > 0.5, rank, -1e4)
    row_number = lax.broadcasted_iota(jnp.int32, (pair_rows, 2 * tok), 0).astype(F32)
    picks = []
    for pair in range(2):
        x_pair = jnp.concatenate(
            [block_refs[2 * pair][:, :width], block_refs[2 * pair + 1][:, :width]], axis=0
        )
        here = []
        for e in range(experts_here):
            low = 2 * pair * experts_here + e
            high = low + experts_here
            place = jnp.concatenate(
                [rank[low : low + 1], rank[high : high + 1] + float(capacity)], axis=1
            )
            here.append(jnp.where(row_number == place, 1.0, 0.0))
        picks.append(here)
        chosen = dot(jnp.concatenate(here, axis=0).astype(BF), x_pair).astype(BF)
        for e in range(experts_here):
            rows_ref[e, pair * pair_rows : (pair + 1) * pair_rows, :] = chosen[
                e * pair_rows : (e + 1) * pair_rows
            ]
    for e in range(experts_here):
        copies[e][0].wait()
        both = dot(rows_ref[e], gate_up_ref[e])
        gate = both[:, :expert_width]
        hidden = (gate / (1.0 + jnp.exp(-gate)) * both[:, expert_width:]).astype(BF)
        copies[e][1].wait()
        back_ref[e] = dot(hidden, down_ref[e]).astype(BF)
    for pair in range(2):
        scaled, rows = [], []
        for e in range(experts_here):
            low = 2 * pair * experts_here + e
            high = low + experts_here
            weight = jnp.concatenate([weights[low], weights[high]], axis=1)
            scaled.append(picks[pair][e] * weight)
            rows.append(back_ref[e, pair * pair_rows : (pair + 1) * pair_rows, :])
        high_part, low_part = split(jnp.concatenate(scaled, axis=0))
        left = jnp.concatenate([high_part, low_part], axis=0)
        right = jnp.concatenate(rows + rows, axis=0)
        summed = lax.dot_general(
            left, right, (((0,), (0,)), ((), ())), preferred_element_type=F32
        ).astype(BF)
        out_refs[2 * pair][...] = summed[:tok]
        out_refs[2 * pair + 1][...] = summed[tok:]


def experts(blocks, first, weights, after, capacity, choose):
    tok, wide = blocks[0].shape
    gate_up_weight, down = weights[:2]
    local_experts, width, double = gate_up_weight.shape
    here = 2 * local_experts
    pair_rows = -(-2 * capacity // 16) * 16
    whole = pl.BlockSpec(memory_space=pltpu.VMEM)
    return pl.pallas_call(
        partial(moe_kernel, capacity, choose),
        in_specs=[pl.BlockSpec(memory_space=pltpu.SMEM)]
        + [whole] * 4
        + [pl.BlockSpec(memory_space=pl.ANY)] * (4 + len(after)),
        out_specs=[whole] * 4,
        out_shape=[jax.ShapeDtypeStruct((tok, width), BF)] * 4,
        scratch_shapes=[
            pltpu.VMEM((here,) + gate_up_weight.shape[1:], BF),
            pltpu.VMEM((here,) + down.shape[1:], BF),
            pltpu.VMEM((here, 2 * pair_rows, width), BF),
            pltpu.VMEM((here, 2 * pair_rows, width), BF),
            pltpu.SemaphoreType.DMA((2, here)),
        ],
        compiler_params=pltpu.CompilerParams(vmem_limit_bytes=VMEM_LIMIT),
        cost_estimate=pl.CostEstimate(
            flops=here * pair_rows * width * double // 4,
            bytes_accessed=tok * width,
            transcendentals=0,
        ),
        name="experts",
    )(first, *blocks, *weights, *after)


def unit_rows(values):
    return values * lax.rsqrt(jnp.sum(values * values, axis=-1, keepdims=True) + 1e-06)


def tiles():
    rows = lax.broadcasted_iota(jnp.int32, (CH, CH), 0)
    columns = lax.broadcasted_iota(jnp.int32, (CH, CH), 1)
    return rows, columns


def against_rows(a, b):
    high, low = split(b)
    right = jnp.concatenate(
        [jnp.concatenate([high, high], axis=1), jnp.concatenate([low, low], axis=1)], axis=0
    )
    both = lax.dot_general(
        left_pair(a), right, (((1,), (1,)), ((), ())), preferred_element_type=F32
    )
    return both[:, : b.shape[0]] + both[:, b.shape[0] :]


def chunk_kernel(place_ref, x_ref, key_w_ref, value_w_ref, sum_ref, rate_ref, *refs):
    k_ref, solved_ref, moved_ref = refs[-3:]
    heads, chunks, _ = sum_ref.shape[1:]
    dim = key_w_ref.shape[2] // heads
    rows, columns = tiles()
    strict = rows > columns
    identity = jnp.where(rows == columns, 1.0, 0.0)
    x = x_ref[...]
    key = dot(x, key_w_ref[0])
    value = dot(x, value_w_ref[0])
    units = [(h, n) for h in range(heads) for n in range(chunks)]

    def part(values, h, n):
        return values[n * CH : (n + 1) * CH, h * dim : (h + 1) * dim]

    keys, values, lowers, rates, growths, remains, wholes = [], [], [], [], [], [], []
    for h, n in units:
        unit = unit_rows(part(key, h, n))
        k_ref[n * CH : (n + 1) * CH, h * dim : (h + 1) * dim] = unit
        keys.append(unit)
        values.append(part(value, h, n))
    for u, (h, n) in enumerate(units):
        across = jnp.broadcast_to(sum_ref[0, h, n : n + 1, :], (CH, CH))
        along = across.T
        rate = jnp.broadcast_to(rate_ref[0, h, n : n + 1, :], (CH, CH)).T
        last = jnp.broadcast_to(along[CH - 1 : CH, :], (CH, CH))
        fade = jnp.exp(jnp.where(strict, along - across, 0.0))
        rates.append(rate)
        growths.append(jnp.exp(along))
        remains.append(jnp.exp(last - along))
        wholes.append(jnp.exp(last))
        lowers.append(jnp.where(strict, rate * fade * against_rows(keys[u], keys[u]), 0.0))

    def ring(size):
        shared = (rows // (2 * size)) == (columns // (2 * size))
        return shared & (rows // size % 2 == 1) & (columns // size % 2 == 0)

    span = range(len(units))
    inverse = [identity - jnp.where(ring(1), lowers[u], 0.0) for u in span]
    size = 2
    while size < CH:
        here = ring(size)
        step = [wide_product(jnp.where(here, lowers[u], 0.0), inverse[u]) for u in span]
        inverse = [inverse[u] - wide_product(inverse[u], step[u]) for u in span]
        size *= 2
    solved = [
        wide_product(
            inverse[u],
            jnp.concatenate([rates[u] * growths[u] * keys[u], rates[u] * values[u]], axis=1),
        )
        for u in span
    ]
    for u, (h, n) in enumerate(units):
        solved_ref[h, n] = solved[u]
        ended = wide_product((remains[u] * keys[u]).T, solved[u])
        moved_ref[h, n, :, :dim] = wholes[u] * identity - ended[:, :dim]
        moved_ref[h, n, :, dim:] = ended[:, dim:]


def chunks_of(x, place, qkv_weight, sums, rates, before):
    rows, width = x.shape
    _, _, columns = qkv_weight.shape
    parts, heads, chunks, _ = sums.shape
    dim = columns // heads
    step = min(4, heads)
    at_rows = pl.BlockSpec((rows, step * dim), lambda i, place: (place[0], i))
    at_chunks = pl.BlockSpec((step, chunks, CH, 2 * dim), lambda i, place: (i, place[0], 0, 0))
    per_head = pl.BlockSpec((1, step, chunks, CH), lambda i, place: (place[0], i, 0, 0))
    return pl.pallas_call(
        chunk_kernel,
        grid_spec=pltpu.PrefetchScalarGridSpec(
            num_scalar_prefetch=1,
            grid=(heads // step,),
            in_specs=[
                pl.BlockSpec((rows, width), lambda i, place: (0, 0)),
                pl.BlockSpec((1, width, step * dim), lambda i, place: (1, 0, i)),
                pl.BlockSpec((1, width, step * dim), lambda i, place: (2, 0, i)),
                per_head,
                per_head,
            ]
            + [pl.BlockSpec(memory_space=pl.ANY)] * len(before),
            out_specs=[at_rows, at_chunks, at_chunks],
        ),
        out_shape=[jax.ShapeDtypeStruct((parts * rows, columns), F32)]
        + [jax.ShapeDtypeStruct((heads, parts * chunks, CH, 2 * dim), F32)] * 2,
        input_output_aliases={6 + i: i for i in range(len(before))},
        compiler_params=pltpu.CompilerParams(vmem_limit_bytes=VMEM_LIMIT),
        name="chunks",
    )(place, x, qkv_weight, qkv_weight, sums, rates, *before)


def chain_kernel(moved_ref, sum_ref, starts_ref, end_ref):
    heads, chunks, dim, _ = moved_ref.shape
    rows, columns = tiles()
    identity = jnp.where(rows == columns, 1.0, 0.0)
    span = range(heads)
    state = [moved_ref[h, 0] for h in span]
    for n in range(1, chunks):
        for h in span:
            starts_ref[h, n - 1] = state[h]
        moved = [wide_product(moved_ref[h, n, :, :dim], state[h]) for h in span]
        state = [
            jnp.concatenate([moved[h][:, :dim], moved[h][:, dim:] + moved_ref[h, n, :, dim:]], axis=1)
            for h in span
        ]
    for h in span:
        decay = sum_ref[h, 0:1, :]
        for n in range(1, chunks):
            decay = decay + sum_ref[h, n : n + 1, :]
        decay = jnp.exp(jnp.broadcast_to(decay, (CH, CH)).T[CH - 1 : CH, :])
        decay = jnp.broadcast_to(decay, (CH, CH))
        end_ref[h, :dim, :dim] = (decay * identity - state[h][:, :dim]).astype(BF)
        end_ref[h, :dim, dim:] = state[h][:, dim:].astype(BF)
        end_ref[h, dim:, :] = left_pair(decay[:16])


def chain(moved, sums):
    heads, chunks, dim, double = moved.shape
    return pl.pallas_call(
        chain_kernel,
        out_shape=[
            jax.ShapeDtypeStruct((heads, chunks - 1, dim, double), F32),
            jax.ShapeDtypeStruct((heads, dim + 16, double), BF),
        ],
        compiler_params=pltpu.CompilerParams(vmem_limit_bytes=VMEM_LIMIT),
        name="chain",
    )(moved, sums)


def read_kernel(place_ref, w_ref, k_ref, solved_ref, starts_ref, sum_ref, *refs):
    x_refs = refs[:-2]
    enter_ref, local_ref = refs[-2:]
    heads, chunks, _ = sum_ref.shape
    dim = starts_ref.shape[2]
    rows, columns = tiles()
    inclusive = rows >= columns
    found = [dot(x_ref[...], w_ref[0]) for x_ref in x_refs]
    queries = []
    for place in range(len(found)):
        query = found[0]
        for i in range(1, len(found)):
            query = jnp.where(place_ref[i] == place, found[i], query)
        queries.append(query)
    each = chunks // len(found)
    units = [(h, n) for h in range(heads) for n in range(chunks)]
    for h, n in units:
        cut = slice(n * CH, (n + 1) * CH), slice(h * dim, (h + 1) * dim)
        across = jnp.broadcast_to(sum_ref[h, n : n + 1, :], (CH, CH))
        along = across.T
        fade = jnp.exp(jnp.where(inclusive, along - across, 0.0))
        query = unit_rows(queries[n // each][n % each * CH : (n % each + 1) * CH, cut[1]])
        masked = jnp.where(inclusive, fade * against_rows(query, k_ref[cut]), 0.0)
        probed = wide_product(masked, solved_ref[h, n])
        entering = jnp.exp(along) * query - probed[:, :dim]
        output = probed[:, dim:]
        if n:
            begun = wide_product(entering, starts_ref[h, n - 1])
            entering = begun[:, :dim]
            output = output + begun[:, dim:]
        enter_ref[cut] = entering
        local_ref[cut] = output


def read(parts, places, qkv_weight, key, solved, starts, sums):
    length, columns = key.shape
    heads, chunks, _ = sums.shape
    dim = columns // heads
    width = qkv_weight.shape[1]
    step = 2 if heads % 2 == 0 else 1
    per_column = pl.BlockSpec((length, step * dim), lambda h: (0, h))
    four = lambda h: (h, 0, 0, 0)
    return pl.pallas_call(
        read_kernel,
        grid=(heads // step,),
        in_specs=[
            pl.BlockSpec(memory_space=pltpu.SMEM),
            pl.BlockSpec((1, width, step * dim), lambda h: (0, 0, h)),
            per_column,
            pl.BlockSpec((step, chunks, CH, 2 * dim), four),
            pl.BlockSpec((step, chunks - 1, dim, 2 * dim), four),
            pl.BlockSpec((step, chunks, CH), lambda h: (h, 0, 0)),
        ]
        + [pl.BlockSpec(x.shape, lambda h: (0, 0)) for x in parts],
        out_specs=[per_column, per_column],
        out_shape=[jax.ShapeDtypeStruct((length, columns), F32)] * 2,
        compiler_params=pltpu.CompilerParams(vmem_limit_bytes=VMEM_LIMIT),
        name="read",
    )(places, qkv_weight, key, solved, starts, sums, *parts)


def carry_kernel(ends_ref, states_ref):
    segments, _, double = ends_ref.shape
    dim = double // 2
    state = jnp.zeros((dim, dim), F32)
    for s in range(segments):
        states_ref[s] = state.astype(BF)
        if s < segments - 1:
            decay = ends_ref[s, dim : dim + 1, :].astype(F32)
            decay = decay[:, :dim] + decay[:, dim:]
            removed = dot(ends_ref[s, :dim, :dim], left_pair(state))
            removed = removed[:, :dim] + removed[:, dim:]
            state = decay * state - removed + ends_ref[s, :dim, dim:].astype(F32)


def carry(ends):
    segments, _, double = ends.shape
    return pl.pallas_call(
        carry_kernel,
        out_shape=jax.ShapeDtypeStruct((segments, double // 2, double // 2), BF),
        compiler_params=pltpu.CompilerParams(vmem_limit_bytes=VMEM_LIMIT),
        name="carry",
    )(ends)


def finish_kernel(enter_ref, local_ref, state_ref, core_ref):
    heads, dim, _ = state_ref.shape
    for h in range(heads):
        cut = slice(h * dim, (h + 1) * dim)
        state = state_ref[h]
        core_ref[:, cut] = local_ref[:, cut] + dot(
            left_pair(enter_ref[:, cut]), jnp.concatenate([state, state], axis=0)
        )


def finish(entering, local_out, states):
    length, columns = entering.shape
    heads, dim, _ = states.shape
    step = 2 if heads % 2 == 0 else 1
    per_column = pl.BlockSpec((length, step * dim), lambda h: (0, h))
    return pl.pallas_call(
        finish_kernel,
        grid=(heads // step,),
        in_specs=[per_column, per_column, pl.BlockSpec((step, dim, dim), lambda h: (h, 0, 0))],
        out_specs=per_column,
        out_shape=jax.ShapeDtypeStruct((length, columns), F32),
        compiler_params=pltpu.CompilerParams(vmem_limit_bytes=VMEM_LIMIT),
        name="finish",
    )(entering, local_out, states)


def relay(ends, seq_count):
    dim = ends.shape[2] // 2
    pairs = [(i, i + 1) for i in range(seq_count - 1)]
    removed, written = ends[:, :dim, :dim].astype(F32), ends[:, :dim, dim:].astype(F32)
    decay = ends[:, dim, :1].astype(F32) + ends[:, dim, dim : dim + 1].astype(F32)

    def step(_, incoming):
        outgoing = decay[:, :, None] * incoming + written
        outgoing = outgoing - jnp.einsum(
            "hij,hjk->hik", removed, incoming, precision=lax.Precision.HIGHEST
        )
        return lax.ppermute(outgoing, "seq", pairs)

    return lax.fori_loop(0, seq_count - 1, step, jnp.zeros_like(written)).astype(BF)


def move(values, change):
    exp_count = lax.axis_size("exp")
    pairs = []
    for s in range(lax.axis_size("seq")):
        for e in range(exp_count):
            to_s, to_e = change(s, e)
            pairs.append((s * exp_count + e, to_s * exp_count + to_e))
    return lax.ppermute(values, ("seq", "exp"), pairs)


def over_x(values):
    return move(values, lambda s, e: (s ^ 1, e))


def over_y(values):
    return move(values, lambda s, e: (s, e ^ 2))


def over_core(values):
    return move(values, lambda s, e: (s, e ^ 1))


def along_z(values, by):
    count = lax.axis_size("seq")
    return move(values, lambda s, e: ((s + 2 * by) % count, e))


def added(*terms):
    total = terms[0].astype(F32)
    for term in terms[1:]:
        total = total + term.astype(F32)
    return total


def route_waves(normed, expert_ids, expert_weights, gate_up_weight, down, capacity):
    tok_rows, width = normed.shape
    choose = expert_ids.shape[1]
    local_experts = gate_up_weight.shape[0]
    me = lax.axis_index("seq") * lax.axis_size("exp") + lax.axis_index("exp")
    first = (jnp.stack([me, me ^ 1]) * local_experts).astype(jnp.int32)
    gap = jnp.zeros((tok_rows, ROUTE_STEP - choose), BF)
    high, low = split(expert_weights)
    tail = jnp.zeros((tok_rows, 128 - 3 * ROUTE_STEP), BF)
    block = jnp.concatenate(
        [normed, expert_ids.astype(BF), gap, high, gap, low, gap, tail], axis=1
    )
    weights = (gate_up_weight, down, over_core(gate_up_weight), over_core(down))
    count = lax.axis_size("seq") // 2
    order = list(range(1, count)) + [0]
    first_way = [over_y if wave == 1 else over_x for wave in range(count)]
    second_way = [over_x if wave == 1 else over_y for wave in range(count)]
    block = [block]
    for wave in range(1, count):
        block.append(along_z(block[-1], 1))
    by_one = [first_way[wave](block[wave]) for wave in range(count)]
    by_two = [second_way[wave](block[wave]) for wave in range(count)]
    diagonal = {wave: second_way[wave](by_one[wave]) for wave in (0, 1)}
    for wave in range(2, count):
        diagonal[wave] = along_z(diagonal[wave - 1], 1)
    due = [() for _ in range(count + 2)]
    for call, wave in enumerate(order):
        if call and wave:
            due[call - 1] += (block[wave],)
        if call > 1:
            due[call - 1 if wave else 0] += (by_one[wave], by_two[wave])
    running = sum_below = None
    for call, wave in enumerate(order):
        own, sum_one, sum_two, sum_both = experts(
            (block[wave], by_one[wave], by_two[wave], diagonal[wave]),
            first,
            weights,
            due[call],
            capacity,
            choose,
        )
        one, two = first_way[wave], second_way[wave]
        due[call + 1] += (own,)
        if sum_below is not None:
            sum_both = added(sum_both, sum_below).astype(BF)
        from_two = two(sum_two)
        if wave:
            sum_below = along_z(sum_both, 1)
            due[call + 2] += (sum_below,)
        else:
            sum_one = added(sum_one, two(sum_both)).astype(BF)
        from_one = one(sum_one)
        due[call + 2] += (from_two, from_one)
        here = added(own, from_two, from_one)
        if running is not None:
            here = here + running.astype(F32)
        if wave:
            running = along_z(here.astype(BF), 1)
    return here


def route_some(normed, expert_ids, expert_weights, gate_up_weight, down, capacity):
    axes = ("seq", "exp")
    tok_rows, width = normed.shape
    choose = expert_ids.shape[1]
    local_experts = gate_up_weight.shape[0]
    expert_width = down.shape[1]
    devices = lax.axis_size("seq") * lax.axis_size("exp")
    experts_all = local_experts * devices
    flat_ids = expert_ids.reshape(-1)
    onehot = (flat_ids[:, None] == jnp.arange(experts_all, dtype=jnp.int32)[None, :]).astype(
        jnp.int32
    )
    rank = jnp.sum(jnp.cumsum(onehot, axis=0) * onehot, axis=1) - 1
    slot = flat_ids * capacity + rank
    token_of = jnp.arange(tok_rows * choose, dtype=jnp.int32) // choose
    send = jnp.zeros((experts_all * capacity, width), BF).at[slot].set(normed[token_of])
    both = jnp.einsum(
        "secd,edf->secf",
        lax.all_to_all(
            send.reshape(devices, local_experts, capacity, width),
            axes,
            split_axis=0,
            concat_axis=0,
            tiled=True,
        ),
        gate_up_weight,
        preferred_element_type=F32,
    )
    hidden = (jax.nn.silu(both[..., :expert_width]) * both[..., expert_width:]).astype(BF)
    back = lax.all_to_all(
        jnp.einsum("secf,efd->secd", hidden, down, preferred_element_type=F32).astype(BF),
        axes,
        split_axis=0,
        concat_axis=0,
        tiled=True,
    )
    back_rows = back.reshape(experts_all * capacity, width)[slot].astype(F32)
    return jnp.sum(
        back_rows.reshape(tok_rows, choose, width) * expert_weights[:, :, None], axis=1
    )


def local(
    stream,
    moe_gain,
    expert_ids,
    expert_weights,
    gate_up_weight,
    down,
    mixer_gain,
    qkv_weight,
    decay_log,
    write_rate,
):
    tok_rows, width = stream.shape
    choose = expert_ids.shape[1]
    seq_count = lax.axis_size("seq")
    devices = seq_count * lax.axis_size("exp")
    experts_all = gate_up_weight.shape[0] * devices
    capacity = max(2, (tok_rows * choose * 6 + experts_all * 5 - 1) // (experts_all * 5))
    normed = rms_scale(stream, moe_gain).astype(BF)
    planes = lax.axis_size("exp") == 4 and seq_count % 4 == 0 and choose <= ROUTE_STEP
    route = route_waves if planes and experts_all <= 256 else route_some
    moe = route(normed, expert_ids, expert_weights, gate_up_weight, down, capacity)
    mixed = (stream.astype(F32) + moe).astype(BF)
    normed_mix = rms_scale(mixed, mixer_gain).astype(BF)
    heads = decay_log.shape[1]
    blocks = decay_log.shape[0] // CH
    sums = jnp.cumsum(decay_log.T.reshape(heads, blocks, CH), axis=-1)
    rates = write_rate.T.reshape(heads, blocks, CH)
    pairs = blocks // 2
    by_pair = lambda values: values.reshape(heads, pairs, 2, CH).transpose(1, 0, 2, 3)
    if planes:
        core = lax.axis_index("exp") % 2
        side = lax.axis_index("exp") // 2
        from_y = over_y(normed_mix)
        both_sides = [(normed_mix, over_core(normed_mix)), (from_y, over_core(from_y))]
        parts = [
            (
                jnp.concatenate([jnp.where(core == 0, a, b), jnp.where(core == 0, b, a)], axis=0),
                place,
            )
            for (a, b), place in zip(both_sides, (side, 1 - side))
        ]
    else:
        gathered = lax.all_gather(normed_mix, "exp", axis=0, tiled=True)
        parts = [(gathered[2 * CH * i : 2 * CH * (i + 1)], jnp.int32(i)) for i in range(pairs)]
    found = ()
    for x, place in parts:
        found = chunks_of(
            x,
            place.astype(jnp.int32).reshape(1),
            qkv_weight,
            by_pair(sums),
            by_pair(rates),
            found,
        )
    key, solved, moved = found
    starts, ends = chain(moved, sums)
    places = jnp.stack([place for _, place in parts]).astype(jnp.int32)
    entering, local_out = read([x for x, _ in parts], places, qkv_weight, key, solved, starts, sums)
    if heads % seq_count == 0:
        dim = ends.shape[2] // 2
        each = heads // seq_count
        held = lax.all_to_all(ends, "seq", split_axis=0, concat_axis=0, tiled=True)
        held = held.reshape(seq_count, each, dim + 16, 2 * dim)
        states = jnp.stack([carry(held[:, i]) for i in range(each)], axis=1)
        arriving = lax.all_to_all(
            states.reshape(seq_count * each, dim, dim), "seq", split_axis=0, concat_axis=0, tiled=True
        )
    else:
        arriving = relay(ends, seq_count)
    return (mixed, finish(entering, local_out, arriving))


def solution(mesh):
    in_specs = (
        P(("seq", "exp"), None),
        P(),
        P(("seq", "exp"), None),
        P(("seq", "exp"), None),
        P(("seq", "exp"), None, None),
        P(("seq", "exp"), None, None),
        P(),
        P(None, None, "exp"),
        P("seq", "exp"),
        P("seq", "exp"),
    )
    out_specs = (P(("seq", "exp"), None), P("seq", "exp"))
    return jax.shard_map(local, mesh=mesh, in_specs=in_specs, out_specs=out_specs, check_vma=False)
```

```python
from functools import partial

import jax
import jax.numpy as jnp
from jax import lax
from jax.experimental import pallas as pl
from jax.experimental.pallas import tpu as pltpu
from jax.sharding import PartitionSpec as P

CH = 128
ROUTE_STEP = 16
VMEM_LIMIT = 56 * 1024 * 1024
BF = jnp.bfloat16
F32 = jnp.float32


def rms_scale(values, gain):
    wide = values.astype(F32)
    return wide * lax.rsqrt(jnp.mean(wide * wide, axis=-1, keepdims=True) + 1e-06) * gain


def dot(a, b):
    return jnp.dot(a, b, preferred_element_type=F32)


def split(a):
    high = a.astype(BF)
    return high, (a - high.astype(F32)).astype(BF)


def rough(a, b):
    return dot(a.astype(BF), b.astype(BF))


def left_pair(a):
    high, low = split(a)
    return jnp.concatenate([high, low], axis=1)


def right_pair(b):
    high, low = split(b)
    row = jnp.concatenate([high, low], axis=1)
    return jnp.concatenate([row, row], axis=0)


def wide_product(a, b):
    columns = b.shape[1]
    both = dot(left_pair(a), right_pair(b))
    return both[:, :columns] + both[:, columns:]


def moe_kernel(capacity, choose, *refs):
    first_ref, *block_refs = refs[:5]
    weight_refs = refs[5:9]
    out_refs = refs[-9:-5]
    gate_up_ref, down_ref, rows_ref, back_ref, sem = refs[-5:]
    tok, wide = block_refs[0].shape
    width = rows_ref.shape[2]
    experts_here = gate_up_ref.shape[0]
    half = experts_here // 2
    expert_width = down_ref.shape[1]
    pair_rows = rows_ref.shape[1] // 2

    copies = []
    for e in range(experts_here):
        side, at = divmod(e, half)
        fetch_in = pltpu.make_async_copy(
            weight_refs[2 * side].at[at], gate_up_ref.at[e], sem.at[0, e]
        )
        fetch_out = pltpu.make_async_copy(
            weight_refs[2 * side + 1].at[at], down_ref.at[e], sem.at[1, e]
        )
        fetch_in.start()
        fetch_out.start()
        copies.append((fetch_in, fetch_out))

    matched, weights = [], []
    for block_ref in block_refs:
        routing = block_ref[:, width:].astype(F32).T
        ids = routing[:choose]
        scale = routing[ROUTE_STEP : ROUTE_STEP + choose]
        scale = scale + routing[2 * ROUTE_STEP : 2 * ROUTE_STEP + choose]
        for e in range(experts_here):
            side, at = divmod(e, half)
            hit = ids == (first_ref[side] + at).astype(F32)
            matched.append(jnp.max(jnp.where(hit, 1.0, 0.0), axis=0, keepdims=True))
            weights.append(jnp.sum(jnp.where(hit, scale, 0.0), axis=0, keepdims=True))
    match = jnp.concatenate(matched, axis=0)
    before = lax.broadcasted_iota(jnp.int32, (tok, tok), 0) < lax.broadcasted_iota(
        jnp.int32, (tok, tok), 1
    )
    rank = dot(match.astype(BF), jnp.where(before, 1.0, 0.0).astype(BF))
    rank = jnp.where(match > 0.5, rank, -1e4)
    row_number = lax.broadcasted_iota(jnp.int32, (pair_rows, 2 * tok), 0).astype(F32)
    picks = []
    for pair in range(2):
        x_pair = jnp.concatenate(
            [block_refs[2 * pair][:, :width], block_refs[2 * pair + 1][:, :width]], axis=0
        )
        here = []
        for e in range(experts_here):
            low = 2 * pair * experts_here + e
            high = low + experts_here
            place = jnp.concatenate(
                [rank[low : low + 1], rank[high : high + 1] + float(capacity)], axis=1
            )
            here.append(jnp.where(row_number == place, 1.0, 0.0))
        picks.append(here)
        chosen = dot(jnp.concatenate(here, axis=0).astype(BF), x_pair).astype(BF)
        for e in range(experts_here):
            rows_ref[e, pair * pair_rows : (pair + 1) * pair_rows, :] = chosen[
                e * pair_rows : (e + 1) * pair_rows
            ]
    for e in range(experts_here):
        copies[e][0].wait()
        both = dot(rows_ref[e], gate_up_ref[e])
        gate = both[:, :expert_width]
        hidden = (gate / (1.0 + jnp.exp(-gate)) * both[:, expert_width:]).astype(BF)
        copies[e][1].wait()
        back_ref[e] = dot(hidden, down_ref[e]).astype(BF)
    for pair in range(2):
        scaled, rows = [], []
        for e in range(experts_here):
            low = 2 * pair * experts_here + e
            high = low + experts_here
            weight = jnp.concatenate([weights[low], weights[high]], axis=1)
            scaled.append(picks[pair][e] * weight)
            rows.append(back_ref[e, pair * pair_rows : (pair + 1) * pair_rows, :])
        high_part, low_part = split(jnp.concatenate(scaled, axis=0))
        left = jnp.concatenate([high_part, low_part], axis=0)
        right = jnp.concatenate(rows + rows, axis=0)
        summed = lax.dot_general(
            left, right, (((0,), (0,)), ((), ())), preferred_element_type=F32
        ).astype(BF)
        out_refs[2 * pair][...] = summed[:tok]
        out_refs[2 * pair + 1][...] = summed[tok:]


def experts(blocks, first, weights, after, capacity, choose):
    tok, wide = blocks[0].shape
    gate_up_weight, down = weights[:2]
    local_experts, width, double = gate_up_weight.shape
    here = 2 * local_experts
    pair_rows = -(-2 * capacity // 16) * 16
    whole = pl.BlockSpec(memory_space=pltpu.VMEM)
    return pl.pallas_call(
        partial(moe_kernel, capacity, choose),
        in_specs=[pl.BlockSpec(memory_space=pltpu.SMEM)]
        + [whole] * 4
        + [pl.BlockSpec(memory_space=pl.ANY)] * (4 + len(after)),
        out_specs=[whole] * 4,
        out_shape=[jax.ShapeDtypeStruct((tok, width), BF)] * 4,
        scratch_shapes=[
            pltpu.VMEM((here,) + gate_up_weight.shape[1:], BF),
            pltpu.VMEM((here,) + down.shape[1:], BF),
            pltpu.VMEM((here, 2 * pair_rows, width), BF),
            pltpu.VMEM((here, 2 * pair_rows, width), BF),
            pltpu.SemaphoreType.DMA((2, here)),
        ],
        compiler_params=pltpu.CompilerParams(vmem_limit_bytes=VMEM_LIMIT),
        cost_estimate=pl.CostEstimate(
            flops=here * pair_rows * width * double // 4,
            bytes_accessed=tok * width,
            transcendentals=0,
        ),
        name="experts",
    )(first, *blocks, *weights, *after)


def unit_rows(values):
    return values * lax.rsqrt(jnp.sum(values * values, axis=-1, keepdims=True) + 1e-06)


def tiles():
    rows = lax.broadcasted_iota(jnp.int32, (CH, CH), 0)
    columns = lax.broadcasted_iota(jnp.int32, (CH, CH), 1)
    return rows, columns


def against_rows(a, b):
    high, low = split(b)
    right = jnp.concatenate(
        [jnp.concatenate([high, high], axis=1), jnp.concatenate([low, low], axis=1)], axis=0
    )
    both = lax.dot_general(
        left_pair(a), right, (((1,), (1,)), ((), ())), preferred_element_type=F32
    )
    return both[:, : b.shape[0]] + both[:, b.shape[0] :]


def chunk_kernel(place_ref, x_ref, key_w_ref, value_w_ref, sum_ref, rate_ref, *refs):
    k_ref, solved_ref, moved_ref = refs[-3:]
    heads, chunks, _ = sum_ref.shape[1:]
    dim = key_w_ref.shape[2] // heads
    rows, columns = tiles()
    strict = rows > columns
    identity = jnp.where(rows == columns, 1.0, 0.0)
    x = x_ref[...]
    key = dot(x, key_w_ref[0])
    value = dot(x, value_w_ref[0])
    units = [(h, n) for h in range(heads) for n in range(chunks)]

    def part(values, h, n):
        return values[n * CH : (n + 1) * CH, h * dim : (h + 1) * dim]

    keys, values, lowers, rates, growths, remains = [], [], [], [], [], []
    for h, n in units:
        unit = unit_rows(part(key, h, n))
        k_ref[n * CH : (n + 1) * CH, h * dim : (h + 1) * dim] = unit
        keys.append(unit)
        values.append(part(value, h, n))
    for u, (h, n) in enumerate(units):
        across = jnp.broadcast_to(sum_ref[0, h, n : n + 1, :], (CH, CH))
        along = across.T
        rate = jnp.broadcast_to(rate_ref[0, h, n : n + 1, :], (CH, CH)).T
        last = jnp.broadcast_to(along[CH - 1 : CH, :], (CH, CH))
        fade = jnp.exp(jnp.where(strict, along - across, 0.0))
        rates.append(rate)
        growths.append(jnp.exp(along))
        remains.append(jnp.exp(last - along))
        unit = keys[u].astype(BF)
        met = lax.dot_general(unit, unit, (((1,), (1,)), ((), ())), preferred_element_type=F32)
        lowers.append(jnp.where(strict, rate * fade * met, 0.0))

    def ring(size):
        shared = (rows // (2 * size)) == (columns // (2 * size))
        return shared & (rows // size % 2 == 1) & (columns // size % 2 == 0)

    span = range(len(units))
    inverse = [identity - jnp.where(ring(1), lowers[u], 0.0) for u in span]
    size = 2
    while size < CH:
        here = ring(size)
        step = [rough(jnp.where(here, lowers[u], 0.0), inverse[u]) for u in span]
        inverse = [inverse[u] - rough(inverse[u], step[u]) for u in span]
        size *= 2
    wanted = [
        jnp.concatenate([rates[u] * growths[u] * keys[u], rates[u] * values[u]], axis=1)
        for u in span
    ]
    solved = [wanted[u] + rough(inverse[u] - identity, wanted[u]) for u in span]
    for u, (h, n) in enumerate(units):
        solved_ref[h, n] = solved[u]
        moved_ref[h, n] = lax.dot_general(
            (remains[u] * keys[u]).astype(BF),
            solved[u].astype(BF),
            (((0,), (0,)), ((), ())),
            preferred_element_type=F32,
        )


def chunks_of(x, place, qkv_weight, sums, rates, before):
    rows, width = x.shape
    _, _, columns = qkv_weight.shape
    parts, heads, chunks, _ = sums.shape
    dim = columns // heads
    step = min(4, heads)
    at_rows = pl.BlockSpec((rows, step * dim), lambda i, place: (place[0], i))
    at_chunks = pl.BlockSpec((step, chunks, CH, 2 * dim), lambda i, place: (i, place[0], 0, 0))
    per_head = pl.BlockSpec((1, step, chunks, CH), lambda i, place: (place[0], i, 0, 0))
    return pl.pallas_call(
        chunk_kernel,
        grid_spec=pltpu.PrefetchScalarGridSpec(
            num_scalar_prefetch=1,
            grid=(heads // step,),
            in_specs=[
                pl.BlockSpec((rows, width), lambda i, place: (0, 0)),
                pl.BlockSpec((1, width, step * dim), lambda i, place: (1, 0, i)),
                pl.BlockSpec((1, width, step * dim), lambda i, place: (2, 0, i)),
                per_head,
                per_head,
            ]
            + [pl.BlockSpec(memory_space=pl.ANY)] * len(before),
            out_specs=[at_rows, at_chunks, at_chunks],
        ),
        out_shape=[jax.ShapeDtypeStruct((parts * rows, columns), F32)]
        + [jax.ShapeDtypeStruct((heads, parts * chunks, CH, 2 * dim), F32)] * 2,
        input_output_aliases={6 + i: i for i in range(len(before))},
        compiler_params=pltpu.CompilerParams(vmem_limit_bytes=VMEM_LIMIT),
        name="chunks",
    )(place, x, qkv_weight, qkv_weight, sums, rates, *before)


def chain_kernel(moved_ref, sum_ref, starts_ref, end_ref):
    heads, chunks, dim, _ = moved_ref.shape
    rows, columns = tiles()
    identity = jnp.where(rows == columns, 1.0, 0.0)
    span = range(heads)

    def spread(total):
        decay = jnp.exp(jnp.broadcast_to(total, (CH, CH)).T[CH - 1 : CH, :])
        return jnp.broadcast_to(decay, (CH, CH))

    wholes = [[spread(sum_ref[h, n : n + 1, :]) for n in range(chunks)] for h in span]
    state = [
        jnp.concatenate(
            [wholes[h][0] * identity - moved_ref[h, 0, :, :dim], moved_ref[h, 0, :, dim:]], axis=1
        )
        for h in span
    ]
    for n in range(1, chunks):
        for h in span:
            starts_ref[h, n - 1] = state[h]
        removed = [rough(moved_ref[h, n, :, :dim], state[h]) for h in span]
        state = [
            jnp.concatenate(
                [
                    wholes[h][n] * state[h][:, :dim] - removed[h][:, :dim],
                    wholes[h][n] * state[h][:, dim:]
                    - removed[h][:, dim:]
                    + moved_ref[h, n, :, dim:],
                ],
                axis=1,
            )
            for h in span
        ]
    for h in span:
        decay = wholes[h][0]
        for n in range(1, chunks):
            decay = decay * wholes[h][n]
        end_ref[h, :dim, :dim] = (decay * identity - state[h][:, :dim]).astype(BF)
        end_ref[h, :dim, dim:] = state[h][:, dim:].astype(BF)
        end_ref[h, dim:, :] = left_pair(decay[:16])


def chain(moved, sums):
    heads, chunks, dim, double = moved.shape
    return pl.pallas_call(
        chain_kernel,
        out_shape=[
            jax.ShapeDtypeStruct((heads, chunks - 1, dim, double), F32),
            jax.ShapeDtypeStruct((heads, dim + 16, double), BF),
        ],
        compiler_params=pltpu.CompilerParams(vmem_limit_bytes=VMEM_LIMIT),
        name="chain",
    )(moved, sums)


def read_kernel(place_ref, w_ref, k_ref, solved_ref, starts_ref, sum_ref, *refs):
    x_refs = refs[:-2]
    enter_ref, local_ref = refs[-2:]
    heads, chunks, _ = sum_ref.shape
    dim = starts_ref.shape[2]
    rows, columns = tiles()
    inclusive = rows >= columns
    found = [dot(x_ref[...], w_ref[0]) for x_ref in x_refs]
    queries = []
    for place in range(len(found)):
        query = found[0]
        for i in range(1, len(found)):
            query = jnp.where(place_ref[i] == place, found[i], query)
        queries.append(query)
    each = chunks // len(found)
    units = [(h, n) for h in range(heads) for n in range(chunks)]
    for h, n in units:
        cut = slice(n * CH, (n + 1) * CH), slice(h * dim, (h + 1) * dim)
        across = jnp.broadcast_to(sum_ref[h, n : n + 1, :], (CH, CH))
        along = across.T
        fade = jnp.exp(jnp.where(inclusive, along - across, 0.0))
        query = unit_rows(queries[n // each][n % each * CH : (n % each + 1) * CH, cut[1]])
        masked = jnp.where(inclusive, fade * against_rows(query, k_ref[cut]), 0.0)
        probed = wide_product(masked, solved_ref[h, n])
        entering = jnp.exp(along) * query - probed[:, :dim]
        output = probed[:, dim:]
        if n:
            begun = wide_product(entering, starts_ref[h, n - 1])
            entering = begun[:, :dim]
            output = output + begun[:, dim:]
        enter_ref[cut] = entering.astype(BF)
        local_ref[cut] = output


def read(parts, places, qkv_weight, key, solved, starts, sums):
    length, columns = key.shape
    heads, chunks, _ = sums.shape
    dim = columns // heads
    width = qkv_weight.shape[1]
    step = 2 if heads % 2 == 0 else 1
    per_column = pl.BlockSpec((length, step * dim), lambda h: (0, h))
    four = lambda h: (h, 0, 0, 0)
    return pl.pallas_call(
        read_kernel,
        grid=(heads // step,),
        in_specs=[
            pl.BlockSpec(memory_space=pltpu.SMEM),
            pl.BlockSpec((1, width, step * dim), lambda h: (0, 0, h)),
            per_column,
            pl.BlockSpec((step, chunks, CH, 2 * dim), four),
            pl.BlockSpec((step, chunks - 1, dim, 2 * dim), four),
            pl.BlockSpec((step, chunks, CH), lambda h: (h, 0, 0)),
        ]
        + [pl.BlockSpec(x.shape, lambda h: (0, 0)) for x in parts],
        out_specs=[per_column, per_column],
        out_shape=[
            jax.ShapeDtypeStruct((length, columns), BF),
            jax.ShapeDtypeStruct((length, columns), F32),
        ],
        compiler_params=pltpu.CompilerParams(vmem_limit_bytes=VMEM_LIMIT),
        name="read",
    )(places, qkv_weight, key, solved, starts, sums, *parts)


def carry_kernel(ends_ref, after_ref, states_ref):
    segments, _, double = ends_ref.shape
    dim = double // 2
    state = jnp.zeros((dim, dim), F32)
    for s in range(segments):
        states_ref[s] = state.astype(BF)
        if s < segments - 1:
            decay = ends_ref[s, dim : dim + 1, :].astype(F32)
            decay = decay[:, :dim] + decay[:, dim:]
            removed = dot(ends_ref[s, :dim, :dim], left_pair(state))
            removed = removed[:, :dim] + removed[:, dim:]
            state = decay * state - removed + ends_ref[s, :dim, dim:].astype(F32)


def carry(ends, after):
    segments, _, double = ends.shape
    return pl.pallas_call(
        carry_kernel,
        in_specs=[pl.BlockSpec(memory_space=pltpu.VMEM), pl.BlockSpec(memory_space=pl.ANY)],
        out_shape=jax.ShapeDtypeStruct((segments, double // 2, double // 2), BF),
        compiler_params=pltpu.CompilerParams(vmem_limit_bytes=VMEM_LIMIT),
        name="carry",
    )(ends, after)


def finish_kernel(enter_ref, local_ref, state_ref, core_ref):
    heads, dim, _ = state_ref.shape
    for h in range(heads):
        cut = slice(h * dim, (h + 1) * dim)
        core_ref[:, cut] = local_ref[:, cut] + dot(enter_ref[:, cut], state_ref[h])


def finish(entering, local_out, states):
    length, columns = entering.shape
    heads, dim, _ = states.shape
    step = 2 if heads % 2 == 0 else 1
    per_column = pl.BlockSpec((length, step * dim), lambda h: (0, h))
    return pl.pallas_call(
        finish_kernel,
        grid=(heads // step,),
        in_specs=[per_column, per_column, pl.BlockSpec((step, dim, dim), lambda h: (h, 0, 0))],
        out_specs=per_column,
        out_shape=jax.ShapeDtypeStruct((length, columns), F32),
        compiler_params=pltpu.CompilerParams(vmem_limit_bytes=VMEM_LIMIT),
        name="finish",
    )(entering, local_out, states)


def relay(ends, seq_count):
    dim = ends.shape[2] // 2
    pairs = [(i, i + 1) for i in range(seq_count - 1)]
    removed, written = ends[:, :dim, :dim].astype(F32), ends[:, :dim, dim:].astype(F32)
    decay = ends[:, dim, :1].astype(F32) + ends[:, dim, dim : dim + 1].astype(F32)

    def step(_, incoming):
        outgoing = decay[:, :, None] * incoming + written
        outgoing = outgoing - jnp.einsum(
            "hij,hjk->hik", removed, incoming, precision=lax.Precision.HIGHEST
        )
        return lax.ppermute(outgoing, "seq", pairs)

    return lax.fori_loop(0, seq_count - 1, step, jnp.zeros_like(written)).astype(BF)


def move(values, change):
    exp_count = lax.axis_size("exp")
    pairs = []
    for s in range(lax.axis_size("seq")):
        for e in range(exp_count):
            to_s, to_e = change(s, e)
            pairs.append((s * exp_count + e, to_s * exp_count + to_e))
    return lax.ppermute(values, ("seq", "exp"), pairs)


def over_x(values):
    return move(values, lambda s, e: (s ^ 1, e))


def over_y(values):
    return move(values, lambda s, e: (s, e ^ 2))


def over_core(values):
    return move(values, lambda s, e: (s, e ^ 1))


def along_z(values, by):
    count = lax.axis_size("seq")
    return move(values, lambda s, e: ((s + 2 * by) % count, e))


def added(*terms):
    total = terms[0].astype(F32)
    for term in terms[1:]:
        total = total + term.astype(F32)
    return total


def route_waves(normed, expert_ids, expert_weights, gate_up_weight, down, capacity):
    tok_rows, width = normed.shape
    choose = expert_ids.shape[1]
    local_experts = gate_up_weight.shape[0]
    me = lax.axis_index("seq") * lax.axis_size("exp") + lax.axis_index("exp")
    first = (jnp.stack([me, me ^ 1]) * local_experts).astype(jnp.int32)
    gap = jnp.zeros((tok_rows, ROUTE_STEP - choose), BF)
    high, low = split(expert_weights)
    tail = jnp.zeros((tok_rows, 128 - 3 * ROUTE_STEP), BF)
    block = jnp.concatenate(
        [normed, expert_ids.astype(BF), gap, high, gap, low, gap, tail], axis=1
    )
    weights = (gate_up_weight, down, over_core(gate_up_weight), over_core(down))
    count = lax.axis_size("seq") // 2
    order = list(range(1, count)) + [0]
    first_way = [over_y if wave == 1 else over_x for wave in range(count)]
    second_way = [over_x if wave == 1 else over_y for wave in range(count)]
    block = [block]
    for wave in range(1, count):
        block.append(along_z(block[-1], 1))
    by_one = [first_way[wave](block[wave]) for wave in range(count)]
    by_two = [second_way[wave](block[wave]) for wave in range(count)]
    diagonal = {wave: second_way[wave](by_one[wave]) for wave in (0, 1)}
    for wave in range(2, count):
        diagonal[wave] = along_z(diagonal[wave - 1], 1)
    due = [() for _ in range(count + 3)]
    for call, wave in enumerate(order):
        if call and wave:
            due[call - 1] += (block[wave],)
        if call > 1:
            due[call - 1 if wave else 0] += (by_one[wave], by_two[wave])
    running = sum_below = None
    for call, wave in enumerate(order):
        own, sum_one, sum_two, sum_both = experts(
            (block[wave], by_one[wave], by_two[wave], diagonal[wave]),
            first,
            weights,
            due[call],
            capacity,
            choose,
        )
        one, two = first_way[wave], second_way[wave]
        due[call + 1] += (own,)
        if sum_below is not None:
            sum_both = added(sum_both, sum_below).astype(BF)
        from_two = two(sum_two)
        if 0 < wave < count - 1:
            sum_below = along_z(sum_both, 1)
            due[call + 2] += (sum_below,)
        else:
            sum_below = None
            sum_one = added(sum_one, two(sum_both)).astype(BF)
        from_one = one(sum_one)
        due[call + 2] += (from_two, from_one)
        here = added(own, from_two, from_one)
        if running is not None:
            here = here + running.astype(F32)
        if wave:
            running = along_z(here.astype(BF), 1)
            due[call + 3] += (running,)
    return here


def route_some(normed, expert_ids, expert_weights, gate_up_weight, down, capacity):
    axes = ("seq", "exp")
    tok_rows, width = normed.shape
    choose = expert_ids.shape[1]
    local_experts = gate_up_weight.shape[0]
    expert_width = down.shape[1]
    devices = lax.axis_size("seq") * lax.axis_size("exp")
    experts_all = local_experts * devices
    flat_ids = expert_ids.reshape(-1)
    onehot = (flat_ids[:, None] == jnp.arange(experts_all, dtype=jnp.int32)[None, :]).astype(
        jnp.int32
    )
    rank = jnp.sum(jnp.cumsum(onehot, axis=0) * onehot, axis=1) - 1
    slot = flat_ids * capacity + rank
    token_of = jnp.arange(tok_rows * choose, dtype=jnp.int32) // choose
    send = jnp.zeros((experts_all * capacity, width), BF).at[slot].set(normed[token_of])
    both = jnp.einsum(
        "secd,edf->secf",
        lax.all_to_all(
            send.reshape(devices, local_experts, capacity, width),
            axes,
            split_axis=0,
            concat_axis=0,
            tiled=True,
        ),
        gate_up_weight,
        preferred_element_type=F32,
    )
    hidden = (jax.nn.silu(both[..., :expert_width]) * both[..., expert_width:]).astype(BF)
    back = lax.all_to_all(
        jnp.einsum("secf,efd->secd", hidden, down, preferred_element_type=F32).astype(BF),
        axes,
        split_axis=0,
        concat_axis=0,
        tiled=True,
    )
    back_rows = back.reshape(experts_all * capacity, width)[slot].astype(F32)
    return jnp.sum(
        back_rows.reshape(tok_rows, choose, width) * expert_weights[:, :, None], axis=1
    )


def local(
    stream,
    moe_gain,
    expert_ids,
    expert_weights,
    gate_up_weight,
    down,
    mixer_gain,
    qkv_weight,
    decay_log,
    write_rate,
):
    tok_rows, width = stream.shape
    choose = expert_ids.shape[1]
    seq_count = lax.axis_size("seq")
    devices = seq_count * lax.axis_size("exp")
    experts_all = gate_up_weight.shape[0] * devices
    capacity = max(2, (tok_rows * choose * 6 + experts_all * 5 - 1) // (experts_all * 5))
    normed = rms_scale(stream, moe_gain).astype(BF)
    planes = lax.axis_size("exp") == 4 and seq_count % 4 == 0 and choose <= ROUTE_STEP
    route = route_waves if planes and experts_all <= 256 else route_some
    moe = route(normed, expert_ids, expert_weights, gate_up_weight, down, capacity)
    mixed = (stream.astype(F32) + moe).astype(BF)
    normed_mix = rms_scale(mixed, mixer_gain).astype(BF)
    heads = decay_log.shape[1]
    blocks = decay_log.shape[0] // CH
    sums = jnp.cumsum(decay_log.T.reshape(heads, blocks, CH), axis=-1)
    rates = write_rate.T.reshape(heads, blocks, CH)
    pairs = blocks // 2
    by_pair = lambda values: values.reshape(heads, pairs, 2, CH).transpose(1, 0, 2, 3)
    if planes:
        core = lax.axis_index("exp") % 2
        side = lax.axis_index("exp") // 2
        from_y = over_y(normed_mix)
        both_sides = [(normed_mix, over_core(normed_mix)), (from_y, over_core(from_y))]
        parts = [
            (
                jnp.concatenate([jnp.where(core == 0, a, b), jnp.where(core == 0, b, a)], axis=0),
                place,
            )
            for (a, b), place in zip(both_sides, (side, 1 - side))
        ]
    else:
        gathered = lax.all_gather(normed_mix, "exp", axis=0, tiled=True)
        parts = [(gathered[2 * CH * i : 2 * CH * (i + 1)], jnp.int32(i)) for i in range(pairs)]
    found = ()
    for x, place in parts:
        found = chunks_of(
            x,
            place.astype(jnp.int32).reshape(1),
            qkv_weight,
            by_pair(sums),
            by_pair(rates),
            found,
        )
    key, solved, moved = found
    starts, ends = chain(moved, sums)
    places = jnp.stack([place for _, place in parts]).astype(jnp.int32)
    entering, local_out = read([x for x, _ in parts], places, qkv_weight, key, solved, starts, sums)
    if heads % seq_count == 0:
        dim = ends.shape[2] // 2
        each = heads // seq_count
        held = lax.all_to_all(ends, "seq", split_axis=0, concat_axis=0, tiled=True)
        held = held.reshape(seq_count, each, dim + 16, 2 * dim)
        states = jnp.stack([carry(held[:, i], entering) for i in range(each)], axis=1)
        arriving = lax.all_to_all(
            states.reshape(seq_count * each, dim, dim), "seq", split_axis=0, concat_axis=0, tiled=True
        )
    else:
        arriving = relay(ends, seq_count)
    return (mixed, finish(entering, local_out, arriving))


def solution(mesh):
    in_specs = (
        P(("seq", "exp"), None),
        P(),
        P(("seq", "exp"), None),
        P(("seq", "exp"), None),
        P(("seq", "exp"), None, None),
        P(("seq", "exp"), None, None),
        P(),
        P(None, None, "exp"),
        P("seq", "exp"),
        P("seq", "exp"),
    )
    out_specs = (P(("seq", "exp"), None), P("seq", "exp"))
    return jax.shard_map(local, mesh=mesh, in_specs=in_specs, out_specs=out_specs, check_vma=False)
```

```python
from functools import partial

import jax
import jax.numpy as jnp
from jax import lax
from jax.experimental import pallas as pl
from jax.experimental.pallas import tpu as pltpu
from jax.sharding import PartitionSpec as P

CH = 128
ROUTE_STEP = 16
SMALL_VMEM = 24 * 1024 * 1024
VMEM_LIMIT = 56 * 1024 * 1024
BF = jnp.bfloat16
F32 = jnp.float32


def rms_scale(values, gain):
    wide = values.astype(F32)
    return wide * lax.rsqrt(jnp.mean(wide * wide, axis=-1, keepdims=True) + 1e-06) * gain


def dot(a, b):
    return jnp.dot(a, b, preferred_element_type=F32)


def split(a):
    high = a.astype(BF)
    return high, (a - high.astype(F32)).astype(BF)


def rough(a, b):
    return dot(a.astype(BF), b.astype(BF))


def left_pair(a):
    high, low = split(a)
    return jnp.concatenate([high, low], axis=1)


def right_pair(b):
    high, low = split(b)
    row = jnp.concatenate([high, low], axis=1)
    return jnp.concatenate([row, row], axis=0)


def wide_product(a, b):
    columns = b.shape[1]
    both = dot(left_pair(a), right_pair(b))
    return both[:, :columns] + both[:, columns:]


def moe_kernel(capacity, choose, *refs):
    first_ref, *block_refs = refs[:5]
    weight_refs = refs[5:9]
    out_refs = refs[-9:-5]
    gate_up_ref, down_ref, rows_ref, back_ref, sem = refs[-5:]
    tok, wide = block_refs[0].shape
    width = rows_ref.shape[2]
    experts_here = gate_up_ref.shape[0]
    half = experts_here // 2
    expert_width = down_ref.shape[1]
    pair_rows = rows_ref.shape[1] // 2

    copies = []
    for e in range(experts_here):
        side, at = divmod(e, half)
        fetch_in = pltpu.make_async_copy(
            weight_refs[2 * side].at[at], gate_up_ref.at[e], sem.at[0, e]
        )
        fetch_out = pltpu.make_async_copy(
            weight_refs[2 * side + 1].at[at], down_ref.at[e], sem.at[1, e]
        )
        fetch_in.start()
        fetch_out.start()
        copies.append((fetch_in, fetch_out))

    matched, weights = [], []
    for block_ref in block_refs:
        routing = block_ref[:, width:].astype(F32).T
        ids = routing[:choose]
        scale = routing[ROUTE_STEP : ROUTE_STEP + choose]
        scale = scale + routing[2 * ROUTE_STEP : 2 * ROUTE_STEP + choose]
        for e in range(experts_here):
            side, at = divmod(e, half)
            hit = ids == (first_ref[side] + at).astype(F32)
            matched.append(jnp.max(jnp.where(hit, 1.0, 0.0), axis=0, keepdims=True))
            weights.append(jnp.sum(jnp.where(hit, scale, 0.0), axis=0, keepdims=True))
    match = jnp.concatenate(matched, axis=0)
    before = lax.broadcasted_iota(jnp.int32, (tok, tok), 0) < lax.broadcasted_iota(
        jnp.int32, (tok, tok), 1
    )
    rank = dot(match.astype(BF), jnp.where(before, 1.0, 0.0).astype(BF))
    rank = jnp.where(match > 0.5, rank, -1e4)
    row_number = lax.broadcasted_iota(jnp.int32, (pair_rows, 2 * tok), 0).astype(F32)
    picks = []
    for pair in range(2):
        x_pair = jnp.concatenate(
            [block_refs[2 * pair][:, :width], block_refs[2 * pair + 1][:, :width]], axis=0
        )
        here = []
        for e in range(experts_here):
            low = 2 * pair * experts_here + e
            high = low + experts_here
            place = jnp.concatenate(
                [rank[low : low + 1], rank[high : high + 1] + float(capacity)], axis=1
            )
            here.append(jnp.where(row_number == place, 1.0, 0.0))
        picks.append(here)
        chosen = dot(jnp.concatenate(here, axis=0).astype(BF), x_pair).astype(BF)
        for e in range(experts_here):
            rows_ref[e, pair * pair_rows : (pair + 1) * pair_rows, :] = chosen[
                e * pair_rows : (e + 1) * pair_rows
            ]
    for e in range(experts_here):
        copies[e][0].wait()
        both = dot(rows_ref[e], gate_up_ref[e])
        gate = both[:, :expert_width]
        hidden = (gate / (1.0 + jnp.exp(-gate)) * both[:, expert_width:]).astype(BF)
        copies[e][1].wait()
        back_ref[e] = dot(hidden, down_ref[e]).astype(BF)
    for pair in range(2):
        scaled, rows = [], []
        for e in range(experts_here):
            low = 2 * pair * experts_here + e
            high = low + experts_here
            weight = jnp.concatenate([weights[low], weights[high]], axis=1)
            scaled.append(picks[pair][e] * weight)
            rows.append(back_ref[e, pair * pair_rows : (pair + 1) * pair_rows, :])
        high_part, low_part = split(jnp.concatenate(scaled, axis=0))
        left = jnp.concatenate([high_part, low_part], axis=0)
        right = jnp.concatenate(rows + rows, axis=0)
        summed = lax.dot_general(
            left, right, (((0,), (0,)), ((), ())), preferred_element_type=F32
        ).astype(BF)
        out_refs[2 * pair][...] = summed[:tok]
        out_refs[2 * pair + 1][...] = summed[tok:]


def experts(blocks, first, weights, after, capacity, choose):
    tok, wide = blocks[0].shape
    gate_up_weight, down = weights[:2]
    local_experts, width, double = gate_up_weight.shape
    here = 2 * local_experts
    pair_rows = -(-2 * capacity // 16) * 16
    whole = pl.BlockSpec(memory_space=pltpu.VMEM)
    return pl.pallas_call(
        partial(moe_kernel, capacity, choose),
        in_specs=[pl.BlockSpec(memory_space=pltpu.SMEM)]
        + [whole] * 4
        + [pl.BlockSpec(memory_space=pl.ANY)] * (4 + len(after)),
        out_specs=[whole] * 4,
        out_shape=[jax.ShapeDtypeStruct((tok, width), BF)] * 4,
        scratch_shapes=[
            pltpu.VMEM((here,) + gate_up_weight.shape[1:], BF),
            pltpu.VMEM((here,) + down.shape[1:], BF),
            pltpu.VMEM((here, 2 * pair_rows, width), BF),
            pltpu.VMEM((here, 2 * pair_rows, width), BF),
            pltpu.SemaphoreType.DMA((2, here)),
        ],
        compiler_params=pltpu.CompilerParams(vmem_limit_bytes=VMEM_LIMIT),
        cost_estimate=pl.CostEstimate(
            flops=here * pair_rows * width * double // 4,
            bytes_accessed=tok * width,
            transcendentals=0,
        ),
        name="experts",
    )(first, *blocks, *weights, *after)


def unit_rows(values):
    return values * lax.rsqrt(jnp.sum(values * values, axis=-1, keepdims=True) + 1e-06)


def tiles():
    rows = lax.broadcasted_iota(jnp.int32, (CH, CH), 0)
    columns = lax.broadcasted_iota(jnp.int32, (CH, CH), 1)
    return rows, columns


def against_rows(a, b):
    high, low = split(b)
    right = jnp.concatenate(
        [jnp.concatenate([high, high], axis=1), jnp.concatenate([low, low], axis=1)], axis=0
    )
    both = lax.dot_general(
        left_pair(a), right, (((1,), (1,)), ((), ())), preferred_element_type=F32
    )
    return both[:, : b.shape[0]] + both[:, b.shape[0] :]


def gate_kernel(sum_ref, rate_ref, solve_ref, read_ref, whole_ref):
    heads, chunks, _ = sum_ref.shape
    rows, columns = tiles()
    for h in range(heads):
        for n in range(chunks):
            across = jnp.broadcast_to(sum_ref[h, n : n + 1, :], (CH, CH))
            along = across.T
            rate = jnp.broadcast_to(rate_ref[h, n : n + 1, :], (CH, CH)).T
            last = along[CH - 1 : CH, :]
            fade = jnp.where(rows >= columns, jnp.exp(jnp.minimum(along - across, 0.0)), 0.0)
            growth = jnp.exp(along)
            solve_ref[n, h, 0] = jnp.where(rows > columns, rate * fade, 0.0)
            solve_ref[n, h, 1] = rate * growth
            solve_ref[n, h, 2] = rate
            solve_ref[n, h, 3] = jnp.exp(last - along)
            read_ref[h, n, 0] = fade
            read_ref[h, n, 1] = growth
            whole_ref[h, n : n + 1, :] = jnp.exp(last)


def gates(sums, rates):
    heads, chunks, _ = sums.shape
    per_head = pl.BlockSpec((1, chunks, CH), lambda h: (h, 0, 0))
    return pl.pallas_call(
        gate_kernel,
        grid=(heads,),
        in_specs=[per_head, per_head],
        out_specs=[
            pl.BlockSpec((chunks, 1, 4, CH, CH), lambda h: (0, h, 0, 0, 0)),
            pl.BlockSpec((1, chunks, 2, CH, CH), lambda h: (h, 0, 0, 0, 0)),
            per_head,
        ],
        out_shape=[
            jax.ShapeDtypeStruct((chunks, heads, 4, CH, CH), F32),
            jax.ShapeDtypeStruct((heads, chunks, 2, CH, CH), F32),
            jax.ShapeDtypeStruct((heads, chunks, CH), F32),
        ],
        compiler_params=pltpu.CompilerParams(vmem_limit_bytes=SMALL_VMEM),
        name="gates",
    )(sums, rates)


def chunk_kernel(place_ref, x_ref, gate_ref, w_ref, *refs):
    k_ref, solved_ref, moved_ref, key_w_ref, value_w_ref, sem = refs[-6:]
    heads = gate_ref.shape[1]
    dim = key_w_ref.shape[1] // heads
    fetch_key = pltpu.make_async_copy(w_ref.at[1], key_w_ref, sem.at[0])
    fetch_value = pltpu.make_async_copy(w_ref.at[2], value_w_ref, sem.at[1])
    fetch_key.start()
    fetch_value.start()
    rows, columns = tiles()
    identity = jnp.where(rows == columns, 1.0, 0.0)
    span = range(heads)
    x = x_ref[...]
    fetch_key.wait()
    projected = dot(x, key_w_ref[...])
    keys, lowers = [], []
    for h in span:
        key = unit_rows(projected[:, h * dim : (h + 1) * dim])
        k_ref[:, h * dim : (h + 1) * dim] = key
        unit = key.astype(BF)
        met = lax.dot_general(unit, unit, (((1,), (1,)), ((), ())), preferred_element_type=F32)
        keys.append(key)
        lowers.append(gate_ref[0, h, 0] * met)

    def ring(size):
        shared = (rows // (2 * size)) == (columns // (2 * size))
        return shared & (rows // size % 2 == 1) & (columns // size % 2 == 0)

    inverse = [identity - jnp.where(ring(1), lowers[h], 0.0) for h in span]
    size = 2
    while size < CH:
        here = ring(size)
        step = [rough(jnp.where(here, lowers[h], 0.0), inverse[h]) for h in span]
        inverse = [inverse[h] - rough(inverse[h], step[h]) for h in span]
        size *= 2
    fetch_value.wait()
    projected = dot(x, value_w_ref[...])
    wanted = [
        jnp.concatenate(
            [
                gate_ref[0, h, 1] * keys[h],
                gate_ref[0, h, 2] * projected[:, h * dim : (h + 1) * dim],
            ],
            axis=1,
        )
        for h in span
    ]
    solved = [wanted[h] + rough(inverse[h] - identity, wanted[h]) for h in span]
    for h in span:
        solved_ref[h, 0] = solved[h]
        moved_ref[h, 0] = lax.dot_general(
            (gate_ref[0, h, 3] * keys[h]).astype(BF),
            solved[h].astype(BF),
            (((0,), (0,)), ((), ())),
            preferred_element_type=F32,
        )


def chunk_of(x, place, qkv_weight, gate, before):
    rows, width = x.shape
    _, _, columns = qkv_weight.shape
    chunks, heads = gate.shape[:2]
    dim = columns // heads
    at_chunk = pl.BlockSpec((heads, 1, CH, 2 * dim), lambda i, place: (0, place[0], 0, 0))
    anywhere = pl.BlockSpec(memory_space=pl.ANY)
    return pl.pallas_call(
        chunk_kernel,
        grid_spec=pltpu.PrefetchScalarGridSpec(
            num_scalar_prefetch=1,
            grid=(1,),
            in_specs=[
                pl.BlockSpec((rows, width), lambda i, place: (0, 0)),
                pl.BlockSpec((1, heads, 4, CH, CH), lambda i, place: (place[0], 0, 0, 0, 0)),
                anywhere,
            ]
            + [anywhere] * len(before),
            out_specs=[
                pl.BlockSpec((rows, columns), lambda i, place: (place[0], 0)),
                at_chunk,
                at_chunk,
            ],
            scratch_shapes=[
                pltpu.VMEM((width, columns), BF),
                pltpu.VMEM((width, columns), BF),
                pltpu.SemaphoreType.DMA((2,)),
            ],
        ),
        out_shape=[jax.ShapeDtypeStruct((chunks * rows, columns), F32)]
        + [jax.ShapeDtypeStruct((heads, chunks, CH, 2 * dim), F32)] * 2,
        input_output_aliases={4 + i: i for i in range(len(before))},
        compiler_params=pltpu.CompilerParams(vmem_limit_bytes=VMEM_LIMIT),
        name="chunk",
    )(place, x, gate, qkv_weight, *before)


def chain_kernel(moved_ref, whole_ref, starts_ref, end_ref):
    heads, chunks, dim, _ = moved_ref.shape
    rows, columns = tiles()
    identity = jnp.where(rows == columns, 1.0, 0.0)
    span = range(heads)

    wholes = [
        [jnp.broadcast_to(whole_ref[h, n : n + 1, :], (CH, CH)) for n in range(chunks)] for h in span
    ]
    state = [
        jnp.concatenate(
            [wholes[h][0] * identity - moved_ref[h, 0, :, :dim], moved_ref[h, 0, :, dim:]], axis=1
        )
        for h in span
    ]
    for n in range(1, chunks):
        for h in span:
            starts_ref[h, n - 1] = state[h]
        removed = [rough(moved_ref[h, n, :, :dim], state[h]) for h in span]
        state = [
            jnp.concatenate(
                [
                    wholes[h][n] * state[h][:, :dim] - removed[h][:, :dim],
                    wholes[h][n] * state[h][:, dim:]
                    - removed[h][:, dim:]
                    + moved_ref[h, n, :, dim:],
                ],
                axis=1,
            )
            for h in span
        ]
    for h in span:
        decay = wholes[h][0]
        for n in range(1, chunks):
            decay = decay * wholes[h][n]
        end_ref[h, :dim, :dim] = (decay * identity - state[h][:, :dim]).astype(BF)
        end_ref[h, :dim, dim:] = state[h][:, dim:].astype(BF)
        end_ref[h, dim:, :] = left_pair(decay[:16])


def chain(moved, whole):
    heads, chunks, dim, double = moved.shape
    return pl.pallas_call(
        chain_kernel,
        out_shape=[
            jax.ShapeDtypeStruct((heads, chunks - 1, dim, double), F32),
            jax.ShapeDtypeStruct((heads, dim + 16, double), BF),
        ],
        compiler_params=pltpu.CompilerParams(vmem_limit_bytes=VMEM_LIMIT),
        name="chain",
    )(moved, whole)


def read_kernel(place_ref, w_ref, k_ref, solved_ref, starts_ref, gate_ref, *refs):
    x_refs = refs[:-2]
    enter_ref, local_ref = refs[-2:]
    heads, chunks = gate_ref.shape[:2]
    dim = starts_ref.shape[2]
    found = dot(jnp.concatenate([x_ref[...] for x_ref in x_refs], axis=0), w_ref[0])
    found = [found[i * CH : (i + 1) * CH] for i in range(chunks)]
    for n in range(chunks):
        projected = found[0]
        for i in range(1, chunks):
            projected = jnp.where(place_ref[i] == n, found[i], projected)
        for h in range(heads):
            cut = slice(n * CH, (n + 1) * CH), slice(h * dim, (h + 1) * dim)
            query = unit_rows(projected[:, cut[1]])
            masked = gate_ref[h, n, 0] * against_rows(query, k_ref[cut])
            probed = wide_product(masked, solved_ref[h, n])
            entering = gate_ref[h, n, 1] * query - probed[:, :dim]
            output = probed[:, dim:]
            if n:
                begun = wide_product(entering, starts_ref[h, n - 1])
                entering = begun[:, :dim]
                output = output + begun[:, dim:]
            enter_ref[cut] = entering.astype(BF)
            local_ref[cut] = output


def read(parts, places, qkv_weight, key, solved, starts, gate):
    length, columns = key.shape
    heads, chunks = gate.shape[:2]
    dim = columns // heads
    width = qkv_weight.shape[1]
    step = 2 if heads % 2 == 0 else 1
    per_column = pl.BlockSpec((length, step * dim), lambda h: (0, h))
    four = lambda h: (h, 0, 0, 0)
    return pl.pallas_call(
        read_kernel,
        grid=(heads // step,),
        in_specs=[
            pl.BlockSpec(memory_space=pltpu.SMEM),
            pl.BlockSpec((1, width, step * dim), lambda h: (0, 0, h)),
            per_column,
            pl.BlockSpec((step, chunks, CH, 2 * dim), four),
            pl.BlockSpec((step, chunks - 1, dim, 2 * dim), four),
            pl.BlockSpec((step, chunks, 2, CH, CH), lambda h: (h, 0, 0, 0, 0)),
        ]
        + [pl.BlockSpec(x.shape, lambda h: (0, 0)) for x in parts],
        out_specs=[per_column, per_column],
        out_shape=[
            jax.ShapeDtypeStruct((length, columns), BF),
            jax.ShapeDtypeStruct((length, columns), F32),
        ],
        compiler_params=pltpu.CompilerParams(vmem_limit_bytes=VMEM_LIMIT),
        name="read",
    )(places, qkv_weight, key, solved, starts, gate, *parts)


def carry_kernel(ends_ref, after_ref, states_ref):
    segments, _, double = ends_ref.shape
    dim = double // 2
    state = jnp.zeros((dim, dim), F32)
    for s in range(segments):
        states_ref[s] = state.astype(BF)
        if s < segments - 1:
            decay = ends_ref[s, dim : dim + 1, :].astype(F32)
            decay = decay[:, :dim] + decay[:, dim:]
            removed = dot(ends_ref[s, :dim, :dim], left_pair(state))
            removed = removed[:, :dim] + removed[:, dim:]
            state = decay * state - removed + ends_ref[s, :dim, dim:].astype(F32)


def carry(ends, after):
    segments, _, double = ends.shape
    return pl.pallas_call(
        carry_kernel,
        in_specs=[pl.BlockSpec(memory_space=pltpu.VMEM), pl.BlockSpec(memory_space=pl.ANY)],
        out_shape=jax.ShapeDtypeStruct((segments, double // 2, double // 2), BF),
        compiler_params=pltpu.CompilerParams(vmem_limit_bytes=VMEM_LIMIT),
        name="carry",
    )(ends, after)


def finish_kernel(enter_ref, local_ref, state_ref, core_ref):
    heads, dim, _ = state_ref.shape
    for h in range(heads):
        cut = slice(h * dim, (h + 1) * dim)
        core_ref[:, cut] = local_ref[:, cut] + dot(enter_ref[:, cut], state_ref[h])


def finish(entering, local_out, states):
    length, columns = entering.shape
    heads, dim, _ = states.shape
    step = 2 if heads % 2 == 0 else 1
    per_column = pl.BlockSpec((length, step * dim), lambda h: (0, h))
    return pl.pallas_call(
        finish_kernel,
        grid=(heads // step,),
        in_specs=[per_column, per_column, pl.BlockSpec((step, dim, dim), lambda h: (h, 0, 0))],
        out_specs=per_column,
        out_shape=jax.ShapeDtypeStruct((length, columns), F32),
        compiler_params=pltpu.CompilerParams(vmem_limit_bytes=VMEM_LIMIT),
        name="finish",
    )(entering, local_out, states)


def relay(ends, seq_count):
    dim = ends.shape[2] // 2
    pairs = [(i, i + 1) for i in range(seq_count - 1)]
    removed, written = ends[:, :dim, :dim].astype(F32), ends[:, :dim, dim:].astype(F32)
    decay = ends[:, dim, :1].astype(F32) + ends[:, dim, dim : dim + 1].astype(F32)

    def step(_, incoming):
        outgoing = decay[:, :, None] * incoming + written
        outgoing = outgoing - jnp.einsum(
            "hij,hjk->hik", removed, incoming, precision=lax.Precision.HIGHEST
        )
        return lax.ppermute(outgoing, "seq", pairs)

    return lax.fori_loop(0, seq_count - 1, step, jnp.zeros_like(written)).astype(BF)


def move(values, change):
    exp_count = lax.axis_size("exp")
    pairs = []
    for s in range(lax.axis_size("seq")):
        for e in range(exp_count):
            to_s, to_e = change(s, e)
            pairs.append((s * exp_count + e, to_s * exp_count + to_e))
    return lax.ppermute(values, ("seq", "exp"), pairs)


def over_x(values):
    return move(values, lambda s, e: (s ^ 1, e))


def over_y(values):
    return move(values, lambda s, e: (s, e ^ 2))


def over_core(values):
    return move(values, lambda s, e: (s, e ^ 1))


def along_z(values, by):
    count = lax.axis_size("seq")
    return move(values, lambda s, e: ((s + 2 * by) % count, e))


def added(*terms):
    total = terms[0].astype(F32)
    for term in terms[1:]:
        total = total + term.astype(F32)
    return total


def route_waves(normed, expert_ids, expert_weights, gate_up_weight, down, capacity, early):
    tok_rows, width = normed.shape
    choose = expert_ids.shape[1]
    local_experts = gate_up_weight.shape[0]
    me = lax.axis_index("seq") * lax.axis_size("exp") + lax.axis_index("exp")
    first = (jnp.stack([me, me ^ 1]) * local_experts).astype(jnp.int32)
    gap = jnp.zeros((tok_rows, ROUTE_STEP - choose), BF)
    high, low = split(expert_weights)
    tail = jnp.zeros((tok_rows, 128 - 3 * ROUTE_STEP), BF)
    block = jnp.concatenate(
        [normed, expert_ids.astype(BF), gap, high, gap, low, gap, tail], axis=1
    )
    weights = (gate_up_weight, down, over_core(gate_up_weight), over_core(down))
    count = lax.axis_size("seq") // 2
    order = list(range(1, count)) + [0]
    first_way = [over_y if wave == 1 else over_x for wave in range(count)]
    second_way = [over_x if wave == 1 else over_y for wave in range(count)]
    block = [block]
    for wave in range(1, count):
        block.append(along_z(block[-1], 1))
    by_one = [first_way[wave](block[wave]) for wave in range(count)]
    by_two = [second_way[wave](block[wave]) for wave in range(count)]
    diagonal = {wave: second_way[wave](by_one[wave]) for wave in (0, 1)}
    for wave in range(2, count):
        diagonal[wave] = along_z(diagonal[wave - 1], 1)
    due = [() for _ in range(count + 3)]
    due[0] = early
    for call, wave in enumerate(order):
        if call and wave:
            due[call - 1] += (block[wave],)
        if call > 1:
            due[call - 1 if wave else 0] += (by_one[wave], by_two[wave])
    running = sum_below = None
    for call, wave in enumerate(order):
        own, sum_one, sum_two, sum_both = experts(
            (block[wave], by_one[wave], by_two[wave], diagonal[wave]),
            first,
            weights,
            due[call],
            capacity,
            choose,
        )
        one, two = first_way[wave], second_way[wave]
        due[call + 1] += (own,)
        if sum_below is not None:
            sum_both = added(sum_both, sum_below).astype(BF)
        from_two = two(sum_two)
        if 0 < wave < count - 1:
            sum_below = along_z(sum_both, 1)
            due[call + 2] += (sum_below,)
        else:
            sum_below = None
            sum_one = added(sum_one, two(sum_both)).astype(BF)
        from_one = one(sum_one)
        due[call + 2] += (from_two, from_one)
        here = added(own, from_two, from_one)
        if running is not None:
            here = here + running.astype(F32)
        if wave:
            running = along_z(here.astype(BF), 1)
            due[call + 3] += (running,)
    return here


def route_some(normed, expert_ids, expert_weights, gate_up_weight, down, capacity, early):
    axes = ("seq", "exp")
    tok_rows, width = normed.shape
    choose = expert_ids.shape[1]
    local_experts = gate_up_weight.shape[0]
    expert_width = down.shape[1]
    devices = lax.axis_size("seq") * lax.axis_size("exp")
    experts_all = local_experts * devices
    flat_ids = expert_ids.reshape(-1)
    onehot = (flat_ids[:, None] == jnp.arange(experts_all, dtype=jnp.int32)[None, :]).astype(
        jnp.int32
    )
    rank = jnp.sum(jnp.cumsum(onehot, axis=0) * onehot, axis=1) - 1
    slot = flat_ids * capacity + rank
    token_of = jnp.arange(tok_rows * choose, dtype=jnp.int32) // choose
    send = jnp.zeros((experts_all * capacity, width), BF).at[slot].set(normed[token_of])
    both = jnp.einsum(
        "secd,edf->secf",
        lax.all_to_all(
            send.reshape(devices, local_experts, capacity, width),
            axes,
            split_axis=0,
            concat_axis=0,
            tiled=True,
        ),
        gate_up_weight,
        preferred_element_type=F32,
    )
    hidden = (jax.nn.silu(both[..., :expert_width]) * both[..., expert_width:]).astype(BF)
    back = lax.all_to_all(
        jnp.einsum("secf,efd->secd", hidden, down, preferred_element_type=F32).astype(BF),
        axes,
        split_axis=0,
        concat_axis=0,
        tiled=True,
    )
    back_rows = back.reshape(experts_all * capacity, width)[slot].astype(F32)
    return jnp.sum(
        back_rows.reshape(tok_rows, choose, width) * expert_weights[:, :, None], axis=1
    )


def local(
    stream,
    moe_gain,
    expert_ids,
    expert_weights,
    gate_up_weight,
    down,
    mixer_gain,
    qkv_weight,
    decay_log,
    write_rate,
):
    tok_rows, width = stream.shape
    choose = expert_ids.shape[1]
    seq_count = lax.axis_size("seq")
    devices = seq_count * lax.axis_size("exp")
    experts_all = gate_up_weight.shape[0] * devices
    capacity = max(2, (tok_rows * choose * 6 + experts_all * 5 - 1) // (experts_all * 5))
    normed = rms_scale(stream, moe_gain).astype(BF)
    planes = lax.axis_size("exp") == 4 and seq_count % 4 == 0 and choose <= ROUTE_STEP
    route = route_waves if planes and experts_all <= 256 else route_some
    heads = decay_log.shape[1]
    blocks = decay_log.shape[0] // CH
    sums = jnp.cumsum(decay_log.T.reshape(heads, blocks, CH), axis=-1)
    rates = write_rate.T.reshape(heads, blocks, CH)
    solve_gate, read_gate, whole = gates(sums, rates)
    moe = route(
        normed, expert_ids, expert_weights, gate_up_weight, down, capacity, (solve_gate,)
    )
    mixed = (stream.astype(F32) + moe).astype(BF)
    normed_mix = rms_scale(mixed, mixer_gain).astype(BF)
    if planes:
        from_y = over_y(normed_mix)
        parts = [normed_mix, over_core(normed_mix), from_y, None]
        places = lax.axis_index("exp") ^ jnp.arange(blocks, dtype=jnp.int32)
    else:
        gathered = lax.all_gather(normed_mix, "exp", axis=0, tiled=True)
        parts = [gathered[CH * i : CH * (i + 1)] for i in range(blocks)]
        places = jnp.arange(blocks, dtype=jnp.int32)
    found = ()
    for i, x in enumerate(parts):
        if i == 1 and planes:
            parts[2], found = lax.optimization_barrier((parts[2], found))
            parts[3] = over_core(parts[2])
        found = chunk_of(x, places[i : i + 1], qkv_weight, solve_gate, found)
    key, solved, moved = found
    starts, ends = chain(moved, whole)
    entering, local_out = read(parts, places, qkv_weight, key, solved, starts, read_gate)
    if heads % seq_count == 0:
        dim = ends.shape[2] // 2
        each = heads // seq_count
        held = lax.all_to_all(ends, "seq", split_axis=0, concat_axis=0, tiled=True)
        held = held.reshape(seq_count, each, dim + 16, 2 * dim)
        states = jnp.stack([carry(held[:, i], entering) for i in range(each)], axis=1)
        arriving = lax.all_to_all(
            states.reshape(seq_count * each, dim, dim), "seq", split_axis=0, concat_axis=0, tiled=True
        )
    else:
        arriving = relay(ends, seq_count)
    return (mixed, finish(entering, local_out, arriving))


def solution(mesh):
    in_specs = (
        P(("seq", "exp"), None),
        P(),
        P(("seq", "exp"), None),
        P(("seq", "exp"), None),
        P(("seq", "exp"), None, None),
        P(("seq", "exp"), None, None),
        P(),
        P(None, None, "exp"),
        P("seq", "exp"),
        P("seq", "exp"),
    )
    out_specs = (P(("seq", "exp"), None), P("seq", "exp"))
    return jax.shard_map(local, mesh=mesh, in_specs=in_specs, out_specs=out_specs, check_vma=False)
```

```python
from functools import partial

import jax
import jax.numpy as jnp
from jax import lax
from jax.experimental import pallas as pl
from jax.experimental.pallas import tpu as pltpu
from jax.sharding import PartitionSpec as P

CH = 128
ROUTE_STEP = 16
EXPERT_VMEM = 16 * 1024 * 1024
VMEM_LIMIT = 56 * 1024 * 1024
BF = jnp.bfloat16
F32 = jnp.float32


def rms_scale(values, gain):
    wide = values.astype(F32)
    return wide * lax.rsqrt(jnp.mean(wide * wide, axis=-1, keepdims=True) + 1e-06) * gain


def dot(a, b):
    return jnp.dot(a, b, preferred_element_type=F32)


def split(a):
    high = a.astype(BF)
    return high, (a - high.astype(F32)).astype(BF)


def rough(a, b):
    return dot(a.astype(BF), b.astype(BF))


def left_pair(a):
    high, low = split(a)
    return jnp.concatenate([high, low], axis=1)


def right_pair(b):
    high, low = split(b)
    row = jnp.concatenate([high, low], axis=1)
    return jnp.concatenate([row, row], axis=0)


def wide_product(a, b):
    columns = b.shape[1]
    both = dot(left_pair(a), right_pair(b))
    return both[:, :columns] + both[:, columns:]


def moe_kernel(capacity, choose, *refs):
    first_ref, *block_refs = refs[:5]
    weight_refs = refs[5:9]
    out_refs = refs[-6:-2]
    rows_ref, back_ref = refs[-2:]
    tok, wide = block_refs[0].shape
    width = rows_ref.shape[2]
    half = weight_refs[0].shape[0]
    experts_here = 2 * half
    expert_width = weight_refs[1].shape[1]
    pair_rows = rows_ref.shape[1] // 2

    matched, weights = [], []
    for block_ref in block_refs:
        routing = block_ref[:, width:].astype(F32).T
        ids = routing[:choose]
        scale = routing[ROUTE_STEP : ROUTE_STEP + choose]
        scale = scale + routing[2 * ROUTE_STEP : 2 * ROUTE_STEP + choose]
        for e in range(experts_here):
            side, at = divmod(e, half)
            hit = ids == (first_ref[side] + at).astype(F32)
            matched.append(jnp.max(jnp.where(hit, 1.0, 0.0), axis=0, keepdims=True))
            weights.append(jnp.sum(jnp.where(hit, scale, 0.0), axis=0, keepdims=True))
    match = jnp.concatenate(matched, axis=0)
    before = lax.broadcasted_iota(jnp.int32, (tok, tok), 0) < lax.broadcasted_iota(
        jnp.int32, (tok, tok), 1
    )
    rank = dot(match.astype(BF), jnp.where(before, 1.0, 0.0).astype(BF))
    rank = jnp.where(match > 0.5, rank, -1e4)
    row_number = lax.broadcasted_iota(jnp.int32, (pair_rows, 2 * tok), 0).astype(F32)
    picks = []
    for pair in range(2):
        x_pair = jnp.concatenate(
            [block_refs[2 * pair][:, :width], block_refs[2 * pair + 1][:, :width]], axis=0
        )
        here = []
        for e in range(experts_here):
            low = 2 * pair * experts_here + e
            high = low + experts_here
            place = jnp.concatenate(
                [rank[low : low + 1], rank[high : high + 1] + float(capacity)], axis=1
            )
            here.append(jnp.where(row_number == place, 1.0, 0.0))
        picks.append(here)
        chosen = dot(jnp.concatenate(here, axis=0).astype(BF), x_pair).astype(BF)
        for e in range(experts_here):
            rows_ref[e, pair * pair_rows : (pair + 1) * pair_rows, :] = chosen[
                e * pair_rows : (e + 1) * pair_rows
            ]
    for e in range(experts_here):
        side, at = divmod(e, half)
        both = dot(rows_ref[e], weight_refs[2 * side][at])
        gate = both[:, :expert_width]
        hidden = (gate / (1.0 + jnp.exp(-gate)) * both[:, expert_width:]).astype(BF)
        back_ref[e] = dot(hidden, weight_refs[2 * side + 1][at]).astype(BF)
    for pair in range(2):
        scaled, rows = [], []
        for e in range(experts_here):
            low = 2 * pair * experts_here + e
            high = low + experts_here
            weight = jnp.concatenate([weights[low], weights[high]], axis=1)
            scaled.append(picks[pair][e] * weight)
            rows.append(back_ref[e, pair * pair_rows : (pair + 1) * pair_rows, :])
        high_part, low_part = split(jnp.concatenate(scaled, axis=0))
        left = jnp.concatenate([high_part, low_part], axis=0)
        right = jnp.concatenate(rows + rows, axis=0)
        summed = lax.dot_general(
            left, right, (((0,), (0,)), ((), ())), preferred_element_type=F32
        ).astype(BF)
        out_refs[2 * pair][...] = summed[:tok]
        out_refs[2 * pair + 1][...] = summed[tok:]


def experts(blocks, first, weights, after, capacity, choose):
    tok, wide = blocks[0].shape
    gate_up_weight, down = weights[:2]
    local_experts, width, double = gate_up_weight.shape
    here = 2 * local_experts
    pair_rows = -(-2 * capacity // 16) * 16
    whole = pl.BlockSpec(memory_space=pltpu.VMEM)
    return pl.pallas_call(
        partial(moe_kernel, capacity, choose),
        in_specs=[pl.BlockSpec(memory_space=pltpu.SMEM)]
        + [whole] * 8
        + [pl.BlockSpec(memory_space=pl.ANY)] * len(after),
        out_specs=[whole] * 4,
        out_shape=[jax.ShapeDtypeStruct((tok, width), BF)] * 4,
        scratch_shapes=[
            pltpu.VMEM((here, 2 * pair_rows, width), BF),
            pltpu.VMEM((here, 2 * pair_rows, width), BF),
        ],
        compiler_params=pltpu.CompilerParams(vmem_limit_bytes=EXPERT_VMEM),
        cost_estimate=pl.CostEstimate(
            flops=here * pair_rows * width * double // 4,
            bytes_accessed=tok * width,
            transcendentals=0,
        ),
        name="experts",
    )(first, *blocks, *weights, *after)


def unit_rows(values):
    return values * lax.rsqrt(jnp.sum(values * values, axis=-1, keepdims=True) + 1e-06)


def tiles():
    rows = lax.broadcasted_iota(jnp.int32, (CH, CH), 0)
    columns = lax.broadcasted_iota(jnp.int32, (CH, CH), 1)
    return rows, columns


def against_rows(a, b):
    high, low = split(b)
    right = jnp.concatenate(
        [jnp.concatenate([high, high], axis=1), jnp.concatenate([low, low], axis=1)], axis=0
    )
    both = lax.dot_general(
        left_pair(a), right, (((1,), (1,)), ((), ())), preferred_element_type=F32
    )
    return both[:, : b.shape[0]] + both[:, b.shape[0] :]


def chunk_kernel(place_ref, x_ref, key_w_ref, value_w_ref, sum_ref, rate_ref, *refs):
    k_ref, solved_ref, moved_ref = refs[-3:]
    heads, chunks, _ = sum_ref.shape[1:]
    dim = key_w_ref.shape[2] // heads
    rows, columns = tiles()
    strict = rows > columns
    identity = jnp.where(rows == columns, 1.0, 0.0)
    x = x_ref[...]
    key = dot(x, key_w_ref[0])
    value = dot(x, value_w_ref[0])
    units = [(h, n) for h in range(heads) for n in range(chunks)]

    def part(values, h, n):
        return values[n * CH : (n + 1) * CH, h * dim : (h + 1) * dim]

    keys, values, lowers, rates, growths, remains = [], [], [], [], [], []
    for h, n in units:
        unit = unit_rows(part(key, h, n))
        k_ref[n * CH : (n + 1) * CH, h * dim : (h + 1) * dim] = unit
        keys.append(unit)
        values.append(part(value, h, n))
    for u, (h, n) in enumerate(units):
        across = jnp.broadcast_to(sum_ref[0, h, n : n + 1, :], (CH, CH))
        along = across.T
        rate = jnp.broadcast_to(rate_ref[0, h, n : n + 1, :], (CH, CH)).T
        last = jnp.broadcast_to(along[CH - 1 : CH, :], (CH, CH))
        fade = jnp.exp(jnp.where(strict, along - across, 0.0))
        rates.append(rate)
        growths.append(jnp.exp(along))
        remains.append(jnp.exp(last - along))
        unit = keys[u].astype(BF)
        met = lax.dot_general(unit, unit, (((1,), (1,)), ((), ())), preferred_element_type=F32)
        lowers.append(jnp.where(strict, rate * fade * met, 0.0))

    def ring(size):
        shared = (rows // (2 * size)) == (columns // (2 * size))
        return shared & (rows // size % 2 == 1) & (columns // size % 2 == 0)

    span = range(len(units))
    inverse = [identity - jnp.where(ring(1), lowers[u], 0.0) for u in span]
    size = 2
    while size < CH:
        here = ring(size)
        step = [rough(jnp.where(here, lowers[u], 0.0), inverse[u]) for u in span]
        inverse = [inverse[u] - rough(inverse[u], step[u]) for u in span]
        size *= 2
    wanted = [
        jnp.concatenate([rates[u] * growths[u] * keys[u], rates[u] * values[u]], axis=1)
        for u in span
    ]
    solved = [wanted[u] + rough(inverse[u] - identity, wanted[u]) for u in span]
    for u, (h, n) in enumerate(units):
        solved_ref[h, n] = solved[u]
        moved_ref[h, n] = lax.dot_general(
            (remains[u] * keys[u]).astype(BF),
            solved[u].astype(BF),
            (((0,), (0,)), ((), ())),
            preferred_element_type=F32,
        )


def chunks_of(x, place, qkv_weight, sums, rates, before):
    rows, width = x.shape
    _, _, columns = qkv_weight.shape
    parts, heads, chunks, _ = sums.shape
    dim = columns // heads
    step = min(4, heads)
    at_rows = pl.BlockSpec((rows, step * dim), lambda i, place: (place[0], i))
    at_chunks = pl.BlockSpec((step, chunks, CH, 2 * dim), lambda i, place: (i, place[0], 0, 0))
    per_head = pl.BlockSpec((1, step, chunks, CH), lambda i, place: (place[0], i, 0, 0))
    return pl.pallas_call(
        chunk_kernel,
        grid_spec=pltpu.PrefetchScalarGridSpec(
            num_scalar_prefetch=1,
            grid=(heads // step,),
            in_specs=[
                pl.BlockSpec((rows, width), lambda i, place: (0, 0)),
                pl.BlockSpec((1, width, step * dim), lambda i, place: (1, 0, i)),
                pl.BlockSpec((1, width, step * dim), lambda i, place: (2, 0, i)),
                per_head,
                per_head,
            ]
            + [pl.BlockSpec(memory_space=pl.ANY)] * len(before),
            out_specs=[at_rows, at_chunks, at_chunks],
        ),
        out_shape=[jax.ShapeDtypeStruct((parts * rows, columns), F32)]
        + [jax.ShapeDtypeStruct((heads, parts * chunks, CH, 2 * dim), F32)] * 2,
        input_output_aliases={6 + i: i for i in range(len(before))},
        compiler_params=pltpu.CompilerParams(vmem_limit_bytes=VMEM_LIMIT),
        name="chunks",
    )(place, x, qkv_weight, qkv_weight, sums, rates, *before)


def chain_kernel(moved_ref, sum_ref, starts_ref, end_ref):
    heads, chunks, dim, _ = moved_ref.shape
    rows, columns = tiles()
    identity = jnp.where(rows == columns, 1.0, 0.0)
    span = range(heads)

    def spread(total):
        decay = jnp.exp(jnp.broadcast_to(total, (CH, CH)).T[CH - 1 : CH, :])
        return jnp.broadcast_to(decay, (CH, CH))

    wholes = [[spread(sum_ref[h, n : n + 1, :]) for n in range(chunks)] for h in span]
    state = [
        jnp.concatenate(
            [wholes[h][0] * identity - moved_ref[h, 0, :, :dim], moved_ref[h, 0, :, dim:]], axis=1
        )
        for h in span
    ]
    for n in range(1, chunks):
        for h in span:
            starts_ref[h, n - 1] = state[h]
        removed = [rough(moved_ref[h, n, :, :dim], state[h]) for h in span]
        state = [
            jnp.concatenate(
                [
                    wholes[h][n] * state[h][:, :dim] - removed[h][:, :dim],
                    wholes[h][n] * state[h][:, dim:]
                    - removed[h][:, dim:]
                    + moved_ref[h, n, :, dim:],
                ],
                axis=1,
            )
            for h in span
        ]
    for h in span:
        decay = wholes[h][0]
        for n in range(1, chunks):
            decay = decay * wholes[h][n]
        end_ref[h, :dim, :dim] = (decay * identity - state[h][:, :dim]).astype(BF)
        end_ref[h, :dim, dim:] = state[h][:, dim:].astype(BF)
        end_ref[h, dim:, :] = left_pair(decay[:16])


def chain(moved, sums):
    heads, chunks, dim, double = moved.shape
    return pl.pallas_call(
        chain_kernel,
        out_shape=[
            jax.ShapeDtypeStruct((heads, chunks - 1, dim, double), F32),
            jax.ShapeDtypeStruct((heads, dim + 16, double), BF),
        ],
        compiler_params=pltpu.CompilerParams(vmem_limit_bytes=VMEM_LIMIT),
        name="chain",
    )(moved, sums)


def read_kernel(place_ref, w_ref, k_ref, solved_ref, starts_ref, sum_ref, *refs):
    x_refs = refs[:-2]
    enter_ref, local_ref = refs[-2:]
    heads, chunks, _ = sum_ref.shape
    dim = starts_ref.shape[2]
    rows, columns = tiles()
    inclusive = rows >= columns
    found = [dot(x_ref[...], w_ref[0]) for x_ref in x_refs]
    queries = []
    for place in range(len(found)):
        query = found[0]
        for i in range(1, len(found)):
            query = jnp.where(place_ref[i] == place, found[i], query)
        queries.append(query)
    each = chunks // len(found)
    units = [(h, n) for h in range(heads) for n in range(chunks)]
    for h, n in units:
        cut = slice(n * CH, (n + 1) * CH), slice(h * dim, (h + 1) * dim)
        across = jnp.broadcast_to(sum_ref[h, n : n + 1, :], (CH, CH))
        along = across.T
        fade = jnp.exp(jnp.where(inclusive, along - across, 0.0))
        query = unit_rows(queries[n // each][n % each * CH : (n % each + 1) * CH, cut[1]])
        masked = jnp.where(inclusive, fade * against_rows(query, k_ref[cut]), 0.0)
        probed = wide_product(masked, solved_ref[h, n])
        entering = jnp.exp(along) * query - probed[:, :dim]
        output = probed[:, dim:]
        if n:
            begun = wide_product(entering, starts_ref[h, n - 1])
            entering = begun[:, :dim]
            output = output + begun[:, dim:]
        enter_ref[cut] = entering.astype(BF)
        local_ref[cut] = output


def read(parts, places, qkv_weight, key, solved, starts, sums):
    length, columns = key.shape
    heads, chunks, _ = sums.shape
    dim = columns // heads
    width = qkv_weight.shape[1]
    step = 2 if heads % 2 == 0 else 1
    per_column = pl.BlockSpec((length, step * dim), lambda h: (0, h))
    four = lambda h: (h, 0, 0, 0)
    return pl.pallas_call(
        read_kernel,
        grid=(heads // step,),
        in_specs=[
            pl.BlockSpec(memory_space=pltpu.SMEM),
            pl.BlockSpec((1, width, step * dim), lambda h: (0, 0, h)),
            per_column,
            pl.BlockSpec((step, chunks, CH, 2 * dim), four),
            pl.BlockSpec((step, chunks - 1, dim, 2 * dim), four),
            pl.BlockSpec((step, chunks, CH), lambda h: (h, 0, 0)),
        ]
        + [pl.BlockSpec(x.shape, lambda h: (0, 0)) for x in parts],
        out_specs=[per_column, per_column],
        out_shape=[
            jax.ShapeDtypeStruct((length, columns), BF),
            jax.ShapeDtypeStruct((length, columns), F32),
        ],
        compiler_params=pltpu.CompilerParams(vmem_limit_bytes=VMEM_LIMIT),
        name="read",
    )(places, qkv_weight, key, solved, starts, sums, *parts)


def carry_kernel(ends_ref, after_ref, states_ref):
    segments, _, double = ends_ref.shape
    dim = double // 2
    state = jnp.zeros((dim, dim), F32)
    for s in range(segments):
        states_ref[s] = state.astype(BF)
        if s < segments - 1:
            decay = ends_ref[s, dim : dim + 1, :].astype(F32)
            decay = decay[:, :dim] + decay[:, dim:]
            removed = dot(ends_ref[s, :dim, :dim], left_pair(state))
            removed = removed[:, :dim] + removed[:, dim:]
            state = decay * state - removed + ends_ref[s, :dim, dim:].astype(F32)


def carry(ends, after):
    segments, _, double = ends.shape
    return pl.pallas_call(
        carry_kernel,
        in_specs=[pl.BlockSpec(memory_space=pltpu.VMEM), pl.BlockSpec(memory_space=pl.ANY)],
        out_shape=jax.ShapeDtypeStruct((segments, double // 2, double // 2), BF),
        compiler_params=pltpu.CompilerParams(vmem_limit_bytes=VMEM_LIMIT),
        name="carry",
    )(ends, after)


def finish_kernel(enter_ref, local_ref, state_ref, core_ref):
    heads, dim, _ = state_ref.shape
    for h in range(heads):
        cut = slice(h * dim, (h + 1) * dim)
        core_ref[:, cut] = local_ref[:, cut] + dot(enter_ref[:, cut], state_ref[h])


def finish(entering, local_out, states):
    length, columns = entering.shape
    heads, dim, _ = states.shape
    step = 2 if heads % 2 == 0 else 1
    per_column = pl.BlockSpec((length, step * dim), lambda h: (0, h))
    return pl.pallas_call(
        finish_kernel,
        grid=(heads // step,),
        in_specs=[per_column, per_column, pl.BlockSpec((step, dim, dim), lambda h: (h, 0, 0))],
        out_specs=per_column,
        out_shape=jax.ShapeDtypeStruct((length, columns), F32),
        compiler_params=pltpu.CompilerParams(vmem_limit_bytes=VMEM_LIMIT),
        name="finish",
    )(entering, local_out, states)


def relay(ends, seq_count):
    dim = ends.shape[2] // 2
    pairs = [(i, i + 1) for i in range(seq_count - 1)]
    removed, written = ends[:, :dim, :dim].astype(F32), ends[:, :dim, dim:].astype(F32)
    decay = ends[:, dim, :1].astype(F32) + ends[:, dim, dim : dim + 1].astype(F32)

    def step(_, incoming):
        outgoing = decay[:, :, None] * incoming + written
        outgoing = outgoing - jnp.einsum(
            "hij,hjk->hik", removed, incoming, precision=lax.Precision.HIGHEST
        )
        return lax.ppermute(outgoing, "seq", pairs)

    return lax.fori_loop(0, seq_count - 1, step, jnp.zeros_like(written)).astype(BF)


def move(values, change):
    exp_count = lax.axis_size("exp")
    pairs = []
    for s in range(lax.axis_size("seq")):
        for e in range(exp_count):
            to_s, to_e = change(s, e)
            pairs.append((s * exp_count + e, to_s * exp_count + to_e))
    return lax.ppermute(values, ("seq", "exp"), pairs)


def over_x(values):
    return move(values, lambda s, e: (s ^ 1, e))


def over_y(values):
    return move(values, lambda s, e: (s, e ^ 2))


def over_core(values):
    return move(values, lambda s, e: (s, e ^ 1))


def along_z(values, by):
    count = lax.axis_size("seq")
    return move(values, lambda s, e: ((s + 2 * by) % count, e))


def added(*terms):
    total = terms[0].astype(F32)
    for term in terms[1:]:
        total = total + term.astype(F32)
    return total


def route_waves(normed, expert_ids, expert_weights, gate_up_weight, down, capacity):
    tok_rows, width = normed.shape
    choose = expert_ids.shape[1]
    local_experts = gate_up_weight.shape[0]
    me = lax.axis_index("seq") * lax.axis_size("exp") + lax.axis_index("exp")
    first = (jnp.stack([me, me ^ 1]) * local_experts).astype(jnp.int32)
    gap = jnp.zeros((tok_rows, ROUTE_STEP - choose), BF)
    high, low = split(expert_weights)
    tail = jnp.zeros((tok_rows, 128 - 3 * ROUTE_STEP), BF)
    block = jnp.concatenate(
        [normed, expert_ids.astype(BF), gap, high, gap, low, gap, tail], axis=1
    )
    weights = (gate_up_weight, down, over_core(gate_up_weight), over_core(down))
    count = lax.axis_size("seq") // 2
    order = list(range(1, count)) + [0]
    first_way = [over_y if wave in (0, 1) else over_x for wave in range(count)]
    second_way = [over_x if wave in (0, 1) else over_y for wave in range(count)]
    block = [block]
    for wave in range(1, count):
        block.append(along_z(block[-1], 1))
    by_one = [first_way[wave](block[wave]) for wave in range(count)]
    by_two = [second_way[wave](block[wave]) for wave in range(count)]
    diagonal = {wave: second_way[wave](by_one[wave]) for wave in (0, 1, 2)}
    for wave in range(3, count):
        diagonal[wave] = along_z(diagonal[wave - 1], 1)
    due = [() for _ in range(count + 3)]
    for call, wave in enumerate(order):
        if call and wave:
            due[call - 1] += (block[wave],)
        if call > 1:
            due[call - 1 if wave else 0] += (by_one[wave], by_two[wave])
    running = sum_below = None
    for call, wave in enumerate(order):
        own, sum_one, sum_two, sum_both = experts(
            (block[wave], by_one[wave], by_two[wave], diagonal[wave]),
            first,
            weights,
            due[call],
            capacity,
            choose,
        )
        one, two = first_way[wave], second_way[wave]
        due[call + 1] += (own,)
        if sum_below is not None:
            sum_both = added(sum_both, sum_below).astype(BF)
        from_two = two(sum_two)
        if 0 < wave < count - 1:
            sum_below = along_z(sum_both, 1)
            due[call + 2] += (sum_below,)
        else:
            sum_below = None
            sum_one = added(sum_one, two(sum_both)).astype(BF)
        from_one = one(sum_one)
        due[call + 2] += (from_two, from_one)
        here = added(own, from_two, from_one)
        if running is not None:
            here = here + running.astype(F32)
        if wave:
            running = along_z(here.astype(BF), 1)
            due[call + 3] += (running,)
    return here


def route_some(normed, expert_ids, expert_weights, gate_up_weight, down, capacity):
    axes = ("seq", "exp")
    tok_rows, width = normed.shape
    choose = expert_ids.shape[1]
    local_experts = gate_up_weight.shape[0]
    expert_width = down.shape[1]
    devices = lax.axis_size("seq") * lax.axis_size("exp")
    experts_all = local_experts * devices
    flat_ids = expert_ids.reshape(-1)
    onehot = (flat_ids[:, None] == jnp.arange(experts_all, dtype=jnp.int32)[None, :]).astype(
        jnp.int32
    )
    rank = jnp.sum(jnp.cumsum(onehot, axis=0) * onehot, axis=1) - 1
    slot = flat_ids * capacity + rank
    token_of = jnp.arange(tok_rows * choose, dtype=jnp.int32) // choose
    send = jnp.zeros((experts_all * capacity, width), BF).at[slot].set(normed[token_of])
    both = jnp.einsum(
        "secd,edf->secf",
        lax.all_to_all(
            send.reshape(devices, local_experts, capacity, width),
            axes,
            split_axis=0,
            concat_axis=0,
            tiled=True,
        ),
        gate_up_weight,
        preferred_element_type=F32,
    )
    hidden = (jax.nn.silu(both[..., :expert_width]) * both[..., expert_width:]).astype(BF)
    back = lax.all_to_all(
        jnp.einsum("secf,efd->secd", hidden, down, preferred_element_type=F32).astype(BF),
        axes,
        split_axis=0,
        concat_axis=0,
        tiled=True,
    )
    back_rows = back.reshape(experts_all * capacity, width)[slot].astype(F32)
    return jnp.sum(
        back_rows.reshape(tok_rows, choose, width) * expert_weights[:, :, None], axis=1
    )


def local(
    stream,
    moe_gain,
    expert_ids,
    expert_weights,
    gate_up_weight,
    down,
    mixer_gain,
    qkv_weight,
    decay_log,
    write_rate,
):
    tok_rows, width = stream.shape
    choose = expert_ids.shape[1]
    seq_count = lax.axis_size("seq")
    devices = seq_count * lax.axis_size("exp")
    experts_all = gate_up_weight.shape[0] * devices
    capacity = max(2, (tok_rows * choose * 6 + experts_all * 5 - 1) // (experts_all * 5))
    normed = rms_scale(stream, moe_gain).astype(BF)
    planes = lax.axis_size("exp") == 4 and seq_count % 4 == 0 and choose <= ROUTE_STEP
    route = route_waves if planes and experts_all <= 256 else route_some
    moe = route(normed, expert_ids, expert_weights, gate_up_weight, down, capacity)
    mixed = (stream.astype(F32) + moe).astype(BF)
    normed_mix = rms_scale(mixed, mixer_gain).astype(BF)
    heads = decay_log.shape[1]
    blocks = decay_log.shape[0] // CH
    sums = jnp.cumsum(decay_log.T.reshape(heads, blocks, CH), axis=-1)
    rates = write_rate.T.reshape(heads, blocks, CH)
    pairs = blocks // 2
    by_pair = lambda values: values.reshape(heads, pairs, 2, CH).transpose(1, 0, 2, 3)
    if planes:
        core = lax.axis_index("exp") % 2
        side = lax.axis_index("exp") // 2
        from_y = over_y(normed_mix)
        both_sides = [(normed_mix, over_core(normed_mix)), (from_y, over_core(from_y))]
        parts = [
            (
                jnp.concatenate([jnp.where(core == 0, a, b), jnp.where(core == 0, b, a)], axis=0),
                place,
            )
            for (a, b), place in zip(both_sides, (side, 1 - side))
        ]
    else:
        gathered = lax.all_gather(normed_mix, "exp", axis=0, tiled=True)
        parts = [(gathered[2 * CH * i : 2 * CH * (i + 1)], jnp.int32(i)) for i in range(pairs)]
    found = ()
    for x, place in parts:
        found = chunks_of(
            x,
            place.astype(jnp.int32).reshape(1),
            qkv_weight,
            by_pair(sums),
            by_pair(rates),
            found,
        )
    key, solved, moved = found
    starts, ends = chain(moved, sums)
    places = jnp.stack([place for _, place in parts]).astype(jnp.int32)
    entering, local_out = read([x for x, _ in parts], places, qkv_weight, key, solved, starts, sums)
    if heads % seq_count == 0:
        dim = ends.shape[2] // 2
        each = heads // seq_count
        held = lax.all_to_all(ends, "seq", split_axis=0, concat_axis=0, tiled=True)
        held = held.reshape(seq_count, each, dim + 16, 2 * dim)
        states = jnp.stack([carry(held[:, i], entering) for i in range(each)], axis=1)
        arriving = lax.all_to_all(
            states.reshape(seq_count * each, dim, dim), "seq", split_axis=0, concat_axis=0, tiled=True
        )
    else:
        arriving = relay(ends, seq_count)
    return (mixed, finish(entering, local_out, arriving))


def solution(mesh):
    in_specs = (
        P(("seq", "exp"), None),
        P(),
        P(("seq", "exp"), None),
        P(("seq", "exp"), None),
        P(("seq", "exp"), None, None),
        P(("seq", "exp"), None, None),
        P(),
        P(None, None, "exp"),
        P("seq", "exp"),
        P("seq", "exp"),
    )
    out_specs = (P(("seq", "exp"), None), P("seq", "exp"))
    return jax.shard_map(local, mesh=mesh, in_specs=in_specs, out_specs=out_specs, check_vma=False)
```

```python
from functools import partial

import jax
import jax.numpy as jnp
from jax import lax
from jax.experimental import pallas as pl
from jax.experimental.pallas import tpu as pltpu
from jax.sharding import PartitionSpec as P

CH = 128
ROUTE_STEP = 16
EXPERT_VMEM = 44 * 1024 * 1024
VMEM_LIMIT = 56 * 1024 * 1024
BF = jnp.bfloat16
F32 = jnp.float32


def rms_scale(values, gain):
    wide = values.astype(F32)
    return wide * lax.rsqrt(jnp.mean(wide * wide, axis=-1, keepdims=True) + 1e-06) * gain


def dot(a, b):
    return jnp.dot(a, b, preferred_element_type=F32)


def split(a):
    high = a.astype(BF)
    return high, (a - high.astype(F32)).astype(BF)


def rough(a, b):
    return dot(a.astype(BF), b.astype(BF))


def left_pair(a):
    high, low = split(a)
    return jnp.concatenate([high, low], axis=1)


def right_pair(b):
    high, low = split(b)
    row = jnp.concatenate([high, low], axis=1)
    return jnp.concatenate([row, row], axis=0)


def wide_product(a, b):
    columns = b.shape[1]
    both = dot(left_pair(a), right_pair(b))
    return both[:, :columns] + both[:, columns:]


def moe_kernel(capacity, choose, cuts, *refs):
    first_ref, *block_refs = refs[:5]
    gate_up_hbm, down_hbm = refs[5:7]
    gate_up_ref, down_ref, rows_ref, back_ref, sem = refs[-5:]
    tok, wide = block_refs[0].shape
    width = rows_ref.shape[2]
    out_refs = refs[-5 - 4 * cuts : -5]
    piece = width // cuts
    experts_here = gate_up_ref.shape[0]
    expert_width = down_ref.shape[1]
    pair_rows = rows_ref.shape[1] // 2

    copies = []
    for e in range(experts_here):
        fetch_in = pltpu.make_async_copy(gate_up_hbm.at[e], gate_up_ref.at[e], sem.at[0, e])
        fetch_out = pltpu.make_async_copy(down_hbm.at[e], down_ref.at[e], sem.at[1, e])
        fetch_in.start()
        fetch_out.start()
        copies.append((fetch_in, fetch_out))

    matched, weights = [], []
    for block_ref in block_refs:
        routing = block_ref[:, width:].astype(F32).T
        ids = routing[:choose]
        scale = routing[ROUTE_STEP : ROUTE_STEP + choose]
        scale = scale + routing[2 * ROUTE_STEP : 2 * ROUTE_STEP + choose]
        for e in range(experts_here):
            hit = ids == (first_ref[0] + e).astype(F32)
            matched.append(jnp.max(jnp.where(hit, 1.0, 0.0), axis=0, keepdims=True))
            weights.append(jnp.sum(jnp.where(hit, scale, 0.0), axis=0, keepdims=True))
    match = jnp.concatenate(matched, axis=0)
    before = lax.broadcasted_iota(jnp.int32, (tok, tok), 0) < lax.broadcasted_iota(
        jnp.int32, (tok, tok), 1
    )
    rank = dot(match.astype(BF), jnp.where(before, 1.0, 0.0).astype(BF))
    rank = jnp.where(match > 0.5, rank, -1e4)
    row_number = lax.broadcasted_iota(jnp.int32, (pair_rows, 2 * tok), 0).astype(F32)
    picks = []
    for pair in range(2):
        x_pair = jnp.concatenate(
            [block_refs[2 * pair][:, :width], block_refs[2 * pair + 1][:, :width]], axis=0
        )
        here = []
        for e in range(experts_here):
            low = 2 * pair * experts_here + e
            high = low + experts_here
            place = jnp.concatenate(
                [rank[low : low + 1], rank[high : high + 1] + float(capacity)], axis=1
            )
            here.append(jnp.where(row_number == place, 1.0, 0.0))
        picks.append(here)
        chosen = dot(jnp.concatenate(here, axis=0).astype(BF), x_pair).astype(BF)
        for e in range(experts_here):
            rows_ref[e, pair * pair_rows : (pair + 1) * pair_rows, :] = chosen[
                e * pair_rows : (e + 1) * pair_rows
            ]
    for e in range(experts_here):
        copies[e][0].wait()
        both = dot(rows_ref[e], gate_up_ref[e])
        gate = both[:, :expert_width]
        hidden = (gate / (1.0 + jnp.exp(-gate)) * both[:, expert_width:]).astype(BF)
        copies[e][1].wait()
        back_ref[e] = dot(hidden, down_ref[e]).astype(BF)
    for pair in range(2):
        scaled, rows = [], []
        for e in range(experts_here):
            low = 2 * pair * experts_here + e
            high = low + experts_here
            weight = jnp.concatenate([weights[low], weights[high]], axis=1)
            scaled.append(picks[pair][e] * weight)
            rows.append(back_ref[e, pair * pair_rows : (pair + 1) * pair_rows, :])
        summed = lax.dot_general(
            jnp.concatenate(scaled, axis=0).astype(BF),
            jnp.concatenate(rows, axis=0),
            (((0,), (0,)), ((), ())),
            preferred_element_type=F32,
        ).astype(BF)
        for cut in range(cuts):
            columns = slice(cut * piece, (cut + 1) * piece)
            out_refs[2 * pair * cuts + cut][...] = summed[:tok, columns]
            out_refs[(2 * pair + 1) * cuts + cut][...] = summed[tok:, columns]


def experts(blocks, first, weights, after, capacity, choose, cuts):
    tok, wide = blocks[0].shape
    here, width, double = weights[0].shape
    pair_rows = -(-2 * capacity // 16) * 16
    whole = pl.BlockSpec(memory_space=pltpu.VMEM)
    return pl.pallas_call(
        partial(moe_kernel, capacity, choose, cuts),
        in_specs=[pl.BlockSpec(memory_space=pltpu.SMEM)]
        + [whole] * 4
        + [pl.BlockSpec(memory_space=pl.ANY)] * (2 + len(after)),
        out_specs=[whole] * (4 * cuts),
        out_shape=[jax.ShapeDtypeStruct((tok, width // cuts), BF)] * (4 * cuts),
        scratch_shapes=[
            pltpu.VMEM(weights[0].shape, BF),
            pltpu.VMEM(weights[1].shape, BF),
            pltpu.VMEM((here, 2 * pair_rows, width), BF),
            pltpu.VMEM((here, 2 * pair_rows, width), BF),
            pltpu.SemaphoreType.DMA((2, here)),
        ],
        compiler_params=pltpu.CompilerParams(vmem_limit_bytes=EXPERT_VMEM),
        cost_estimate=pl.CostEstimate(
            flops=here * pair_rows * width * double // 4,
            bytes_accessed=tok * width,
            transcendentals=0,
        ),
        name="experts",
    )(first, *blocks, *weights, *after)


def unit_rows(values):
    return values * lax.rsqrt(jnp.sum(values * values, axis=-1, keepdims=True) + 1e-06)


def tiles():
    rows = lax.broadcasted_iota(jnp.int32, (CH, CH), 0)
    columns = lax.broadcasted_iota(jnp.int32, (CH, CH), 1)
    return rows, columns


def against_rows(a, b):
    high, low = split(b)
    right = jnp.concatenate(
        [jnp.concatenate([high, high], axis=1), jnp.concatenate([low, low], axis=1)], axis=0
    )
    both = lax.dot_general(
        left_pair(a), right, (((1,), (1,)), ((), ())), preferred_element_type=F32
    )
    return both[:, : b.shape[0]] + both[:, b.shape[0] :]


def chunk_kernel(place_ref, x_ref, key_w_ref, value_w_ref, sum_ref, rate_ref, *refs):
    k_ref, solved_ref, moved_ref = refs[-3:]
    heads, chunks, _ = sum_ref.shape[1:]
    dim = key_w_ref.shape[2] // heads
    rows, columns = tiles()
    strict = rows > columns
    identity = jnp.where(rows == columns, 1.0, 0.0)
    x = x_ref[...]
    key = dot(x, key_w_ref[0])
    value = dot(x, value_w_ref[0])
    units = [(h, n) for h in range(heads) for n in range(chunks)]

    def part(values, h, n):
        return values[n * CH : (n + 1) * CH, h * dim : (h + 1) * dim]

    keys, values, lowers, rates, growths, remains = [], [], [], [], [], []
    for h, n in units:
        unit = unit_rows(part(key, h, n))
        k_ref[n * CH : (n + 1) * CH, h * dim : (h + 1) * dim] = unit
        keys.append(unit)
        values.append(part(value, h, n))
    for u, (h, n) in enumerate(units):
        across = jnp.broadcast_to(sum_ref[0, h, n : n + 1, :], (CH, CH))
        along = across.T
        rate = jnp.broadcast_to(rate_ref[0, h, n : n + 1, :], (CH, CH)).T
        last = jnp.broadcast_to(along[CH - 1 : CH, :], (CH, CH))
        fade = jnp.exp(jnp.where(strict, along - across, 0.0))
        rates.append(rate)
        growths.append(jnp.exp(along))
        remains.append(jnp.exp(last - along))
        unit = keys[u].astype(BF)
        met = lax.dot_general(unit, unit, (((1,), (1,)), ((), ())), preferred_element_type=F32)
        lowers.append(jnp.where(strict, rate * fade * met, 0.0))

    def ring(size):
        shared = (rows // (2 * size)) == (columns // (2 * size))
        return shared & (rows // size % 2 == 1) & (columns // size % 2 == 0)

    span = range(len(units))
    inverse = [identity - jnp.where(ring(1), lowers[u], 0.0) for u in span]
    size = 2
    while size < CH:
        here = ring(size)
        step = [rough(jnp.where(here, lowers[u], 0.0), inverse[u]) for u in span]
        inverse = [inverse[u] - rough(inverse[u], step[u]) for u in span]
        size *= 2
    wanted = [
        jnp.concatenate([rates[u] * growths[u] * keys[u], rates[u] * values[u]], axis=1)
        for u in span
    ]
    solved = [wanted[u] + rough(inverse[u] - identity, wanted[u]) for u in span]
    for u, (h, n) in enumerate(units):
        solved_ref[h, n] = solved[u]
        moved_ref[h, n] = lax.dot_general(
            (remains[u] * keys[u]).astype(BF),
            solved[u].astype(BF),
            (((0,), (0,)), ((), ())),
            preferred_element_type=F32,
        )


def chunks_of(x, place, qkv_weight, sums, rates, before):
    rows, width = x.shape
    _, _, columns = qkv_weight.shape
    parts, heads, chunks, _ = sums.shape
    dim = columns // heads
    step = min(4, heads)
    at_rows = pl.BlockSpec((rows, step * dim), lambda i, place: (place[0], i))
    at_chunks = pl.BlockSpec((step, chunks, CH, 2 * dim), lambda i, place: (i, place[0], 0, 0))
    per_head = pl.BlockSpec((1, step, chunks, CH), lambda i, place: (place[0], i, 0, 0))
    return pl.pallas_call(
        chunk_kernel,
        grid_spec=pltpu.PrefetchScalarGridSpec(
            num_scalar_prefetch=1,
            grid=(heads // step,),
            in_specs=[
                pl.BlockSpec((rows, width), lambda i, place: (0, 0)),
                pl.BlockSpec((1, width, step * dim), lambda i, place: (1, 0, i)),
                pl.BlockSpec((1, width, step * dim), lambda i, place: (2, 0, i)),
                per_head,
                per_head,
            ]
            + [pl.BlockSpec(memory_space=pl.ANY)] * len(before),
            out_specs=[at_rows, at_chunks, at_chunks],
        ),
        out_shape=[jax.ShapeDtypeStruct((parts * rows, columns), F32)]
        + [jax.ShapeDtypeStruct((heads, parts * chunks, CH, 2 * dim), F32)] * 2,
        input_output_aliases={6 + i: i for i in range(len(before))},
        compiler_params=pltpu.CompilerParams(vmem_limit_bytes=VMEM_LIMIT),
        name="chunks",
    )(place, x, qkv_weight, qkv_weight, sums, rates, *before)


def chain_kernel(moved_ref, sum_ref, starts_ref, end_ref):
    heads, chunks, dim, _ = moved_ref.shape
    rows, columns = tiles()
    identity = jnp.where(rows == columns, 1.0, 0.0)
    span = range(heads)

    def spread(total):
        decay = jnp.exp(jnp.broadcast_to(total, (CH, CH)).T[CH - 1 : CH, :])
        return jnp.broadcast_to(decay, (CH, CH))

    wholes = [[spread(sum_ref[h, n : n + 1, :]) for n in range(chunks)] for h in span]
    state = [
        jnp.concatenate(
            [wholes[h][0] * identity - moved_ref[h, 0, :, :dim], moved_ref[h, 0, :, dim:]], axis=1
        )
        for h in span
    ]
    for n in range(1, chunks):
        for h in span:
            starts_ref[h, n - 1] = state[h]
        removed = [rough(moved_ref[h, n, :, :dim], state[h]) for h in span]
        state = [
            jnp.concatenate(
                [
                    wholes[h][n] * state[h][:, :dim] - removed[h][:, :dim],
                    wholes[h][n] * state[h][:, dim:]
                    - removed[h][:, dim:]
                    + moved_ref[h, n, :, dim:],
                ],
                axis=1,
            )
            for h in span
        ]
    for h in span:
        decay = wholes[h][0]
        for n in range(1, chunks):
            decay = decay * wholes[h][n]
        end_ref[h, :dim, :dim] = (decay * identity - state[h][:, :dim]).astype(BF)
        end_ref[h, :dim, dim:] = state[h][:, dim:].astype(BF)
        end_ref[h, dim:, :] = left_pair(decay[:16])


def chain(moved, sums):
    heads, chunks, dim, double = moved.shape
    return pl.pallas_call(
        chain_kernel,
        out_shape=[
            jax.ShapeDtypeStruct((heads, chunks - 1, dim, double), F32),
            jax.ShapeDtypeStruct((heads, dim + 16, double), BF),
        ],
        compiler_params=pltpu.CompilerParams(vmem_limit_bytes=VMEM_LIMIT),
        name="chain",
    )(moved, sums)


def read_kernel(place_ref, w_ref, k_ref, solved_ref, starts_ref, sum_ref, *refs):
    x_refs = refs[:-2]
    enter_ref, local_ref = refs[-2:]
    heads, chunks, _ = sum_ref.shape
    dim = starts_ref.shape[2]
    rows, columns = tiles()
    inclusive = rows >= columns
    found = [dot(x_ref[...], w_ref[0]) for x_ref in x_refs]
    queries = []
    for place in range(len(found)):
        query = found[0]
        for i in range(1, len(found)):
            query = jnp.where(place_ref[i] == place, found[i], query)
        queries.append(query)
    each = chunks // len(found)
    units = [(h, n) for h in range(heads) for n in range(chunks)]
    for h, n in units:
        cut = slice(n * CH, (n + 1) * CH), slice(h * dim, (h + 1) * dim)
        across = jnp.broadcast_to(sum_ref[h, n : n + 1, :], (CH, CH))
        along = across.T
        fade = jnp.exp(jnp.where(inclusive, along - across, 0.0))
        query = unit_rows(queries[n // each][n % each * CH : (n % each + 1) * CH, cut[1]])
        masked = jnp.where(inclusive, fade * against_rows(query, k_ref[cut]), 0.0)
        probed = wide_product(masked, solved_ref[h, n])
        entering = jnp.exp(along) * query - probed[:, :dim]
        output = probed[:, dim:]
        if n:
            begun = wide_product(entering, starts_ref[h, n - 1])
            entering = begun[:, :dim]
            output = output + begun[:, dim:]
        enter_ref[cut] = entering.astype(BF)
        local_ref[cut] = output


def read(parts, places, qkv_weight, key, solved, starts, sums):
    length, columns = key.shape
    heads, chunks, _ = sums.shape
    dim = columns // heads
    width = qkv_weight.shape[1]
    step = 2 if heads % 2 == 0 else 1
    per_column = pl.BlockSpec((length, step * dim), lambda h: (0, h))
    four = lambda h: (h, 0, 0, 0)
    return pl.pallas_call(
        read_kernel,
        grid=(heads // step,),
        in_specs=[
            pl.BlockSpec(memory_space=pltpu.SMEM),
            pl.BlockSpec((1, width, step * dim), lambda h: (0, 0, h)),
            per_column,
            pl.BlockSpec((step, chunks, CH, 2 * dim), four),
            pl.BlockSpec((step, chunks - 1, dim, 2 * dim), four),
            pl.BlockSpec((step, chunks, CH), lambda h: (h, 0, 0)),
        ]
        + [pl.BlockSpec(x.shape, lambda h: (0, 0)) for x in parts],
        out_specs=[per_column, per_column],
        out_shape=[
            jax.ShapeDtypeStruct((length, columns), BF),
            jax.ShapeDtypeStruct((length, columns), F32),
        ],
        compiler_params=pltpu.CompilerParams(vmem_limit_bytes=VMEM_LIMIT),
        name="read",
    )(places, qkv_weight, key, solved, starts, sums, *parts)


def carry_kernel(ends_ref, after_ref, states_ref):
    segments, _, double = ends_ref.shape
    dim = double // 2
    state = jnp.zeros((dim, dim), F32)
    for s in range(segments):
        states_ref[s] = state.astype(BF)
        if s < segments - 1:
            decay = ends_ref[s, dim : dim + 1, :].astype(F32)
            decay = decay[:, :dim] + decay[:, dim:]
            removed = dot(ends_ref[s, :dim, :dim], left_pair(state))
            removed = removed[:, :dim] + removed[:, dim:]
            state = decay * state - removed + ends_ref[s, :dim, dim:].astype(F32)


def carry(ends, after):
    segments, _, double = ends.shape
    return pl.pallas_call(
        carry_kernel,
        in_specs=[pl.BlockSpec(memory_space=pltpu.VMEM), pl.BlockSpec(memory_space=pl.ANY)],
        out_shape=jax.ShapeDtypeStruct((segments, double // 2, double // 2), BF),
        compiler_params=pltpu.CompilerParams(vmem_limit_bytes=VMEM_LIMIT),
        name="carry",
    )(ends, after)


def finish_kernel(enter_ref, local_ref, state_ref, core_ref):
    heads, dim, _ = state_ref.shape
    for h in range(heads):
        cut = slice(h * dim, (h + 1) * dim)
        core_ref[:, cut] = local_ref[:, cut] + dot(enter_ref[:, cut], state_ref[h])


def finish(entering, local_out, states):
    length, columns = entering.shape
    heads, dim, _ = states.shape
    step = 2 if heads % 2 == 0 else 1
    per_column = pl.BlockSpec((length, step * dim), lambda h: (0, h))
    return pl.pallas_call(
        finish_kernel,
        grid=(heads // step,),
        in_specs=[per_column, per_column, pl.BlockSpec((step, dim, dim), lambda h: (h, 0, 0))],
        out_specs=per_column,
        out_shape=jax.ShapeDtypeStruct((length, columns), F32),
        compiler_params=pltpu.CompilerParams(vmem_limit_bytes=VMEM_LIMIT),
        name="finish",
    )(entering, local_out, states)


def relay(ends, seq_count):
    dim = ends.shape[2] // 2
    pairs = [(i, i + 1) for i in range(seq_count - 1)]
    removed, written = ends[:, :dim, :dim].astype(F32), ends[:, :dim, dim:].astype(F32)
    decay = ends[:, dim, :1].astype(F32) + ends[:, dim, dim : dim + 1].astype(F32)

    def step(_, incoming):
        outgoing = decay[:, :, None] * incoming + written
        outgoing = outgoing - jnp.einsum(
            "hij,hjk->hik", removed, incoming, precision=lax.Precision.HIGHEST
        )
        return lax.ppermute(outgoing, "seq", pairs)

    return lax.fori_loop(0, seq_count - 1, step, jnp.zeros_like(written)).astype(BF)


def move(values, change):
    exp_count = lax.axis_size("exp")
    pairs = []
    for s in range(lax.axis_size("seq")):
        for e in range(exp_count):
            to_s, to_e = change(s, e)
            pairs.append((s * exp_count + e, to_s * exp_count + to_e))
    return lax.ppermute(values, ("seq", "exp"), pairs)


def over_x(values):
    return move(values, lambda s, e: (s ^ 1, e))


def over_y(values):
    return move(values, lambda s, e: (s, e ^ 2))


def over_core(values):
    return move(values, lambda s, e: (s, e ^ 1))


def along_z(values, by):
    count = lax.axis_size("seq")
    return move(values, lambda s, e: ((s + 2 * by) % count, e))


def added(*terms):
    total = terms[0].astype(F32)
    for term in terms[1:]:
        total = total + term.astype(F32)
    return total


def route_waves(normed, expert_ids, expert_weights, gate_up_weight, down, capacity):
    tok_rows, width = normed.shape
    choose = expert_ids.shape[1]
    local_experts = gate_up_weight.shape[0]
    me = lax.axis_index("seq") * lax.axis_size("exp") + lax.axis_index("exp")
    first = (me // 2 * 2 * local_experts).astype(jnp.int32).reshape(1)
    gap = jnp.zeros((tok_rows, ROUTE_STEP - choose), BF)
    high, low = split(expert_weights)
    tail = jnp.zeros((tok_rows, 128 - 3 * ROUTE_STEP), BF)
    block = jnp.concatenate(
        [normed, expert_ids.astype(BF), gap, high, gap, low, gap, tail], axis=1
    )
    chips = lax.axis_size("exp") // 2
    pairs = [[2 * chip, 2 * chip + 1] for chip in range(chips)]
    weights = [
        lax.all_gather(values, "exp", axis=0, tiled=True, axis_index_groups=pairs)
        for values in (gate_up_weight, down)
    ]
    count = lax.axis_size("seq") // 2
    first_way = [over_y if wave % 2 else over_x for wave in range(count)]
    second_way = [over_x if wave % 2 else over_y for wave in range(count)]
    block = [block, along_z(block, 1)]
    by_one, by_two = [first_way[0](block[0])], [second_way[0](block[0])]
    block[1], by_one[0], by_two[0] = lax.optimization_barrier((block[1], by_one[0], by_two[0]))
    diagonal = [second_way[0](by_one[0])]
    block.append(along_z(block[1], 1))
    for wave in range(1, count):
        by_one.append(first_way[wave](block[wave]))
        by_two.append(second_way[wave](block[wave]))
        if wave == 1:
            diagonal.append(second_way[1](by_one[1]))
            block[2], diagonal[0] = lax.optimization_barrier((block[2], diagonal[0]))
        else:
            diagonal.append(along_z(diagonal[-1], 1))
        if 1 < wave + 1 < count and len(block) < wave + 3 and len(block) < count:
            block.append(along_z(block[-1], 1))
    due = [() for _ in range(count + 3)]
    for wave in range(1, count):
        due[wave - 1] += (by_one[wave], by_two[wave])
        if wave > 1:
            due[wave - 2] += (block[wave],)
    running = sum_below = None
    for wave in range(count):
        cuts = 2 if wave == count - 1 else 1
        found = experts(
            (block[wave], by_one[wave], by_two[wave], diagonal[wave]),
            first,
            weights,
            due[wave],
            capacity,
            choose,
            cuts,
        )
        one, two = first_way[wave], second_way[wave]
        due[wave + 1] += (found[0],)
        if sum_below is not None:
            sum_below = jnp.split(sum_below, cuts, axis=1)
        if running is not None:
            arrived = jnp.split(running[0], cuts, axis=1)
        pieces = []
        for cut in range(cuts):
            own, sum_one, sum_two, sum_both = found[cut::cuts]
            if sum_below is not None:
                sum_both = added(sum_both, sum_below[cut]).astype(BF)
            if 0 < wave < count - 1:
                sum_below = along_z(sum_both, 1)
                due[wave + 2] += (sum_below,)
            else:
                sum_one = added(sum_one, two(sum_both)).astype(BF)
                due[wave + 2] += (sum_one,)
            from_two = two(sum_two)
            from_one = one(sum_one)
            due[wave + 2] += (from_two,)
            due[wave + (2 if wave else 3)] += (from_one,)
            if pieces:
                from_one, _ = lax.optimization_barrier((from_one, pieces[-1]))
            here = added(own, from_two, from_one)
            if running is not None:
                here = here + arrived[cut].astype(F32)
            pieces.append(here.astype(BF) if wave else here)
        if wave == 0:
            home = pieces
        else:
            running = [along_z(piece, 1) for piece in pieces]
    return home[0] + jnp.concatenate(running, axis=1).astype(F32)


def route_some(normed, expert_ids, expert_weights, gate_up_weight, down, capacity):
    axes = ("seq", "exp")
    tok_rows, width = normed.shape
    choose = expert_ids.shape[1]
    local_experts = gate_up_weight.shape[0]
    expert_width = down.shape[1]
    devices = lax.axis_size("seq") * lax.axis_size("exp")
    experts_all = local_experts * devices
    flat_ids = expert_ids.reshape(-1)
    onehot = (flat_ids[:, None] == jnp.arange(experts_all, dtype=jnp.int32)[None, :]).astype(
        jnp.int32
    )
    rank = jnp.sum(jnp.cumsum(onehot, axis=0) * onehot, axis=1) - 1
    slot = flat_ids * capacity + rank
    token_of = jnp.arange(tok_rows * choose, dtype=jnp.int32) // choose
    send = jnp.zeros((experts_all * capacity, width), BF).at[slot].set(normed[token_of])
    both = jnp.einsum(
        "secd,edf->secf",
        lax.all_to_all(
            send.reshape(devices, local_experts, capacity, width),
            axes,
            split_axis=0,
            concat_axis=0,
            tiled=True,
        ),
        gate_up_weight,
        preferred_element_type=F32,
    )
    hidden = (jax.nn.silu(both[..., :expert_width]) * both[..., expert_width:]).astype(BF)
    back = lax.all_to_all(
        jnp.einsum("secf,efd->secd", hidden, down, preferred_element_type=F32).astype(BF),
        axes,
        split_axis=0,
        concat_axis=0,
        tiled=True,
    )
    back_rows = back.reshape(experts_all * capacity, width)[slot].astype(F32)
    return jnp.sum(
        back_rows.reshape(tok_rows, choose, width) * expert_weights[:, :, None], axis=1
    )


def local(
    stream,
    moe_gain,
    expert_ids,
    expert_weights,
    gate_up_weight,
    down,
    mixer_gain,
    qkv_weight,
    decay_log,
    write_rate,
):
    tok_rows, width = stream.shape
    choose = expert_ids.shape[1]
    seq_count = lax.axis_size("seq")
    devices = seq_count * lax.axis_size("exp")
    experts_all = gate_up_weight.shape[0] * devices
    capacity = max(2, (tok_rows * choose * 6 + experts_all * 5 - 1) // (experts_all * 5))
    normed = rms_scale(stream, moe_gain).astype(BF)
    planes = lax.axis_size("exp") == 4 and seq_count % 4 == 0 and choose <= ROUTE_STEP
    route = route_waves if planes and experts_all <= 256 else route_some
    moe = route(normed, expert_ids, expert_weights, gate_up_weight, down, capacity)
    mixed = (stream.astype(F32) + moe).astype(BF)
    normed_mix = rms_scale(mixed, mixer_gain).astype(BF)
    heads = decay_log.shape[1]
    blocks = decay_log.shape[0] // CH
    sums = jnp.cumsum(decay_log.T.reshape(heads, blocks, CH), axis=-1)
    rates = write_rate.T.reshape(heads, blocks, CH)
    pairs = blocks // 2
    by_pair = lambda values: values.reshape(heads, pairs, 2, CH).transpose(1, 0, 2, 3)
    if planes:
        core = lax.axis_index("exp") % 2
        side = lax.axis_index("exp") // 2
        from_y = over_y(normed_mix)
        both_sides = [(normed_mix, over_core(normed_mix)), (from_y, over_core(from_y))]
        parts = [
            (
                jnp.concatenate([jnp.where(core == 0, a, b), jnp.where(core == 0, b, a)], axis=0),
                place,
            )
            for (a, b), place in zip(both_sides, (side, 1 - side))
        ]
    else:
        gathered = lax.all_gather(normed_mix, "exp", axis=0, tiled=True)
        parts = [(gathered[2 * CH * i : 2 * CH * (i + 1)], jnp.int32(i)) for i in range(pairs)]
    found = ()
    for x, place in parts:
        found = chunks_of(
            x,
            place.astype(jnp.int32).reshape(1),
            qkv_weight,
            by_pair(sums),
            by_pair(rates),
            found,
        )
    key, solved, moved = found
    starts, ends = chain(moved, sums)
    places = jnp.stack([place for _, place in parts]).astype(jnp.int32)
    entering, local_out = read([x for x, _ in parts], places, qkv_weight, key, solved, starts, sums)
    if heads % seq_count == 0:
        dim = ends.shape[2] // 2
        each = heads // seq_count
        held = lax.all_to_all(ends, "seq", split_axis=0, concat_axis=0, tiled=True)
        held = held.reshape(seq_count, each, dim + 16, 2 * dim)
        states = jnp.stack([carry(held[:, i], entering) for i in range(each)], axis=1)
        arriving = lax.all_to_all(
            states.reshape(seq_count * each, dim, dim), "seq", split_axis=0, concat_axis=0, tiled=True
        )
    else:
        arriving = relay(ends, seq_count)
    return (mixed, finish(entering, local_out, arriving))


def solution(mesh):
    in_specs = (
        P(("seq", "exp"), None),
        P(),
        P(("seq", "exp"), None),
        P(("seq", "exp"), None),
        P(("seq", "exp"), None, None),
        P(("seq", "exp"), None, None),
        P(),
        P(None, None, "exp"),
        P("seq", "exp"),
        P("seq", "exp"),
    )
    out_specs = (P(("seq", "exp"), None), P("seq", "exp"))
    return jax.shard_map(local, mesh=mesh, in_specs=in_specs, out_specs=out_specs, check_vma=False)
```

```python
from functools import partial

import jax
import jax.numpy as jnp
from jax import lax
from jax.experimental import pallas as pl
from jax.experimental.pallas import tpu as pltpu
from jax.sharding import PartitionSpec as P

CH = 128
ROUTE_STEP = 16
VMEM_LIMIT = 56 * 1024 * 1024
BF = jnp.bfloat16
F32 = jnp.float32


def rms_scale(values, gain):
    wide = values.astype(F32)
    return wide * lax.rsqrt(jnp.mean(wide * wide, axis=-1, keepdims=True) + 1e-06) * gain


def dot(a, b):
    return jnp.dot(a, b, preferred_element_type=F32)


def split(a):
    high = a.astype(BF)
    return high, (a - high.astype(F32)).astype(BF)


def rough(a, b):
    return dot(a.astype(BF), b.astype(BF))


def left_pair(a):
    high, low = split(a)
    return jnp.concatenate([high, low], axis=1)


def right_pair(b):
    high, low = split(b)
    row = jnp.concatenate([high, low], axis=1)
    return jnp.concatenate([row, row], axis=0)


def wide_product(a, b):
    columns = b.shape[1]
    both = dot(left_pair(a), right_pair(b))
    return both[:, :columns] + both[:, columns:]


def moe_kernel(capacity, choose, cuts, *refs):
    first_ref, *block_refs = refs[:5]
    weight_refs = refs[5:9]
    gate_up_ref, down_ref, rows_ref, back_ref, sem = refs[-5:]
    tok, wide = block_refs[0].shape
    width = rows_ref.shape[2]
    out_refs = refs[-5 - 4 * cuts : -5]
    piece = width // cuts
    experts_here = gate_up_ref.shape[0]
    half = experts_here // 2
    expert_width = down_ref.shape[1]
    pair_rows = rows_ref.shape[1] // 2

    copies = []
    for e in range(experts_here):
        side, at = divmod(e, half)
        fetch_in = pltpu.make_async_copy(
            weight_refs[2 * side].at[at], gate_up_ref.at[e], sem.at[0, e]
        )
        fetch_out = pltpu.make_async_copy(
            weight_refs[2 * side + 1].at[at], down_ref.at[e], sem.at[1, e]
        )
        fetch_in.start()
        fetch_out.start()
        copies.append((fetch_in, fetch_out))

    matched, weights = [], []
    for block_ref in block_refs:
        routing = block_ref[:, width:].astype(F32).T
        ids = routing[:choose]
        scale = routing[ROUTE_STEP : ROUTE_STEP + choose]
        scale = scale + routing[2 * ROUTE_STEP : 2 * ROUTE_STEP + choose]
        for e in range(experts_here):
            side, at = divmod(e, half)
            hit = ids == (first_ref[side] + at).astype(F32)
            matched.append(jnp.max(jnp.where(hit, 1.0, 0.0), axis=0, keepdims=True))
            weights.append(jnp.sum(jnp.where(hit, scale, 0.0), axis=0, keepdims=True))
    match = jnp.concatenate(matched, axis=0)
    before = lax.broadcasted_iota(jnp.int32, (tok, tok), 0) < lax.broadcasted_iota(
        jnp.int32, (tok, tok), 1
    )
    rank = dot(match.astype(BF), jnp.where(before, 1.0, 0.0).astype(BF))
    rank = jnp.where(match > 0.5, rank, -1e4)
    row_number = lax.broadcasted_iota(jnp.int32, (pair_rows, 2 * tok), 0).astype(F32)
    picks = []
    for pair in range(2):
        x_pair = jnp.concatenate(
            [block_refs[2 * pair][:, :width], block_refs[2 * pair + 1][:, :width]], axis=0
        )
        here = []
        for e in range(experts_here):
            low = 2 * pair * experts_here + e
            high = low + experts_here
            place = jnp.concatenate(
                [rank[low : low + 1], rank[high : high + 1] + float(capacity)], axis=1
            )
            here.append(jnp.where(row_number == place, 1.0, 0.0))
        picks.append(here)
        chosen = dot(jnp.concatenate(here, axis=0).astype(BF), x_pair).astype(BF)
        for e in range(experts_here):
            rows_ref[e, pair * pair_rows : (pair + 1) * pair_rows, :] = chosen[
                e * pair_rows : (e + 1) * pair_rows
            ]
    for e in range(experts_here):
        copies[e][0].wait()
        both = dot(rows_ref[e], gate_up_ref[e])
        gate = both[:, :expert_width]
        hidden = (gate / (1.0 + jnp.exp(-gate)) * both[:, expert_width:]).astype(BF)
        copies[e][1].wait()
        back_ref[e] = dot(hidden, down_ref[e]).astype(BF)
    for pair in range(2):
        scaled, rows = [], []
        for e in range(experts_here):
            low = 2 * pair * experts_here + e
            high = low + experts_here
            weight = jnp.concatenate([weights[low], weights[high]], axis=1)
            scaled.append(picks[pair][e] * weight)
            rows.append(back_ref[e, pair * pair_rows : (pair + 1) * pair_rows, :])
        summed = lax.dot_general(
            jnp.concatenate(scaled, axis=0).astype(BF),
            jnp.concatenate(rows, axis=0),
            (((0,), (0,)), ((), ())),
            preferred_element_type=F32,
        ).astype(BF)
        for cut in range(cuts):
            columns = slice(cut * piece, (cut + 1) * piece)
            out_refs[2 * pair * cuts + cut][...] = summed[:tok, columns]
            out_refs[(2 * pair + 1) * cuts + cut][...] = summed[tok:, columns]


def experts(blocks, first, weights, after, capacity, choose, cuts):
    tok, wide = blocks[0].shape
    gate_up_weight, down = weights[:2]
    local_experts, width, double = gate_up_weight.shape
    here = 2 * local_experts
    pair_rows = -(-2 * capacity // 16) * 16
    whole = pl.BlockSpec(memory_space=pltpu.VMEM)
    return pl.pallas_call(
        partial(moe_kernel, capacity, choose, cuts),
        in_specs=[pl.BlockSpec(memory_space=pltpu.SMEM)]
        + [whole] * 4
        + [pl.BlockSpec(memory_space=pl.ANY)] * (4 + len(after)),
        out_specs=[whole] * (4 * cuts),
        out_shape=[jax.ShapeDtypeStruct((tok, width // cuts), BF)] * (4 * cuts),
        scratch_shapes=[
            pltpu.VMEM((here,) + gate_up_weight.shape[1:], BF),
            pltpu.VMEM((here,) + down.shape[1:], BF),
            pltpu.VMEM((here, 2 * pair_rows, width), BF),
            pltpu.VMEM((here, 2 * pair_rows, width), BF),
            pltpu.SemaphoreType.DMA((2, here)),
        ],
        compiler_params=pltpu.CompilerParams(vmem_limit_bytes=VMEM_LIMIT),
        cost_estimate=pl.CostEstimate(
            flops=here * pair_rows * width * double // 4,
            bytes_accessed=tok * width,
            transcendentals=0,
        ),
        name="experts",
    )(first, *blocks, *weights, *after)


def unit_rows(values):
    return values * lax.rsqrt(jnp.sum(values * values, axis=-1, keepdims=True) + 1e-06)


def tiles():
    rows = lax.broadcasted_iota(jnp.int32, (CH, CH), 0)
    columns = lax.broadcasted_iota(jnp.int32, (CH, CH), 1)
    return rows, columns


def against_rows(a, b):
    high, low = split(b)
    right = jnp.concatenate(
        [jnp.concatenate([high, high], axis=1), jnp.concatenate([low, low], axis=1)], axis=0
    )
    both = lax.dot_general(
        left_pair(a), right, (((1,), (1,)), ((), ())), preferred_element_type=F32
    )
    return both[:, : b.shape[0]] + both[:, b.shape[0] :]


def chunk_kernel(place_ref, x_ref, key_w_ref, value_w_ref, sum_ref, rate_ref, *refs):
    k_ref, solved_ref, moved_ref = refs[-3:]
    heads, chunks, _ = sum_ref.shape[1:]
    dim = key_w_ref.shape[2] // heads
    rows, columns = tiles()
    strict = rows > columns
    identity = jnp.where(rows == columns, 1.0, 0.0)
    x = x_ref[...]
    key = dot(x, key_w_ref[0])
    value = dot(x, value_w_ref[0])
    units = [(h, n) for h in range(heads) for n in range(chunks)]

    def part(values, h, n):
        return values[n * CH : (n + 1) * CH, h * dim : (h + 1) * dim]

    keys, values, lowers, rates, growths, remains = [], [], [], [], [], []
    for h, n in units:
        unit = unit_rows(part(key, h, n))
        k_ref[n * CH : (n + 1) * CH, h * dim : (h + 1) * dim] = unit
        keys.append(unit)
        values.append(part(value, h, n))
    for u, (h, n) in enumerate(units):
        across = jnp.broadcast_to(sum_ref[0, h, n : n + 1, :], (CH, CH))
        along = across.T
        rate = jnp.broadcast_to(rate_ref[0, h, n : n + 1, :], (CH, CH)).T
        last = jnp.broadcast_to(along[CH - 1 : CH, :], (CH, CH))
        fade = jnp.exp(jnp.where(strict, along - across, 0.0))
        rates.append(rate)
        growths.append(jnp.exp(along))
        remains.append(jnp.exp(last - along))
        unit = keys[u].astype(BF)
        met = lax.dot_general(unit, unit, (((1,), (1,)), ((), ())), preferred_element_type=F32)
        lowers.append(jnp.where(strict, rate * fade * met, 0.0))

    def ring(size):
        shared = (rows // (2 * size)) == (columns // (2 * size))
        return shared & (rows // size % 2 == 1) & (columns // size % 2 == 0)

    span = range(len(units))
    inverse = [identity - jnp.where(ring(1), lowers[u], 0.0) for u in span]
    size = 2
    while size < CH and size < 16:
        here = ring(size)
        step = [rough(jnp.where(here, lowers[u], 0.0), inverse[u]) for u in span]
        inverse = [inverse[u] - rough(inverse[u], step[u]) for u in span]
        size *= 2
    while size < CH:
        starts = range(0, CH, 2 * size)

        def odd(values):
            return jnp.concatenate([values[s + size : s + 2 * size] for s in starts], axis=0)

        def woven(even, odds):
            rows_of = []
            for i, s in enumerate(starts):
                rows_of += [even[s : s + size], odds[i * size : (i + 1) * size]]
            return jnp.concatenate(rows_of, axis=0)

        here = odd(jnp.where(ring(size), 1.0, 0.0))
        nothing = jnp.zeros((CH, CH), F32)
        step = [woven(nothing, rough(here * odd(lowers[u]), inverse[u])) for u in span]
        inverse = [
            woven(inverse[u], odd(inverse[u]) - rough(odd(inverse[u]), step[u])) for u in span
        ]
        size *= 2
    wanted = [
        jnp.concatenate([rates[u] * growths[u] * keys[u], rates[u] * values[u]], axis=1)
        for u in span
    ]
    solved = [wanted[u] + rough(inverse[u] - identity, wanted[u]) for u in span]
    for u, (h, n) in enumerate(units):
        solved_ref[h, n] = solved[u]
        moved_ref[h, n] = lax.dot_general(
            (remains[u] * keys[u]).astype(BF),
            solved[u].astype(BF),
            (((0,), (0,)), ((), ())),
            preferred_element_type=F32,
        )


def chunks_of(x, place, qkv_weight, sums, rates, before):
    rows, width = x.shape
    _, _, columns = qkv_weight.shape
    parts, heads, chunks, _ = sums.shape
    dim = columns // heads
    step = min(4, heads)
    at_rows = pl.BlockSpec((rows, step * dim), lambda i, place: (place[0], i))
    at_chunks = pl.BlockSpec((step, chunks, CH, 2 * dim), lambda i, place: (i, place[0], 0, 0))
    per_head = pl.BlockSpec((1, step, chunks, CH), lambda i, place: (place[0], i, 0, 0))
    return pl.pallas_call(
        chunk_kernel,
        grid_spec=pltpu.PrefetchScalarGridSpec(
            num_scalar_prefetch=1,
            grid=(heads // step,),
            in_specs=[
                pl.BlockSpec((rows, width), lambda i, place: (0, 0)),
                pl.BlockSpec((1, width, step * dim), lambda i, place: (1, 0, i)),
                pl.BlockSpec((1, width, step * dim), lambda i, place: (2, 0, i)),
                per_head,
                per_head,
            ]
            + [pl.BlockSpec(memory_space=pl.ANY)] * len(before),
            out_specs=[at_rows, at_chunks, at_chunks],
        ),
        out_shape=[jax.ShapeDtypeStruct((parts * rows, columns), F32)]
        + [jax.ShapeDtypeStruct((heads, parts * chunks, CH, 2 * dim), F32)] * 2,
        input_output_aliases={6 + i: i for i in range(len(before))},
        compiler_params=pltpu.CompilerParams(vmem_limit_bytes=VMEM_LIMIT),
        name="chunks",
    )(place, x, qkv_weight, qkv_weight, sums, rates, *before)


def chain_kernel(moved_ref, sum_ref, starts_ref, end_ref):
    heads, chunks, dim, _ = moved_ref.shape
    rows, columns = tiles()
    identity = jnp.where(rows == columns, 1.0, 0.0)
    span = range(heads)

    def spread(total):
        return jnp.broadcast_to(jnp.exp(total[:, CH - 1 :]), (CH, CH))

    wholes = [[spread(sum_ref[h, n : n + 1, :]) for n in range(chunks)] for h in span]
    state = [
        jnp.concatenate(
            [wholes[h][0] * identity - moved_ref[h, 0, :, :dim], moved_ref[h, 0, :, dim:]], axis=1
        )
        for h in span
    ]
    for n in range(1, chunks):
        for h in span:
            starts_ref[h, n - 1] = state[h]
        removed = [rough(moved_ref[h, n, :, :dim], state[h]) for h in span]
        state = [
            jnp.concatenate(
                [
                    wholes[h][n] * state[h][:, :dim] - removed[h][:, :dim],
                    wholes[h][n] * state[h][:, dim:]
                    - removed[h][:, dim:]
                    + moved_ref[h, n, :, dim:],
                ],
                axis=1,
            )
            for h in span
        ]
    for h in span:
        decay = wholes[h][0]
        for n in range(1, chunks):
            decay = decay * wholes[h][n]
        end_ref[h, :dim, :dim] = (decay * identity - state[h][:, :dim]).astype(BF)
        end_ref[h, :dim, dim:] = state[h][:, dim:].astype(BF)
        end_ref[h, dim:, :] = left_pair(decay[:16])


def chain(moved, sums):
    heads, chunks, dim, double = moved.shape
    return pl.pallas_call(
        chain_kernel,
        out_shape=[
            jax.ShapeDtypeStruct((heads, chunks - 1, dim, double), F32),
            jax.ShapeDtypeStruct((heads, dim + 16, double), BF),
        ],
        compiler_params=pltpu.CompilerParams(vmem_limit_bytes=VMEM_LIMIT),
        name="chain",
    )(moved, sums)


def read_kernel(place_ref, w_ref, k_ref, solved_ref, starts_ref, sum_ref, *refs):
    x_refs = refs[:-2]
    enter_ref, local_ref = refs[-2:]
    heads, chunks, _ = sum_ref.shape
    dim = starts_ref.shape[2]
    rows, columns = tiles()
    inclusive = rows >= columns
    found = [dot(x_ref[...], w_ref[0]) for x_ref in x_refs]
    queries = []
    for place in range(len(found)):
        query = found[0]
        for i in range(1, len(found)):
            query = jnp.where(place_ref[i] == place, found[i], query)
        queries.append(query)
    each = chunks // len(found)
    units = [(h, n) for h in range(heads) for n in range(chunks)]
    for h, n in units:
        cut = slice(n * CH, (n + 1) * CH), slice(h * dim, (h + 1) * dim)
        across = jnp.broadcast_to(sum_ref[h, n : n + 1, :], (CH, CH))
        along = across.T
        fade = jnp.exp(jnp.where(inclusive, along - across, 0.0))
        query = unit_rows(queries[n // each][n % each * CH : (n % each + 1) * CH, cut[1]])
        masked = jnp.where(inclusive, fade * against_rows(query, k_ref[cut]), 0.0)
        probed = wide_product(masked, solved_ref[h, n])
        entering = jnp.exp(along) * query - probed[:, :dim]
        output = probed[:, dim:]
        if n:
            begun = wide_product(entering, starts_ref[h, n - 1])
            entering = begun[:, :dim]
            output = output + begun[:, dim:]
        enter_ref[cut] = entering.astype(BF)
        local_ref[cut] = output


def read(parts, places, qkv_weight, key, solved, starts, sums):
    length, columns = key.shape
    heads, chunks, _ = sums.shape
    dim = columns // heads
    width = qkv_weight.shape[1]
    step = 2 if heads % 2 == 0 else 1
    per_column = pl.BlockSpec((length, step * dim), lambda h: (0, h))
    four = lambda h: (h, 0, 0, 0)
    return pl.pallas_call(
        read_kernel,
        grid=(heads // step,),
        in_specs=[
            pl.BlockSpec(memory_space=pltpu.SMEM),
            pl.BlockSpec((1, width, step * dim), lambda h: (0, 0, h)),
            per_column,
            pl.BlockSpec((step, chunks, CH, 2 * dim), four),
            pl.BlockSpec((step, chunks - 1, dim, 2 * dim), four),
            pl.BlockSpec((step, chunks, CH), lambda h: (h, 0, 0)),
        ]
        + [pl.BlockSpec(x.shape, lambda h: (0, 0)) for x in parts],
        out_specs=[per_column, per_column],
        out_shape=[
            jax.ShapeDtypeStruct((length, columns), BF),
            jax.ShapeDtypeStruct((length, columns), F32),
        ],
        compiler_params=pltpu.CompilerParams(vmem_limit_bytes=VMEM_LIMIT),
        name="read",
    )(places, qkv_weight, key, solved, starts, sums, *parts)


def carry_kernel(ends_ref, after_ref, states_ref):
    segments, _, double = ends_ref.shape
    dim = double // 2
    state = jnp.zeros((dim, dim), F32)
    for s in range(segments):
        states_ref[s] = state.astype(BF)
        if s < segments - 1:
            decay = ends_ref[s, dim : dim + 1, :].astype(F32)
            decay = decay[:, :dim] + decay[:, dim:]
            removed = dot(ends_ref[s, :dim, :dim], left_pair(state))
            removed = removed[:, :dim] + removed[:, dim:]
            state = decay * state - removed + ends_ref[s, :dim, dim:].astype(F32)


def carry(ends, after):
    segments, _, double = ends.shape
    return pl.pallas_call(
        carry_kernel,
        in_specs=[pl.BlockSpec(memory_space=pltpu.VMEM), pl.BlockSpec(memory_space=pl.ANY)],
        out_shape=jax.ShapeDtypeStruct((segments, double // 2, double // 2), BF),
        compiler_params=pltpu.CompilerParams(vmem_limit_bytes=VMEM_LIMIT),
        name="carry",
    )(ends, after)


def finish_kernel(enter_ref, local_ref, state_ref, core_ref):
    heads, dim, _ = state_ref.shape
    for h in range(heads):
        cut = slice(h * dim, (h + 1) * dim)
        core_ref[:, cut] = local_ref[:, cut] + dot(enter_ref[:, cut], state_ref[h])


def finish(entering, local_out, states):
    length, columns = entering.shape
    heads, dim, _ = states.shape
    step = 2 if heads % 2 == 0 else 1
    per_column = pl.BlockSpec((length, step * dim), lambda h: (0, h))
    return pl.pallas_call(
        finish_kernel,
        grid=(heads // step,),
        in_specs=[per_column, per_column, pl.BlockSpec((step, dim, dim), lambda h: (h, 0, 0))],
        out_specs=per_column,
        out_shape=jax.ShapeDtypeStruct((length, columns), F32),
        compiler_params=pltpu.CompilerParams(vmem_limit_bytes=VMEM_LIMIT),
        name="finish",
    )(entering, local_out, states)


def relay(ends, seq_count):
    dim = ends.shape[2] // 2
    pairs = [(i, i + 1) for i in range(seq_count - 1)]
    removed, written = ends[:, :dim, :dim].astype(F32), ends[:, :dim, dim:].astype(F32)
    decay = ends[:, dim, :1].astype(F32) + ends[:, dim, dim : dim + 1].astype(F32)

    def step(_, incoming):
        outgoing = decay[:, :, None] * incoming + written
        outgoing = outgoing - jnp.einsum(
            "hij,hjk->hik", removed, incoming, precision=lax.Precision.HIGHEST
        )
        return lax.ppermute(outgoing, "seq", pairs)

    return lax.fori_loop(0, seq_count - 1, step, jnp.zeros_like(written)).astype(BF)


def move(values, change):
    exp_count = lax.axis_size("exp")
    pairs = []
    for s in range(lax.axis_size("seq")):
        for e in range(exp_count):
            to_s, to_e = change(s, e)
            pairs.append((s * exp_count + e, to_s * exp_count + to_e))
    return lax.ppermute(values, ("seq", "exp"), pairs)


def over_x(values):
    return move(values, lambda s, e: (s ^ 1, e))


def over_y(values):
    return move(values, lambda s, e: (s, e ^ 2))


def over_core(values):
    return move(values, lambda s, e: (s, e ^ 1))


def along_z(values, by):
    count = lax.axis_size("seq")
    return move(values, lambda s, e: ((s + 2 * by) % count, e))


def added(*terms):
    total = terms[0].astype(F32)
    for term in terms[1:]:
        total = total + term.astype(F32)
    return total


def route_waves(normed, expert_ids, expert_weights, gate_up_weight, down, capacity):
    tok_rows, width = normed.shape
    choose = expert_ids.shape[1]
    local_experts = gate_up_weight.shape[0]
    me = lax.axis_index("seq") * lax.axis_size("exp") + lax.axis_index("exp")
    first = (jnp.stack([me, me ^ 1]) * local_experts).astype(jnp.int32)
    gap = jnp.zeros((tok_rows, ROUTE_STEP - choose), BF)
    high, low = split(expert_weights)
    tail = jnp.zeros((tok_rows, 128 - 3 * ROUTE_STEP), BF)
    block = jnp.concatenate(
        [normed, expert_ids.astype(BF), gap, high, gap, low, gap, tail], axis=1
    )
    weights = (gate_up_weight, down, over_core(gate_up_weight), over_core(down))
    count = lax.axis_size("seq") // 2
    order = list(range(1, count)) + [0]
    first_way = [over_y if wave == 1 else over_x for wave in range(count)]
    second_way = [over_x if wave == 1 else over_y for wave in range(count)]
    block = [block]
    for wave in range(1, count):
        block.append(along_z(block[-1], 1))
    by_one = [first_way[wave](block[wave]) for wave in range(count)]
    by_two = [second_way[wave](block[wave]) for wave in range(count)]
    diagonal = {wave: second_way[wave](by_one[wave]) for wave in (0, 1)}
    for wave in range(2, count):
        diagonal[wave] = along_z(diagonal[wave - 1], 1)
    due = [() for _ in range(count + 3)]
    for call, wave in enumerate(order):
        if call and wave:
            due[call - 1] += (block[wave],)
        if call > 1:
            due[call - 1 if wave else 0] += (by_one[wave], by_two[wave])
    running = sum_below = None
    for call, wave in enumerate(order):
        cuts = 2 if call > count - 3 else 1
        found = experts(
            (block[wave], by_one[wave], by_two[wave], diagonal[wave]),
            first,
            weights,
            due[call],
            capacity,
            choose,
            cuts,
        )
        one, two = first_way[wave], second_way[wave]
        if wave == 0:
            one, two = two, one
        due[call + 1] += (found[0],)
        below = None if sum_below is None else jnp.split(sum_below, cuts, axis=1)
        sum_below = None
        if running is not None and len(running) < cuts:
            running = jnp.split(running[0], cuts, axis=1)
        pieces = []
        for cut in range(cuts):
            own, sum_one, sum_two, sum_both = found[cut::cuts]
            if wave == 0:
                sum_one, sum_two = sum_two, sum_one
            if below is not None:
                sum_both = added(sum_both, below[cut]).astype(BF)
            if 0 < wave < count - 1:
                sum_below = along_z(sum_both, 1)
                due[call + 2] += (sum_below,)
            else:
                sum_one = added(sum_one, two(sum_both)).astype(BF)
            from_two = two(sum_two)
            from_one = one(sum_one)
            due[call + 2] += (from_two, from_one)
            if pieces:
                from_one, _ = lax.optimization_barrier((from_one, pieces[-1]))
            here = added(own, from_two, from_one)
            if running is not None:
                here = added(here, running[cut])
            pieces.append(here.astype(BF) if wave else here)
        if wave:
            running = [along_z(piece, 1) for piece in pieces]
    return jnp.concatenate(pieces, axis=1)


def route_some(normed, expert_ids, expert_weights, gate_up_weight, down, capacity):
    axes = ("seq", "exp")
    tok_rows, width = normed.shape
    choose = expert_ids.shape[1]
    local_experts = gate_up_weight.shape[0]
    expert_width = down.shape[1]
    devices = lax.axis_size("seq") * lax.axis_size("exp")
    experts_all = local_experts * devices
    flat_ids = expert_ids.reshape(-1)
    onehot = (flat_ids[:, None] == jnp.arange(experts_all, dtype=jnp.int32)[None, :]).astype(
        jnp.int32
    )
    rank = jnp.sum(jnp.cumsum(onehot, axis=0) * onehot, axis=1) - 1
    slot = flat_ids * capacity + rank
    token_of = jnp.arange(tok_rows * choose, dtype=jnp.int32) // choose
    send = jnp.zeros((experts_all * capacity, width), BF).at[slot].set(normed[token_of])
    both = jnp.einsum(
        "secd,edf->secf",
        lax.all_to_all(
            send.reshape(devices, local_experts, capacity, width),
            axes,
            split_axis=0,
            concat_axis=0,
            tiled=True,
        ),
        gate_up_weight,
        preferred_element_type=F32,
    )
    hidden = (jax.nn.silu(both[..., :expert_width]) * both[..., expert_width:]).astype(BF)
    back = lax.all_to_all(
        jnp.einsum("secf,efd->secd", hidden, down, preferred_element_type=F32).astype(BF),
        axes,
        split_axis=0,
        concat_axis=0,
        tiled=True,
    )
    back_rows = back.reshape(experts_all * capacity, width)[slot].astype(F32)
    return jnp.sum(
        back_rows.reshape(tok_rows, choose, width) * expert_weights[:, :, None], axis=1
    )


def local(
    stream,
    moe_gain,
    expert_ids,
    expert_weights,
    gate_up_weight,
    down,
    mixer_gain,
    qkv_weight,
    decay_log,
    write_rate,
):
    tok_rows, width = stream.shape
    choose = expert_ids.shape[1]
    seq_count = lax.axis_size("seq")
    devices = seq_count * lax.axis_size("exp")
    experts_all = gate_up_weight.shape[0] * devices
    capacity = max(2, (tok_rows * choose * 6 + experts_all * 5 - 1) // (experts_all * 5))
    normed = rms_scale(stream, moe_gain).astype(BF)
    planes = lax.axis_size("exp") == 4 and seq_count % 4 == 0 and choose <= ROUTE_STEP
    route = route_waves if planes and experts_all <= 256 else route_some
    moe = route(normed, expert_ids, expert_weights, gate_up_weight, down, capacity)
    mixed = (stream.astype(F32) + moe).astype(BF)
    normed_mix = rms_scale(mixed, mixer_gain).astype(BF)
    heads = decay_log.shape[1]
    blocks = decay_log.shape[0] // CH
    sums = jnp.cumsum(decay_log.T.reshape(heads, blocks, CH), axis=-1)
    rates = write_rate.T.reshape(heads, blocks, CH)
    pairs = blocks // 2
    by_pair = lambda values: values.reshape(heads, pairs, 2, CH).transpose(1, 0, 2, 3)
    if planes:
        core = lax.axis_index("exp") % 2
        side = lax.axis_index("exp") // 2
        from_y = over_y(normed_mix)
        both_sides = [(normed_mix, over_core(normed_mix)), (from_y, over_core(from_y))]
        parts = [
            (
                jnp.concatenate([jnp.where(core == 0, a, b), jnp.where(core == 0, b, a)], axis=0),
                place,
            )
            for (a, b), place in zip(both_sides, (side, 1 - side))
        ]
    else:
        gathered = lax.all_gather(normed_mix, "exp", axis=0, tiled=True)
        parts = [(gathered[2 * CH * i : 2 * CH * (i + 1)], jnp.int32(i)) for i in range(pairs)]
    found = ()
    for x, place in parts:
        found = chunks_of(
            x,
            place.astype(jnp.int32).reshape(1),
            qkv_weight,
            by_pair(sums),
            by_pair(rates),
            found,
        )
    key, solved, moved = found
    starts, ends = chain(moved, sums)
    places = jnp.stack([place for _, place in parts]).astype(jnp.int32)
    entering, local_out = read([x for x, _ in parts], places, qkv_weight, key, solved, starts, sums)
    if heads % seq_count == 0:
        dim = ends.shape[2] // 2
        each = heads // seq_count
        held = lax.all_to_all(ends, "seq", split_axis=0, concat_axis=0, tiled=True)
        held = held.reshape(seq_count, each, dim + 16, 2 * dim)
        states = jnp.stack([carry(held[:, i], entering) for i in range(each)], axis=1)
        arriving = lax.all_to_all(
            states.reshape(seq_count * each, dim, dim), "seq", split_axis=0, concat_axis=0, tiled=True
        )
    else:
        arriving = relay(ends, seq_count)
    return (mixed, finish(entering, local_out, arriving))


def solution(mesh):
    in_specs = (
        P(("seq", "exp"), None),
        P(),
        P(("seq", "exp"), None),
        P(("seq", "exp"), None),
        P(("seq", "exp"), None, None),
        P(("seq", "exp"), None, None),
        P(),
        P(None, None, "exp"),
        P("seq", "exp"),
        P("seq", "exp"),
    )
    out_specs = (P(("seq", "exp"), None), P("seq", "exp"))
    return jax.shard_map(local, mesh=mesh, in_specs=in_specs, out_specs=out_specs, check_vma=False)
```

```python
from functools import partial

import jax
import jax.numpy as jnp
from jax import lax
from jax.experimental import pallas as pl
from jax.experimental.pallas import tpu as pltpu
from jax.sharding import PartitionSpec as P

CH = 128
ROUTE_STEP = 16
VMEM_LIMIT = 56 * 1024 * 1024
BF = jnp.bfloat16
F32 = jnp.float32


def rms_scale(values, gain):
    wide = values.astype(F32)
    return wide * lax.rsqrt(jnp.mean(wide * wide, axis=-1, keepdims=True) + 1e-06) * gain


def dot(a, b):
    return jnp.dot(a, b, preferred_element_type=F32)


def split(a):
    high = a.astype(BF)
    return high, (a - high.astype(F32)).astype(BF)


def rough(a, b):
    return dot(a.astype(BF), b.astype(BF))


def left_pair(a):
    high, low = split(a)
    return jnp.concatenate([high, low], axis=1)


def right_pair(b):
    high, low = split(b)
    row = jnp.concatenate([high, low], axis=1)
    return jnp.concatenate([row, row], axis=0)


def wide_product(a, b):
    columns = b.shape[1]
    both = dot(left_pair(a), right_pair(b))
    return both[:, :columns] + both[:, columns:]


def moe_kernel(capacity, choose, *refs):
    first_ref, *block_refs = refs[:5]
    weight_refs = refs[5:9]
    out_refs = refs[-9:-5]
    gate_up_ref, down_ref, rows_ref, back_ref, sem = refs[-5:]
    tok, wide = block_refs[0].shape
    width = rows_ref.shape[2]
    experts_here = gate_up_ref.shape[0]
    half = experts_here // 2
    expert_width = down_ref.shape[1]
    pair_rows = rows_ref.shape[1] // 2

    copies = []
    for e in range(experts_here):
        side, at = divmod(e, half)
        fetch_in = pltpu.make_async_copy(
            weight_refs[2 * side].at[at], gate_up_ref.at[e], sem.at[0, e]
        )
        fetch_out = pltpu.make_async_copy(
            weight_refs[2 * side + 1].at[at], down_ref.at[e], sem.at[1, e]
        )
        fetch_in.start()
        fetch_out.start()
        copies.append((fetch_in, fetch_out))

    matched, weights = [], []
    for block_ref in block_refs:
        routing = block_ref[:, width:].astype(F32).T
        ids = routing[:choose]
        scale = routing[ROUTE_STEP : ROUTE_STEP + choose]
        scale = scale + routing[2 * ROUTE_STEP : 2 * ROUTE_STEP + choose]
        for e in range(experts_here):
            side, at = divmod(e, half)
            hit = ids == (first_ref[side] + at).astype(F32)
            matched.append(jnp.max(jnp.where(hit, 1.0, 0.0), axis=0, keepdims=True))
            weights.append(jnp.sum(jnp.where(hit, scale, 0.0), axis=0, keepdims=True))
    match = jnp.concatenate(matched, axis=0)
    before = lax.broadcasted_iota(jnp.int32, (tok, tok), 0) < lax.broadcasted_iota(
        jnp.int32, (tok, tok), 1
    )
    rank = dot(match.astype(BF), jnp.where(before, 1.0, 0.0).astype(BF))
    rank = jnp.where(match > 0.5, rank, -1e4)
    row_number = lax.broadcasted_iota(jnp.int32, (pair_rows, 2 * tok), 0).astype(F32)
    picks = []
    for pair in range(2):
        x_pair = jnp.concatenate(
            [block_refs[2 * pair][:, :width], block_refs[2 * pair + 1][:, :width]], axis=0
        )
        here = []
        for e in range(experts_here):
            low = 2 * pair * experts_here + e
            high = low + experts_here
            place = jnp.concatenate(
                [rank[low : low + 1], rank[high : high + 1] + float(capacity)], axis=1
            )
            here.append(jnp.where(row_number == place, 1.0, 0.0))
        picks.append(here)
        chosen = dot(jnp.concatenate(here, axis=0).astype(BF), x_pair).astype(BF)
        for e in range(experts_here):
            rows_ref[e, pair * pair_rows : (pair + 1) * pair_rows, :] = chosen[
                e * pair_rows : (e + 1) * pair_rows
            ]
    for e in range(experts_here):
        copies[e][0].wait()
        both = dot(rows_ref[e], gate_up_ref[e])
        gate = both[:, :expert_width]
        hidden = (gate / (1.0 + jnp.exp(-gate)) * both[:, expert_width:]).astype(BF)
        copies[e][1].wait()
        back_ref[e] = dot(hidden, down_ref[e]).astype(BF)
    for pair in range(2):
        scaled, rows = [], []
        for e in range(experts_here):
            low = 2 * pair * experts_here + e
            high = low + experts_here
            weight = jnp.concatenate([weights[low], weights[high]], axis=1)
            scaled.append(picks[pair][e] * weight)
            rows.append(back_ref[e, pair * pair_rows : (pair + 1) * pair_rows, :])
        summed = lax.dot_general(
            jnp.concatenate(scaled, axis=0).astype(BF),
            jnp.concatenate(rows, axis=0),
            (((0,), (0,)), ((), ())),
            preferred_element_type=F32,
        ).astype(BF)
        out_refs[2 * pair][...] = summed[:tok]
        out_refs[2 * pair + 1][...] = summed[tok:]


def experts(blocks, first, weights, after, capacity, choose):
    tok, wide = blocks[0].shape
    gate_up_weight, down = weights[:2]
    local_experts, width, double = gate_up_weight.shape
    here = 2 * local_experts
    pair_rows = -(-2 * capacity // 16) * 16
    whole = pl.BlockSpec(memory_space=pltpu.VMEM)
    return pl.pallas_call(
        partial(moe_kernel, capacity, choose),
        in_specs=[pl.BlockSpec(memory_space=pltpu.SMEM)]
        + [whole] * 4
        + [pl.BlockSpec(memory_space=pl.ANY)] * (4 + len(after)),
        out_specs=[whole] * 4,
        out_shape=[jax.ShapeDtypeStruct((tok, width), BF)] * 4,
        scratch_shapes=[
            pltpu.VMEM((here,) + gate_up_weight.shape[1:], BF),
            pltpu.VMEM((here,) + down.shape[1:], BF),
            pltpu.VMEM((here, 2 * pair_rows, width), BF),
            pltpu.VMEM((here, 2 * pair_rows, width), BF),
            pltpu.SemaphoreType.DMA((2, here)),
        ],
        compiler_params=pltpu.CompilerParams(vmem_limit_bytes=VMEM_LIMIT),
        cost_estimate=pl.CostEstimate(
            flops=here * pair_rows * width * double // 4,
            bytes_accessed=tok * width,
            transcendentals=0,
        ),
        name="experts",
    )(first, *blocks, *weights, *after)


def unit_rows(values):
    return values * lax.rsqrt(jnp.sum(values * values, axis=-1, keepdims=True) + 1e-06)


def tiles():
    rows = lax.broadcasted_iota(jnp.int32, (CH, CH), 0)
    columns = lax.broadcasted_iota(jnp.int32, (CH, CH), 1)
    return rows, columns


def against_rows(a, b):
    high, low = split(b)
    right = jnp.concatenate(
        [jnp.concatenate([high, high], axis=1), jnp.concatenate([low, low], axis=1)], axis=0
    )
    both = lax.dot_general(
        left_pair(a), right, (((1,), (1,)), ((), ())), preferred_element_type=F32
    )
    return both[:, : b.shape[0]] + both[:, b.shape[0] :]


def chunk_kernel(place_ref, a_ref, b_ref, key_w_ref, value_w_ref, sum_ref, rate_ref, *refs):
    k_ref, solved_ref, moved_ref = refs[-3:]
    heads, chunks, _ = sum_ref.shape[1:]
    dim = key_w_ref.shape[2] // heads
    rows, columns = tiles()
    strict = rows > columns
    identity = jnp.where(rows == columns, 1.0, 0.0)
    swapped = place_ref[1] == 1
    x = jnp.concatenate(
        [
            jnp.where(swapped, b_ref[...], a_ref[...]),
            jnp.where(swapped, a_ref[...], b_ref[...]),
        ],
        axis=0,
    )
    key = dot(x, key_w_ref[0])
    value = dot(x, value_w_ref[0])
    units = [(h, n) for h in range(heads) for n in range(chunks)]

    def part(values, h, n):
        return values[n * CH : (n + 1) * CH, h * dim : (h + 1) * dim]

    keys, values, lowers, rates, growths, remains = [], [], [], [], [], []
    for h, n in units:
        unit = unit_rows(part(key, h, n))
        k_ref[n * CH : (n + 1) * CH, h * dim : (h + 1) * dim] = unit
        keys.append(unit)
        values.append(part(value, h, n))
    for u, (h, n) in enumerate(units):
        across = jnp.broadcast_to(sum_ref[0, h, n : n + 1, :], (CH, CH))
        along = across.T
        rate = jnp.broadcast_to(rate_ref[0, h, n : n + 1, :], (CH, CH)).T
        last = jnp.broadcast_to(along[CH - 1 : CH, :], (CH, CH))
        fade = jnp.exp(jnp.where(strict, along - across, 0.0))
        rates.append(rate)
        growths.append(jnp.exp(along))
        remains.append(jnp.exp(last - along))
        unit = keys[u].astype(BF)
        met = lax.dot_general(unit, unit, (((1,), (1,)), ((), ())), preferred_element_type=F32)
        lowers.append(jnp.where(strict, rate * fade * met, 0.0))

    def ring(size):
        shared = (rows // (2 * size)) == (columns // (2 * size))
        return shared & (rows // size % 2 == 1) & (columns // size % 2 == 0)

    span = range(len(units))
    inverse = [identity - jnp.where(ring(1), lowers[u], 0.0) for u in span]
    size = 2
    while size < CH:
        here = ring(size)
        step = [rough(jnp.where(here, lowers[u], 0.0), inverse[u]) for u in span]
        inverse = [inverse[u] - rough(inverse[u], step[u]) for u in span]
        size *= 2
    wanted = [
        jnp.concatenate([rates[u] * growths[u] * keys[u], rates[u] * values[u]], axis=1)
        for u in span
    ]
    solved = [wanted[u] + rough(inverse[u] - identity, wanted[u]) for u in span]
    for u, (h, n) in enumerate(units):
        solved_ref[h, n] = solved[u]
        moved_ref[h, n] = lax.dot_general(
            (remains[u] * keys[u]).astype(BF),
            solved[u].astype(BF),
            (((0,), (0,)), ((), ())),
            preferred_element_type=F32,
        )


def chunks_of(blocks, place, qkv_weight, sums, rates, before, steps):
    rows, width = blocks[0].shape
    rows *= 2
    _, _, columns = qkv_weight.shape
    parts, heads, chunks, _ = sums.shape
    dim = columns // heads
    step = head_step(heads)
    start = steps[0]
    at_rows = pl.BlockSpec((rows, step * dim), lambda i, place: (place[0], i + start))
    at_chunks = pl.BlockSpec(
        (step, chunks, CH, 2 * dim), lambda i, place: (i + start, place[0], 0, 0)
    )
    per_head = pl.BlockSpec((1, step, chunks, CH), lambda i, place: (place[0], i + start, 0, 0))
    block = pl.BlockSpec(blocks[0].shape, lambda i, place: (0, 0))
    return pl.pallas_call(
        chunk_kernel,
        grid_spec=pltpu.PrefetchScalarGridSpec(
            num_scalar_prefetch=1,
            grid=(len(steps),),
            in_specs=[
                block,
                block,
                pl.BlockSpec((1, width, step * dim), lambda i, place: (1, 0, i + start)),
                pl.BlockSpec((1, width, step * dim), lambda i, place: (2, 0, i + start)),
                per_head,
                per_head,
            ]
            + [pl.BlockSpec(memory_space=pl.ANY)] * len(before),
            out_specs=[at_rows, at_chunks, at_chunks],
        ),
        out_shape=[jax.ShapeDtypeStruct((parts * rows, columns), F32)]
        + [jax.ShapeDtypeStruct((heads, parts * chunks, CH, 2 * dim), F32)] * 2,
        input_output_aliases={7 + i: i for i in range(len(before))},
        compiler_params=pltpu.CompilerParams(vmem_limit_bytes=VMEM_LIMIT),
        name="chunks",
    )(place, *blocks, qkv_weight, qkv_weight, sums, rates, *before)


def head_step(heads):
    return min(4, heads)


def chain_kernel(moved_ref, sum_ref, starts_ref, end_ref):
    heads, chunks, dim, _ = moved_ref.shape
    rows, columns = tiles()
    identity = jnp.where(rows == columns, 1.0, 0.0)
    span = range(heads)

    def spread(total):
        decay = jnp.exp(jnp.broadcast_to(total, (CH, CH)).T[CH - 1 : CH, :])
        return jnp.broadcast_to(decay, (CH, CH))

    wholes = [[spread(sum_ref[h, n : n + 1, :]) for n in range(chunks)] for h in span]
    state = [
        jnp.concatenate(
            [wholes[h][0] * identity - moved_ref[h, 0, :, :dim], moved_ref[h, 0, :, dim:]], axis=1
        )
        for h in span
    ]
    for n in range(1, chunks):
        for h in span:
            starts_ref[h, n - 1] = state[h]
        removed = [rough(moved_ref[h, n, :, :dim], state[h]) for h in span]
        state = [
            jnp.concatenate(
                [
                    wholes[h][n] * state[h][:, :dim] - removed[h][:, :dim],
                    wholes[h][n] * state[h][:, dim:]
                    - removed[h][:, dim:]
                    + moved_ref[h, n, :, dim:],
                ],
                axis=1,
            )
            for h in span
        ]
    for h in span:
        decay = wholes[h][0]
        for n in range(1, chunks):
            decay = decay * wholes[h][n]
        end_ref[h, :dim, :dim] = (decay * identity - state[h][:, :dim]).astype(BF)
        end_ref[h, :dim, dim:] = state[h][:, dim:].astype(BF)
        end_ref[h, dim:, :] = left_pair(decay[:16])


def chain(moved, sums):
    heads, chunks, dim, double = moved.shape
    return pl.pallas_call(
        chain_kernel,
        out_shape=[
            jax.ShapeDtypeStruct((heads, chunks - 1, dim, double), F32),
            jax.ShapeDtypeStruct((heads, dim + 16, double), BF),
        ],
        compiler_params=pltpu.CompilerParams(vmem_limit_bytes=VMEM_LIMIT),
        name="chain",
    )(moved, sums)


def read_kernel(place_ref, w_ref, k_ref, solved_ref, starts_ref, sum_ref, *refs):
    x_refs = refs[:-2]
    chunk_places = len(x_refs)
    enter_ref, local_ref = refs[-2:]
    heads, chunks, _ = sum_ref.shape
    dim = starts_ref.shape[2]
    rows, columns = tiles()
    inclusive = rows >= columns
    found = dot(jnp.concatenate([x_ref[...] for x_ref in x_refs], axis=0), w_ref[0])
    found = [found[i * CH : (i + 1) * CH] for i in range(chunk_places)]
    queries = []
    for place in range(chunk_places):
        query = found[0]
        for i in range(1, chunk_places):
            query = jnp.where(place_ref[i] == place, found[i], query)
        queries.append(query)
    units = [(h, n) for h in range(heads) for n in range(chunks)]
    for h, n in units:
        cut = slice(n * CH, (n + 1) * CH), slice(h * dim, (h + 1) * dim)
        across = jnp.broadcast_to(sum_ref[h, n : n + 1, :], (CH, CH))
        along = across.T
        fade = jnp.exp(jnp.where(inclusive, along - across, 0.0))
        query = unit_rows(queries[n][:, cut[1]])
        masked = jnp.where(inclusive, fade * against_rows(query, k_ref[cut]), 0.0)
        probed = wide_product(masked, solved_ref[h, n])
        entering = jnp.exp(along) * query - probed[:, :dim]
        output = probed[:, dim:]
        if n:
            begun = wide_product(entering, starts_ref[h, n - 1])
            entering = begun[:, :dim]
            output = output + begun[:, dim:]
        enter_ref[cut] = entering.astype(BF)
        local_ref[cut] = output


def read(parts, places, qkv_weight, key, solved, starts, sums):
    length, columns = key.shape
    heads, chunks, _ = sums.shape
    dim = columns // heads
    width = qkv_weight.shape[1]
    step = 2 if heads % 2 == 0 else 1
    per_column = pl.BlockSpec((length, step * dim), lambda h: (0, h))
    four = lambda h: (h, 0, 0, 0)
    return pl.pallas_call(
        read_kernel,
        grid=(heads // step,),
        in_specs=[
            pl.BlockSpec(memory_space=pltpu.SMEM),
            pl.BlockSpec((1, width, step * dim), lambda h: (0, 0, h)),
            per_column,
            pl.BlockSpec((step, chunks, CH, 2 * dim), four),
            pl.BlockSpec((step, chunks - 1, dim, 2 * dim), four),
            pl.BlockSpec((step, chunks, CH), lambda h: (h, 0, 0)),
        ]
        + [pl.BlockSpec(x.shape, lambda h: (0, 0)) for x in parts],
        out_specs=[per_column, per_column],
        out_shape=[
            jax.ShapeDtypeStruct((length, columns), BF),
            jax.ShapeDtypeStruct((length, columns), F32),
        ],
        compiler_params=pltpu.CompilerParams(vmem_limit_bytes=VMEM_LIMIT),
        name="read",
    )(places, qkv_weight, key, solved, starts, sums, *parts)


def carry_kernel(ends_ref, after_ref, states_ref):
    segments, _, double = ends_ref.shape
    dim = double // 2
    state = jnp.zeros((dim, dim), F32)
    for s in range(segments):
        states_ref[s] = state.astype(BF)
        if s < segments - 1:
            decay = ends_ref[s, dim : dim + 1, :].astype(F32)
            decay = decay[:, :dim] + decay[:, dim:]
            removed = dot(ends_ref[s, :dim, :dim], left_pair(state))
            removed = removed[:, :dim] + removed[:, dim:]
            state = decay * state - removed + ends_ref[s, :dim, dim:].astype(F32)


def carry(ends, after):
    segments, _, double = ends.shape
    return pl.pallas_call(
        carry_kernel,
        in_specs=[pl.BlockSpec(memory_space=pltpu.VMEM), pl.BlockSpec(memory_space=pl.ANY)],
        out_shape=jax.ShapeDtypeStruct((segments, double // 2, double // 2), BF),
        compiler_params=pltpu.CompilerParams(vmem_limit_bytes=VMEM_LIMIT),
        name="carry",
    )(ends, after)


def finish_kernel(enter_ref, local_ref, state_ref, core_ref):
    heads, dim, _ = state_ref.shape
    for h in range(heads):
        cut = slice(h * dim, (h + 1) * dim)
        core_ref[:, cut] = local_ref[:, cut] + dot(enter_ref[:, cut], state_ref[h])


def finish(entering, local_out, states):
    length, columns = entering.shape
    heads, dim, _ = states.shape
    step = 2 if heads % 2 == 0 else 1
    per_column = pl.BlockSpec((length, step * dim), lambda h: (0, h))
    return pl.pallas_call(
        finish_kernel,
        grid=(heads // step,),
        in_specs=[per_column, per_column, pl.BlockSpec((step, dim, dim), lambda h: (h, 0, 0))],
        out_specs=per_column,
        out_shape=jax.ShapeDtypeStruct((length, columns), F32),
        compiler_params=pltpu.CompilerParams(vmem_limit_bytes=VMEM_LIMIT),
        name="finish",
    )(entering, local_out, states)


def relay(ends, seq_count):
    dim = ends.shape[2] // 2
    pairs = [(i, i + 1) for i in range(seq_count - 1)]
    removed, written = ends[:, :dim, :dim].astype(F32), ends[:, :dim, dim:].astype(F32)
    decay = ends[:, dim, :1].astype(F32) + ends[:, dim, dim : dim + 1].astype(F32)

    def step(_, incoming):
        outgoing = decay[:, :, None] * incoming + written
        outgoing = outgoing - jnp.einsum(
            "hij,hjk->hik", removed, incoming, precision=lax.Precision.HIGHEST
        )
        return lax.ppermute(outgoing, "seq", pairs)

    return lax.fori_loop(0, seq_count - 1, step, jnp.zeros_like(written)).astype(BF)


def move(values, change):
    exp_count = lax.axis_size("exp")
    pairs = []
    for s in range(lax.axis_size("seq")):
        for e in range(exp_count):
            to_s, to_e = change(s, e)
            pairs.append((s * exp_count + e, to_s * exp_count + to_e))
    return lax.ppermute(values, ("seq", "exp"), pairs)


def over_x(values):
    return move(values, lambda s, e: (s ^ 1, e))


def over_y(values):
    return move(values, lambda s, e: (s, e ^ 2))


def over_core(values):
    return move(values, lambda s, e: (s, e ^ 1))


def along_z(values, by):
    count = lax.axis_size("seq")
    return move(values, lambda s, e: ((s + 2 * by) % count, e))


def added(*terms):
    total = terms[0].astype(F32)
    for term in terms[1:]:
        total = total + term.astype(F32)
    return total


def route_waves(normed, expert_ids, expert_weights, gate_up_weight, down, capacity):
    tok_rows, width = normed.shape
    choose = expert_ids.shape[1]
    local_experts = gate_up_weight.shape[0]
    me = lax.axis_index("seq") * lax.axis_size("exp") + lax.axis_index("exp")
    first = (jnp.stack([me, me ^ 1]) * local_experts).astype(jnp.int32)
    gap = jnp.zeros((tok_rows, ROUTE_STEP - choose), BF)
    high, low = split(expert_weights)
    tail = jnp.zeros((tok_rows, 128 - 3 * ROUTE_STEP), BF)
    block = jnp.concatenate(
        [normed, expert_ids.astype(BF), gap, high, gap, low, gap, tail], axis=1
    )
    weights = (gate_up_weight, down, over_core(gate_up_weight), over_core(down))
    count = lax.axis_size("seq") // 2
    order = [1, 0] + list(range(2, count))
    first_way = [over_y if wave == 1 else over_x for wave in range(count)]
    second_way = [over_x if wave == 1 else over_y for wave in range(count)]
    block = [block]
    for wave in range(1, count):
        block.append(along_z(block[-1], 1))
    by_one = [first_way[wave](block[wave]) for wave in range(count)]
    by_two = [second_way[wave](block[wave]) for wave in range(count)]
    diagonal = [second_way[wave](by_one[wave]) for wave in (0, 1)]
    for wave in range(2, count):
        diagonal.append(along_z(diagonal[wave - 1], 1))
    due = [() for _ in range(count + 4)]
    due[0] = (by_one[0], by_two[0], block[2])
    due[1] = (by_one[2], by_two[2], block[3])
    due[2] = (by_one[3], by_two[3])
    running = sum_below = None
    for call, wave in enumerate(order):
        own, sum_one, sum_two, sum_both = experts(
            (block[wave], by_one[wave], by_two[wave], diagonal[wave]),
            first,
            weights,
            due[call],
            capacity,
            choose,
        )
        one, two = first_way[wave], second_way[wave]
        due[call + 1] += (own,)
        if wave:
            if sum_below is not None:
                sum_both = added(sum_both, sum_below).astype(BF)
            if wave < count - 1:
                sum_below = along_z(sum_both, 1)
                due[call + 2] += (sum_below,)
            else:
                far = move(sum_both, lambda s, e: (((s ^ 1) + 2) % (2 * count), e ^ 2))
        else:
            sum_one = added(sum_one, two(sum_both)).astype(BF)
            due[call + 2] += (sum_one,)
        from_two = two(sum_two)
        from_one = one(sum_one)
        due[call + 2] += (from_two, from_one) if wave else (from_two,)
        here = added(own, from_two, from_one)
        if wave:
            if running is not None:
                here = added(here, running)
            running = along_z(here.astype(BF), 1)
            due[call + 3] += (running,)
        else:
            home = here
    return added(home, running, far)


def route_some(normed, expert_ids, expert_weights, gate_up_weight, down, capacity):
    axes = ("seq", "exp")
    tok_rows, width = normed.shape
    choose = expert_ids.shape[1]
    local_experts = gate_up_weight.shape[0]
    expert_width = down.shape[1]
    devices = lax.axis_size("seq") * lax.axis_size("exp")
    experts_all = local_experts * devices
    flat_ids = expert_ids.reshape(-1)
    onehot = (flat_ids[:, None] == jnp.arange(experts_all, dtype=jnp.int32)[None, :]).astype(
        jnp.int32
    )
    rank = jnp.sum(jnp.cumsum(onehot, axis=0) * onehot, axis=1) - 1
    slot = flat_ids * capacity + rank
    token_of = jnp.arange(tok_rows * choose, dtype=jnp.int32) // choose
    send = jnp.zeros((experts_all * capacity, width), BF).at[slot].set(normed[token_of])
    both = jnp.einsum(
        "secd,edf->secf",
        lax.all_to_all(
            send.reshape(devices, local_experts, capacity, width),
            axes,
            split_axis=0,
            concat_axis=0,
            tiled=True,
        ),
        gate_up_weight,
        preferred_element_type=F32,
    )
    hidden = (jax.nn.silu(both[..., :expert_width]) * both[..., expert_width:]).astype(BF)
    back = lax.all_to_all(
        jnp.einsum("secf,efd->secd", hidden, down, preferred_element_type=F32).astype(BF),
        axes,
        split_axis=0,
        concat_axis=0,
        tiled=True,
    )
    back_rows = back.reshape(experts_all * capacity, width)[slot].astype(F32)
    return jnp.sum(
        back_rows.reshape(tok_rows, choose, width) * expert_weights[:, :, None], axis=1
    )


def local(
    stream,
    moe_gain,
    expert_ids,
    expert_weights,
    gate_up_weight,
    down,
    mixer_gain,
    qkv_weight,
    decay_log,
    write_rate,
):
    tok_rows, width = stream.shape
    choose = expert_ids.shape[1]
    seq_count = lax.axis_size("seq")
    devices = seq_count * lax.axis_size("exp")
    experts_all = gate_up_weight.shape[0] * devices
    capacity = max(2, (tok_rows * choose * 6 + experts_all * 5 - 1) // (experts_all * 5))
    normed = rms_scale(stream, moe_gain).astype(BF)
    planes = lax.axis_size("exp") == 4 and seq_count % 4 == 0 and choose <= ROUTE_STEP
    route = route_waves if planes and experts_all <= 256 else route_some
    moe = route(normed, expert_ids, expert_weights, gate_up_weight, down, capacity)
    mixed = (stream.astype(F32) + moe).astype(BF)
    normed_mix = rms_scale(mixed, mixer_gain).astype(BF)
    heads = decay_log.shape[1]
    blocks = decay_log.shape[0] // CH
    sums = jnp.cumsum(decay_log.T.reshape(heads, blocks, CH), axis=-1)
    rates = write_rate.T.reshape(heads, blocks, CH)
    pairs = blocks // 2
    by_pair = lambda values: values.reshape(heads, pairs, 2, CH).transpose(1, 0, 2, 3)
    steps = list(range(heads // head_step(heads)))
    found = ()
    if planes:
        me = lax.axis_index("exp")
        from_y = over_y(normed_mix)
        parts = [normed_mix, over_core(normed_mix), from_y, None]
        places = me ^ jnp.arange(blocks, dtype=jnp.int32)
        for i, step in enumerate(steps):
            if i == len(steps) - 1:
                parts[2], found = lax.optimization_barrier((from_y, found))
                parts[3] = over_core(parts[2])
            found = chunks_of(
                parts[:2],
                jnp.stack([me // 2, me % 2]),
                qkv_weight,
                by_pair(sums),
                by_pair(rates),
                found,
                [step],
            )
        found = chunks_of(
            parts[2:],
            jnp.stack([1 - me // 2, me % 2]),
            qkv_weight,
            by_pair(sums),
            by_pair(rates),
            found,
            steps,
        )
    else:
        gathered = lax.all_gather(normed_mix, "exp", axis=0, tiled=True)
        parts = [gathered[CH * i : CH * (i + 1)] for i in range(blocks)]
        places = jnp.arange(blocks, dtype=jnp.int32)
        for i in range(pairs):
            found = chunks_of(
                parts[2 * i : 2 * i + 2],
                jnp.array([i, 0], jnp.int32),
                qkv_weight,
                by_pair(sums),
                by_pair(rates),
                found,
                steps,
            )
    key, solved, moved = found
    starts, ends = chain(moved, sums)
    entering, local_out = read(parts, places, qkv_weight, key, solved, starts, sums)
    if heads % seq_count == 0:
        dim = ends.shape[2] // 2
        each = heads // seq_count
        held = lax.all_to_all(ends, "seq", split_axis=0, concat_axis=0, tiled=True)
        held = held.reshape(seq_count, each, dim + 16, 2 * dim)
        states = jnp.stack([carry(held[:, i], entering) for i in range(each)], axis=1)
        arriving = lax.all_to_all(
            states.reshape(seq_count * each, dim, dim), "seq", split_axis=0, concat_axis=0, tiled=True
        )
    else:
        arriving = relay(ends, seq_count)
    return (mixed, finish(entering, local_out, arriving))


def solution(mesh):
    in_specs = (
        P(("seq", "exp"), None),
        P(),
        P(("seq", "exp"), None),
        P(("seq", "exp"), None),
        P(("seq", "exp"), None, None),
        P(("seq", "exp"), None, None),
        P(),
        P(None, None, "exp"),
        P("seq", "exp"),
        P("seq", "exp"),
    )
    out_specs = (P(("seq", "exp"), None), P("seq", "exp"))
    return jax.shard_map(local, mesh=mesh, in_specs=in_specs, out_specs=out_specs, check_vma=False)
```

```python
from functools import partial

import jax
import jax.numpy as jnp
from jax import lax
from jax.experimental import pallas as pl
from jax.experimental.pallas import tpu as pltpu
from jax.sharding import PartitionSpec as P

CH = 128
ROUTE_STEP = 16
VMEM_LIMIT = 56 * 1024 * 1024
BF = jnp.bfloat16
F32 = jnp.float32


def rms_scale(values, gain):
    wide = values.astype(F32)
    return wide * lax.rsqrt(jnp.mean(wide * wide, axis=-1, keepdims=True) + 1e-06) * gain


def dot(a, b):
    return jnp.dot(a, b, preferred_element_type=F32)


def split(a):
    high = a.astype(BF)
    return high, (a - high.astype(F32)).astype(BF)


def rough(a, b):
    return dot(a.astype(BF), b.astype(BF))


def left_pair(a):
    high, low = split(a)
    return jnp.concatenate([high, low], axis=1)


def right_pair(b):
    high, low = split(b)
    row = jnp.concatenate([high, low], axis=1)
    return jnp.concatenate([row, row], axis=0)


def wide_product(a, b):
    columns = b.shape[1]
    both = dot(left_pair(a), right_pair(b))
    return both[:, :columns] + both[:, columns:]


def moe_kernel(capacity, choose, cuts, *refs):
    first_ref, *block_refs = refs[:5]
    weight_refs = refs[5:9]
    gate_up_ref, down_ref, rows_ref, back_ref, sem = refs[-5:]
    tok, wide = block_refs[0].shape
    width = rows_ref.shape[2]
    out_refs = refs[-5 - 4 * cuts : -5]
    piece = width // cuts
    experts_here = gate_up_ref.shape[0]
    half = experts_here // 2
    expert_width = down_ref.shape[1]
    pair_rows = rows_ref.shape[1] // 2

    copies = []
    for e in range(experts_here):
        side, at = divmod(e, half)
        fetch_in = pltpu.make_async_copy(
            weight_refs[2 * side].at[at], gate_up_ref.at[e], sem.at[0, e]
        )
        fetch_out = pltpu.make_async_copy(
            weight_refs[2 * side + 1].at[at], down_ref.at[e], sem.at[1, e]
        )
        fetch_in.start()
        fetch_out.start()
        copies.append((fetch_in, fetch_out))

    matched, weights = [], []
    for block_ref in block_refs:
        routing = block_ref[:, width:].astype(F32).T
        ids = routing[:choose]
        scale = routing[ROUTE_STEP : ROUTE_STEP + choose]
        scale = scale + routing[2 * ROUTE_STEP : 2 * ROUTE_STEP + choose]
        for e in range(experts_here):
            side, at = divmod(e, half)
            hit = ids == (first_ref[side] + at).astype(F32)
            matched.append(jnp.max(jnp.where(hit, 1.0, 0.0), axis=0, keepdims=True))
            weights.append(jnp.sum(jnp.where(hit, scale, 0.0), axis=0, keepdims=True))
    match = jnp.concatenate(matched, axis=0)
    before = lax.broadcasted_iota(jnp.int32, (tok, tok), 0) < lax.broadcasted_iota(
        jnp.int32, (tok, tok), 1
    )
    rank = dot(match.astype(BF), jnp.where(before, 1.0, 0.0).astype(BF))
    rank = jnp.where(match > 0.5, rank, -1e4)
    row_number = lax.broadcasted_iota(jnp.int32, (pair_rows, 2 * tok), 0).astype(F32)
    picks = []
    for pair in range(2):
        x_pair = jnp.concatenate(
            [block_refs[2 * pair][:, :width], block_refs[2 * pair + 1][:, :width]], axis=0
        )
        here = []
        for e in range(experts_here):
            low = 2 * pair * experts_here + e
            high = low + experts_here
            place = jnp.concatenate(
                [rank[low : low + 1], rank[high : high + 1] + float(capacity)], axis=1
            )
            here.append(jnp.where(row_number == place, 1.0, 0.0))
        picks.append(here)
        chosen = dot(jnp.concatenate(here, axis=0).astype(BF), x_pair).astype(BF)
        for e in range(experts_here):
            rows_ref[e, pair * pair_rows : (pair + 1) * pair_rows, :] = chosen[
                e * pair_rows : (e + 1) * pair_rows
            ]
    for e in range(experts_here):
        copies[e][0].wait()
        both = dot(rows_ref[e], gate_up_ref[e])
        gate = both[:, :expert_width]
        hidden = (gate / (1.0 + jnp.exp(-gate)) * both[:, expert_width:]).astype(BF)
        copies[e][1].wait()
        back_ref[e] = dot(hidden, down_ref[e]).astype(BF)
    for pair in range(2):
        scaled, rows = [], []
        for e in range(experts_here):
            low = 2 * pair * experts_here + e
            high = low + experts_here
            weight = jnp.concatenate([weights[low], weights[high]], axis=1)
            scaled.append(picks[pair][e] * weight)
            rows.append(back_ref[e, pair * pair_rows : (pair + 1) * pair_rows, :])
        summed = lax.dot_general(
            jnp.concatenate(scaled, axis=0).astype(BF),
            jnp.concatenate(rows, axis=0),
            (((0,), (0,)), ((), ())),
            preferred_element_type=F32,
        ).astype(BF)
        for cut in range(cuts):
            columns = slice(cut * piece, (cut + 1) * piece)
            out_refs[2 * pair * cuts + cut][...] = summed[:tok, columns]
            out_refs[(2 * pair + 1) * cuts + cut][...] = summed[tok:, columns]


def experts(blocks, first, weights, after, capacity, choose, cuts):
    tok, wide = blocks[0].shape
    gate_up_weight, down = weights[:2]
    local_experts, width, double = gate_up_weight.shape
    here = 2 * local_experts
    pair_rows = -(-2 * capacity // 16) * 16
    whole = pl.BlockSpec(memory_space=pltpu.VMEM)
    return pl.pallas_call(
        partial(moe_kernel, capacity, choose, cuts),
        in_specs=[pl.BlockSpec(memory_space=pltpu.SMEM)]
        + [whole] * 4
        + [pl.BlockSpec(memory_space=pl.ANY)] * (4 + len(after)),
        out_specs=[whole] * (4 * cuts),
        out_shape=[jax.ShapeDtypeStruct((tok, width // cuts), BF)] * (4 * cuts),
        scratch_shapes=[
            pltpu.VMEM((here,) + gate_up_weight.shape[1:], BF),
            pltpu.VMEM((here,) + down.shape[1:], BF),
            pltpu.VMEM((here, 2 * pair_rows, width), BF),
            pltpu.VMEM((here, 2 * pair_rows, width), BF),
            pltpu.SemaphoreType.DMA((2, here)),
        ],
        compiler_params=pltpu.CompilerParams(vmem_limit_bytes=VMEM_LIMIT),
        cost_estimate=pl.CostEstimate(
            flops=here * pair_rows * width * double // 4,
            bytes_accessed=tok * width,
            transcendentals=0,
        ),
        name="experts",
    )(first, *blocks, *weights, *after)


def unit_rows(values):
    return values * lax.rsqrt(jnp.sum(values * values, axis=-1, keepdims=True) + 1e-06)


def tiles():
    rows = lax.broadcasted_iota(jnp.int32, (CH, CH), 0)
    columns = lax.broadcasted_iota(jnp.int32, (CH, CH), 1)
    return rows, columns


def against_rows(a, b):
    high, low = split(b)
    right = jnp.concatenate(
        [jnp.concatenate([high, high], axis=1), jnp.concatenate([low, low], axis=1)], axis=0
    )
    both = lax.dot_general(
        left_pair(a), right, (((1,), (1,)), ((), ())), preferred_element_type=F32
    )
    return both[:, : b.shape[0]] + both[:, b.shape[0] :]


def chunk_kernel(place_ref, x_ref, key_w_ref, value_w_ref, sum_ref, rate_ref, *refs):
    k_ref, solved_ref, moved_ref = refs[-3:]
    heads, chunks, _ = sum_ref.shape[1:]
    dim = key_w_ref.shape[2] // heads
    rows, columns = tiles()
    strict = rows > columns
    identity = jnp.where(rows == columns, 1.0, 0.0)
    x = x_ref[...]
    key = dot(x, key_w_ref[0])
    value = dot(x, value_w_ref[0])
    units = [(h, n) for h in range(heads) for n in range(chunks)]

    def part(values, h, n):
        return values[n * CH : (n + 1) * CH, h * dim : (h + 1) * dim]

    keys, values, lowers, rates, growths, remains = [], [], [], [], [], []
    for h, n in units:
        unit = unit_rows(part(key, h, n))
        k_ref[n * CH : (n + 1) * CH, h * dim : (h + 1) * dim] = unit
        keys.append(unit)
        values.append(part(value, h, n))
    for u, (h, n) in enumerate(units):
        across = jnp.broadcast_to(sum_ref[0, h, n : n + 1, :], (CH, CH))
        along = across.T
        rate = jnp.broadcast_to(rate_ref[0, h, n : n + 1, :], (CH, CH)).T
        last = jnp.broadcast_to(along[CH - 1 : CH, :], (CH, CH))
        fade = jnp.exp(jnp.where(strict, along - across, 0.0))
        rates.append(rate)
        growths.append(jnp.exp(along))
        remains.append(jnp.exp(last - along))
        unit = keys[u].astype(BF)
        met = lax.dot_general(unit, unit, (((1,), (1,)), ((), ())), preferred_element_type=F32)
        lowers.append(jnp.where(strict, rate * fade * met, 0.0))

    def ring(size):
        shared = (rows // (2 * size)) == (columns // (2 * size))
        return shared & (rows // size % 2 == 1) & (columns // size % 2 == 0)

    span = range(len(units))
    inverse = [identity - jnp.where(ring(1), lowers[u], 0.0) for u in span]
    size = 2
    while size < CH and size < 16:
        here = ring(size)
        step = [rough(jnp.where(here, lowers[u], 0.0), inverse[u]) for u in span]
        inverse = [inverse[u] - rough(inverse[u], step[u]) for u in span]
        size *= 2
    while size < CH:
        starts = range(0, CH, 2 * size)

        def odd(values):
            return jnp.concatenate([values[s + size : s + 2 * size] for s in starts], axis=0)

        def woven(even, odds):
            rows_of = []
            for i, s in enumerate(starts):
                rows_of += [even[s : s + size], odds[i * size : (i + 1) * size]]
            return jnp.concatenate(rows_of, axis=0)

        here = odd(jnp.where(ring(size), 1.0, 0.0))
        nothing = jnp.zeros((CH, CH), F32)
        step = [woven(nothing, rough(here * odd(lowers[u]), inverse[u])) for u in span]
        inverse = [
            woven(inverse[u], odd(inverse[u]) - rough(odd(inverse[u]), step[u])) for u in span
        ]
        size *= 2
    wanted = [
        jnp.concatenate([rates[u] * growths[u] * keys[u], rates[u] * values[u]], axis=1)
        for u in span
    ]
    solved = [wanted[u] + rough(inverse[u] - identity, wanted[u]) for u in span]
    for u, (h, n) in enumerate(units):
        solved_ref[h, n] = solved[u]
        moved_ref[h, n] = lax.dot_general(
            (remains[u] * keys[u]).astype(BF),
            solved[u].astype(BF),
            (((0,), (0,)), ((), ())),
            preferred_element_type=F32,
        )


def chunks_of(x, place, qkv_weight, sums, rates, before):
    rows, width = x.shape
    _, _, columns = qkv_weight.shape
    parts, heads, chunks, _ = sums.shape
    dim = columns // heads
    step = min(4, heads)
    at_rows = pl.BlockSpec((rows, step * dim), lambda i, place: (place[0], i))
    at_chunks = pl.BlockSpec((step, chunks, CH, 2 * dim), lambda i, place: (i, place[0], 0, 0))
    per_head = pl.BlockSpec((1, step, chunks, CH), lambda i, place: (place[0], i, 0, 0))
    return pl.pallas_call(
        chunk_kernel,
        grid_spec=pltpu.PrefetchScalarGridSpec(
            num_scalar_prefetch=1,
            grid=(heads // step,),
            in_specs=[
                pl.BlockSpec((rows, width), lambda i, place: (0, 0)),
                pl.BlockSpec((1, width, step * dim), lambda i, place: (1, 0, i)),
                pl.BlockSpec((1, width, step * dim), lambda i, place: (2, 0, i)),
                per_head,
                per_head,
            ]
            + [pl.BlockSpec(memory_space=pl.ANY)] * len(before),
            out_specs=[at_rows, at_chunks, at_chunks],
        ),
        out_shape=[jax.ShapeDtypeStruct((parts * rows, columns), F32)]
        + [jax.ShapeDtypeStruct((heads, parts * chunks, CH, 2 * dim), F32)] * 2,
        input_output_aliases={6 + i: i for i in range(len(before))},
        compiler_params=pltpu.CompilerParams(vmem_limit_bytes=VMEM_LIMIT),
        name="chunks",
    )(place, x, qkv_weight, qkv_weight, sums, rates, *before)


def chain_kernel(moved_ref, sum_ref, starts_ref, end_ref):
    heads, chunks, dim, _ = moved_ref.shape
    rows, columns = tiles()
    identity = jnp.where(rows == columns, 1.0, 0.0)
    span = range(heads)

    def spread(total):
        return jnp.broadcast_to(jnp.exp(total[:, CH - 1 :]), (CH, CH))

    wholes = [[spread(sum_ref[h, n : n + 1, :]) for n in range(chunks)] for h in span]
    state = [
        jnp.concatenate(
            [wholes[h][0] * identity - moved_ref[h, 0, :, :dim], moved_ref[h, 0, :, dim:]], axis=1
        )
        for h in span
    ]
    for n in range(1, chunks):
        for h in span:
            starts_ref[h, n - 1] = state[h]
        removed = [rough(moved_ref[h, n, :, :dim], state[h]) for h in span]
        state = [
            jnp.concatenate(
                [
                    wholes[h][n] * state[h][:, :dim] - removed[h][:, :dim],
                    wholes[h][n] * state[h][:, dim:]
                    - removed[h][:, dim:]
                    + moved_ref[h, n, :, dim:],
                ],
                axis=1,
            )
            for h in span
        ]
    for h in span:
        decay = wholes[h][0]
        for n in range(1, chunks):
            decay = decay * wholes[h][n]
        end_ref[h, :dim, :dim] = (decay * identity - state[h][:, :dim]).astype(BF)
        end_ref[h, :dim, dim:] = state[h][:, dim:].astype(BF)
        end_ref[h, dim:, :] = left_pair(decay[:16])


def chain(moved, sums):
    heads, chunks, dim, double = moved.shape
    step = min(4, heads)
    return pl.pallas_call(
        chain_kernel,
        grid=(heads // step,),
        in_specs=[
            pl.BlockSpec((step, chunks, dim, double), lambda i: (i, 0, 0, 0)),
            pl.BlockSpec((step, chunks, CH), lambda i: (i, 0, 0)),
        ],
        out_specs=[
            pl.BlockSpec((step, chunks - 1, dim, double), lambda i: (i, 0, 0, 0)),
            pl.BlockSpec((step, dim + 16, double), lambda i: (i, 0, 0)),
        ],
        out_shape=[
            jax.ShapeDtypeStruct((heads, chunks - 1, dim, double), F32),
            jax.ShapeDtypeStruct((heads, dim + 16, double), BF),
        ],
        compiler_params=pltpu.CompilerParams(vmem_limit_bytes=VMEM_LIMIT),
        name="chain",
    )(moved, sums)


def read_kernel(place_ref, w_ref, k_ref, solved_ref, starts_ref, sum_ref, *refs):
    x_refs = refs[:-2]
    enter_ref, local_ref = refs[-2:]
    heads, chunks, _ = sum_ref.shape
    dim = starts_ref.shape[2]
    rows, columns = tiles()
    inclusive = rows >= columns
    found = [dot(x_ref[...], w_ref[0]) for x_ref in x_refs]
    queries = []
    for place in range(len(found)):
        query = found[0]
        for i in range(1, len(found)):
            query = jnp.where(place_ref[i] == place, found[i], query)
        queries.append(query)
    each = chunks // len(found)
    units = [(h, n) for h in range(heads) for n in range(chunks)]
    for h, n in units:
        cut = slice(n * CH, (n + 1) * CH), slice(h * dim, (h + 1) * dim)
        across = jnp.broadcast_to(sum_ref[h, n : n + 1, :], (CH, CH))
        along = across.T
        fade = jnp.exp(jnp.where(inclusive, along - across, 0.0))
        query = unit_rows(queries[n // each][n % each * CH : (n % each + 1) * CH, cut[1]])
        masked = jnp.where(inclusive, fade * against_rows(query, k_ref[cut]), 0.0)
        probed = wide_product(masked, solved_ref[h, n])
        entering = jnp.exp(along) * query - probed[:, :dim]
        output = probed[:, dim:]
        if n:
            begun = wide_product(entering, starts_ref[h, n - 1])
            entering = begun[:, :dim]
            output = output + begun[:, dim:]
        enter_ref[cut] = entering.astype(BF)
        local_ref[cut] = output


def read(parts, places, qkv_weight, key, solved, starts, sums):
    length, columns = key.shape
    heads, chunks, _ = sums.shape
    dim = columns // heads
    width = qkv_weight.shape[1]
    step = 2 if heads % 2 == 0 else 1
    per_column = pl.BlockSpec((length, step * dim), lambda h: (0, h))
    four = lambda h: (h, 0, 0, 0)
    return pl.pallas_call(
        read_kernel,
        grid=(heads // step,),
        in_specs=[
            pl.BlockSpec(memory_space=pltpu.SMEM),
            pl.BlockSpec((1, width, step * dim), lambda h: (0, 0, h)),
            per_column,
            pl.BlockSpec((step, chunks, CH, 2 * dim), four),
            pl.BlockSpec((step, chunks - 1, dim, 2 * dim), four),
            pl.BlockSpec((step, chunks, CH), lambda h: (h, 0, 0)),
        ]
        + [pl.BlockSpec(x.shape, lambda h: (0, 0)) for x in parts],
        out_specs=[per_column, per_column],
        out_shape=[
            jax.ShapeDtypeStruct((length, columns), BF),
            jax.ShapeDtypeStruct((length, columns), F32),
        ],
        compiler_params=pltpu.CompilerParams(vmem_limit_bytes=VMEM_LIMIT),
        name="read",
    )(places, qkv_weight, key, solved, starts, sums, *parts)


def carry_kernel(ends_ref, after_ref, states_ref):
    segments, _, double = ends_ref.shape
    dim = double // 2
    state = jnp.zeros((dim, dim), F32)
    for s in range(segments):
        states_ref[s] = state.astype(BF)
        if s < segments - 1:
            decay = ends_ref[s, dim : dim + 1, :].astype(F32)
            decay = decay[:, :dim] + decay[:, dim:]
            removed = dot(ends_ref[s, :dim, :dim], left_pair(state))
            removed = removed[:, :dim] + removed[:, dim:]
            state = decay * state - removed + ends_ref[s, :dim, dim:].astype(F32)


def carry(ends, after):
    segments, _, double = ends.shape
    return pl.pallas_call(
        carry_kernel,
        in_specs=[pl.BlockSpec(memory_space=pltpu.VMEM), pl.BlockSpec(memory_space=pl.ANY)],
        out_shape=jax.ShapeDtypeStruct((segments, double // 2, double // 2), BF),
        compiler_params=pltpu.CompilerParams(vmem_limit_bytes=VMEM_LIMIT),
        name="carry",
    )(ends, after)


def finish_kernel(enter_ref, local_ref, state_ref, core_ref):
    heads, dim, _ = state_ref.shape
    for h in range(heads):
        cut = slice(h * dim, (h + 1) * dim)
        core_ref[:, cut] = local_ref[:, cut] + dot(enter_ref[:, cut], state_ref[h])


def finish(entering, local_out, states):
    length, columns = entering.shape
    heads, dim, _ = states.shape
    step = 2 if heads % 2 == 0 else 1
    per_column = pl.BlockSpec((length, step * dim), lambda h: (0, h))
    return pl.pallas_call(
        finish_kernel,
        grid=(heads // step,),
        in_specs=[per_column, per_column, pl.BlockSpec((step, dim, dim), lambda h: (h, 0, 0))],
        out_specs=per_column,
        out_shape=jax.ShapeDtypeStruct((length, columns), F32),
        compiler_params=pltpu.CompilerParams(vmem_limit_bytes=VMEM_LIMIT),
        name="finish",
    )(entering, local_out, states)


def relay(ends, seq_count):
    dim = ends.shape[2] // 2
    pairs = [(i, i + 1) for i in range(seq_count - 1)]
    removed, written = ends[:, :dim, :dim].astype(F32), ends[:, :dim, dim:].astype(F32)
    decay = ends[:, dim, :1].astype(F32) + ends[:, dim, dim : dim + 1].astype(F32)

    def step(_, incoming):
        outgoing = decay[:, :, None] * incoming + written
        outgoing = outgoing - jnp.einsum(
            "hij,hjk->hik", removed, incoming, precision=lax.Precision.HIGHEST
        )
        return lax.ppermute(outgoing, "seq", pairs)

    return lax.fori_loop(0, seq_count - 1, step, jnp.zeros_like(written)).astype(BF)


def move(values, change):
    exp_count = lax.axis_size("exp")
    pairs = []
    for s in range(lax.axis_size("seq")):
        for e in range(exp_count):
            to_s, to_e = change(s, e)
            pairs.append((s * exp_count + e, to_s * exp_count + to_e))
    return lax.ppermute(values, ("seq", "exp"), pairs)


def over_x(values):
    return move(values, lambda s, e: (s ^ 1, e))


def over_y(values):
    return move(values, lambda s, e: (s, e ^ 2))


def over_core(values):
    return move(values, lambda s, e: (s, e ^ 1))


def along_z(values, by):
    count = lax.axis_size("seq")
    return move(values, lambda s, e: ((s + 2 * by) % count, e))


def added(*terms):
    total = terms[0].astype(F32)
    for term in terms[1:]:
        total = total + term.astype(F32)
    return total


def route_waves(normed, expert_ids, expert_weights, gate_up_weight, down, capacity):
    tok_rows, width = normed.shape
    choose = expert_ids.shape[1]
    local_experts = gate_up_weight.shape[0]
    me = lax.axis_index("seq") * lax.axis_size("exp") + lax.axis_index("exp")
    first = (jnp.stack([me, me ^ 1]) * local_experts).astype(jnp.int32)
    gap = jnp.zeros((tok_rows, ROUTE_STEP - choose), BF)
    high, low = split(expert_weights)
    tail = jnp.zeros((tok_rows, 128 - 3 * ROUTE_STEP), BF)
    block = jnp.concatenate(
        [normed, expert_ids.astype(BF), gap, high, gap, low, gap, tail], axis=1
    )
    weights = (gate_up_weight, down, over_core(gate_up_weight), over_core(down))
    count = lax.axis_size("seq") // 2
    order = list(range(1, count)) + [0]
    first_way = [over_y if wave == 1 else over_x for wave in range(count)]
    second_way = [over_x if wave == 1 else over_y for wave in range(count)]
    block = [block]
    for wave in range(1, count):
        block.append(along_z(block[-1], 1))
    by_one = [first_way[wave](block[wave]) for wave in range(count)]
    by_two = [second_way[wave](block[wave]) for wave in range(count)]
    diagonal = {wave: second_way[wave](by_one[wave]) for wave in (0, 1)}
    for wave in range(2, count):
        diagonal[wave] = along_z(diagonal[wave - 1], 1)
    due = [() for _ in range(count + 3)]
    for call, wave in enumerate(order):
        if call and wave:
            due[call - 1] += (block[wave],)
        if call > 1:
            due[call - 1 if wave else 0] += (by_one[wave], by_two[wave])
    running = sum_below = None
    for call, wave in enumerate(order):
        cuts = 1
        found = experts(
            (block[wave], by_one[wave], by_two[wave], diagonal[wave]),
            first,
            weights,
            due[call],
            capacity,
            choose,
            cuts,
        )
        one, two = first_way[wave], second_way[wave]
        if wave == 0:
            one, two = two, one
        due[call + 1] += (found[0],)
        below = None if sum_below is None else jnp.split(sum_below, cuts, axis=1)
        sum_below = None
        if running is not None and len(running) < cuts:
            running = jnp.split(running[0], cuts, axis=1)
        pieces = []
        for cut in range(cuts):
            own, sum_one, sum_two, sum_both = found[cut::cuts]
            if wave == 0:
                sum_one, sum_two = sum_two, sum_one
            if below is not None:
                sum_both = added(sum_both, below[cut]).astype(BF)
            if 0 < wave < count - 1:
                sum_below = along_z(sum_both, 1)
                due[call + 2] += (sum_below,)
            else:
                sum_one = added(sum_one, two(sum_both)).astype(BF)
            from_two = two(sum_two)
            from_one = one(sum_one)
            due[call + 2] += (from_two, from_one)
            if pieces:
                from_one, _ = lax.optimization_barrier((from_one, pieces[-1]))
            here = added(own, from_two, from_one)
            if running is not None:
                here = added(here, running[cut])
            pieces.append(here.astype(BF) if wave else here)
        if wave:
            running = [along_z(piece, 1) for piece in pieces]
    return jnp.concatenate(pieces, axis=1)


def route_some(normed, expert_ids, expert_weights, gate_up_weight, down, capacity):
    axes = ("seq", "exp")
    tok_rows, width = normed.shape
    choose = expert_ids.shape[1]
    local_experts = gate_up_weight.shape[0]
    expert_width = down.shape[1]
    devices = lax.axis_size("seq") * lax.axis_size("exp")
    experts_all = local_experts * devices
    flat_ids = expert_ids.reshape(-1)
    onehot = (flat_ids[:, None] == jnp.arange(experts_all, dtype=jnp.int32)[None, :]).astype(
        jnp.int32
    )
    rank = jnp.sum(jnp.cumsum(onehot, axis=0) * onehot, axis=1) - 1
    slot = flat_ids * capacity + rank
    token_of = jnp.arange(tok_rows * choose, dtype=jnp.int32) // choose
    send = jnp.zeros((experts_all * capacity, width), BF).at[slot].set(normed[token_of])
    both = jnp.einsum(
        "secd,edf->secf",
        lax.all_to_all(
            send.reshape(devices, local_experts, capacity, width),
            axes,
            split_axis=0,
            concat_axis=0,
            tiled=True,
        ),
        gate_up_weight,
        preferred_element_type=F32,
    )
    hidden = (jax.nn.silu(both[..., :expert_width]) * both[..., expert_width:]).astype(BF)
    back = lax.all_to_all(
        jnp.einsum("secf,efd->secd", hidden, down, preferred_element_type=F32).astype(BF),
        axes,
        split_axis=0,
        concat_axis=0,
        tiled=True,
    )
    back_rows = back.reshape(experts_all * capacity, width)[slot].astype(F32)
    return jnp.sum(
        back_rows.reshape(tok_rows, choose, width) * expert_weights[:, :, None], axis=1
    )


def local(
    stream,
    moe_gain,
    expert_ids,
    expert_weights,
    gate_up_weight,
    down,
    mixer_gain,
    qkv_weight,
    decay_log,
    write_rate,
):
    tok_rows, width = stream.shape
    choose = expert_ids.shape[1]
    seq_count = lax.axis_size("seq")
    devices = seq_count * lax.axis_size("exp")
    experts_all = gate_up_weight.shape[0] * devices
    capacity = max(2, (tok_rows * choose * 6 + experts_all * 5 - 1) // (experts_all * 5))
    normed = rms_scale(stream, moe_gain).astype(BF)
    planes = lax.axis_size("exp") == 4 and seq_count % 4 == 0 and choose <= ROUTE_STEP
    route = route_waves if planes and experts_all <= 256 else route_some
    moe = route(normed, expert_ids, expert_weights, gate_up_weight, down, capacity)
    mixed = (stream.astype(F32) + moe).astype(BF)
    normed_mix = rms_scale(mixed, mixer_gain).astype(BF)
    heads = decay_log.shape[1]
    blocks = decay_log.shape[0] // CH
    sums = jnp.cumsum(decay_log.T.reshape(heads, blocks, CH), axis=-1)
    rates = write_rate.T.reshape(heads, blocks, CH)
    pairs = blocks // 2
    by_pair = lambda values: values.reshape(heads, pairs, 2, CH).transpose(1, 0, 2, 3)
    if planes:
        core = lax.axis_index("exp") % 2
        side = lax.axis_index("exp") // 2
        from_y = over_y(normed_mix)
        both_sides = [(normed_mix, over_core(normed_mix)), (from_y, over_core(from_y))]
        parts = [
            (
                jnp.concatenate([jnp.where(core == 0, a, b), jnp.where(core == 0, b, a)], axis=0),
                place,
            )
            for (a, b), place in zip(both_sides, (side, 1 - side))
        ]
    else:
        gathered = lax.all_gather(normed_mix, "exp", axis=0, tiled=True)
        parts = [(gathered[2 * CH * i : 2 * CH * (i + 1)], jnp.int32(i)) for i in range(pairs)]
    found = ()
    for x, place in parts:
        found = chunks_of(
            x,
            place.astype(jnp.int32).reshape(1),
            qkv_weight,
            by_pair(sums),
            by_pair(rates),
            found,
        )
    key, solved, moved = found
    starts, ends = chain(moved, sums)
    places = jnp.stack([place for _, place in parts]).astype(jnp.int32)
    entering, local_out = read([x for x, _ in parts], places, qkv_weight, key, solved, starts, sums)
    if heads % seq_count == 0:
        dim = ends.shape[2] // 2
        each = heads // seq_count
        held = lax.all_to_all(ends, "seq", split_axis=0, concat_axis=0, tiled=True)
        held = held.reshape(seq_count, each, dim + 16, 2 * dim)
        states = jnp.stack([carry(held[:, i], entering) for i in range(each)], axis=1)
        arriving = lax.all_to_all(
            states.reshape(seq_count * each, dim, dim), "seq", split_axis=0, concat_axis=0, tiled=True
        )
    else:
        arriving = relay(ends, seq_count)
    return (mixed, finish(entering, local_out, arriving))


def solution(mesh):
    in_specs = (
        P(("seq", "exp"), None),
        P(),
        P(("seq", "exp"), None),
        P(("seq", "exp"), None),
        P(("seq", "exp"), None, None),
        P(("seq", "exp"), None, None),
        P(),
        P(None, None, "exp"),
        P("seq", "exp"),
        P("seq", "exp"),
    )
    out_specs = (P(("seq", "exp"), None), P("seq", "exp"))
    return jax.shard_map(local, mesh=mesh, in_specs=in_specs, out_specs=out_specs, check_vma=False)
```

```python
from functools import partial

import jax
import jax.numpy as jnp
from jax import lax
from jax.experimental import pallas as pl
from jax.experimental.pallas import tpu as pltpu
from jax.sharding import PartitionSpec as P

CH = 128
ROUTE_STEP = 16
VMEM_LIMIT = 56 * 1024 * 1024
BF = jnp.bfloat16
F32 = jnp.float32


def rms_scale(values, gain):
    wide = values.astype(F32)
    return wide * lax.rsqrt(jnp.mean(wide * wide, axis=-1, keepdims=True) + 1e-06) * gain


def dot(a, b):
    return jnp.dot(a, b, preferred_element_type=F32)


def split(a):
    high = a.astype(BF)
    return high, (a - high.astype(F32)).astype(BF)


def rough(a, b):
    return dot(a.astype(BF), b.astype(BF))


def left_pair(a):
    high, low = split(a)
    return jnp.concatenate([high, low], axis=1)


def right_pair(b):
    high, low = split(b)
    row = jnp.concatenate([high, low], axis=1)
    return jnp.concatenate([row, row], axis=0)


def wide_product(a, b):
    columns = b.shape[1]
    both = dot(left_pair(a), right_pair(b))
    return both[:, :columns] + both[:, columns:]


def moe_kernel(capacity, choose, cuts, *refs):
    first_ref, *block_refs = refs[:5]
    weight_refs = refs[5:9]
    gate_up_ref, down_ref, rows_ref, back_ref, sem = refs[-5:]
    tok, wide = block_refs[0].shape
    width = rows_ref.shape[2]
    out_refs = refs[-5 - 4 * cuts : -5]
    piece = width // cuts
    experts_here = gate_up_ref.shape[0]
    half = experts_here // 2
    expert_width = down_ref.shape[1]
    pair_rows = rows_ref.shape[1] // 2

    copies = []
    for e in range(experts_here):
        side, at = divmod(e, half)
        fetch_in = pltpu.make_async_copy(
            weight_refs[2 * side].at[at], gate_up_ref.at[e], sem.at[0, e]
        )
        fetch_out = pltpu.make_async_copy(
            weight_refs[2 * side + 1].at[at], down_ref.at[e], sem.at[1, e]
        )
        fetch_in.start()
        fetch_out.start()
        copies.append((fetch_in, fetch_out))

    matched, weights = [], []
    for block_ref in block_refs:
        routing = block_ref[:, width:].astype(F32).T
        ids = routing[:choose]
        scale = routing[ROUTE_STEP : ROUTE_STEP + choose]
        scale = scale + routing[2 * ROUTE_STEP : 2 * ROUTE_STEP + choose]
        for e in range(experts_here):
            side, at = divmod(e, half)
            hit = ids == (first_ref[side] + at).astype(F32)
            matched.append(jnp.max(jnp.where(hit, 1.0, 0.0), axis=0, keepdims=True))
            weights.append(jnp.sum(jnp.where(hit, scale, 0.0), axis=0, keepdims=True))
    match = jnp.concatenate(matched, axis=0)
    before = lax.broadcasted_iota(jnp.int32, (tok, tok), 0) < lax.broadcasted_iota(
        jnp.int32, (tok, tok), 1
    )
    rank = dot(match.astype(BF), jnp.where(before, 1.0, 0.0).astype(BF))
    rank = jnp.where(match > 0.5, rank, -1e4)
    row_number = lax.broadcasted_iota(jnp.int32, (pair_rows, 2 * tok), 0).astype(F32)
    picks = []
    for pair in range(2):
        x_pair = jnp.concatenate(
            [block_refs[2 * pair][:, :width], block_refs[2 * pair + 1][:, :width]], axis=0
        )
        here = []
        for e in range(experts_here):
            low = 2 * pair * experts_here + e
            high = low + experts_here
            place = jnp.concatenate(
                [rank[low : low + 1], rank[high : high + 1] + float(capacity)], axis=1
            )
            here.append(jnp.where(row_number == place, 1.0, 0.0))
        picks.append(here)
        chosen = dot(jnp.concatenate(here, axis=0).astype(BF), x_pair).astype(BF)
        for e in range(experts_here):
            rows_ref[e, pair * pair_rows : (pair + 1) * pair_rows, :] = chosen[
                e * pair_rows : (e + 1) * pair_rows
            ]
    for e in range(experts_here):
        copies[e][0].wait()
        both = dot(rows_ref[e], gate_up_ref[e])
        gate = both[:, :expert_width]
        hidden = (gate / (1.0 + jnp.exp(-gate)) * both[:, expert_width:]).astype(BF)
        copies[e][1].wait()
        back_ref[e] = dot(hidden, down_ref[e]).astype(BF)
    for pair in range(2):
        scaled, rows = [], []
        for e in range(experts_here):
            low = 2 * pair * experts_here + e
            high = low + experts_here
            weight = jnp.concatenate([weights[low], weights[high]], axis=1)
            scaled.append(picks[pair][e] * weight)
            rows.append(back_ref[e, pair * pair_rows : (pair + 1) * pair_rows, :])
        summed = lax.dot_general(
            jnp.concatenate(scaled, axis=0).astype(BF),
            jnp.concatenate(rows, axis=0),
            (((0,), (0,)), ((), ())),
            preferred_element_type=F32,
        ).astype(BF)
        for cut in range(cuts):
            columns = slice(cut * piece, (cut + 1) * piece)
            out_refs[2 * pair * cuts + cut][...] = summed[:tok, columns]
            out_refs[(2 * pair + 1) * cuts + cut][...] = summed[tok:, columns]


def experts(blocks, first, weights, after, capacity, choose, cuts):
    tok, wide = blocks[0].shape
    gate_up_weight, down = weights[:2]
    local_experts, width, double = gate_up_weight.shape
    here = 2 * local_experts
    pair_rows = -(-2 * capacity // 16) * 16
    whole = pl.BlockSpec(memory_space=pltpu.VMEM)
    return pl.pallas_call(
        partial(moe_kernel, capacity, choose, cuts),
        in_specs=[pl.BlockSpec(memory_space=pltpu.SMEM)]
        + [whole] * 4
        + [pl.BlockSpec(memory_space=pl.ANY)] * (4 + len(after)),
        out_specs=[whole] * (4 * cuts),
        out_shape=[jax.ShapeDtypeStruct((tok, width // cuts), BF)] * (4 * cuts),
        scratch_shapes=[
            pltpu.VMEM((here,) + gate_up_weight.shape[1:], BF),
            pltpu.VMEM((here,) + down.shape[1:], BF),
            pltpu.VMEM((here, 2 * pair_rows, width), BF),
            pltpu.VMEM((here, 2 * pair_rows, width), BF),
            pltpu.SemaphoreType.DMA((2, here)),
        ],
        compiler_params=pltpu.CompilerParams(vmem_limit_bytes=VMEM_LIMIT),
        cost_estimate=pl.CostEstimate(
            flops=here * pair_rows * width * double // 4,
            bytes_accessed=tok * width,
            transcendentals=0,
        ),
        name="experts",
    )(first, *blocks, *weights, *after)


def unit_rows(values):
    return values * lax.rsqrt(jnp.sum(values * values, axis=-1, keepdims=True) + 1e-06)


def tiles():
    rows = lax.broadcasted_iota(jnp.int32, (CH, CH), 0)
    columns = lax.broadcasted_iota(jnp.int32, (CH, CH), 1)
    return rows, columns


def against_rows(a, b):
    high, low = split(b)
    right = jnp.concatenate(
        [jnp.concatenate([high, high], axis=1), jnp.concatenate([low, low], axis=1)], axis=0
    )
    both = lax.dot_general(
        left_pair(a), right, (((1,), (1,)), ((), ())), preferred_element_type=F32
    )
    return both[:, : b.shape[0]] + both[:, b.shape[0] :]


def chunk_kernel(place_ref, x_ref, key_w_ref, value_w_ref, sum_ref, rate_ref, *refs):
    k_ref, solved_ref, moved_ref = refs[-3:]
    heads, chunks, _ = sum_ref.shape[1:]
    dim = key_w_ref.shape[2] // heads
    rows, columns = tiles()
    strict = rows > columns
    identity = jnp.where(rows == columns, 1.0, 0.0)
    x = x_ref[...]
    key = dot(x, key_w_ref[0])
    value = dot(x, value_w_ref[0])
    units = [(h, n) for h in range(heads) for n in range(chunks)]

    def part(values, h, n):
        return values[n * CH : (n + 1) * CH, h * dim : (h + 1) * dim]

    keys, values, lowers, rates, growths, remains = [], [], [], [], [], []
    for h, n in units:
        unit = unit_rows(part(key, h, n))
        k_ref[n * CH : (n + 1) * CH, h * dim : (h + 1) * dim] = unit
        keys.append(unit)
        values.append(part(value, h, n))
    for u, (h, n) in enumerate(units):
        across = jnp.broadcast_to(sum_ref[0, h, n : n + 1, :], (CH, CH))
        along = across.T
        rate = jnp.broadcast_to(rate_ref[0, h, n : n + 1, :], (CH, CH)).T
        last = jnp.broadcast_to(along[CH - 1 : CH, :], (CH, CH))
        fade = jnp.exp(jnp.where(strict, along - across, 0.0))
        rates.append(rate)
        growths.append(jnp.exp(along))
        remains.append(jnp.exp(last - along))
        unit = keys[u].astype(BF)
        met = lax.dot_general(unit, unit, (((1,), (1,)), ((), ())), preferred_element_type=F32)
        lowers.append(jnp.where(strict, rate * fade * met, 0.0))

    def ring(size):
        shared = (rows // (2 * size)) == (columns // (2 * size))
        return shared & (rows // size % 2 == 1) & (columns // size % 2 == 0)

    span = range(len(units))
    inverse = [identity - jnp.where(ring(1), lowers[u], 0.0) for u in span]
    size = 2
    while size < CH and size < 16:
        here = ring(size)
        step = [rough(jnp.where(here, lowers[u], 0.0), inverse[u]) for u in span]
        inverse = [inverse[u] - rough(inverse[u], step[u]) for u in span]
        size *= 2
    while size < CH:
        starts = range(0, CH, 2 * size)

        def odd(values):
            return jnp.concatenate([values[s + size : s + 2 * size] for s in starts], axis=0)

        def woven(even, odds):
            rows_of = []
            for i, s in enumerate(starts):
                rows_of += [even[s : s + size], odds[i * size : (i + 1) * size]]
            return jnp.concatenate(rows_of, axis=0)

        here = odd(jnp.where(ring(size), 1.0, 0.0))
        nothing = jnp.zeros((CH, CH), F32)
        step = [woven(nothing, rough(here * odd(lowers[u]), inverse[u])) for u in span]
        inverse = [
            woven(inverse[u], odd(inverse[u]) - rough(odd(inverse[u]), step[u])) for u in span
        ]
        size *= 2
    wanted = [
        jnp.concatenate([rates[u] * growths[u] * keys[u], rates[u] * values[u]], axis=1)
        for u in span
    ]
    solved = [wanted[u] + rough(inverse[u] - identity, wanted[u]) for u in span]
    for u, (h, n) in enumerate(units):
        solved_ref[h, n] = solved[u]
        moved_ref[h, n] = lax.dot_general(
            (remains[u] * keys[u]).astype(BF),
            solved[u].astype(BF),
            (((0,), (0,)), ((), ())),
            preferred_element_type=F32,
        )


def head_step(heads):
    return min(4, heads)


def chunks_of(x, place, qkv_weight, sums, rates, before, steps):
    start = steps[0]
    rows, width = x.shape
    _, _, columns = qkv_weight.shape
    parts, heads, chunks, _ = sums.shape
    dim = columns // heads
    step = head_step(heads)
    at_rows = pl.BlockSpec((rows, step * dim), lambda i, place: (place[0], i + start))
    at_chunks = pl.BlockSpec(
        (step, chunks, CH, 2 * dim), lambda i, place: (i + start, place[0], 0, 0)
    )
    per_head = pl.BlockSpec((1, step, chunks, CH), lambda i, place: (place[0], i + start, 0, 0))
    return pl.pallas_call(
        chunk_kernel,
        grid_spec=pltpu.PrefetchScalarGridSpec(
            num_scalar_prefetch=1,
            grid=(len(steps),),
            in_specs=[
                pl.BlockSpec((rows, width), lambda i, place: (0, 0)),
                pl.BlockSpec((1, width, step * dim), lambda i, place: (1, 0, i + start)),
                pl.BlockSpec((1, width, step * dim), lambda i, place: (2, 0, i + start)),
                per_head,
                per_head,
            ]
            + [pl.BlockSpec(memory_space=pl.ANY)] * len(before),
            out_specs=[at_rows, at_chunks, at_chunks],
        ),
        out_shape=[jax.ShapeDtypeStruct((parts * rows, columns), F32)]
        + [jax.ShapeDtypeStruct((heads, parts * chunks, CH, 2 * dim), F32)] * 2,
        input_output_aliases={6 + i: i for i in range(len(before))},
        compiler_params=pltpu.CompilerParams(vmem_limit_bytes=VMEM_LIMIT),
        name="chunks",
    )(place, x, qkv_weight, qkv_weight, sums, rates, *before)


def chain_kernel(moved_ref, sum_ref, starts_ref, end_ref):
    heads, chunks, dim, _ = moved_ref.shape
    rows, columns = tiles()
    identity = jnp.where(rows == columns, 1.0, 0.0)
    span = range(heads)

    def spread(total):
        return jnp.broadcast_to(jnp.exp(total[:, CH - 1 :]), (CH, CH))

    wholes = [[spread(sum_ref[h, n : n + 1, :]) for n in range(chunks)] for h in span]
    state = [
        jnp.concatenate(
            [wholes[h][0] * identity - moved_ref[h, 0, :, :dim], moved_ref[h, 0, :, dim:]], axis=1
        )
        for h in span
    ]
    for n in range(1, chunks):
        for h in span:
            starts_ref[h, n - 1] = state[h]
        removed = [rough(moved_ref[h, n, :, :dim], state[h]) for h in span]
        state = [
            jnp.concatenate(
                [
                    wholes[h][n] * state[h][:, :dim] - removed[h][:, :dim],
                    wholes[h][n] * state[h][:, dim:]
                    - removed[h][:, dim:]
                    + moved_ref[h, n, :, dim:],
                ],
                axis=1,
            )
            for h in span
        ]
    for h in span:
        decay = wholes[h][0]
        for n in range(1, chunks):
            decay = decay * wholes[h][n]
        end_ref[h, :dim, :dim] = (decay * identity - state[h][:, :dim]).astype(BF)
        end_ref[h, :dim, dim:] = state[h][:, dim:].astype(BF)
        end_ref[h, dim:, :] = left_pair(decay[:16])


def chain(moved, sums):
    heads, chunks, dim, double = moved.shape
    step = min(4, heads)
    return pl.pallas_call(
        chain_kernel,
        grid=(heads // step,),
        in_specs=[
            pl.BlockSpec((step, chunks, dim, double), lambda i: (i, 0, 0, 0)),
            pl.BlockSpec((step, chunks, CH), lambda i: (i, 0, 0)),
        ],
        out_specs=[
            pl.BlockSpec((step, chunks - 1, dim, double), lambda i: (i, 0, 0, 0)),
            pl.BlockSpec((step, dim + 16, double), lambda i: (i, 0, 0)),
        ],
        out_shape=[
            jax.ShapeDtypeStruct((heads, chunks - 1, dim, double), F32),
            jax.ShapeDtypeStruct((heads, dim + 16, double), BF),
        ],
        compiler_params=pltpu.CompilerParams(vmem_limit_bytes=VMEM_LIMIT),
        name="chain",
    )(moved, sums)


def read_kernel(place_ref, w_ref, k_ref, solved_ref, starts_ref, sum_ref, *refs):
    x_refs = refs[:-2]
    enter_ref, local_ref = refs[-2:]
    heads, chunks, _ = sum_ref.shape
    dim = starts_ref.shape[2]
    rows, columns = tiles()
    inclusive = rows >= columns
    found = [dot(x_ref[...], w_ref[0]) for x_ref in x_refs]
    queries = []
    for place in range(len(found)):
        query = found[0]
        for i in range(1, len(found)):
            query = jnp.where(place_ref[i] == place, found[i], query)
        queries.append(query)
    each = chunks // len(found)
    units = [(h, n) for h in range(heads) for n in range(chunks)]
    for h, n in units:
        cut = slice(n * CH, (n + 1) * CH), slice(h * dim, (h + 1) * dim)
        across = jnp.broadcast_to(sum_ref[h, n : n + 1, :], (CH, CH))
        along = across.T
        fade = jnp.exp(jnp.where(inclusive, along - across, 0.0))
        query = unit_rows(queries[n // each][n % each * CH : (n % each + 1) * CH, cut[1]])
        masked = jnp.where(inclusive, fade * against_rows(query, k_ref[cut]), 0.0)
        probed = wide_product(masked, solved_ref[h, n])
        entering = jnp.exp(along) * query - probed[:, :dim]
        output = probed[:, dim:]
        if n:
            begun = wide_product(entering, starts_ref[h, n - 1])
            entering = begun[:, :dim]
            output = output + begun[:, dim:]
        enter_ref[cut] = entering.astype(BF)
        local_ref[cut] = output


def read(parts, places, qkv_weight, key, solved, starts, sums):
    length, columns = key.shape
    heads, chunks, _ = sums.shape
    dim = columns // heads
    width = qkv_weight.shape[1]
    step = 2 if heads % 2 == 0 else 1
    per_column = pl.BlockSpec((length, step * dim), lambda h: (0, h))
    four = lambda h: (h, 0, 0, 0)
    return pl.pallas_call(
        read_kernel,
        grid=(heads // step,),
        in_specs=[
            pl.BlockSpec(memory_space=pltpu.SMEM),
            pl.BlockSpec((1, width, step * dim), lambda h: (0, 0, h)),
            per_column,
            pl.BlockSpec((step, chunks, CH, 2 * dim), four),
            pl.BlockSpec((step, chunks - 1, dim, 2 * dim), four),
            pl.BlockSpec((step, chunks, CH), lambda h: (h, 0, 0)),
        ]
        + [pl.BlockSpec(x.shape, lambda h: (0, 0)) for x in parts],
        out_specs=[per_column, per_column],
        out_shape=[
            jax.ShapeDtypeStruct((length, columns), BF),
            jax.ShapeDtypeStruct((length, columns), F32),
        ],
        compiler_params=pltpu.CompilerParams(vmem_limit_bytes=VMEM_LIMIT),
        name="read",
    )(places, qkv_weight, key, solved, starts, sums, *parts)


def carry_kernel(ends_ref, after_ref, states_ref):
    segments, _, double = ends_ref.shape
    dim = double // 2
    state = jnp.zeros((dim, dim), F32)
    for s in range(segments):
        states_ref[s] = state.astype(BF)
        if s < segments - 1:
            decay = ends_ref[s, dim : dim + 1, :].astype(F32)
            decay = decay[:, :dim] + decay[:, dim:]
            removed = dot(ends_ref[s, :dim, :dim], left_pair(state))
            removed = removed[:, :dim] + removed[:, dim:]
            state = decay * state - removed + ends_ref[s, :dim, dim:].astype(F32)


def carry(ends, after):
    segments, _, double = ends.shape
    return pl.pallas_call(
        carry_kernel,
        in_specs=[pl.BlockSpec(memory_space=pltpu.VMEM), pl.BlockSpec(memory_space=pl.ANY)],
        out_shape=jax.ShapeDtypeStruct((segments, double // 2, double // 2), BF),
        compiler_params=pltpu.CompilerParams(vmem_limit_bytes=VMEM_LIMIT),
        name="carry",
    )(ends, after)


def finish_kernel(enter_ref, local_ref, state_ref, core_ref):
    heads, dim, _ = state_ref.shape
    for h in range(heads):
        cut = slice(h * dim, (h + 1) * dim)
        core_ref[:, cut] = local_ref[:, cut] + dot(enter_ref[:, cut], state_ref[h])


def finish(entering, local_out, states):
    length, columns = entering.shape
    heads, dim, _ = states.shape
    step = 2 if heads % 2 == 0 else 1
    per_column = pl.BlockSpec((length, step * dim), lambda h: (0, h))
    return pl.pallas_call(
        finish_kernel,
        grid=(heads // step,),
        in_specs=[per_column, per_column, pl.BlockSpec((step, dim, dim), lambda h: (h, 0, 0))],
        out_specs=per_column,
        out_shape=jax.ShapeDtypeStruct((length, columns), F32),
        compiler_params=pltpu.CompilerParams(vmem_limit_bytes=VMEM_LIMIT),
        name="finish",
    )(entering, local_out, states)


def relay(ends, seq_count):
    dim = ends.shape[2] // 2
    pairs = [(i, i + 1) for i in range(seq_count - 1)]
    removed, written = ends[:, :dim, :dim].astype(F32), ends[:, :dim, dim:].astype(F32)
    decay = ends[:, dim, :1].astype(F32) + ends[:, dim, dim : dim + 1].astype(F32)

    def step(_, incoming):
        outgoing = decay[:, :, None] * incoming + written
        outgoing = outgoing - jnp.einsum(
            "hij,hjk->hik", removed, incoming, precision=lax.Precision.HIGHEST
        )
        return lax.ppermute(outgoing, "seq", pairs)

    return lax.fori_loop(0, seq_count - 1, step, jnp.zeros_like(written)).astype(BF)


def move(values, change):
    exp_count = lax.axis_size("exp")
    pairs = []
    for s in range(lax.axis_size("seq")):
        for e in range(exp_count):
            to_s, to_e = change(s, e)
            pairs.append((s * exp_count + e, to_s * exp_count + to_e))
    return lax.ppermute(values, ("seq", "exp"), pairs)


def over_x(values):
    return move(values, lambda s, e: (s ^ 1, e))


def over_y(values):
    return move(values, lambda s, e: (s, e ^ 2))


def over_core(values):
    return move(values, lambda s, e: (s, e ^ 1))


def along_z(values, by):
    count = lax.axis_size("seq")
    return move(values, lambda s, e: ((s + 2 * by) % count, e))


def added(*terms):
    total = terms[0].astype(F32)
    for term in terms[1:]:
        total = total + term.astype(F32)
    return total


def route_waves(normed, expert_ids, expert_weights, gate_up_weight, down, capacity):
    tok_rows, width = normed.shape
    choose = expert_ids.shape[1]
    local_experts = gate_up_weight.shape[0]
    me = lax.axis_index("seq") * lax.axis_size("exp") + lax.axis_index("exp")
    first = (jnp.stack([me, me ^ 1]) * local_experts).astype(jnp.int32)
    gap = jnp.zeros((tok_rows, ROUTE_STEP - choose), BF)
    high, low = split(expert_weights)
    tail = jnp.zeros((tok_rows, 128 - 3 * ROUTE_STEP), BF)
    block = jnp.concatenate(
        [normed, expert_ids.astype(BF), gap, high, gap, low, gap, tail], axis=1
    )
    weights = (gate_up_weight, down, over_core(gate_up_weight), over_core(down))
    count = lax.axis_size("seq") // 2
    order = list(range(1, count)) + [0]
    first_way = [over_y if wave == 1 else over_x for wave in range(count)]
    second_way = [over_x if wave == 1 else over_y for wave in range(count)]
    block = [block]
    for wave in range(1, count):
        block.append(along_z(block[-1], 1))
    by_one = [first_way[wave](block[wave]) for wave in range(count)]
    by_two = [second_way[wave](block[wave]) for wave in range(count)]
    diagonal = {wave: second_way[wave](by_one[wave]) for wave in (0, 1)}
    for wave in range(2, count):
        diagonal[wave] = along_z(diagonal[wave - 1], 1)
    due = [() for _ in range(count + 3)]
    for call, wave in enumerate(order):
        if call and wave:
            due[call - 1] += (block[wave],)
        if call > 1:
            due[call - 1 if wave else 0] += (by_one[wave], by_two[wave])
    running = sum_below = None
    for call, wave in enumerate(order):
        own, sum_one, sum_two, sum_both = experts(
            (block[wave], by_one[wave], by_two[wave], diagonal[wave]),
            first,
            weights,
            due[call],
            capacity,
            choose,
            1,
        )
        one, two = first_way[wave], second_way[wave]
        due[call + 1] += (own,)
        if sum_below is not None:
            sum_both = added(sum_both, sum_below).astype(BF)
            sum_below = None
        if wave == 0:
            near = move(sum_both, lambda s, e: (s ^ 1, e ^ 2))
        elif wave == count - 1:
            far = move(sum_both, lambda s, e: (((s ^ 1) + 2) % (2 * count), e ^ 2))
        else:
            sum_below = along_z(sum_both, 1)
            due[call + 2] += (sum_below,)
        from_two = two(sum_two)
        from_one = one(sum_one)
        due[call + 2] += (from_two, from_one)
        here = added(own, from_two, from_one)
        if running is not None and wave:
            here = added(here, running)
        if wave:
            running = here.astype(BF)
            if wave == count - 1:
                running, far = lax.optimization_barrier((running, far))
            running = along_z(running, 1)
    return added(here, near, far, running)


def route_some(normed, expert_ids, expert_weights, gate_up_weight, down, capacity):
    axes = ("seq", "exp")
    tok_rows, width = normed.shape
    choose = expert_ids.shape[1]
    local_experts = gate_up_weight.shape[0]
    expert_width = down.shape[1]
    devices = lax.axis_size("seq") * lax.axis_size("exp")
    experts_all = local_experts * devices
    flat_ids = expert_ids.reshape(-1)
    onehot = (flat_ids[:, None] == jnp.arange(experts_all, dtype=jnp.int32)[None, :]).astype(
        jnp.int32
    )
    rank = jnp.sum(jnp.cumsum(onehot, axis=0) * onehot, axis=1) - 1
    slot = flat_ids * capacity + rank
    token_of = jnp.arange(tok_rows * choose, dtype=jnp.int32) // choose
    send = jnp.zeros((experts_all * capacity, width), BF).at[slot].set(normed[token_of])
    both = jnp.einsum(
        "secd,edf->secf",
        lax.all_to_all(
            send.reshape(devices, local_experts, capacity, width),
            axes,
            split_axis=0,
            concat_axis=0,
            tiled=True,
        ),
        gate_up_weight,
        preferred_element_type=F32,
    )
    hidden = (jax.nn.silu(both[..., :expert_width]) * both[..., expert_width:]).astype(BF)
    back = lax.all_to_all(
        jnp.einsum("secf,efd->secd", hidden, down, preferred_element_type=F32).astype(BF),
        axes,
        split_axis=0,
        concat_axis=0,
        tiled=True,
    )
    back_rows = back.reshape(experts_all * capacity, width)[slot].astype(F32)
    return jnp.sum(
        back_rows.reshape(tok_rows, choose, width) * expert_weights[:, :, None], axis=1
    )


def local(
    stream,
    moe_gain,
    expert_ids,
    expert_weights,
    gate_up_weight,
    down,
    mixer_gain,
    qkv_weight,
    decay_log,
    write_rate,
):
    tok_rows, width = stream.shape
    choose = expert_ids.shape[1]
    seq_count = lax.axis_size("seq")
    devices = seq_count * lax.axis_size("exp")
    experts_all = gate_up_weight.shape[0] * devices
    capacity = max(2, (tok_rows * choose * 6 + experts_all * 5 - 1) // (experts_all * 5))
    normed = rms_scale(stream, moe_gain).astype(BF)
    planes = lax.axis_size("exp") == 4 and seq_count % 4 == 0 and choose <= ROUTE_STEP
    route = route_waves if planes and experts_all <= 256 else route_some
    moe = route(normed, expert_ids, expert_weights, gate_up_weight, down, capacity)
    mixed = (stream.astype(F32) + moe).astype(BF)
    normed_mix = rms_scale(mixed, mixer_gain).astype(BF)
    heads = decay_log.shape[1]
    blocks = decay_log.shape[0] // CH
    sums = jnp.cumsum(decay_log.T.reshape(heads, blocks, CH), axis=-1)
    rates = write_rate.T.reshape(heads, blocks, CH)
    pairs = blocks // 2
    by_pair = lambda values: values.reshape(heads, pairs, 2, CH).transpose(1, 0, 2, 3)
    groups = list(range(heads // head_step(heads)))
    found = ()

    def work(x, place, steps):
        return chunks_of(
            x,
            place.astype(jnp.int32).reshape(1),
            qkv_weight,
            by_pair(sums),
            by_pair(rates),
            found,
            steps,
        )

    if planes:
        core = lax.axis_index("exp") % 2
        side = lax.axis_index("exp") // 2

        def in_order(a, b):
            return jnp.concatenate(
                [jnp.where(core == 0, a, b), jnp.where(core == 0, b, a)], axis=0
            )

        from_y = over_y(normed_mix)
        parts = [(in_order(normed_mix, over_core(normed_mix)), side)]
        found = work(*parts[0], groups[:1])
        from_y, found = lax.optimization_barrier((from_y, found))
        parts.append((in_order(from_y, over_core(from_y)), 1 - side))
        if groups[1:]:
            found = work(*parts[0], groups[1:])
        found = work(*parts[1], groups)
    else:
        gathered = lax.all_gather(normed_mix, "exp", axis=0, tiled=True)
        parts = [(gathered[2 * CH * i : 2 * CH * (i + 1)], jnp.int32(i)) for i in range(pairs)]
        for x, place in parts:
            found = work(x, place, groups)
    key, solved, moved = found
    starts, ends = chain(moved, sums)
    places = jnp.stack([place for _, place in parts]).astype(jnp.int32)
    entering, local_out = read([x for x, _ in parts], places, qkv_weight, key, solved, starts, sums)
    if heads % seq_count == 0:
        dim = ends.shape[2] // 2
        each = heads // seq_count
        held = lax.all_to_all(ends, "seq", split_axis=0, concat_axis=0, tiled=True)
        held = held.reshape(seq_count, each, dim + 16, 2 * dim)
        states = jnp.stack([carry(held[:, i], entering) for i in range(each)], axis=1)
        arriving = lax.all_to_all(
            states.reshape(seq_count * each, dim, dim), "seq", split_axis=0, concat_axis=0, tiled=True
        )
    else:
        arriving = relay(ends, seq_count)
    return (mixed, finish(entering, local_out, arriving))


def solution(mesh):
    in_specs = (
        P(("seq", "exp"), None),
        P(),
        P(("seq", "exp"), None),
        P(("seq", "exp"), None),
        P(("seq", "exp"), None, None),
        P(("seq", "exp"), None, None),
        P(),
        P(None, None, "exp"),
        P("seq", "exp"),
        P("seq", "exp"),
    )
    out_specs = (P(("seq", "exp"), None), P("seq", "exp"))
    return jax.shard_map(local, mesh=mesh, in_specs=in_specs, out_specs=out_specs, check_vma=False)
```

```python
from functools import partial

import jax
import jax.numpy as jnp
from jax import lax
from jax.experimental import pallas as pl
from jax.experimental.pallas import tpu as pltpu
from jax.sharding import PartitionSpec as P

CH = 128
ROUTE_STEP = 16
VMEM_LIMIT = 56 * 1024 * 1024
BF = jnp.bfloat16
F32 = jnp.float32


def rms_scale(values, gain):
    wide = values.astype(F32)
    return wide * lax.rsqrt(jnp.mean(wide * wide, axis=-1, keepdims=True) + 1e-06) * gain


def dot(a, b):
    return jnp.dot(a, b, preferred_element_type=F32)


def split(a):
    high = a.astype(BF)
    return high, (a - high.astype(F32)).astype(BF)


def rough(a, b):
    return dot(a.astype(BF), b.astype(BF))


def left_pair(a):
    high, low = split(a)
    return jnp.concatenate([high, low], axis=1)


def right_pair(b):
    high, low = split(b)
    row = jnp.concatenate([high, low], axis=1)
    return jnp.concatenate([row, row], axis=0)


def wide_product(a, b):
    columns = b.shape[1]
    both = dot(left_pair(a), right_pair(b))
    return both[:, :columns] + both[:, columns:]


def moe_kernel(capacity, choose, cuts, *refs):
    first_ref, *block_refs = refs[:5]
    weight_refs = refs[5:9]
    gate_up_ref, down_ref, rows_ref, back_ref, sem = refs[-5:]
    tok, wide = block_refs[0].shape
    width = rows_ref.shape[2]
    out_refs = refs[-5 - 4 * cuts : -5]
    piece = width // cuts
    experts_here = gate_up_ref.shape[0]
    half = experts_here // 2
    expert_width = down_ref.shape[1]
    pair_rows = rows_ref.shape[1] // 2

    copies = []
    for e in range(experts_here):
        side, at = divmod(e, half)
        fetch_in = pltpu.make_async_copy(
            weight_refs[2 * side].at[at], gate_up_ref.at[e], sem.at[0, e]
        )
        fetch_out = pltpu.make_async_copy(
            weight_refs[2 * side + 1].at[at], down_ref.at[e], sem.at[1, e]
        )
        copies.append((fetch_in, fetch_out))
    for e in range(min(2, experts_here)):
        copies[e][0].start()
        copies[e][1].start()

    matched, weights = [], []
    for block_ref in block_refs:
        routing = block_ref[:, width:].astype(F32).T
        ids = routing[:choose]
        scale = routing[ROUTE_STEP : ROUTE_STEP + choose]
        scale = scale + routing[2 * ROUTE_STEP : 2 * ROUTE_STEP + choose]
        for e in range(experts_here):
            side, at = divmod(e, half)
            hit = ids == (first_ref[side] + at).astype(F32)
            matched.append(jnp.max(jnp.where(hit, 1.0, 0.0), axis=0, keepdims=True))
            weights.append(jnp.sum(jnp.where(hit, scale, 0.0), axis=0, keepdims=True))
    match = jnp.concatenate(matched, axis=0)
    before = lax.broadcasted_iota(jnp.int32, (tok, tok), 0) < lax.broadcasted_iota(
        jnp.int32, (tok, tok), 1
    )
    rank = dot(match.astype(BF), jnp.where(before, 1.0, 0.0).astype(BF))
    rank = jnp.where(match > 0.5, rank, -1e4)
    row_number = lax.broadcasted_iota(jnp.int32, (pair_rows, 2 * tok), 0).astype(F32)
    picks = []
    for pair in range(2):
        x_pair = jnp.concatenate(
            [block_refs[2 * pair][:, :width], block_refs[2 * pair + 1][:, :width]], axis=0
        )
        here = []
        for e in range(experts_here):
            low = 2 * pair * experts_here + e
            high = low + experts_here
            place = jnp.concatenate(
                [rank[low : low + 1], rank[high : high + 1] + float(capacity)], axis=1
            )
            here.append(jnp.where(row_number == place, 1.0, 0.0))
        picks.append(here)
        chosen = dot(jnp.concatenate(here, axis=0).astype(BF), x_pair).astype(BF)
        for e in range(experts_here):
            rows_ref[e, pair * pair_rows : (pair + 1) * pair_rows, :] = chosen[
                e * pair_rows : (e + 1) * pair_rows
            ]
    for e in range(experts_here):
        if e + 2 < experts_here:
            copies[e + 2][0].start()
            copies[e + 2][1].start()
        copies[e][0].wait()
        both = dot(rows_ref[e], gate_up_ref[e])
        gate = both[:, :expert_width]
        hidden = (gate / (1.0 + jnp.exp(-gate)) * both[:, expert_width:]).astype(BF)
        copies[e][1].wait()
        back_ref[e] = dot(hidden, down_ref[e]).astype(BF)
    for pair in range(2):
        scaled, rows = [], []
        for e in range(experts_here):
            low = 2 * pair * experts_here + e
            high = low + experts_here
            weight = jnp.concatenate([weights[low], weights[high]], axis=1)
            scaled.append(picks[pair][e] * weight)
            rows.append(back_ref[e, pair * pair_rows : (pair + 1) * pair_rows, :])
        summed = lax.dot_general(
            jnp.concatenate(scaled, axis=0).astype(BF),
            jnp.concatenate(rows, axis=0),
            (((0,), (0,)), ((), ())),
            preferred_element_type=F32,
        ).astype(BF)
        for cut in range(cuts):
            columns = slice(cut * piece, (cut + 1) * piece)
            out_refs[2 * pair * cuts + cut][...] = summed[:tok, columns]
            out_refs[(2 * pair + 1) * cuts + cut][...] = summed[tok:, columns]


def experts(blocks, first, weights, after, capacity, choose, cuts):
    tok, wide = blocks[0].shape
    gate_up_weight, down = weights[:2]
    local_experts, width, double = gate_up_weight.shape
    here = 2 * local_experts
    pair_rows = -(-2 * capacity // 16) * 16
    whole = pl.BlockSpec(memory_space=pltpu.VMEM)
    return pl.pallas_call(
        partial(moe_kernel, capacity, choose, cuts),
        in_specs=[pl.BlockSpec(memory_space=pltpu.SMEM)]
        + [whole] * 4
        + [pl.BlockSpec(memory_space=pl.ANY)] * (4 + len(after)),
        out_specs=[whole] * (4 * cuts),
        out_shape=[jax.ShapeDtypeStruct((tok, width // cuts), BF)] * (4 * cuts),
        scratch_shapes=[
            pltpu.VMEM((here,) + gate_up_weight.shape[1:], BF),
            pltpu.VMEM((here,) + down.shape[1:], BF),
            pltpu.VMEM((here, 2 * pair_rows, width), BF),
            pltpu.VMEM((here, 2 * pair_rows, width), BF),
            pltpu.SemaphoreType.DMA((2, here)),
        ],
        compiler_params=pltpu.CompilerParams(vmem_limit_bytes=VMEM_LIMIT),
        cost_estimate=pl.CostEstimate(
            flops=here * pair_rows * width * double // 4,
            bytes_accessed=tok * width,
            transcendentals=0,
        ),
        name="experts",
    )(first, *blocks, *weights, *after)


def unit_rows(values):
    return values * lax.rsqrt(jnp.sum(values * values, axis=-1, keepdims=True) + 1e-06)


def tiles():
    rows = lax.broadcasted_iota(jnp.int32, (CH, CH), 0)
    columns = lax.broadcasted_iota(jnp.int32, (CH, CH), 1)
    return rows, columns


def against_rows(a, b):
    high, low = split(b)
    right = jnp.concatenate(
        [jnp.concatenate([high, high], axis=1), jnp.concatenate([low, low], axis=1)], axis=0
    )
    both = lax.dot_general(
        left_pair(a), right, (((1,), (1,)), ((), ())), preferred_element_type=F32
    )
    return both[:, : b.shape[0]] + both[:, b.shape[0] :]


def chunk_kernel(place_ref, x_ref, key_w_ref, value_w_ref, sum_ref, rate_ref, *refs):
    k_ref, solved_ref, moved_ref = refs[-3:]
    heads, chunks, _ = sum_ref.shape[1:]
    dim = key_w_ref.shape[2] // heads
    rows, columns = tiles()
    strict = rows > columns
    identity = jnp.where(rows == columns, 1.0, 0.0)
    x = x_ref[...]
    key = dot(x, key_w_ref[0])
    value = dot(x, value_w_ref[0])
    units = [(h, n) for h in range(heads) for n in range(chunks)]

    def part(values, h, n):
        return values[n * CH : (n + 1) * CH, h * dim : (h + 1) * dim]

    keys, values, lowers, rates, growths, remains = [], [], [], [], [], []
    for h, n in units:
        unit = unit_rows(part(key, h, n))
        k_ref[n * CH : (n + 1) * CH, h * dim : (h + 1) * dim] = unit
        keys.append(unit)
        values.append(part(value, h, n))
    for u, (h, n) in enumerate(units):
        across = jnp.broadcast_to(sum_ref[0, h, n : n + 1, :], (CH, CH))
        along = across.T
        rate = jnp.broadcast_to(rate_ref[0, h, n : n + 1, :], (CH, CH)).T
        last = jnp.broadcast_to(along[CH - 1 : CH, :], (CH, CH))
        fade = jnp.exp(jnp.where(strict, along - across, 0.0))
        rates.append(rate)
        growths.append(jnp.exp(along))
        remains.append(jnp.exp(last - along))
        unit = keys[u].astype(BF)
        met = lax.dot_general(unit, unit, (((1,), (1,)), ((), ())), preferred_element_type=F32)
        lowers.append(jnp.where(strict, rate * fade * met, 0.0))

    def ring(size):
        shared = (rows // (2 * size)) == (columns // (2 * size))
        return shared & (rows // size % 2 == 1) & (columns // size % 2 == 0)

    span = range(len(units))
    inverse = [identity - jnp.where(ring(1), lowers[u], 0.0) for u in span]
    size = 2
    while size < CH and size < 16:
        here = ring(size)
        step = [rough(jnp.where(here, lowers[u], 0.0), inverse[u]) for u in span]
        inverse = [inverse[u] - rough(inverse[u], step[u]) for u in span]
        size *= 2
    while size < CH:
        starts = range(0, CH, 2 * size)

        def odd(values):
            return jnp.concatenate([values[s + size : s + 2 * size] for s in starts], axis=0)

        def woven(even, odds):
            rows_of = []
            for i, s in enumerate(starts):
                rows_of += [even[s : s + size], odds[i * size : (i + 1) * size]]
            return jnp.concatenate(rows_of, axis=0)

        here = odd(jnp.where(ring(size), 1.0, 0.0))
        nothing = jnp.zeros((CH, CH), F32)
        step = [woven(nothing, rough(here * odd(lowers[u]), inverse[u])) for u in span]
        inverse = [
            woven(inverse[u], odd(inverse[u]) - rough(odd(inverse[u]), step[u])) for u in span
        ]
        size *= 2
    wanted = [
        jnp.concatenate([rates[u] * growths[u] * keys[u], rates[u] * values[u]], axis=1)
        for u in span
    ]
    solved = [wanted[u] + rough(inverse[u] - identity, wanted[u]) for u in span]
    for u, (h, n) in enumerate(units):
        solved_ref[h, n] = solved[u]
        moved_ref[h, n] = lax.dot_general(
            (remains[u] * keys[u]).astype(BF),
            solved[u].astype(BF),
            (((0,), (0,)), ((), ())),
            preferred_element_type=F32,
        )


def chunks_of(x, place, qkv_weight, sums, rates, before):
    rows, width = x.shape
    _, _, columns = qkv_weight.shape
    parts, heads, chunks, _ = sums.shape
    dim = columns // heads
    step = min(4, heads)
    at_rows = pl.BlockSpec((rows, step * dim), lambda i, place: (place[0], i))
    at_chunks = pl.BlockSpec((step, chunks, CH, 2 * dim), lambda i, place: (i, place[0], 0, 0))
    per_head = pl.BlockSpec((1, step, chunks, CH), lambda i, place: (place[0], i, 0, 0))
    return pl.pallas_call(
        chunk_kernel,
        grid_spec=pltpu.PrefetchScalarGridSpec(
            num_scalar_prefetch=1,
            grid=(heads // step,),
            in_specs=[
                pl.BlockSpec((rows, width), lambda i, place: (0, 0)),
                pl.BlockSpec((1, width, step * dim), lambda i, place: (1, 0, i)),
                pl.BlockSpec((1, width, step * dim), lambda i, place: (2, 0, i)),
                per_head,
                per_head,
            ]
            + [pl.BlockSpec(memory_space=pl.ANY)] * len(before),
            out_specs=[at_rows, at_chunks, at_chunks],
        ),
        out_shape=[jax.ShapeDtypeStruct((parts * rows, columns), F32)]
        + [jax.ShapeDtypeStruct((heads, parts * chunks, CH, 2 * dim), F32)] * 2,
        input_output_aliases={6 + i: i for i in range(len(before))},
        compiler_params=pltpu.CompilerParams(vmem_limit_bytes=VMEM_LIMIT),
        name="chunks",
    )(place, x, qkv_weight, qkv_weight, sums, rates, *before)


def chain_kernel(moved_ref, sum_ref, starts_ref, end_ref):
    heads, chunks, dim, _ = moved_ref.shape
    rows, columns = tiles()
    identity = jnp.where(rows == columns, 1.0, 0.0)
    span = range(heads)

    def spread(total):
        return jnp.broadcast_to(jnp.exp(total[:, CH - 1 :]), (CH, CH))

    wholes = [[spread(sum_ref[h, n : n + 1, :]) for n in range(chunks)] for h in span]
    state = [
        jnp.concatenate(
            [wholes[h][0] * identity - moved_ref[h, 0, :, :dim], moved_ref[h, 0, :, dim:]], axis=1
        )
        for h in span
    ]
    for n in range(1, chunks):
        for h in span:
            starts_ref[h, n - 1] = state[h]
        removed = [rough(moved_ref[h, n, :, :dim], state[h]) for h in span]
        state = [
            jnp.concatenate(
                [
                    wholes[h][n] * state[h][:, :dim] - removed[h][:, :dim],
                    wholes[h][n] * state[h][:, dim:]
                    - removed[h][:, dim:]
                    + moved_ref[h, n, :, dim:],
                ],
                axis=1,
            )
            for h in span
        ]
    for h in span:
        decay = wholes[h][0]
        for n in range(1, chunks):
            decay = decay * wholes[h][n]
        end_ref[h, :dim, :dim] = (decay * identity - state[h][:, :dim]).astype(BF)
        end_ref[h, :dim, dim:] = state[h][:, dim:].astype(BF)
        end_ref[h, dim:, :] = left_pair(decay[:16])


def chain(moved, sums):
    heads, chunks, dim, double = moved.shape
    step = min(4, heads)
    return pl.pallas_call(
        chain_kernel,
        grid=(heads // step,),
        in_specs=[
            pl.BlockSpec((step, chunks, dim, double), lambda i: (i, 0, 0, 0)),
            pl.BlockSpec((step, chunks, CH), lambda i: (i, 0, 0)),
        ],
        out_specs=[
            pl.BlockSpec((step, chunks - 1, dim, double), lambda i: (i, 0, 0, 0)),
            pl.BlockSpec((step, dim + 16, double), lambda i: (i, 0, 0)),
        ],
        out_shape=[
            jax.ShapeDtypeStruct((heads, chunks - 1, dim, double), F32),
            jax.ShapeDtypeStruct((heads, dim + 16, double), BF),
        ],
        compiler_params=pltpu.CompilerParams(vmem_limit_bytes=VMEM_LIMIT),
        name="chain",
    )(moved, sums)


def read_kernel(place_ref, w_ref, k_ref, solved_ref, starts_ref, sum_ref, *refs):
    x_refs = refs[:-2]
    enter_ref, local_ref = refs[-2:]
    heads, chunks, _ = sum_ref.shape
    dim = starts_ref.shape[2]
    rows, columns = tiles()
    inclusive = rows >= columns
    found = [dot(x_ref[...], w_ref[0]) for x_ref in x_refs]
    queries = []
    for place in range(len(found)):
        query = found[0]
        for i in range(1, len(found)):
            query = jnp.where(place_ref[i] == place, found[i], query)
        queries.append(query)
    each = chunks // len(found)
    units = [(h, n) for h in range(heads) for n in range(chunks)]
    for h, n in units:
        cut = slice(n * CH, (n + 1) * CH), slice(h * dim, (h + 1) * dim)
        across = jnp.broadcast_to(sum_ref[h, n : n + 1, :], (CH, CH))
        along = across.T
        fade = jnp.exp(jnp.where(inclusive, along - across, 0.0))
        query = unit_rows(queries[n // each][n % each * CH : (n % each + 1) * CH, cut[1]])
        masked = jnp.where(inclusive, fade * against_rows(query, k_ref[cut]), 0.0)
        probed = wide_product(masked, solved_ref[h, n])
        entering = jnp.exp(along) * query - probed[:, :dim]
        output = probed[:, dim:]
        if n:
            begun = wide_product(entering, starts_ref[h, n - 1])
            entering = begun[:, :dim]
            output = output + begun[:, dim:]
        enter_ref[cut] = entering.astype(BF)
        local_ref[cut] = output


def read(parts, places, qkv_weight, key, solved, starts, sums):
    length, columns = key.shape
    heads, chunks, _ = sums.shape
    dim = columns // heads
    width = qkv_weight.shape[1]
    step = 2 if heads % 2 == 0 else 1
    per_column = pl.BlockSpec((length, step * dim), lambda h: (0, h))
    four = lambda h: (h, 0, 0, 0)
    return pl.pallas_call(
        read_kernel,
        grid=(heads // step,),
        in_specs=[
            pl.BlockSpec(memory_space=pltpu.SMEM),
            pl.BlockSpec((1, width, step * dim), lambda h: (0, 0, h)),
            per_column,
            pl.BlockSpec((step, chunks, CH, 2 * dim), four),
            pl.BlockSpec((step, chunks - 1, dim, 2 * dim), four),
            pl.BlockSpec((step, chunks, CH), lambda h: (h, 0, 0)),
        ]
        + [pl.BlockSpec(x.shape, lambda h: (0, 0)) for x in parts],
        out_specs=[per_column, per_column],
        out_shape=[
            jax.ShapeDtypeStruct((length, columns), BF),
            jax.ShapeDtypeStruct((length, columns), F32),
        ],
        compiler_params=pltpu.CompilerParams(vmem_limit_bytes=VMEM_LIMIT),
        name="read",
    )(places, qkv_weight, key, solved, starts, sums, *parts)


def carry_kernel(ends_ref, after_ref, states_ref):
    segments, _, double = ends_ref.shape
    dim = double // 2
    state = jnp.zeros((dim, dim), F32)
    for s in range(segments):
        states_ref[s] = state.astype(BF)
        if s < segments - 1:
            decay = ends_ref[s, dim : dim + 1, :].astype(F32)
            decay = decay[:, :dim] + decay[:, dim:]
            removed = dot(ends_ref[s, :dim, :dim], left_pair(state))
            removed = removed[:, :dim] + removed[:, dim:]
            state = decay * state - removed + ends_ref[s, :dim, dim:].astype(F32)


def carry(ends, after):
    segments, _, double = ends.shape
    return pl.pallas_call(
        carry_kernel,
        in_specs=[pl.BlockSpec(memory_space=pltpu.VMEM), pl.BlockSpec(memory_space=pl.ANY)],
        out_shape=jax.ShapeDtypeStruct((segments, double // 2, double // 2), BF),
        compiler_params=pltpu.CompilerParams(vmem_limit_bytes=VMEM_LIMIT),
        name="carry",
    )(ends, after)


def finish_kernel(enter_ref, local_ref, state_ref, core_ref):
    heads, dim, _ = state_ref.shape
    for h in range(heads):
        cut = slice(h * dim, (h + 1) * dim)
        core_ref[:, cut] = local_ref[:, cut] + dot(enter_ref[:, cut], state_ref[h])


def finish(entering, local_out, states):
    length, columns = entering.shape
    heads, dim, _ = states.shape
    step = 2 if heads % 2 == 0 else 1
    per_column = pl.BlockSpec((length, step * dim), lambda h: (0, h))
    return pl.pallas_call(
        finish_kernel,
        grid=(heads // step,),
        in_specs=[per_column, per_column, pl.BlockSpec((step, dim, dim), lambda h: (h, 0, 0))],
        out_specs=per_column,
        out_shape=jax.ShapeDtypeStruct((length, columns), F32),
        compiler_params=pltpu.CompilerParams(vmem_limit_bytes=VMEM_LIMIT),
        name="finish",
    )(entering, local_out, states)


def relay(ends, seq_count):
    dim = ends.shape[2] // 2
    pairs = [(i, i + 1) for i in range(seq_count - 1)]
    removed, written = ends[:, :dim, :dim].astype(F32), ends[:, :dim, dim:].astype(F32)
    decay = ends[:, dim, :1].astype(F32) + ends[:, dim, dim : dim + 1].astype(F32)

    def step(_, incoming):
        outgoing = decay[:, :, None] * incoming + written
        outgoing = outgoing - jnp.einsum(
            "hij,hjk->hik", removed, incoming, precision=lax.Precision.HIGHEST
        )
        return lax.ppermute(outgoing, "seq", pairs)

    return lax.fori_loop(0, seq_count - 1, step, jnp.zeros_like(written)).astype(BF)


def move(values, change):
    exp_count = lax.axis_size("exp")
    pairs = []
    for s in range(lax.axis_size("seq")):
        for e in range(exp_count):
            to_s, to_e = change(s, e)
            pairs.append((s * exp_count + e, to_s * exp_count + to_e))
    return lax.ppermute(values, ("seq", "exp"), pairs)


def over_x(values):
    return move(values, lambda s, e: (s ^ 1, e))


def over_y(values):
    return move(values, lambda s, e: (s, e ^ 2))


def over_core(values):
    return move(values, lambda s, e: (s, e ^ 1))


def along_z(values, by):
    count = lax.axis_size("seq")
    return move(values, lambda s, e: ((s + 2 * by) % count, e))


def added(*terms):
    total = terms[0].astype(F32)
    for term in terms[1:]:
        total = total + term.astype(F32)
    return total


def route_waves(normed, expert_ids, expert_weights, gate_up_weight, down, capacity):
    tok_rows, width = normed.shape
    choose = expert_ids.shape[1]
    local_experts = gate_up_weight.shape[0]
    me = lax.axis_index("seq") * lax.axis_size("exp") + lax.axis_index("exp")
    first = (jnp.stack([me, me ^ 1]) * local_experts).astype(jnp.int32)
    gap = jnp.zeros((tok_rows, ROUTE_STEP - choose), BF)
    high, low = split(expert_weights)
    tail = jnp.zeros((tok_rows, 128 - 3 * ROUTE_STEP), BF)
    block = jnp.concatenate(
        [normed, expert_ids.astype(BF), gap, high, gap, low, gap, tail], axis=1
    )
    weights = (gate_up_weight, down, over_core(gate_up_weight), over_core(down))
    count = lax.axis_size("seq") // 2
    order = list(range(1, count)) + [0]
    first_way = [over_y if wave == 1 else over_x for wave in range(count)]
    second_way = [over_x if wave == 1 else over_y for wave in range(count)]
    block = [block]
    for wave in range(1, count):
        block.append(along_z(block[-1], 1))
    by_one = [first_way[wave](block[wave]) for wave in range(count)]
    by_two = [second_way[wave](block[wave]) for wave in range(count)]
    diagonal = {wave: second_way[wave](by_one[wave]) for wave in (0, 1)}
    for wave in range(2, count):
        diagonal[wave] = along_z(diagonal[wave - 1], 1)
    due = [() for _ in range(count + 3)]
    for call, wave in enumerate(order):
        if call and wave:
            due[call - 1] += (block[wave],)
        if call > 1:
            due[call - 1 if wave else 0] += (by_one[wave], by_two[wave])
    running = sum_below = None
    for call, wave in enumerate(order):
        cuts = 1
        found = experts(
            (block[wave], by_one[wave], by_two[wave], diagonal[wave]),
            first,
            weights,
            due[call],
            capacity,
            choose,
            cuts,
        )
        one, two = first_way[wave], second_way[wave]
        due[call + 1] += (found[0],)
        below = None if sum_below is None else jnp.split(sum_below, cuts, axis=1)
        sum_below = None
        if running is not None and len(running) < cuts:
            running = jnp.split(running[0], cuts, axis=1)
        pieces = []
        for cut in range(cuts):
            own, sum_one, sum_two, sum_both = found[cut::cuts]
            if below is not None:
                sum_both = added(sum_both, below[cut]).astype(BF)
            if 0 < wave < count - 1:
                sum_below = along_z(sum_both, 1)
                due[call + 2] += (sum_below,)
            else:
                sum_one = added(sum_one, two(sum_both)).astype(BF)
            from_two = two(sum_two)
            from_one = one(sum_one)
            due[call + 2] += (from_two, from_one)
            if pieces:
                from_one, _ = lax.optimization_barrier((from_one, pieces[-1]))
            here = added(own, from_two, from_one)
            if running is not None:
                here = added(here, running[cut])
            pieces.append(here.astype(BF) if wave else here)
        if wave:
            running = [along_z(piece, 1) for piece in pieces]
    return jnp.concatenate(pieces, axis=1)


def route_some(normed, expert_ids, expert_weights, gate_up_weight, down, capacity):
    axes = ("seq", "exp")
    tok_rows, width = normed.shape
    choose = expert_ids.shape[1]
    local_experts = gate_up_weight.shape[0]
    expert_width = down.shape[1]
    devices = lax.axis_size("seq") * lax.axis_size("exp")
    experts_all = local_experts * devices
    flat_ids = expert_ids.reshape(-1)
    onehot = (flat_ids[:, None] == jnp.arange(experts_all, dtype=jnp.int32)[None, :]).astype(
        jnp.int32
    )
    rank = jnp.sum(jnp.cumsum(onehot, axis=0) * onehot, axis=1) - 1
    slot = flat_ids * capacity + rank
    token_of = jnp.arange(tok_rows * choose, dtype=jnp.int32) // choose
    send = jnp.zeros((experts_all * capacity, width), BF).at[slot].set(normed[token_of])
    both = jnp.einsum(
        "secd,edf->secf",
        lax.all_to_all(
            send.reshape(devices, local_experts, capacity, width),
            axes,
            split_axis=0,
            concat_axis=0,
            tiled=True,
        ),
        gate_up_weight,
        preferred_element_type=F32,
    )
    hidden = (jax.nn.silu(both[..., :expert_width]) * both[..., expert_width:]).astype(BF)
    back = lax.all_to_all(
        jnp.einsum("secf,efd->secd", hidden, down, preferred_element_type=F32).astype(BF),
        axes,
        split_axis=0,
        concat_axis=0,
        tiled=True,
    )
    back_rows = back.reshape(experts_all * capacity, width)[slot].astype(F32)
    return jnp.sum(
        back_rows.reshape(tok_rows, choose, width) * expert_weights[:, :, None], axis=1
    )


def local(
    stream,
    moe_gain,
    expert_ids,
    expert_weights,
    gate_up_weight,
    down,
    mixer_gain,
    qkv_weight,
    decay_log,
    write_rate,
):
    tok_rows, width = stream.shape
    choose = expert_ids.shape[1]
    seq_count = lax.axis_size("seq")
    devices = seq_count * lax.axis_size("exp")
    experts_all = gate_up_weight.shape[0] * devices
    capacity = max(2, (tok_rows * choose * 6 + experts_all * 5 - 1) // (experts_all * 5))
    normed = rms_scale(stream, moe_gain).astype(BF)
    planes = lax.axis_size("exp") == 4 and seq_count % 4 == 0 and choose <= ROUTE_STEP
    route = route_waves if planes and experts_all <= 256 else route_some
    moe = route(normed, expert_ids, expert_weights, gate_up_weight, down, capacity)
    mixed = (stream.astype(F32) + moe).astype(BF)
    normed_mix = rms_scale(mixed, mixer_gain).astype(BF)
    heads = decay_log.shape[1]
    blocks = decay_log.shape[0] // CH
    sums = jnp.cumsum(decay_log.T.reshape(heads, blocks, CH), axis=-1)
    rates = write_rate.T.reshape(heads, blocks, CH)
    pairs = blocks // 2
    by_pair = lambda values: values.reshape(heads, pairs, 2, CH).transpose(1, 0, 2, 3)
    if planes:
        core = lax.axis_index("exp") % 2
        side = lax.axis_index("exp") // 2
        from_y = over_y(normed_mix)
        both_sides = [(normed_mix, over_core(normed_mix)), (from_y, over_core(from_y))]
        parts = [
            (
                jnp.concatenate([jnp.where(core == 0, a, b), jnp.where(core == 0, b, a)], axis=0),
                place,
            )
            for (a, b), place in zip(both_sides, (side, 1 - side))
        ]
    else:
        gathered = lax.all_gather(normed_mix, "exp", axis=0, tiled=True)
        parts = [(gathered[2 * CH * i : 2 * CH * (i + 1)], jnp.int32(i)) for i in range(pairs)]
    found = ()
    for x, place in parts:
        found = chunks_of(
            x,
            place.astype(jnp.int32).reshape(1),
            qkv_weight,
            by_pair(sums),
            by_pair(rates),
            found,
        )
    key, solved, moved = found
    starts, ends = chain(moved, sums)
    places = jnp.stack([place for _, place in parts]).astype(jnp.int32)
    entering, local_out = read([x for x, _ in parts], places, qkv_weight, key, solved, starts, sums)
    if heads % seq_count == 0:
        dim = ends.shape[2] // 2
        each = heads // seq_count
        held = lax.all_to_all(ends, "seq", split_axis=0, concat_axis=0, tiled=True)
        held = held.reshape(seq_count, each, dim + 16, 2 * dim)
        states = jnp.stack([carry(held[:, i], entering) for i in range(each)], axis=1)
        arriving = lax.all_to_all(
            states.reshape(seq_count * each, dim, dim), "seq", split_axis=0, concat_axis=0, tiled=True
        )
    else:
        arriving = relay(ends, seq_count)
    return (mixed, finish(entering, local_out, arriving))


def solution(mesh):
    in_specs = (
        P(("seq", "exp"), None),
        P(),
        P(("seq", "exp"), None),
        P(("seq", "exp"), None),
        P(("seq", "exp"), None, None),
        P(("seq", "exp"), None, None),
        P(),
        P(None, None, "exp"),
        P("seq", "exp"),
        P("seq", "exp"),
    )
    out_specs = (P(("seq", "exp"), None), P("seq", "exp"))
    return jax.shard_map(local, mesh=mesh, in_specs=in_specs, out_specs=out_specs, check_vma=False)
```

```python
from functools import partial

import jax
import jax.numpy as jnp
from jax import lax
from jax.experimental import pallas as pl
from jax.experimental.pallas import tpu as pltpu
from jax.sharding import PartitionSpec as P

CH = 128
ROUTE_STEP = 16
MIB = 1024 * 1024
EXPERT_VMEM = 44 * MIB
CHUNK_VMEM = 28 * MIB
READ_VMEM = 20 * MIB
SMALL_VMEM = 16 * MIB
BF = jnp.bfloat16
F32 = jnp.float32


def rms_scale(values, gain):
    wide = values.astype(F32)
    return wide * lax.rsqrt(jnp.mean(wide * wide, axis=-1, keepdims=True) + 1e-06) * gain


def dot(a, b):
    return jnp.dot(a, b, preferred_element_type=F32)


def split(a):
    high = a.astype(BF)
    return high, (a - high.astype(F32)).astype(BF)


def rough(a, b):
    return dot(a.astype(BF), b.astype(BF))


def left_pair(a):
    high, low = split(a)
    return jnp.concatenate([high, low], axis=1)


def right_pair(b):
    high, low = split(b)
    row = jnp.concatenate([high, low], axis=1)
    return jnp.concatenate([row, row], axis=0)


def wide_product(a, b):
    columns = b.shape[1]
    both = dot(left_pair(a), right_pair(b))
    return both[:, :columns] + both[:, columns:]


def moe_kernel(capacity, choose, cuts, *refs):
    first_ref, *block_refs = refs[:5]
    weight_refs = refs[5:9]
    gate_up_ref, down_ref, rows_ref, back_ref, sem = refs[-5:]
    tok, wide = block_refs[0].shape
    width = rows_ref.shape[2]
    out_refs = refs[-5 - 4 * cuts : -5]
    piece = width // cuts
    experts_here = gate_up_ref.shape[0]
    half = experts_here // 2
    expert_width = down_ref.shape[1]
    pair_rows = rows_ref.shape[1] // 2

    copies = []
    for e in range(experts_here):
        side, at = divmod(e, half)
        fetch_in = pltpu.make_async_copy(
            weight_refs[2 * side].at[at], gate_up_ref.at[e], sem.at[0, e]
        )
        fetch_out = pltpu.make_async_copy(
            weight_refs[2 * side + 1].at[at], down_ref.at[e], sem.at[1, e]
        )
        copies.append((fetch_in, fetch_out))
    for e in range(min(2, experts_here)):
        copies[e][0].start()
        copies[e][1].start()

    matched, weights = [], []
    for block_ref in block_refs:
        routing = block_ref[:, width:].astype(F32).T
        ids = routing[:choose]
        scale = routing[ROUTE_STEP : ROUTE_STEP + choose]
        scale = scale + routing[2 * ROUTE_STEP : 2 * ROUTE_STEP + choose]
        for e in range(experts_here):
            side, at = divmod(e, half)
            hit = ids == (first_ref[side] + at).astype(F32)
            matched.append(jnp.max(jnp.where(hit, 1.0, 0.0), axis=0, keepdims=True))
            weights.append(jnp.sum(jnp.where(hit, scale, 0.0), axis=0, keepdims=True))
    match = jnp.concatenate(matched, axis=0)
    before = lax.broadcasted_iota(jnp.int32, (tok, tok), 0) < lax.broadcasted_iota(
        jnp.int32, (tok, tok), 1
    )
    rank = dot(match.astype(BF), jnp.where(before, 1.0, 0.0).astype(BF))
    rank = jnp.where(match > 0.5, rank, -1e4)
    row_number = lax.broadcasted_iota(jnp.int32, (pair_rows, 2 * tok), 0).astype(F32)
    picks = []
    for pair in range(2):
        x_pair = jnp.concatenate(
            [block_refs[2 * pair][:, :width], block_refs[2 * pair + 1][:, :width]], axis=0
        )
        here = []
        for e in range(experts_here):
            low = 2 * pair * experts_here + e
            high = low + experts_here
            place = jnp.concatenate(
                [rank[low : low + 1], rank[high : high + 1] + float(capacity)], axis=1
            )
            here.append(jnp.where(row_number == place, 1.0, 0.0))
        picks.append(here)
        chosen = dot(jnp.concatenate(here, axis=0).astype(BF), x_pair).astype(BF)
        for e in range(experts_here):
            rows_ref[e, pair * pair_rows : (pair + 1) * pair_rows, :] = chosen[
                e * pair_rows : (e + 1) * pair_rows
            ]
    for e in range(experts_here):
        if e + 2 < experts_here:
            copies[e + 2][0].start()
            copies[e + 2][1].start()
        copies[e][0].wait()
        both = dot(rows_ref[e], gate_up_ref[e])
        gate = both[:, :expert_width]
        hidden = (gate / (1.0 + jnp.exp(-gate)) * both[:, expert_width:]).astype(BF)
        copies[e][1].wait()
        back_ref[e] = dot(hidden, down_ref[e]).astype(BF)
    for pair in range(2):
        scaled, rows = [], []
        for e in range(experts_here):
            low = 2 * pair * experts_here + e
            high = low + experts_here
            weight = jnp.concatenate([weights[low], weights[high]], axis=1)
            scaled.append(picks[pair][e] * weight)
            rows.append(back_ref[e, pair * pair_rows : (pair + 1) * pair_rows, :])
        summed = lax.dot_general(
            jnp.concatenate(scaled, axis=0).astype(BF),
            jnp.concatenate(rows, axis=0),
            (((0,), (0,)), ((), ())),
            preferred_element_type=F32,
        ).astype(BF)
        for cut in range(cuts):
            columns = slice(cut * piece, (cut + 1) * piece)
            out_refs[2 * pair * cuts + cut][...] = summed[:tok, columns]
            out_refs[(2 * pair + 1) * cuts + cut][...] = summed[tok:, columns]


def experts(blocks, first, weights, after, capacity, choose, cuts):
    tok, wide = blocks[0].shape
    gate_up_weight, down = weights[:2]
    local_experts, width, double = gate_up_weight.shape
    here = 2 * local_experts
    pair_rows = -(-2 * capacity // 16) * 16
    whole = pl.BlockSpec(memory_space=pltpu.VMEM)
    return pl.pallas_call(
        partial(moe_kernel, capacity, choose, cuts),
        in_specs=[pl.BlockSpec(memory_space=pltpu.SMEM)]
        + [whole] * 4
        + [pl.BlockSpec(memory_space=pl.ANY)] * (4 + len(after)),
        out_specs=[whole] * (4 * cuts),
        out_shape=[jax.ShapeDtypeStruct((tok, width // cuts), BF)] * (4 * cuts),
        scratch_shapes=[
            pltpu.VMEM((here,) + gate_up_weight.shape[1:], BF),
            pltpu.VMEM((here,) + down.shape[1:], BF),
            pltpu.VMEM((here, 2 * pair_rows, width), BF),
            pltpu.VMEM((here, 2 * pair_rows, width), BF),
            pltpu.SemaphoreType.DMA((2, here)),
        ],
        compiler_params=pltpu.CompilerParams(vmem_limit_bytes=EXPERT_VMEM),
        cost_estimate=pl.CostEstimate(
            flops=here * pair_rows * width * double // 4,
            bytes_accessed=tok * width,
            transcendentals=0,
        ),
        name="experts",
    )(first, *blocks, *weights, *after)


def unit_rows(values):
    return values * lax.rsqrt(jnp.sum(values * values, axis=-1, keepdims=True) + 1e-06)


def tiles():
    rows = lax.broadcasted_iota(jnp.int32, (CH, CH), 0)
    columns = lax.broadcasted_iota(jnp.int32, (CH, CH), 1)
    return rows, columns


def against_rows(a, b):
    high, low = split(b)
    right = jnp.concatenate(
        [jnp.concatenate([high, high], axis=1), jnp.concatenate([low, low], axis=1)], axis=0
    )
    both = lax.dot_general(
        left_pair(a), right, (((1,), (1,)), ((), ())), preferred_element_type=F32
    )
    return both[:, : b.shape[0]] + both[:, b.shape[0] :]


def chunk_kernel(place_ref, x_ref, key_w_ref, value_w_ref, sum_ref, rate_ref, *refs):
    k_ref, solved_ref, moved_ref = refs[-3:]
    heads, chunks, _ = sum_ref.shape[1:]
    dim = key_w_ref.shape[2] // heads
    rows, columns = tiles()
    strict = rows > columns
    identity = jnp.where(rows == columns, 1.0, 0.0)
    x = x_ref[...]
    key = dot(x, key_w_ref[0])
    value = dot(x, value_w_ref[0])
    units = [(h, n) for h in range(heads) for n in range(chunks)]

    def part(values, h, n):
        return values[n * CH : (n + 1) * CH, h * dim : (h + 1) * dim]

    keys, values, lowers, rates, growths, remains = [], [], [], [], [], []
    for h, n in units:
        unit = unit_rows(part(key, h, n))
        k_ref[n * CH : (n + 1) * CH, h * dim : (h + 1) * dim] = unit
        keys.append(unit)
        values.append(part(value, h, n))
    for u, (h, n) in enumerate(units):
        across = jnp.broadcast_to(sum_ref[0, h, n : n + 1, :], (CH, CH))
        along = across.T
        rate = jnp.broadcast_to(rate_ref[0, h, n : n + 1, :], (CH, CH)).T
        last = jnp.broadcast_to(along[CH - 1 : CH, :], (CH, CH))
        fade = jnp.exp(jnp.where(strict, along - across, 0.0))
        rates.append(rate)
        growths.append(jnp.exp(along))
        remains.append(jnp.exp(last - along))
        unit = keys[u].astype(BF)
        met = lax.dot_general(unit, unit, (((1,), (1,)), ((), ())), preferred_element_type=F32)
        lowers.append(jnp.where(strict, rate * fade * met, 0.0))

    def ring(size):
        shared = (rows // (2 * size)) == (columns // (2 * size))
        return shared & (rows // size % 2 == 1) & (columns // size % 2 == 0)

    span = range(len(units))
    inverse = [identity - jnp.where(ring(1), lowers[u], 0.0) for u in span]
    size = 2
    while size < CH and size < 16:
        here = ring(size)
        step = [rough(jnp.where(here, lowers[u], 0.0), inverse[u]) for u in span]
        inverse = [inverse[u] - rough(inverse[u], step[u]) for u in span]
        size *= 2
    while size < CH:
        starts = range(0, CH, 2 * size)

        def odd(values):
            return jnp.concatenate([values[s + size : s + 2 * size] for s in starts], axis=0)

        def woven(even, odds):
            rows_of = []
            for i, s in enumerate(starts):
                rows_of += [even[s : s + size], odds[i * size : (i + 1) * size]]
            return jnp.concatenate(rows_of, axis=0)

        here = odd(jnp.where(ring(size), 1.0, 0.0))
        nothing = jnp.zeros((CH, CH), F32)
        step = [woven(nothing, rough(here * odd(lowers[u]), inverse[u])) for u in span]
        inverse = [
            woven(inverse[u], odd(inverse[u]) - rough(odd(inverse[u]), step[u])) for u in span
        ]
        size *= 2
    wanted = [
        jnp.concatenate([rates[u] * growths[u] * keys[u], rates[u] * values[u]], axis=1)
        for u in span
    ]
    solved = [wanted[u] + rough(inverse[u] - identity, wanted[u]) for u in span]
    for u, (h, n) in enumerate(units):
        solved_ref[h, n] = solved[u]
        moved_ref[h, n] = lax.dot_general(
            (remains[u] * keys[u]).astype(BF),
            solved[u].astype(BF),
            (((0,), (0,)), ((), ())),
            preferred_element_type=F32,
        )


def chunks_of(x, place, qkv_weight, sums, rates, before):
    rows, width = x.shape
    _, _, columns = qkv_weight.shape
    parts, heads, chunks, _ = sums.shape
    dim = columns // heads
    step = min(4, heads)
    at_rows = pl.BlockSpec((rows, step * dim), lambda i, place: (place[0], i))
    at_chunks = pl.BlockSpec((step, chunks, CH, 2 * dim), lambda i, place: (i, place[0], 0, 0))
    per_head = pl.BlockSpec((1, step, chunks, CH), lambda i, place: (place[0], i, 0, 0))
    return pl.pallas_call(
        chunk_kernel,
        grid_spec=pltpu.PrefetchScalarGridSpec(
            num_scalar_prefetch=1,
            grid=(heads // step,),
            in_specs=[
                pl.BlockSpec((rows, width), lambda i, place: (0, 0)),
                pl.BlockSpec((1, width, step * dim), lambda i, place: (1, 0, i)),
                pl.BlockSpec((1, width, step * dim), lambda i, place: (2, 0, i)),
                per_head,
                per_head,
            ]
            + [pl.BlockSpec(memory_space=pl.ANY)] * len(before),
            out_specs=[at_rows, at_chunks, at_chunks],
        ),
        out_shape=[jax.ShapeDtypeStruct((parts * rows, columns), F32)]
        + [jax.ShapeDtypeStruct((heads, parts * chunks, CH, 2 * dim), F32)] * 2,
        input_output_aliases={6 + i: i for i in range(len(before))},
        compiler_params=pltpu.CompilerParams(vmem_limit_bytes=CHUNK_VMEM),
        name="chunks",
    )(place, x, qkv_weight, qkv_weight, sums, rates, *before)


def chain_kernel(moved_ref, sum_ref, starts_ref, end_ref):
    heads, chunks, dim, _ = moved_ref.shape
    rows, columns = tiles()
    identity = jnp.where(rows == columns, 1.0, 0.0)
    span = range(heads)

    def spread(total):
        return jnp.broadcast_to(jnp.exp(total[:, CH - 1 :]), (CH, CH))

    wholes = [[spread(sum_ref[h, n : n + 1, :]) for n in range(chunks)] for h in span]
    state = [
        jnp.concatenate(
            [wholes[h][0] * identity - moved_ref[h, 0, :, :dim], moved_ref[h, 0, :, dim:]], axis=1
        )
        for h in span
    ]
    for n in range(1, chunks):
        for h in span:
            starts_ref[h, n - 1] = state[h]
        removed = [rough(moved_ref[h, n, :, :dim], state[h]) for h in span]
        state = [
            jnp.concatenate(
                [
                    wholes[h][n] * state[h][:, :dim] - removed[h][:, :dim],
                    wholes[h][n] * state[h][:, dim:]
                    - removed[h][:, dim:]
                    + moved_ref[h, n, :, dim:],
                ],
                axis=1,
            )
            for h in span
        ]
    for h in span:
        decay = wholes[h][0]
        for n in range(1, chunks):
            decay = decay * wholes[h][n]
        end_ref[h, :dim, :dim] = (decay * identity - state[h][:, :dim]).astype(BF)
        end_ref[h, :dim, dim:] = state[h][:, dim:].astype(BF)
        end_ref[h, dim:, :] = left_pair(decay[:16])


def chain(moved, sums):
    heads, chunks, dim, double = moved.shape
    step = min(4, heads)
    return pl.pallas_call(
        chain_kernel,
        grid=(heads // step,),
        in_specs=[
            pl.BlockSpec((step, chunks, dim, double), lambda i: (i, 0, 0, 0)),
            pl.BlockSpec((step, chunks, CH), lambda i: (i, 0, 0)),
        ],
        out_specs=[
            pl.BlockSpec((step, chunks - 1, dim, double), lambda i: (i, 0, 0, 0)),
            pl.BlockSpec((step, dim + 16, double), lambda i: (i, 0, 0)),
        ],
        out_shape=[
            jax.ShapeDtypeStruct((heads, chunks - 1, dim, double), F32),
            jax.ShapeDtypeStruct((heads, dim + 16, double), BF),
        ],
        compiler_params=pltpu.CompilerParams(vmem_limit_bytes=SMALL_VMEM),
        name="chain",
    )(moved, sums)


def read_kernel(place_ref, w_ref, k_ref, solved_ref, starts_ref, sum_ref, *refs):
    x_refs = refs[:-2]
    enter_ref, local_ref = refs[-2:]
    heads, chunks, _ = sum_ref.shape
    dim = starts_ref.shape[2]
    rows, columns = tiles()
    inclusive = rows >= columns
    found = [dot(x_ref[...], w_ref[0]) for x_ref in x_refs]
    queries = []
    for place in range(len(found)):
        query = found[0]
        for i in range(1, len(found)):
            query = jnp.where(place_ref[i] == place, found[i], query)
        queries.append(query)
    each = chunks // len(found)
    units = [(h, n) for h in range(heads) for n in range(chunks)]
    for h, n in units:
        cut = slice(n * CH, (n + 1) * CH), slice(h * dim, (h + 1) * dim)
        across = jnp.broadcast_to(sum_ref[h, n : n + 1, :], (CH, CH))
        along = across.T
        fade = jnp.exp(jnp.where(inclusive, along - across, 0.0))
        query = unit_rows(queries[n // each][n % each * CH : (n % each + 1) * CH, cut[1]])
        masked = jnp.where(inclusive, fade * against_rows(query, k_ref[cut]), 0.0)
        probed = wide_product(masked, solved_ref[h, n])
        entering = jnp.exp(along) * query - probed[:, :dim]
        output = probed[:, dim:]
        if n:
            begun = wide_product(entering, starts_ref[h, n - 1])
            entering = begun[:, :dim]
            output = output + begun[:, dim:]
        enter_ref[cut] = entering.astype(BF)
        local_ref[cut] = output


def read(parts, places, qkv_weight, key, solved, starts, sums):
    length, columns = key.shape
    heads, chunks, _ = sums.shape
    dim = columns // heads
    width = qkv_weight.shape[1]
    step = 2 if heads % 2 == 0 else 1
    per_column = pl.BlockSpec((length, step * dim), lambda h: (0, h))
    four = lambda h: (h, 0, 0, 0)
    return pl.pallas_call(
        read_kernel,
        grid=(heads // step,),
        in_specs=[
            pl.BlockSpec(memory_space=pltpu.SMEM),
            pl.BlockSpec((1, width, step * dim), lambda h: (0, 0, h)),
            per_column,
            pl.BlockSpec((step, chunks, CH, 2 * dim), four),
            pl.BlockSpec((step, chunks - 1, dim, 2 * dim), four),
            pl.BlockSpec((step, chunks, CH), lambda h: (h, 0, 0)),
        ]
        + [pl.BlockSpec(x.shape, lambda h: (0, 0)) for x in parts],
        out_specs=[per_column, per_column],
        out_shape=[
            jax.ShapeDtypeStruct((length, columns), BF),
            jax.ShapeDtypeStruct((length, columns), F32),
        ],
        compiler_params=pltpu.CompilerParams(vmem_limit_bytes=READ_VMEM),
        name="read",
    )(places, qkv_weight, key, solved, starts, sums, *parts)


def carry_kernel(ends_ref, after_ref, states_ref):
    segments, _, double = ends_ref.shape
    dim = double // 2
    state = jnp.zeros((dim, dim), F32)
    for s in range(segments):
        states_ref[s] = state.astype(BF)
        if s < segments - 1:
            decay = ends_ref[s, dim : dim + 1, :].astype(F32)
            decay = decay[:, :dim] + decay[:, dim:]
            removed = dot(ends_ref[s, :dim, :dim], left_pair(state))
            removed = removed[:, :dim] + removed[:, dim:]
            state = decay * state - removed + ends_ref[s, :dim, dim:].astype(F32)


def carry(ends, after):
    segments, _, double = ends.shape
    return pl.pallas_call(
        carry_kernel,
        in_specs=[pl.BlockSpec(memory_space=pltpu.VMEM), pl.BlockSpec(memory_space=pl.ANY)],
        out_shape=jax.ShapeDtypeStruct((segments, double // 2, double // 2), BF),
        compiler_params=pltpu.CompilerParams(vmem_limit_bytes=SMALL_VMEM),
        name="carry",
    )(ends, after)


def finish_kernel(enter_ref, local_ref, state_ref, core_ref):
    heads, dim, _ = state_ref.shape
    for h in range(heads):
        cut = slice(h * dim, (h + 1) * dim)
        core_ref[:, cut] = local_ref[:, cut] + dot(enter_ref[:, cut], state_ref[h])


def finish(entering, local_out, states):
    length, columns = entering.shape
    heads, dim, _ = states.shape
    step = 2 if heads % 2 == 0 else 1
    per_column = pl.BlockSpec((length, step * dim), lambda h: (0, h))
    return pl.pallas_call(
        finish_kernel,
        grid=(heads // step,),
        in_specs=[per_column, per_column, pl.BlockSpec((step, dim, dim), lambda h: (h, 0, 0))],
        out_specs=per_column,
        out_shape=jax.ShapeDtypeStruct((length, columns), F32),
        compiler_params=pltpu.CompilerParams(vmem_limit_bytes=SMALL_VMEM),
        name="finish",
    )(entering, local_out, states)


def relay(ends, seq_count):
    dim = ends.shape[2] // 2
    pairs = [(i, i + 1) for i in range(seq_count - 1)]
    removed, written = ends[:, :dim, :dim].astype(F32), ends[:, :dim, dim:].astype(F32)
    decay = ends[:, dim, :1].astype(F32) + ends[:, dim, dim : dim + 1].astype(F32)

    def step(_, incoming):
        outgoing = decay[:, :, None] * incoming + written
        outgoing = outgoing - jnp.einsum(
            "hij,hjk->hik", removed, incoming, precision=lax.Precision.HIGHEST
        )
        return lax.ppermute(outgoing, "seq", pairs)

    return lax.fori_loop(0, seq_count - 1, step, jnp.zeros_like(written)).astype(BF)


def move(values, change):
    exp_count = lax.axis_size("exp")
    pairs = []
    for s in range(lax.axis_size("seq")):
        for e in range(exp_count):
            to_s, to_e = change(s, e)
            pairs.append((s * exp_count + e, to_s * exp_count + to_e))
    return lax.ppermute(values, ("seq", "exp"), pairs)


def over_x(values):
    return move(values, lambda s, e: (s ^ 1, e))


def over_y(values):
    return move(values, lambda s, e: (s, e ^ 2))


def over_core(values):
    return move(values, lambda s, e: (s, e ^ 1))


def along_z(values, by):
    count = lax.axis_size("seq")
    return move(values, lambda s, e: ((s + 2 * by) % count, e))


def added(*terms):
    total = terms[0].astype(F32)
    for term in terms[1:]:
        total = total + term.astype(F32)
    return total


def route_waves(normed, expert_ids, expert_weights, gate_up_weight, down, capacity):
    tok_rows, width = normed.shape
    choose = expert_ids.shape[1]
    local_experts = gate_up_weight.shape[0]
    me = lax.axis_index("seq") * lax.axis_size("exp") + lax.axis_index("exp")
    first = (jnp.stack([me, me ^ 1]) * local_experts).astype(jnp.int32)
    gap = jnp.zeros((tok_rows, ROUTE_STEP - choose), BF)
    high, low = split(expert_weights)
    tail = jnp.zeros((tok_rows, 128 - 3 * ROUTE_STEP), BF)
    block = jnp.concatenate(
        [normed, expert_ids.astype(BF), gap, high, gap, low, gap, tail], axis=1
    )
    weights = (gate_up_weight, down, over_core(gate_up_weight), over_core(down))
    count = lax.axis_size("seq") // 2
    order = list(range(1, count)) + [0]
    first_way = [over_y if wave == 1 else over_x for wave in range(count)]
    second_way = [over_x if wave == 1 else over_y for wave in range(count)]
    block = [block]
    for wave in range(1, count):
        block.append(along_z(block[-1], 1))
    by_one = [first_way[wave](block[wave]) for wave in range(count)]
    by_two = [second_way[wave](block[wave]) for wave in range(count)]
    diagonal = {wave: second_way[wave](by_one[wave]) for wave in (0, 1)}
    for wave in range(2, count):
        diagonal[wave] = along_z(diagonal[wave - 1], 1)
    due = [() for _ in range(count + 3)]
    for call, wave in enumerate(order):
        if call and wave:
            due[call - 1] += (block[wave],)
        if call > 1:
            due[call - 1 if wave else 0] += (by_one[wave], by_two[wave])
    running = sum_below = None
    for call, wave in enumerate(order):
        cuts = 1
        found = experts(
            (block[wave], by_one[wave], by_two[wave], diagonal[wave]),
            first,
            weights,
            due[call],
            capacity,
            choose,
            cuts,
        )
        one, two = first_way[wave], second_way[wave]
        due[call + 1] += (found[0],)
        below = None if sum_below is None else jnp.split(sum_below, cuts, axis=1)
        sum_below = None
        if running is not None and len(running) < cuts:
            running = jnp.split(running[0], cuts, axis=1)
        pieces = []
        for cut in range(cuts):
            own, sum_one, sum_two, sum_both = found[cut::cuts]
            if below is not None:
                sum_both = added(sum_both, below[cut]).astype(BF)
            if 0 < wave < count - 1:
                sum_below = along_z(sum_both, 1)
                due[call + 2] += (sum_below,)
            else:
                sum_one = added(sum_one, two(sum_both)).astype(BF)
            from_two = two(sum_two)
            from_one = one(sum_one)
            due[call + 2] += (from_two, from_one)
            if pieces:
                from_one, _ = lax.optimization_barrier((from_one, pieces[-1]))
            here = added(own, from_two, from_one)
            if running is not None:
                here = added(here, running[cut])
            pieces.append(here.astype(BF) if wave else here)
        if wave:
            running = [along_z(piece, 1) for piece in pieces]
    return jnp.concatenate(pieces, axis=1)


def route_some(normed, expert_ids, expert_weights, gate_up_weight, down, capacity):
    axes = ("seq", "exp")
    tok_rows, width = normed.shape
    choose = expert_ids.shape[1]
    local_experts = gate_up_weight.shape[0]
    expert_width = down.shape[1]
    devices = lax.axis_size("seq") * lax.axis_size("exp")
    experts_all = local_experts * devices
    flat_ids = expert_ids.reshape(-1)
    onehot = (flat_ids[:, None] == jnp.arange(experts_all, dtype=jnp.int32)[None, :]).astype(
        jnp.int32
    )
    rank = jnp.sum(jnp.cumsum(onehot, axis=0) * onehot, axis=1) - 1
    slot = flat_ids * capacity + rank
    token_of = jnp.arange(tok_rows * choose, dtype=jnp.int32) // choose
    send = jnp.zeros((experts_all * capacity, width), BF).at[slot].set(normed[token_of])
    both = jnp.einsum(
        "secd,edf->secf",
        lax.all_to_all(
            send.reshape(devices, local_experts, capacity, width),
            axes,
            split_axis=0,
            concat_axis=0,
            tiled=True,
        ),
        gate_up_weight,
        preferred_element_type=F32,
    )
    hidden = (jax.nn.silu(both[..., :expert_width]) * both[..., expert_width:]).astype(BF)
    back = lax.all_to_all(
        jnp.einsum("secf,efd->secd", hidden, down, preferred_element_type=F32).astype(BF),
        axes,
        split_axis=0,
        concat_axis=0,
        tiled=True,
    )
    back_rows = back.reshape(experts_all * capacity, width)[slot].astype(F32)
    return jnp.sum(
        back_rows.reshape(tok_rows, choose, width) * expert_weights[:, :, None], axis=1
    )


def local(
    stream,
    moe_gain,
    expert_ids,
    expert_weights,
    gate_up_weight,
    down,
    mixer_gain,
    qkv_weight,
    decay_log,
    write_rate,
):
    tok_rows, width = stream.shape
    choose = expert_ids.shape[1]
    seq_count = lax.axis_size("seq")
    devices = seq_count * lax.axis_size("exp")
    experts_all = gate_up_weight.shape[0] * devices
    capacity = max(2, (tok_rows * choose * 6 + experts_all * 5 - 1) // (experts_all * 5))
    normed = rms_scale(stream, moe_gain).astype(BF)
    planes = lax.axis_size("exp") == 4 and seq_count % 4 == 0 and choose <= ROUTE_STEP
    route = route_waves if planes and experts_all <= 256 else route_some
    moe = route(normed, expert_ids, expert_weights, gate_up_weight, down, capacity)
    mixed = (stream.astype(F32) + moe).astype(BF)
    normed_mix = rms_scale(mixed, mixer_gain).astype(BF)
    heads = decay_log.shape[1]
    blocks = decay_log.shape[0] // CH
    sums = jnp.cumsum(decay_log.T.reshape(heads, blocks, CH), axis=-1)
    rates = write_rate.T.reshape(heads, blocks, CH)
    pairs = blocks // 2
    by_pair = lambda values: values.reshape(heads, pairs, 2, CH).transpose(1, 0, 2, 3)
    if planes:
        core = lax.axis_index("exp") % 2
        side = lax.axis_index("exp") // 2
        from_y = over_y(normed_mix)
        both_sides = [(normed_mix, over_core(normed_mix)), (from_y, over_core(from_y))]
        parts = [
            (
                jnp.concatenate([jnp.where(core == 0, a, b), jnp.where(core == 0, b, a)], axis=0),
                place,
            )
            for (a, b), place in zip(both_sides, (side, 1 - side))
        ]
    else:
        gathered = lax.all_gather(normed_mix, "exp", axis=0, tiled=True)
        parts = [(gathered[2 * CH * i : 2 * CH * (i + 1)], jnp.int32(i)) for i in range(pairs)]
    found = ()
    for x, place in parts:
        found = chunks_of(
            x,
            place.astype(jnp.int32).reshape(1),
            qkv_weight,
            by_pair(sums),
            by_pair(rates),
            found,
        )
    key, solved, moved = found
    starts, ends = chain(moved, sums)
    places = jnp.stack([place for _, place in parts]).astype(jnp.int32)
    entering, local_out = read([x for x, _ in parts], places, qkv_weight, key, solved, starts, sums)
    if heads % seq_count == 0:
        dim = ends.shape[2] // 2
        each = heads // seq_count
        held = lax.all_to_all(ends, "seq", split_axis=0, concat_axis=0, tiled=True)
        held = held.reshape(seq_count, each, dim + 16, 2 * dim)
        states = jnp.stack([carry(held[:, i], entering) for i in range(each)], axis=1)
        arriving = lax.all_to_all(
            states.reshape(seq_count * each, dim, dim), "seq", split_axis=0, concat_axis=0, tiled=True
        )
    else:
        arriving = relay(ends, seq_count)
    return (mixed, finish(entering, local_out, arriving))


def solution(mesh):
    in_specs = (
        P(("seq", "exp"), None),
        P(),
        P(("seq", "exp"), None),
        P(("seq", "exp"), None),
        P(("seq", "exp"), None, None),
        P(("seq", "exp"), None, None),
        P(),
        P(None, None, "exp"),
        P("seq", "exp"),
        P("seq", "exp"),
    )
    out_specs = (P(("seq", "exp"), None), P("seq", "exp"))
    return jax.shard_map(local, mesh=mesh, in_specs=in_specs, out_specs=out_specs, check_vma=False)
```

```python
from functools import partial

import jax
import jax.numpy as jnp
from jax import lax
from jax.experimental import pallas as pl
from jax.experimental.pallas import tpu as pltpu
from jax.sharding import PartitionSpec as P

CH = 128
ROUTE_STEP = 16
MIB = 1024 * 1024
VMEM_LIMIT = 56 * MIB
READ_VMEM = 44 * MIB
SMALL_VMEM = 16 * MIB
BF = jnp.bfloat16
F32 = jnp.float32


def rms_scale(values, gain):
    wide = values.astype(F32)
    return wide * lax.rsqrt(jnp.mean(wide * wide, axis=-1, keepdims=True) + 1e-06) * gain


def dot(a, b):
    return jnp.dot(a, b, preferred_element_type=F32)


def split(a):
    high = a.astype(BF)
    return high, (a - high.astype(F32)).astype(BF)


def rough(a, b):
    return dot(a.astype(BF), b.astype(BF))


def left_pair(a):
    high, low = split(a)
    return jnp.concatenate([high, low], axis=1)


def right_pair(b):
    high, low = split(b)
    row = jnp.concatenate([high, low], axis=1)
    return jnp.concatenate([row, row], axis=0)


def wide_product(a, b):
    columns = b.shape[1]
    both = dot(left_pair(a), right_pair(b))
    return both[:, :columns] + both[:, columns:]


def moe_kernel(capacity, choose, cuts, *refs):
    first_ref, *block_refs = refs[:5]
    weight_refs = refs[5:9]
    gate_up_ref, down_ref, rows_ref, back_ref, sem = refs[-5:]
    tok, wide = block_refs[0].shape
    width = rows_ref.shape[2]
    out_refs = refs[-5 - 4 * cuts : -5]
    piece = width // cuts
    experts_here = gate_up_ref.shape[0]
    half = experts_here // 2
    expert_width = down_ref.shape[1]
    pair_rows = rows_ref.shape[1] // 2

    copies = []
    for e in range(experts_here):
        side, at = divmod(e, half)
        fetch_in = pltpu.make_async_copy(
            weight_refs[2 * side].at[at], gate_up_ref.at[e], sem.at[0, e]
        )
        fetch_out = pltpu.make_async_copy(
            weight_refs[2 * side + 1].at[at], down_ref.at[e], sem.at[1, e]
        )
        copies.append((fetch_in, fetch_out))
    for e in range(min(2, experts_here)):
        copies[e][0].start()
        copies[e][1].start()

    matched, weights = [], []
    for block_ref in block_refs:
        routing = block_ref[:, width:].astype(F32).T
        ids = routing[:choose]
        scale = routing[ROUTE_STEP : ROUTE_STEP + choose]
        scale = scale + routing[2 * ROUTE_STEP : 2 * ROUTE_STEP + choose]
        for e in range(experts_here):
            side, at = divmod(e, half)
            hit = ids == (first_ref[side] + at).astype(F32)
            matched.append(jnp.max(jnp.where(hit, 1.0, 0.0), axis=0, keepdims=True))
            weights.append(jnp.sum(jnp.where(hit, scale, 0.0), axis=0, keepdims=True))
    match = jnp.concatenate(matched, axis=0)
    before = lax.broadcasted_iota(jnp.int32, (tok, tok), 0) < lax.broadcasted_iota(
        jnp.int32, (tok, tok), 1
    )
    rank = dot(match.astype(BF), jnp.where(before, 1.0, 0.0).astype(BF))
    rank = jnp.where(match > 0.5, rank, -1e4)
    row_number = lax.broadcasted_iota(jnp.int32, (pair_rows, 2 * tok), 0).astype(F32)
    picks = []
    for pair in range(2):
        x_pair = jnp.concatenate(
            [block_refs[2 * pair][:, :width], block_refs[2 * pair + 1][:, :width]], axis=0
        )
        here = []
        for e in range(experts_here):
            low = 2 * pair * experts_here + e
            high = low + experts_here
            place = jnp.concatenate(
                [rank[low : low + 1], rank[high : high + 1] + float(capacity)], axis=1
            )
            here.append(jnp.where(row_number == place, 1.0, 0.0))
        picks.append(here)
        chosen = dot(jnp.concatenate(here, axis=0).astype(BF), x_pair).astype(BF)
        for e in range(experts_here):
            rows_ref[e, pair * pair_rows : (pair + 1) * pair_rows, :] = chosen[
                e * pair_rows : (e + 1) * pair_rows
            ]
    for e in range(experts_here):
        if e + 2 < experts_here:
            copies[e + 2][0].start()
            copies[e + 2][1].start()
        copies[e][0].wait()
        both = dot(rows_ref[e], gate_up_ref[e])
        gate = both[:, :expert_width]
        hidden = (gate / (1.0 + jnp.exp(-gate)) * both[:, expert_width:]).astype(BF)
        copies[e][1].wait()
        back_ref[e] = dot(hidden, down_ref[e]).astype(BF)
    for pair in range(2):
        scaled, rows = [], []
        for e in range(experts_here):
            low = 2 * pair * experts_here + e
            high = low + experts_here
            weight = jnp.concatenate([weights[low], weights[high]], axis=1)
            scaled.append(picks[pair][e] * weight)
            rows.append(back_ref[e, pair * pair_rows : (pair + 1) * pair_rows, :])
        summed = lax.dot_general(
            jnp.concatenate(scaled, axis=0).astype(BF),
            jnp.concatenate(rows, axis=0),
            (((0,), (0,)), ((), ())),
            preferred_element_type=F32,
        ).astype(BF)
        for cut in range(cuts):
            columns = slice(cut * piece, (cut + 1) * piece)
            out_refs[2 * pair * cuts + cut][...] = summed[:tok, columns]
            out_refs[(2 * pair + 1) * cuts + cut][...] = summed[tok:, columns]


def experts(blocks, first, weights, after, capacity, choose, cuts):
    tok, wide = blocks[0].shape
    gate_up_weight, down = weights[:2]
    local_experts, width, double = gate_up_weight.shape
    here = 2 * local_experts
    pair_rows = -(-2 * capacity // 16) * 16
    whole = pl.BlockSpec(memory_space=pltpu.VMEM)
    return pl.pallas_call(
        partial(moe_kernel, capacity, choose, cuts),
        in_specs=[pl.BlockSpec(memory_space=pltpu.SMEM)]
        + [whole] * 4
        + [pl.BlockSpec(memory_space=pl.ANY)] * (4 + len(after)),
        out_specs=[whole] * (4 * cuts),
        out_shape=[jax.ShapeDtypeStruct((tok, width // cuts), BF)] * (4 * cuts),
        scratch_shapes=[
            pltpu.VMEM((here,) + gate_up_weight.shape[1:], BF),
            pltpu.VMEM((here,) + down.shape[1:], BF),
            pltpu.VMEM((here, 2 * pair_rows, width), BF),
            pltpu.VMEM((here, 2 * pair_rows, width), BF),
            pltpu.SemaphoreType.DMA((2, here)),
        ],
        compiler_params=pltpu.CompilerParams(vmem_limit_bytes=VMEM_LIMIT),
        cost_estimate=pl.CostEstimate(
            flops=here * pair_rows * width * double // 4,
            bytes_accessed=tok * width,
            transcendentals=0,
        ),
        name="experts",
    )(first, *blocks, *weights, *after)


def unit_rows(values):
    return values * lax.rsqrt(jnp.sum(values * values, axis=-1, keepdims=True) + 1e-06)


def tiles():
    rows = lax.broadcasted_iota(jnp.int32, (CH, CH), 0)
    columns = lax.broadcasted_iota(jnp.int32, (CH, CH), 1)
    return rows, columns


def against_rows(a, b):
    high, low = split(b)
    right = jnp.concatenate(
        [jnp.concatenate([high, high], axis=1), jnp.concatenate([low, low], axis=1)], axis=0
    )
    both = lax.dot_general(
        left_pair(a), right, (((1,), (1,)), ((), ())), preferred_element_type=F32
    )
    return both[:, : b.shape[0]] + both[:, b.shape[0] :]


def chunk_kernel(place_ref, x_ref, key_w_ref, value_w_ref, sum_ref, rate_ref, *refs):
    k_ref, solved_ref, moved_ref = refs[-3:]
    heads, chunks, _ = sum_ref.shape[1:]
    dim = key_w_ref.shape[2] // heads
    rows, columns = tiles()
    strict = rows > columns
    identity = jnp.where(rows == columns, 1.0, 0.0)
    x = x_ref[...]
    key = dot(x, key_w_ref[0])
    value = dot(x, value_w_ref[0])
    units = [(h, n) for h in range(heads) for n in range(chunks)]

    def part(values, h, n):
        return values[n * CH : (n + 1) * CH, h * dim : (h + 1) * dim]

    keys, values, lowers, rates, growths, remains = [], [], [], [], [], []
    for h, n in units:
        unit = unit_rows(part(key, h, n))
        k_ref[n * CH : (n + 1) * CH, h * dim : (h + 1) * dim] = unit
        keys.append(unit)
        values.append(part(value, h, n))
    for u, (h, n) in enumerate(units):
        across = jnp.broadcast_to(sum_ref[0, h, n : n + 1, :], (CH, CH))
        along = across.T
        rate = jnp.broadcast_to(rate_ref[0, h, n : n + 1, :], (CH, CH)).T
        last = jnp.broadcast_to(along[CH - 1 : CH, :], (CH, CH))
        fade = jnp.exp(jnp.where(strict, along - across, 0.0))
        rates.append(rate)
        growths.append(jnp.exp(along))
        remains.append(jnp.exp(last - along))
        unit = keys[u].astype(BF)
        met = lax.dot_general(unit, unit, (((1,), (1,)), ((), ())), preferred_element_type=F32)
        lowers.append(jnp.where(strict, rate * fade * met, 0.0))

    def ring(size):
        shared = (rows // (2 * size)) == (columns // (2 * size))
        return shared & (rows // size % 2 == 1) & (columns // size % 2 == 0)

    span = range(len(units))
    inverse = [identity - jnp.where(ring(1), lowers[u], 0.0) for u in span]
    size = 2
    while size < CH and size < 16:
        here = ring(size)
        step = [rough(jnp.where(here, lowers[u], 0.0), inverse[u]) for u in span]
        inverse = [inverse[u] - rough(inverse[u], step[u]) for u in span]
        size *= 2
    while size < CH:
        starts = range(0, CH, 2 * size)

        def odd(values):
            return jnp.concatenate([values[s + size : s + 2 * size] for s in starts], axis=0)

        def woven(even, odds):
            rows_of = []
            for i, s in enumerate(starts):
                rows_of += [even[s : s + size], odds[i * size : (i + 1) * size]]
            return jnp.concatenate(rows_of, axis=0)

        here = odd(jnp.where(ring(size), 1.0, 0.0))
        nothing = jnp.zeros((CH, CH), F32)
        step = [woven(nothing, rough(here * odd(lowers[u]), inverse[u])) for u in span]
        inverse = [
            woven(inverse[u], odd(inverse[u]) - rough(odd(inverse[u]), step[u])) for u in span
        ]
        size *= 2
    wanted = [
        jnp.concatenate([rates[u] * growths[u] * keys[u], rates[u] * values[u]], axis=1)
        for u in span
    ]
    solved = [wanted[u] + rough(inverse[u] - identity, wanted[u]) for u in span]
    for u, (h, n) in enumerate(units):
        solved_ref[h, n] = solved[u]
        moved_ref[h, n] = lax.dot_general(
            (remains[u] * keys[u]).astype(BF),
            solved[u].astype(BF),
            (((0,), (0,)), ((), ())),
            preferred_element_type=F32,
        )


def chunks_of(x, place, qkv_weight, sums, rates, before):
    rows, width = x.shape
    _, _, columns = qkv_weight.shape
    parts, heads, chunks, _ = sums.shape
    dim = columns // heads
    step = min(4, heads)
    at_rows = pl.BlockSpec((rows, step * dim), lambda i, place: (place[0], i))
    at_chunks = pl.BlockSpec((step, chunks, CH, 2 * dim), lambda i, place: (i, place[0], 0, 0))
    per_head = pl.BlockSpec((1, step, chunks, CH), lambda i, place: (place[0], i, 0, 0))
    return pl.pallas_call(
        chunk_kernel,
        grid_spec=pltpu.PrefetchScalarGridSpec(
            num_scalar_prefetch=1,
            grid=(heads // step,),
            in_specs=[
                pl.BlockSpec((rows, width), lambda i, place: (0, 0)),
                pl.BlockSpec((1, width, step * dim), lambda i, place: (1, 0, i)),
                pl.BlockSpec((1, width, step * dim), lambda i, place: (2, 0, i)),
                per_head,
                per_head,
            ]
            + [pl.BlockSpec(memory_space=pl.ANY)] * len(before),
            out_specs=[at_rows, at_chunks, at_chunks],
        ),
        out_shape=[jax.ShapeDtypeStruct((parts * rows, columns), F32)]
        + [jax.ShapeDtypeStruct((heads, parts * chunks, CH, 2 * dim), F32)] * 2,
        input_output_aliases={6 + i: i for i in range(len(before))},
        compiler_params=pltpu.CompilerParams(vmem_limit_bytes=VMEM_LIMIT),
        name="chunks",
    )(place, x, qkv_weight, qkv_weight, sums, rates, *before)


def chain_kernel(moved_ref, sum_ref, starts_ref, end_ref):
    heads, chunks, dim, _ = moved_ref.shape
    rows, columns = tiles()
    identity = jnp.where(rows == columns, 1.0, 0.0)
    span = range(heads)

    def spread(total):
        return jnp.broadcast_to(jnp.exp(total[:, CH - 1 :]), (CH, CH))

    wholes = [[spread(sum_ref[h, n : n + 1, :]) for n in range(chunks)] for h in span]
    state = [
        jnp.concatenate(
            [wholes[h][0] * identity - moved_ref[h, 0, :, :dim], moved_ref[h, 0, :, dim:]], axis=1
        )
        for h in span
    ]
    for n in range(1, chunks):
        for h in span:
            starts_ref[h, n - 1] = state[h]
        removed = [rough(moved_ref[h, n, :, :dim], state[h]) for h in span]
        state = [
            jnp.concatenate(
                [
                    wholes[h][n] * state[h][:, :dim] - removed[h][:, :dim],
                    wholes[h][n] * state[h][:, dim:]
                    - removed[h][:, dim:]
                    + moved_ref[h, n, :, dim:],
                ],
                axis=1,
            )
            for h in span
        ]
    for h in span:
        decay = wholes[h][0]
        for n in range(1, chunks):
            decay = decay * wholes[h][n]
        end_ref[h, :dim, :dim] = (decay * identity - state[h][:, :dim]).astype(BF)
        end_ref[h, :dim, dim:] = state[h][:, dim:].astype(BF)
        end_ref[h, dim:, :] = left_pair(decay[:16])


def chain(moved, sums):
    heads, chunks, dim, double = moved.shape
    step = min(4, heads)
    return pl.pallas_call(
        chain_kernel,
        grid=(heads // step,),
        in_specs=[
            pl.BlockSpec((step, chunks, dim, double), lambda i: (i, 0, 0, 0)),
            pl.BlockSpec((step, chunks, CH), lambda i: (i, 0, 0)),
        ],
        out_specs=[
            pl.BlockSpec((step, chunks - 1, dim, double), lambda i: (i, 0, 0, 0)),
            pl.BlockSpec((step, dim + 16, double), lambda i: (i, 0, 0)),
        ],
        out_shape=[
            jax.ShapeDtypeStruct((heads, chunks - 1, dim, double), F32),
            jax.ShapeDtypeStruct((heads, dim + 16, double), BF),
        ],
        compiler_params=pltpu.CompilerParams(vmem_limit_bytes=VMEM_LIMIT),
        name="chain",
    )(moved, sums)


def read_kernel(place_ref, w_ref, k_ref, solved_ref, starts_ref, sum_ref, *refs):
    x_refs = refs[:-2]
    enter_ref, local_ref = refs[-2:]
    heads, chunks, _ = sum_ref.shape
    dim = starts_ref.shape[2]
    rows, columns = tiles()
    inclusive = rows >= columns
    found = [dot(x_ref[...], w_ref[0]) for x_ref in x_refs]
    queries = []
    for place in range(len(found)):
        query = found[0]
        for i in range(1, len(found)):
            query = jnp.where(place_ref[i] == place, found[i], query)
        queries.append(query)
    each = chunks // len(found)
    units = [(h, n) for h in range(heads) for n in range(chunks)]
    for h, n in units:
        cut = slice(n * CH, (n + 1) * CH), slice(h * dim, (h + 1) * dim)
        across = jnp.broadcast_to(sum_ref[h, n : n + 1, :], (CH, CH))
        along = across.T
        fade = jnp.exp(jnp.where(inclusive, along - across, 0.0))
        query = unit_rows(queries[n // each][n % each * CH : (n % each + 1) * CH, cut[1]])
        masked = jnp.where(inclusive, fade * against_rows(query, k_ref[cut]), 0.0)
        probed = wide_product(masked, solved_ref[h, n])
        entering = jnp.exp(along) * query - probed[:, :dim]
        output = probed[:, dim:]
        if n:
            begun = wide_product(entering, starts_ref[h, n - 1])
            entering = begun[:, :dim]
            output = output + begun[:, dim:]
        enter_ref[cut] = entering.astype(BF)
        local_ref[cut] = output


def read(parts, places, qkv_weight, key, solved, starts, sums):
    length, columns = key.shape
    heads, chunks, _ = sums.shape
    dim = columns // heads
    width = qkv_weight.shape[1]
    step = 2 if heads % 2 == 0 else 1
    per_column = pl.BlockSpec((length, step * dim), lambda h: (0, h))
    four = lambda h: (h, 0, 0, 0)
    return pl.pallas_call(
        read_kernel,
        grid=(heads // step,),
        in_specs=[
            pl.BlockSpec(memory_space=pltpu.SMEM),
            pl.BlockSpec((1, width, step * dim), lambda h: (0, 0, h)),
            per_column,
            pl.BlockSpec((step, chunks, CH, 2 * dim), four),
            pl.BlockSpec((step, chunks - 1, dim, 2 * dim), four),
            pl.BlockSpec((step, chunks, CH), lambda h: (h, 0, 0)),
        ]
        + [pl.BlockSpec(x.shape, lambda h: (0, 0)) for x in parts],
        out_specs=[per_column, per_column],
        out_shape=[
            jax.ShapeDtypeStruct((length, columns), BF),
            jax.ShapeDtypeStruct((length, columns), F32),
        ],
        compiler_params=pltpu.CompilerParams(vmem_limit_bytes=READ_VMEM),
        name="read",
    )(places, qkv_weight, key, solved, starts, sums, *parts)


def carry_kernel(ends_ref, after_ref, states_ref):
    segments, _, double = ends_ref.shape
    dim = double // 2
    state = jnp.zeros((dim, dim), F32)
    for s in range(segments):
        states_ref[s] = state.astype(BF)
        if s < segments - 1:
            decay = ends_ref[s, dim : dim + 1, :].astype(F32)
            decay = decay[:, :dim] + decay[:, dim:]
            removed = dot(ends_ref[s, :dim, :dim], left_pair(state))
            removed = removed[:, :dim] + removed[:, dim:]
            state = decay * state - removed + ends_ref[s, :dim, dim:].astype(F32)


def carry(ends, after):
    segments, _, double = ends.shape
    return pl.pallas_call(
        carry_kernel,
        in_specs=[pl.BlockSpec(memory_space=pltpu.VMEM), pl.BlockSpec(memory_space=pl.ANY)],
        out_shape=jax.ShapeDtypeStruct((segments, double // 2, double // 2), BF),
        compiler_params=pltpu.CompilerParams(vmem_limit_bytes=SMALL_VMEM),
        name="carry",
    )(ends, after)


def finish_kernel(enter_ref, local_ref, state_ref, core_ref):
    heads, dim, _ = state_ref.shape
    for h in range(heads):
        cut = slice(h * dim, (h + 1) * dim)
        core_ref[:, cut] = local_ref[:, cut] + dot(enter_ref[:, cut], state_ref[h])


def finish(entering, local_out, states):
    length, columns = entering.shape
    heads, dim, _ = states.shape
    step = 2 if heads % 2 == 0 else 1
    per_column = pl.BlockSpec((length, step * dim), lambda h: (0, h))
    return pl.pallas_call(
        finish_kernel,
        grid=(heads // step,),
        in_specs=[per_column, per_column, pl.BlockSpec((step, dim, dim), lambda h: (h, 0, 0))],
        out_specs=per_column,
        out_shape=jax.ShapeDtypeStruct((length, columns), F32),
        compiler_params=pltpu.CompilerParams(vmem_limit_bytes=SMALL_VMEM),
        name="finish",
    )(entering, local_out, states)


def relay(ends, seq_count):
    dim = ends.shape[2] // 2
    pairs = [(i, i + 1) for i in range(seq_count - 1)]
    removed, written = ends[:, :dim, :dim].astype(F32), ends[:, :dim, dim:].astype(F32)
    decay = ends[:, dim, :1].astype(F32) + ends[:, dim, dim : dim + 1].astype(F32)

    def step(_, incoming):
        outgoing = decay[:, :, None] * incoming + written
        outgoing = outgoing - jnp.einsum(
            "hij,hjk->hik", removed, incoming, precision=lax.Precision.HIGHEST
        )
        return lax.ppermute(outgoing, "seq", pairs)

    return lax.fori_loop(0, seq_count - 1, step, jnp.zeros_like(written)).astype(BF)


def move(values, change):
    exp_count = lax.axis_size("exp")
    pairs = []
    for s in range(lax.axis_size("seq")):
        for e in range(exp_count):
            to_s, to_e = change(s, e)
            pairs.append((s * exp_count + e, to_s * exp_count + to_e))
    return lax.ppermute(values, ("seq", "exp"), pairs)


def over_x(values):
    return move(values, lambda s, e: (s ^ 1, e))


def over_y(values):
    return move(values, lambda s, e: (s, e ^ 2))


def over_core(values):
    return move(values, lambda s, e: (s, e ^ 1))


def along_z(values, by):
    count = lax.axis_size("seq")
    return move(values, lambda s, e: ((s + 2 * by) % count, e))


def added(*terms):
    total = terms[0].astype(F32)
    for term in terms[1:]:
        total = total + term.astype(F32)
    return total


def route_waves(normed, expert_ids, expert_weights, gate_up_weight, down, capacity):
    tok_rows, width = normed.shape
    choose = expert_ids.shape[1]
    local_experts = gate_up_weight.shape[0]
    me = lax.axis_index("seq") * lax.axis_size("exp") + lax.axis_index("exp")
    first = (jnp.stack([me, me ^ 1]) * local_experts).astype(jnp.int32)
    gap = jnp.zeros((tok_rows, ROUTE_STEP - choose), BF)
    high, low = split(expert_weights)
    tail = jnp.zeros((tok_rows, 128 - 3 * ROUTE_STEP), BF)
    block = jnp.concatenate(
        [normed, expert_ids.astype(BF), gap, high, gap, low, gap, tail], axis=1
    )
    weights = (gate_up_weight, down, over_core(gate_up_weight), over_core(down))
    count = lax.axis_size("seq") // 2
    order = list(range(1, count)) + [0]
    first_way = [over_y if wave == 1 else over_x for wave in range(count)]
    second_way = [over_x if wave == 1 else over_y for wave in range(count)]
    block = [block]
    for wave in range(1, count):
        block.append(along_z(block[-1], 1))
    by_one = [first_way[wave](block[wave]) for wave in range(count)]
    by_two = [second_way[wave](block[wave]) for wave in range(count)]
    diagonal = {wave: second_way[wave](by_one[wave]) for wave in (0, 1)}
    for wave in range(2, count):
        diagonal[wave] = along_z(diagonal[wave - 1], 1)
    due = [() for _ in range(count + 3)]
    for call, wave in enumerate(order):
        if call and wave:
            due[call - 1] += (block[wave],)
        if call > 1:
            due[call - 1 if wave else 0] += (by_one[wave], by_two[wave])
    running = sum_below = None
    for call, wave in enumerate(order):
        cuts = 1
        found = experts(
            (block[wave], by_one[wave], by_two[wave], diagonal[wave]),
            first,
            weights,
            due[call],
            capacity,
            choose,
            cuts,
        )
        one, two = first_way[wave], second_way[wave]
        due[call + 1] += (found[0],)
        below = None if sum_below is None else jnp.split(sum_below, cuts, axis=1)
        sum_below = None
        if running is not None and len(running) < cuts:
            running = jnp.split(running[0], cuts, axis=1)
        pieces = []
        for cut in range(cuts):
            own, sum_one, sum_two, sum_both = found[cut::cuts]
            if below is not None:
                sum_both = added(sum_both, below[cut]).astype(BF)
            if 0 < wave < count - 1:
                sum_below = along_z(sum_both, 1)
                due[call + 2] += (sum_below,)
            else:
                sum_one = added(sum_one, two(sum_both)).astype(BF)
            from_two = two(sum_two)
            from_one = one(sum_one)
            due[call + 2] += (from_two, from_one)
            if pieces:
                from_one, _ = lax.optimization_barrier((from_one, pieces[-1]))
            here = added(own, from_two, from_one)
            if running is not None:
                here = added(here, running[cut])
            pieces.append(here.astype(BF) if wave else here)
        if wave:
            running = [along_z(piece, 1) for piece in pieces]
    return jnp.concatenate(pieces, axis=1)


def route_some(normed, expert_ids, expert_weights, gate_up_weight, down, capacity):
    axes = ("seq", "exp")
    tok_rows, width = normed.shape
    choose = expert_ids.shape[1]
    local_experts = gate_up_weight.shape[0]
    expert_width = down.shape[1]
    devices = lax.axis_size("seq") * lax.axis_size("exp")
    experts_all = local_experts * devices
    flat_ids = expert_ids.reshape(-1)
    onehot = (flat_ids[:, None] == jnp.arange(experts_all, dtype=jnp.int32)[None, :]).astype(
        jnp.int32
    )
    rank = jnp.sum(jnp.cumsum(onehot, axis=0) * onehot, axis=1) - 1
    slot = flat_ids * capacity + rank
    token_of = jnp.arange(tok_rows * choose, dtype=jnp.int32) // choose
    send = jnp.zeros((experts_all * capacity, width), BF).at[slot].set(normed[token_of])
    both = jnp.einsum(
        "secd,edf->secf",
        lax.all_to_all(
            send.reshape(devices, local_experts, capacity, width),
            axes,
            split_axis=0,
            concat_axis=0,
            tiled=True,
        ),
        gate_up_weight,
        preferred_element_type=F32,
    )
    hidden = (jax.nn.silu(both[..., :expert_width]) * both[..., expert_width:]).astype(BF)
    back = lax.all_to_all(
        jnp.einsum("secf,efd->secd", hidden, down, preferred_element_type=F32).astype(BF),
        axes,
        split_axis=0,
        concat_axis=0,
        tiled=True,
    )
    back_rows = back.reshape(experts_all * capacity, width)[slot].astype(F32)
    return jnp.sum(
        back_rows.reshape(tok_rows, choose, width) * expert_weights[:, :, None], axis=1
    )


def local(
    stream,
    moe_gain,
    expert_ids,
    expert_weights,
    gate_up_weight,
    down,
    mixer_gain,
    qkv_weight,
    decay_log,
    write_rate,
):
    tok_rows, width = stream.shape
    choose = expert_ids.shape[1]
    seq_count = lax.axis_size("seq")
    devices = seq_count * lax.axis_size("exp")
    experts_all = gate_up_weight.shape[0] * devices
    capacity = max(2, (tok_rows * choose * 6 + experts_all * 5 - 1) // (experts_all * 5))
    normed = rms_scale(stream, moe_gain).astype(BF)
    planes = lax.axis_size("exp") == 4 and seq_count % 4 == 0 and choose <= ROUTE_STEP
    route = route_waves if planes and experts_all <= 256 else route_some
    moe = route(normed, expert_ids, expert_weights, gate_up_weight, down, capacity)
    mixed = (stream.astype(F32) + moe).astype(BF)
    normed_mix = rms_scale(mixed, mixer_gain).astype(BF)
    heads = decay_log.shape[1]
    blocks = decay_log.shape[0] // CH
    sums = jnp.cumsum(decay_log.T.reshape(heads, blocks, CH), axis=-1)
    rates = write_rate.T.reshape(heads, blocks, CH)
    pairs = blocks // 2
    by_pair = lambda values: values.reshape(heads, pairs, 2, CH).transpose(1, 0, 2, 3)
    if planes:
        core = lax.axis_index("exp") % 2
        side = lax.axis_index("exp") // 2
        from_y = over_y(normed_mix)
        both_sides = [(normed_mix, over_core(normed_mix)), (from_y, over_core(from_y))]
        parts = [
            (
                jnp.concatenate([jnp.where(core == 0, a, b), jnp.where(core == 0, b, a)], axis=0),
                place,
            )
            for (a, b), place in zip(both_sides, (side, 1 - side))
        ]
    else:
        gathered = lax.all_gather(normed_mix, "exp", axis=0, tiled=True)
        parts = [(gathered[2 * CH * i : 2 * CH * (i + 1)], jnp.int32(i)) for i in range(pairs)]
    found = ()
    for x, place in parts:
        found = chunks_of(
            x,
            place.astype(jnp.int32).reshape(1),
            qkv_weight,
            by_pair(sums),
            by_pair(rates),
            found,
        )
    key, solved, moved = found
    starts, ends = chain(moved, sums)
    places = jnp.stack([place for _, place in parts]).astype(jnp.int32)
    entering, local_out = read([x for x, _ in parts], places, qkv_weight, key, solved, starts, sums)
    if heads % seq_count == 0:
        dim = ends.shape[2] // 2
        each = heads // seq_count
        held = lax.all_to_all(ends, "seq", split_axis=0, concat_axis=0, tiled=True)
        held = held.reshape(seq_count, each, dim + 16, 2 * dim)
        states = jnp.stack([carry(held[:, i], entering) for i in range(each)], axis=1)
        arriving = lax.all_to_all(
            states.reshape(seq_count * each, dim, dim), "seq", split_axis=0, concat_axis=0, tiled=True
        )
    else:
        arriving = relay(ends, seq_count)
    return (mixed, finish(entering, local_out, arriving))


def solution(mesh):
    in_specs = (
        P(("seq", "exp"), None),
        P(),
        P(("seq", "exp"), None),
        P(("seq", "exp"), None),
        P(("seq", "exp"), None, None),
        P(("seq", "exp"), None, None),
        P(),
        P(None, None, "exp"),
        P("seq", "exp"),
        P("seq", "exp"),
    )
    out_specs = (P(("seq", "exp"), None), P("seq", "exp"))
    return jax.shard_map(local, mesh=mesh, in_specs=in_specs, out_specs=out_specs, check_vma=False)
```
